32 devices in a mesh: dp: 8 (over y, x, core), tensor: 4 (over z).
Axes of the slice: x: 2, y: 2, z: 4, core: 2. Of those that a mesh axis runs over, the one named last changes fastest.
Arguments:
- tokens: bfloat16 [16384, 1024], P(('dp', 'tensor')), may hold values from -6 to 6
- group_bucket: int32 [8], P('dp'), may hold values from 0 to 1
- gain_one: float32 [1024], replicated, may hold values from 0.25 to 1.75
- shift_one: float32 [1024], replicated, may hold values from -3 to 3
- w_qkv: bfloat16 [1024, 3, 1024], P(None, None, 'tensor'), may hold values from -0.1875 to 0.1875
- w_out: bfloat16 [1024, 1024], P('tensor'), may hold values from -6 to 6
- gain_two: float32 [1024], replicated, may hold values from 0.25 to 1.75
- shift_two: float32 [1024], replicated, may hold values from -3 to 3
- w_gate_up: bfloat16 [1024, 2, 4096], P(None, None, 'tensor'), may hold values from -0.1875 to 0.1875
- w_down: bfloat16 [4096, 1024], P('tensor'), may hold values from -0.1875 to 0.1875
- cotangent: bfloat16 [16384, 1024], P(('dp', 'tensor')), may hold values from -6 to 6
Outputs:
- layer_out: bfloat16 [16384, 1024], P(('dp', 'tensor'))
- token_grad: float32 [16384, 1024], P(('dp', 'tensor'))
- gain_one_grad: float32 [1024], replicated
- shift_one_grad: float32 [1024], replicated
- qkv_grad: float32 [1024, 3, 1024], P(None, None, 'tensor')
- out_grad: float32 [1024, 1024], P('tensor')
- gain_two_grad: float32 [1024], replicated
- shift_two_grad: float32 [1024], replicated
- gate_up_grad: float32 [1024, 2, 4096], P(None, None, 'tensor')
- down_grad: float32 [4096, 1024], P('tensor')
The draws below stay inside these ranges and needn't reach their ends.
Inputs may be any that keep to these rules, and one draw needn't show every extreme that they name: `group_bucket`: 1 makes all windows of the group 2048 tokens long; 0 makes them 1000 tokens long, the rest of the group's rows one more window.
All inputs are finite; a program needn't handle non-finite values.
Results may differ from the reference program's by a relative error of at most 0.023.
Values may be sent and summed in bfloat16 or wider, within the bound.
A program may use at most 192 MiB of HBM per device.

```python
import jax
import jax.numpy as jnp
from jax import lax

D = 1024
HEADS = 16
FF = 4096
HEAD_DIM = 64
LONG_LEN = 2048
SHORT_LEN = 1000
TOK_GROUP = 2048
TOKENS = 16384
N_DP = 8
N_TENSOR = 4


def set_ends(values, key, least, top_value):
    longest = values.shape.index(max(values.shape))
    spots = []
    for shift in (0, 1):
        where = [jax.random.randint(jax.random.fold_in(key, axis), (), 0, length) for axis, length in enumerate(values.shape)]
        where[longest] = (where[longest] + shift) % values.shape[longest]
        spots.append(tuple(where))
    return values.at[spots[0]].set(least).at[spots[1]].set(top_value)


def shard_levels(own_key, extent, pieces, smallest, top_value):
    level, own = 1.0, jax.random.fold_in(own_key, 6)
    for axis_at, shards_of in pieces:
        draws = jnp.exp(jax.random.uniform(jax.random.fold_in(own, axis_at), (shards_of,), jnp.float32, smallest / len(pieces), top_value / len(pieces)))
        level = level * jnp.repeat(draws, extent[axis_at] // shards_of).reshape([-1 if axis == axis_at else 1 for axis in range(len(extent))])
    return level


def bell_draw(rng, shape, width, bound, pieces=(), kind=jnp.bfloat16):
    values = width * jax.random.normal(rng, shape, jnp.float32)
    if pieces:
        values = values * shard_levels(rng, shape, pieces, -0.22, 0.18)
    return jnp.clip(values, -bound, bound).astype(kind)


def setup_inputs(seed: int = 0) -> dict:
    key_of = jax.random.split(jax.random.key(seed), 12)
    return {
        "tokens": bell_draw(key_of[0], (TOKENS, D), 1.0, 6.0, ((0, 32),)),
        "group_bucket": set_ends(jax.random.randint(key_of[1], (N_DP,), 0, 2), jax.random.fold_in(key_of[1], 1), 0, 1).astype(jnp.int32),
        "gain_one": jnp.clip(1.0 + 0.15 * jax.random.normal(key_of[2], (D,), jnp.float32), 0.25, 1.75),
        "shift_one": bell_draw(key_of[3], (D,), 0.5, 3.0, (), jnp.float32),
        "w_qkv": bell_draw(key_of[4], (D, 3, D), D ** -0.5, 0.1875, ((2, 4),)),
        "w_out": bell_draw(key_of[5], (D, D), (max(1, D // LONG_LEN)) ** -0.5, 6.0, ((0, 4),)),
        "gain_two": jnp.clip(1.0 + 0.15 * jax.random.normal(key_of[6], (D,), jnp.float32), 0.25, 1.75),
        "shift_two": bell_draw(key_of[7], (D,), 0.5, 3.0, (), jnp.float32),
        "w_gate_up": bell_draw(key_of[8], (D, 2, FF), D ** -0.5, 0.1875, ((2, 4),)),
        "w_down": bell_draw(key_of[9], (FF, D), (FF // 4) ** -0.5, 0.1875, ((0, 4),)),
        "cotangent": bell_draw(key_of[10], (TOKENS, D), 1.0, 6.0, ((0, 32),)),
    }


@jax.custom_vjp
def low(v):
    return lax.optimization_barrier(v.astype(jnp.bfloat16)).astype(jnp.float32)

@jax.custom_vjp
def low_back(v):
    return v

def low_keep(v):
    return (low(v), None)

def low_pass(kept, grad):
    return (grad,)

def back_keep(v):
    return (v, None)

def back_low(kept, grad):
    return (low(grad),)
low.defvjp(low_keep, low_pass)
low_back.defvjp(back_keep, back_low)
norm_eps = 1e-05
mask_fill = -1e+30
rope_base = 10000.0
highest = lax.Precision.HIGHEST

def layout(bucket_id):
    positions = jnp.arange(TOK_GROUP, dtype=jnp.int32)
    span_len = jnp.where(bucket_id == 1, LONG_LEN, SHORT_LEN).astype(jnp.int32)
    window_ids = positions // span_len
    return (window_ids, positions - window_ids * span_len)

def rotary_tables(places):
    half_dim = HEAD_DIM // 2
    exponents = jnp.arange(half_dim, dtype=jnp.float32) * (-2.0 / HEAD_DIM)
    freqs = jnp.exp(exponents * jnp.log(jnp.float32(rope_base)))
    angles = places.astype(jnp.float32)[:, None] * freqs[None, :]
    return (jnp.cos(angles), jnp.sin(angles))

def rotate(vectors, cos_table, sine_table):
    half_dim = vectors.shape[-1] // 2
    first, second = (vectors[..., :half_dim], vectors[..., half_dim:])
    cos_rows = cos_table[:, None, :]
    sine_rows = sine_table[:, None, :]
    return jnp.concatenate([first * cos_rows - second * sine_rows, second * cos_rows + first * sine_rows], axis=-1)

def layer_norm(values, gain, shift):
    average = lax.optimization_barrier(jnp.mean(values, axis=-1, keepdims=True))
    centred = values - average
    spread_sq = lax.optimization_barrier(jnp.mean(centred * centred, axis=-1, keepdims=True))
    return centred * lax.rsqrt(spread_sq + norm_eps) * gain + shift

def attend_rows(query_block, window_block, key_rows, value_rows, window_ids):
    scores = jnp.einsum('qhd,khd->hqk', query_block, key_rows, precision=highest) * HEAD_DIM ** (-0.5)
    scores = low_back(scores)
    same_window = window_block[None, :, None] == window_ids[None, None, :]
    scores = jnp.where(same_window, scores, mask_fill)
    row_max = lax.optimization_barrier(jnp.max(scores, axis=-1, keepdims=True))
    weights = jnp.exp(scores - row_max)
    probs = low(weights / lax.optimization_barrier(jnp.sum(weights, axis=-1, keepdims=True)))
    return jnp.einsum('hqk,khd->qhd', probs, value_rows, precision=highest)

def blocked_sum(values, weights, block_width):
    parts = jnp.einsum('snw,nwd->nsd', values.reshape(TOK_GROUP, N_TENSOR, block_width), weights.reshape(N_TENSOR, block_width, D), precision=highest)
    return lax.optimization_barrier(jnp.sum(low(parts), axis=0))

def copies_of(values):
    return low_back(jnp.broadcast_to(values[None], (N_TENSOR, TOK_GROUP, D)))

def group_forward(rows_in, gain_one, shift_one, w_qkv, w_out, gain_two, shift_two, w_gate_up, w_down, bucket_id):
    window_ids, places = layout(bucket_id)
    cos_table, sine_table = rotary_tables(places)
    feat_block = D // N_TENSOR
    unit_block = FF // N_TENSOR
    normed_one = low(layer_norm(rows_in, gain_one, shift_one))
    mixed = jnp.einsum('nsd,dcnw->scnw', copies_of(normed_one), w_qkv.reshape(D, 3, N_TENSOR, feat_block), precision=highest)
    mixed = low_back(mixed.reshape(TOK_GROUP, 3 * D))
    mixed = mixed.reshape(TOK_GROUP, 3, HEADS, HEAD_DIM)
    queries = low(rotate(mixed[:, 0], cos_table, sine_table))
    key_rows = low(rotate(mixed[:, 1], cos_table, sine_table))
    value_rows = low(mixed[:, 2])
    block_rows = min(512, TOK_GROUP)
    block_count = TOK_GROUP // block_rows

    def one_block(inputs):
        return attend_rows(inputs[0], inputs[1], key_rows, value_rows, window_ids)
    attended = lax.map(jax.checkpoint(one_block), (queries.reshape(block_count, block_rows, HEADS, HEAD_DIM), window_ids.reshape(block_count, block_rows)))
    attended = low_back(low(attended.reshape(TOK_GROUP, D)))
    attn_out = low_back(blocked_sum(attended, w_out, feat_block))
    resid = rows_in + attn_out
    normed_two = low(layer_norm(resid, gain_two, shift_two))
    both = jnp.einsum('nsd,dcnf->scnf', copies_of(normed_two), w_gate_up.reshape(D, 2, N_TENSOR, unit_block), precision=highest).reshape(TOK_GROUP, 2, FF)
    gate_vals = low_back(both[:, 0])
    up_vals = low_back(both[:, 1])
    hidden = low(jax.nn.silu(gate_vals) * up_vals)
    ffn_out = low_back(blocked_sum(hidden, w_down, unit_block))
    return resid + ffn_out

def reference(tokens, group_bucket, gain_one, shift_one, w_qkv, w_out, gain_two, shift_two, w_gate_up, w_down, cotangent):
    params = tuple((p.astype(jnp.float32) for p in (gain_one, shift_one, w_qkv, w_out, gain_two, shift_two, w_gate_up, w_down)))
    group_rows = tokens.astype(jnp.float32).reshape(N_DP, TOK_GROUP, D)
    group_cots = cotangent.astype(jnp.float32).reshape(N_DP, TOK_GROUP, D)

    def one_group(totals, inputs):
        rows_in, cot_rows, bucket_id = inputs

        def forward(rows_arg, *param_args):
            return group_forward(rows_arg, *param_args, bucket_id)
        result, pull_back = jax.vjp(forward, rows_in, *params)
        grads = pull_back(cot_rows)
        new_totals = tuple((a + b for a, b in zip(totals, grads[1:])))
        return (new_totals, (result.astype(jnp.bfloat16), grads[0]))
    zeros = tuple((jnp.zeros_like(p) for p in params))
    totals, (outputs, token_grads) = lax.scan(one_group, zeros, (group_rows, group_cots, group_bucket))
    layer_out = outputs.reshape(TOKENS, D)
    token_grad = token_grads.reshape(TOKENS, D)
    return (layer_out, token_grad, totals[0], totals[1], totals[2], totals[3], totals[4], totals[5], totals[6], totals[7])
```

```python
import functools

import jax
import jax.numpy as jnp
from jax import lax
from jax.experimental import pallas as pl
from jax.experimental.pallas import tpu as pltpu
from jax.sharding import PartitionSpec as P

HEADS = 16
LONG_LEN = 2048
SHORT_LEN = 1000

norm_eps = 1e-05
mask_fill = -1e30
rope_base = 10000.0
MIB = 2**20
F32 = jnp.float32
BF16 = jnp.bfloat16


def dot_nn(a, b):
    return jnp.dot(a, b, preferred_element_type=F32)


def dot_nt(a, b):
    return lax.dot_general(a, b, (((1,), (1,)), ((), ())), preferred_element_type=F32)


def dot_tn(a, b):
    return lax.dot_general(a, b, (((0,), (0,)), ((), ())), preferred_element_type=F32)


def rotary_wide(bucket_id, group_rows, head_dim, width):
    positions = jnp.arange(group_rows, dtype=jnp.int32)
    span_len = jnp.where(bucket_id == 1, LONG_LEN, SHORT_LEN).astype(jnp.int32)
    places = positions - (positions // span_len) * span_len
    half_dim = head_dim // 2
    exponents = jnp.arange(half_dim, dtype=F32) * (-2.0 / head_dim)
    freqs = jnp.exp(exponents * jnp.log(F32(rope_base)))
    angles = places.astype(F32)[:, None] * freqs[None, :]
    cos_table, sine_table = jnp.cos(angles), jnp.sin(angles)
    heads = width // head_dim
    cos_wide = jnp.tile(jnp.concatenate([cos_table, cos_table], axis=1), (1, heads))
    sine_wide = jnp.tile(jnp.concatenate([-sine_table, sine_table], axis=1), (1, heads))
    return cos_wide, sine_wide


def norm_forward(values, gain, shift):
    average = jnp.mean(values, axis=-1, keepdims=True)
    centred = values - average
    spread_sq = jnp.mean(centred * centred, axis=-1, keepdims=True)
    inv_root = lax.rsqrt(spread_sq + norm_eps)
    unit_rows = centred * inv_root
    return (unit_rows * gain + shift, unit_rows, inv_root)


def norm_backward(out_grad_rows, unit_rows, inv_root, gain):
    scaled = out_grad_rows * gain
    first_mean = jnp.mean(scaled, axis=-1, keepdims=True)
    second_mean = jnp.mean(scaled * unit_rows, axis=-1, keepdims=True)
    in_grad = inv_root * (scaled - first_mean - unit_rows * second_mean)
    return (in_grad, jnp.sum(out_grad_rows * unit_rows, axis=0), jnp.sum(out_grad_rows, axis=0))


def swap_halves(x, head_dim):
    half = head_dim // 2
    width = x.shape[1]
    lane = lax.broadcasted_iota(jnp.int32, x.shape, 1) % head_dim
    return jnp.where(lane < half, pltpu.roll(x, width - half, 1), pltpu.roll(x, half, 1))


def head_mask(x, h, head_dim):
    lane = lax.broadcasted_iota(jnp.int32, x.shape, 1)
    return jnp.where((lane >= h * head_dim) & (lane < (h + 1) * head_dim), x, jnp.zeros_like(x))


def project_kernel(head_dim, x_ref, w_ref, cos_ref, sin_ref, q_ref, k_ref, v_ref, kt_ref, vt_ref):
    width = q_ref.shape[1]
    mixed = dot_nn(x_ref[...], w_ref[...])
    cos, sin = cos_ref[...], sin_ref[...]
    q = mixed[:, :width]
    k = mixed[:, width : 2 * width]
    v = mixed[:, 2 * width :].astype(BF16)
    q = q * cos + swap_halves(q, head_dim) * sin
    k = k * cos + swap_halves(k, head_dim) * sin
    k_low = k.astype(BF16)
    q_ref[...] = (q.astype(BF16).astype(F32) * head_dim ** (-0.5)).astype(BF16)
    k_ref[...] = k_low
    v_ref[...] = v
    kt_ref[...] = k_low.T
    vt_ref[...] = v.T


def project(rows, qkv_matrix, cos_wide, sine_wide, head_dim):
    n, d = rows.shape
    width = qkv_matrix.shape[1] // 3
    block = min(512, n)
    row = pl.BlockSpec((block, width), lambda i: (i, 0))
    col = pl.BlockSpec((width, block), lambda i: (0, i))
    return pl.pallas_call(
        functools.partial(project_kernel, head_dim),
        grid=(n // block,),
        in_specs=[
            pl.BlockSpec((block, d), lambda i: (i, 0)),
            pl.BlockSpec((d, 3 * width), lambda i: (0, 0)),
            row,
            row,
        ],
        out_specs=[row, row, row, col, col],
        out_shape=[jax.ShapeDtypeStruct((n, width), BF16)] * 3
        + [jax.ShapeDtypeStruct((width, n), BF16)] * 2,
        compiler_params=pltpu.CompilerParams(vmem_limit_bytes=40 * MIB),
        cost_estimate=pl.CostEstimate(
            flops=6 * n * d * width, bytes_accessed=2 * n * d + 18 * n * width, transcendentals=0
        ),
        name="project",
    )(rows, qkv_matrix, cos_wide, sine_wide)


def key_range(start, block, total):
    first = (start // SHORT_LEN) * SHORT_LEN
    last = min(total, ((start + block - 1) // SHORT_LEN + 1) * SHORT_LEN)
    return (first // 256) * 256, min(total, -(-last // 256) * 256)


def window_bias(key_start, keys, row_start, rows, total):
    key_at = lax.broadcasted_iota(jnp.int32, (keys, rows), 0) + key_start
    row_at = lax.broadcasted_iota(jnp.int32, (keys, rows), 1) + row_start
    key_window = jnp.zeros_like(key_at)
    row_window = jnp.zeros_like(row_at)
    for edge in range(SHORT_LEN, total, SHORT_LEN):
        key_window += (key_at >= edge).astype(jnp.int32)
        row_window += (row_at >= edge).astype(jnp.int32)
    return jnp.where(key_window == row_window, 0.0, mask_fill)


def attend_kernel(head_dim, bucket_ref, q_ref, k_ref, vt_ref, o_ref, ot_ref, l_ref, bias_ref):
    rows, width = q_ref.shape
    total = k_ref.shape[0]
    heads = width // head_dim
    step = pl.program_id(0)

    def block(at, first, last, masked):
        @pl.loop(0, heads)
        def _(h):
            hs = pl.ds(pl.multiple_of(h * head_dim, head_dim), head_dim)
            scores = dot_nt(k_ref[first:last, :], head_mask(q_ref[at, :], h, head_dim))
            if masked:
                scores = scores + bias_ref[: last - first, :]
            top = jnp.max(scores, axis=0, keepdims=True)
            weights = jnp.exp(scores - top)
            totals = jnp.sum(weights, axis=0, keepdims=True)
            ot_ref[hs, at] = dot_nn(vt_ref[hs, first:last], weights.astype(BF16)) / totals
            l_ref[pl.ds(h, 1), at] = top + jnp.log(totals)

    @pl.when(bucket_ref[0] == 1)
    def _():
        block(slice(0, rows), 0, total, False)

    sub = bias_ref.shape[1]
    for start in range(0, total, sub):
        first, last = key_range(start, sub, total)

        @pl.when((bucket_ref[0] != 1) & (step == start // rows))
        def _():
            bias_ref[: last - first, :] = window_bias(first, last - first, start, sub, total)
            block(slice(start % rows, start % rows + sub), first, last, True)

    o_ref[...] = ot_ref[...].T.astype(BF16)


def attend(bucket, q, k, vt, head_dim):
    n, width = q.shape
    heads = width // head_dim
    block = min(1024, n)
    pairs = n * n * heads
    lanes = -(-heads // 8) * 8
    row = pl.BlockSpec((block, width), lambda i, *_: (i, 0))
    col = pl.BlockSpec((width, block), lambda i, *_: (0, i))
    return pl.pallas_call(
        functools.partial(attend_kernel, head_dim),
        grid_spec=pltpu.PrefetchScalarGridSpec(
            num_scalar_prefetch=1,
            grid=(n // block,),
            in_specs=[
                row,
                pl.BlockSpec((n, width), lambda i, *_: (0, 0)),
                pl.BlockSpec((width, n), lambda i, *_: (0, 0)),
            ],
            out_specs=[row, col, pl.BlockSpec((lanes, block), lambda i, *_: (0, i))],
            scratch_shapes=[pltpu.VMEM((n, min(512, block)), F32)],
        ),
        out_shape=[
            jax.ShapeDtypeStruct((n, width), BF16),
            jax.ShapeDtypeStruct((width, n), F32),
            jax.ShapeDtypeStruct((lanes, n), F32),
        ],
        compiler_params=pltpu.CompilerParams(vmem_limit_bytes=56 * MIB),
        cost_estimate=pl.CostEstimate(
            flops=pairs * 1024, bytes_accessed=10 * n * width, transcendentals=pairs
        ),
        name="attend",
    )(bucket, q, k, vt)


def attend_back_kernel(
    head_dim,
    bucket_ref,
    q_ref,
    k_ref,
    kt_ref,
    v_ref,
    g_ref,
    ot_ref,
    l_ref,
    dq_ref,
    dk_ref,
    dv_ref,
    bias_ref,
    gt_ref,
):
    rows, width = q_ref.shape
    total = k_ref.shape[0]
    heads = width // head_dim
    step = pl.program_id(0)

    @pl.when(step == 0)
    def _():
        dk_ref[...] = jnp.zeros_like(dk_ref)
        dv_ref[...] = jnp.zeros_like(dv_ref)

    gt_ref[...] = g_ref[...].astype(F32).T * ot_ref[...]

    def block(first, last, masked):
        keys = slice(first, last)

        @pl.loop(0, heads)
        def _(h):
            hs = pl.ds(pl.multiple_of(h * head_dim, head_dim), head_dim)
            qh, gh = head_mask(q_ref[...], h, head_dim), head_mask(g_ref[...], h, head_dim)
            scores = dot_nt(k_ref[keys, :], qh)
            if masked:
                scores = scores + bias_ref[: last - first, :]
            probs = jnp.exp(scores - l_ref[pl.ds(h, 1), :])
            prob_grad = dot_nt(v_ref[keys, :], gh)
            delta = jnp.sum(gt_ref[hs, :], axis=0, keepdims=True)
            score_grad = (probs * (prob_grad - delta)).astype(BF16)
            dv_ref[keys, :] += dot_nn(probs.astype(BF16), gh)
            dk_ref[keys, :] += dot_nn(score_grad, qh)
            dq_ref[hs, :] = dot_nn(kt_ref[hs, keys], score_grad)

    @pl.when(bucket_ref[0] == 1)
    def _():
        block(0, total, False)

    for start in range(0, total, rows):
        first, last = key_range(start, rows, total)

        @pl.when((bucket_ref[0] != 1) & (step == start // rows))
        def _():
            bias_ref[: last - first, :] = window_bias(first, last - first, start, rows, total)
            block(first, last, True)


def attend_back(bucket, q, k, kt, v, g, ot, log_totals, head_dim):
    n, width = q.shape
    heads = width // head_dim
    block = min(512, n)
    pairs = n * n * heads
    row = pl.BlockSpec((block, width), lambda i, *_: (i, 0))
    col = pl.BlockSpec((width, block), lambda i, *_: (0, i))
    full = pl.BlockSpec((n, width), lambda i, *_: (0, 0))
    return pl.pallas_call(
        functools.partial(attend_back_kernel, head_dim),
        grid_spec=pltpu.PrefetchScalarGridSpec(
            num_scalar_prefetch=1,
            grid=(n // block,),
            in_specs=[
                row,
                full,
                pl.BlockSpec((width, n), lambda i, *_: (0, 0)),
                full,
                row,
                col,
                pl.BlockSpec((log_totals.shape[0], block), lambda i, *_: (0, i)),
            ],
            out_specs=[col, full, full],
            scratch_shapes=[pltpu.VMEM((n, block), F32), pltpu.VMEM((width, block), F32)],
        ),
        out_shape=[
            jax.ShapeDtypeStruct((width, n), F32),
            jax.ShapeDtypeStruct((n, width), F32),
            jax.ShapeDtypeStruct((n, width), F32),
        ],
        compiler_params=pltpu.CompilerParams(vmem_limit_bytes=56 * MIB),
        cost_estimate=pl.CostEstimate(
            flops=pairs * 2560, bytes_accessed=24 * n * width, transcendentals=pairs
        ),
        name="attend_back",
    )(bucket, q, k, kt, v, g, ot, log_totals)


def unrotate_kernel(head_dim, dq_ref, dk_ref, dv_ref, cos_ref, sin_ref, out_ref):
    width = dk_ref.shape[1]
    cos, sin = cos_ref[...], sin_ref[...]
    dq = dq_ref[...].T * head_dim ** (-0.5)
    dk = dk_ref[...]
    out_ref[:, :width] = (dq * cos - swap_halves(dq, head_dim) * sin).astype(BF16)
    out_ref[:, width : 2 * width] = (dk * cos - swap_halves(dk, head_dim) * sin).astype(BF16)
    out_ref[:, 2 * width :] = dv_ref[...].astype(BF16)


def unrotate(dq_t, dk, dv, cos_wide, sine_wide, head_dim):
    n, width = dk.shape
    block = min(512, n)
    row = pl.BlockSpec((block, width), lambda i: (i, 0))
    return pl.pallas_call(
        functools.partial(unrotate_kernel, head_dim),
        grid=(n // block,),
        in_specs=[pl.BlockSpec((width, block), lambda i: (0, i)), row, row, row, row],
        out_specs=pl.BlockSpec((block, 3 * width), lambda i: (i, 0)),
        out_shape=jax.ShapeDtypeStruct((n, 3 * width), BF16),
        compiler_params=pltpu.CompilerParams(vmem_limit_bytes=40 * MIB),
        cost_estimate=pl.CostEstimate(flops=0, bytes_accessed=26 * n * width, transcendentals=0),
        name="unrotate",
    )(dq_t, dk, dv, cos_wide, sine_wide)


def feed_kernel(x_ref, c_ref, wgu_ref, wd_ref, h_ref, b_ref, n_ref):
    units = wd_ref.shape[0]
    both = dot_nn(x_ref[...], wgu_ref[...])
    gate, up = both[:, :units], both[:, units:]
    sig = jax.nn.sigmoid(gate)
    silu = gate * sig
    h_ref[...] = (silu * up).astype(BF16)
    hidden_grad = dot_nt(c_ref[...], wd_ref[...])
    b_ref[:, :units] = (hidden_grad * up * sig * (1.0 + gate * (1.0 - sig))).astype(BF16)
    b_ref[:, units:] = (hidden_grad * silu).astype(BF16)
    n_ref[...] = dot_nt(b_ref[...], wgu_ref[...]).astype(BF16)


def feed(x, cot, wgu, wd):
    n, d = x.shape
    units = wd.shape[0]
    block = min(256, n)
    row = lambda w: pl.BlockSpec((block, w), lambda i: (i, 0))
    return pl.pallas_call(
        feed_kernel,
        grid=(n // block,),
        in_specs=[
            row(d),
            row(d),
            pl.BlockSpec((d, 2 * units), lambda i: (0, 0)),
            pl.BlockSpec((units, d), lambda i: (0, 0)),
        ],
        out_specs=[row(units), row(2 * units), row(d)],
        out_shape=[
            jax.ShapeDtypeStruct((n, units), BF16),
            jax.ShapeDtypeStruct((n, 2 * units), BF16),
            jax.ShapeDtypeStruct((n, d), BF16),
        ],
        compiler_params=pltpu.CompilerParams(vmem_limit_bytes=40 * MIB),
        cost_estimate=pl.CostEstimate(
            flops=10 * n * d * units, bytes_accessed=8 * n * d, transcendentals=n * units
        ),
        name="feed",
    )(x, cot, wgu, wd)


def hop(x, bit):
    size = lax.axis_size("dp")
    return lax.ppermute(x, "dp", [(i, i ^ bit) for i in range(size)])


def gather_plane(a):
    size = lax.axis_size("dp")
    if size != 8:
        return [lax.all_gather(a, "dp", axis=0, tiled=True)]
    half = a.shape[0] // 2
    from_x, from_y = hop(a, 2), hop(a, 4)
    own_pair = jnp.concatenate([a, hop(a, 1)])
    low, high = hop(from_y[:half], 2), hop(from_x[half:], 4)
    x_pair = jnp.concatenate([from_x, hop(from_x, 1)])
    y_pair = jnp.concatenate([from_y, hop(from_y, 1)])
    far = jnp.concatenate([low, high])
    far_pair = jnp.concatenate([far, hop(far, 1)])
    return [own_pair, x_pair, y_pair, far_pair]


def add_low(*terms):
    return sum(t.astype(F32) for t in terms).astype(BF16)


def scatter_plane(parts):
    size = lax.axis_size("dp")
    if size != 8:
        return lax.psum_scatter(parts[0], "dp", scatter_dimension=0, tiled=True).astype(F32)
    rows = parts[0].shape[0] // 2
    half = rows // 2
    own, x, y, far = (add_low(p[:rows], hop(p[rows:], 1)) for p in parts)
    to_x, to_y = hop(far[:half], 2), hop(far[half:], 4)
    y = jnp.concatenate([add_low(y[:half], to_x), y[half:]])
    x = jnp.concatenate([x[:half], add_low(x[half:], to_y)])
    return own.astype(F32) + hop(x, 2).astype(F32) + hop(y, 4).astype(F32)


def shards(
    tokens,
    group_bucket,
    gain_one,
    shift_one,
    w_qkv,
    w_out,
    gain_two,
    shift_two,
    w_gate_up,
    w_down,
    cotangent,
):
    ways = lax.axis_size("tensor")
    replicas = lax.axis_size("dp")
    replica = lax.axis_index("dp")
    own_rows, d = tokens.shape
    group_rows = own_rows * ways
    local_width = w_out.shape[0]
    head_dim = d // HEADS
    hidden_width = w_down.shape[0]
    units = hidden_width // replicas
    out_rows = local_width // replicas
    qkv_matrix = w_qkv.reshape(d, 3 * local_width)
    cos_wide, sine_wide = rotary_wide(group_bucket[0], group_rows, head_dim, local_width)

    rows_in = tokens.astype(F32)
    normed_one, unit_one, root_one = norm_forward(rows_in, gain_one, shift_one)
    normed_one_low = normed_one.astype(BF16)
    rows_one = lax.all_gather(normed_one_low, "tensor", axis=0, tiled=True)

    gate_up_slice = lax.dynamic_slice_in_dim(w_gate_up, replica * units, units, axis=2)
    down_slice = lax.dynamic_slice_in_dim(w_down, replica * units, units, axis=0)
    out_slice = lax.dynamic_slice_in_dim(w_out, replica * out_rows, out_rows, axis=0)
    gate_up_all = lax.all_gather(gate_up_slice.reshape(d, 2 * units), "tensor", axis=0)
    down_all = lax.all_gather(down_slice, "tensor", axis=0, tiled=True)
    out_part = lax.all_gather(out_slice, "tensor", axis=0)
    out_full = lax.all_gather(out_part, "dp", axis=1).reshape(d, d)
    wgu = gate_up_all.reshape(ways, d, 2, units).transpose(1, 2, 0, 3).reshape(d, 2 * ways * units)
    cot_pieces = gather_plane(cotangent)

    q, k, v, kt, vt = project(rows_one, qkv_matrix, cos_wide, sine_wide, head_dim)
    attended, attended_t, log_totals = attend(group_bucket, q, k, vt, head_dim)
    attended_own = lax.all_to_all(attended, "tensor", 0, 1, tiled=True)
    resid = rows_in + dot_nn(attended_own, out_full)

    normed_two, unit_two, root_two = norm_forward(resid, gain_two, shift_two)
    row_pieces = gather_plane(normed_two.astype(BF16))
    fed = [feed(x, c, wgu, down_all) for x, c in zip(row_pieces, cot_pieces)]
    normed_two_grad = scatter_plane([f[2] for f in fed])
    hidden = [f[0] for f in fed]
    branch = [f[1] for f in fed]
    ffn_out = scatter_plane([dot_nn(h, down_all).astype(BF16) for h in hidden])
    layer_out = (resid + ffn_out).astype(BF16)
    down_grad = sum(dot_tn(h, c) for h, c in zip(hidden, cot_pieces)).astype(BF16)
    gate_up_grad = sum(dot_tn(x, b) for x, b in zip(row_pieces, branch)).astype(BF16)
    gate_up_grad = gate_up_grad.reshape(d, 2, ways, units).transpose(2, 0, 1, 3)
    gate_up_grad = gate_up_grad.reshape(ways, d, 2 * units)
    gate_up_grad = lax.psum_scatter(gate_up_grad, "tensor", scatter_dimension=0)
    down_grad = lax.psum_scatter(down_grad, "tensor", scatter_dimension=0, tiled=True)
    gate_up_grad = lax.all_gather(gate_up_grad, "dp", axis=0)
    down_grad = lax.all_gather(down_grad, "dp", axis=0, tiled=True).astype(F32)
    gate_up_grad = gate_up_grad.reshape(replicas, d, 2, units).transpose(1, 2, 0, 3)
    gate_up_grad = gate_up_grad.reshape(d, 2, hidden_width).astype(F32)

    resid_part, gain_two_grad, shift_two_grad = norm_backward(
        normed_two_grad, unit_two, root_two, gain_two
    )
    resid_grad = cotangent.astype(F32) + resid_part
    attn_grad = resid_grad.astype(BF16)

    attended_grad_own = dot_nt(attn_grad, out_full).astype(BF16)
    attended_grad = lax.all_to_all(attended_grad_own, "tensor", 1, 0, tiled=True)
    out_grad = dot_tn(attended_own, attn_grad).astype(BF16).reshape(ways, replicas, out_rows, d)
    out_grad = lax.psum_scatter(out_grad, "dp", scatter_dimension=1)
    out_grad = lax.psum_scatter(out_grad, "tensor", scatter_dimension=0)
    out_grad = lax.all_gather(out_grad, "dp", axis=0, tiled=True).astype(F32)
    dq_t, dk, dv = attend_back(
        group_bucket, q, k, kt, v, attended_grad, attended_t, log_totals, head_dim
    )
    mixed_grad = unrotate(dq_t, dk, dv, cos_wide, sine_wide, head_dim)
    normed_one_grad = lax.psum_scatter(
        dot_nt(mixed_grad, qkv_matrix).astype(BF16), "tensor", scatter_dimension=0, tiled=True
    ).astype(F32)
    qkv_grad = lax.psum(dot_tn(rows_one, mixed_grad).astype(BF16), "dp").astype(F32)
    qkv_grad = qkv_grad.reshape(d, 3, local_width)
    input_part, gain_one_grad, shift_one_grad = norm_backward(
        normed_one_grad, unit_one, root_one, gain_one
    )
    token_grad = resid_grad + input_part
    gain_one_grad, shift_one_grad, gain_two_grad, shift_two_grad = lax.psum(
        jnp.stack([gain_one_grad, shift_one_grad, gain_two_grad, shift_two_grad]), ("dp", "tensor")
    )
    return (
        layer_out,
        token_grad,
        gain_one_grad,
        shift_one_grad,
        qkv_grad,
        out_grad,
        gain_two_grad,
        shift_two_grad,
        gate_up_grad,
        down_grad,
    )


def solution(mesh):
    in_specs = (
        P(("dp", "tensor"), None),
        P("dp"),
        P(),
        P(),
        P(None, None, "tensor"),
        P("tensor", None),
        P(),
        P(),
        P(None, None, "tensor"),
        P("tensor", None),
        P(("dp", "tensor"), None),
    )
    out_specs = (
        P(("dp", "tensor"), None),
        P(("dp", "tensor"), None),
        P(),
        P(),
        P(None, None, "tensor"),
        P("tensor", None),
        P(),
        P(),
        P(None, None, "tensor"),
        P("tensor", None),
    )
    return jax.shard_map(shards, mesh=mesh, in_specs=in_specs, out_specs=out_specs, check_vma=False)
```

```python
import functools

import jax
import jax.numpy as jnp
from jax import lax
from jax.experimental import pallas as pl
from jax.experimental.pallas import tpu as pltpu
from jax.sharding import PartitionSpec as P

HEADS = 16
LONG_LEN = 2048
SHORT_LEN = 1000

norm_eps = 1e-05
mask_fill = -1e30
rope_base = 10000.0
MIB = 2**20
F32 = jnp.float32
BF16 = jnp.bfloat16


def dot_nn(a, b):
    return jnp.dot(a, b, preferred_element_type=F32)


def dot_nt(a, b):
    return lax.dot_general(a, b, (((1,), (1,)), ((), ())), preferred_element_type=F32)


def dot_tn(a, b):
    return lax.dot_general(a, b, (((0,), (0,)), ((), ())), preferred_element_type=F32)


def rotary_wide(bucket_id, group_rows, head_dim, width):
    positions = jnp.arange(group_rows, dtype=jnp.int32)
    span_len = jnp.where(bucket_id == 1, LONG_LEN, SHORT_LEN).astype(jnp.int32)
    places = positions - (positions // span_len) * span_len
    half_dim = head_dim // 2
    exponents = jnp.arange(half_dim, dtype=F32) * (-2.0 / head_dim)
    freqs = jnp.exp(exponents * jnp.log(F32(rope_base)))
    heads = width // head_dim
    signs = jnp.tile(jnp.repeat(jnp.array([-1.0, 1.0], F32), half_dim), heads)
    angles = places.astype(F32)[:, None] * jnp.tile(freqs, 2 * heads)[None, :]
    return jnp.cos(angles), jnp.sin(angles) * signs


def norm_forward(values, gain, shift):
    average = jnp.mean(values, axis=-1, keepdims=True)
    centred = values - average
    spread_sq = jnp.mean(centred * centred, axis=-1, keepdims=True)
    inv_root = lax.rsqrt(spread_sq + norm_eps)
    unit_rows = centred * inv_root
    return (unit_rows * gain + shift, unit_rows, inv_root)


def norm_backward(out_grad_rows, unit_rows, inv_root, gain):
    scaled = out_grad_rows * gain
    first_mean = jnp.mean(scaled, axis=-1, keepdims=True)
    second_mean = jnp.mean(scaled * unit_rows, axis=-1, keepdims=True)
    in_grad = inv_root * (scaled - first_mean - unit_rows * second_mean)
    return (in_grad, jnp.sum(out_grad_rows * unit_rows, axis=0), jnp.sum(out_grad_rows, axis=0))


def swap_halves(x, head_dim):
    half = head_dim // 2
    width = x.shape[1]
    lane = lax.broadcasted_iota(jnp.int32, x.shape, 1) % head_dim
    return jnp.where(lane < half, pltpu.roll(x, width - half, 1), pltpu.roll(x, half, 1))


def head_mask(x, h, head_dim):
    lane = lax.broadcasted_iota(jnp.int32, x.shape, 1)
    return jnp.where((lane >= h * head_dim) & (lane < (h + 1) * head_dim), x, jnp.zeros_like(x))


def widen(table, width):
    return jnp.concatenate([table] * (width // table.shape[1]), axis=1)


def project_kernel(head_dim, x_ref, w_ref, cos_ref, sin_ref, q_ref, k_ref, v_ref, kt_ref, vt_ref):
    width = q_ref.shape[1]
    x = x_ref[...]
    cos, sin = widen(cos_ref[...], width), widen(sin_ref[...], width)
    q, k, v = (dot_nn(x, w_ref[j]) for j in range(3))
    v = v.astype(BF16)
    q = q * cos + swap_halves(q, head_dim) * sin
    k = k * cos + swap_halves(k, head_dim) * sin
    k_low = k.astype(BF16)
    q_ref[...] = (q.astype(BF16).astype(F32) * head_dim ** (-0.5)).astype(BF16)
    k_ref[...] = k_low
    v_ref[...] = v
    kt_ref[...] = k_low.T
    vt_ref[...] = v.T


def project(rows, w, cos_wide, sine_wide, head_dim):
    n, d = rows.shape
    width = w.shape[2]
    block = min(512, n)
    row = pl.BlockSpec((block, width), lambda i: (i, 0))
    col = pl.BlockSpec((width, block), lambda i: (0, i))
    table = pl.BlockSpec((block, cos_wide.shape[1]), lambda i: (i, 0))
    return pl.pallas_call(
        functools.partial(project_kernel, head_dim),
        grid=(n // block,),
        in_specs=[
            pl.BlockSpec((block, d), lambda i: (i, 0)),
            pl.BlockSpec((3, d, width), lambda i: (0, 0, 0)),
            table,
            table,
        ],
        out_specs=[row, row, row, col, col],
        out_shape=[jax.ShapeDtypeStruct((n, width), BF16)] * 3
        + [jax.ShapeDtypeStruct((width, n), BF16)] * 2,
        compiler_params=pltpu.CompilerParams(vmem_limit_bytes=40 * MIB),
        cost_estimate=pl.CostEstimate(
            flops=6 * n * d * width, bytes_accessed=2 * n * d + 18 * n * width, transcendentals=0
        ),
        name="project",
    )(rows, w, cos_wide, sine_wide)


def key_range(start, block, total):
    first = (start // SHORT_LEN) * SHORT_LEN
    last = min(total, ((start + block - 1) // SHORT_LEN + 1) * SHORT_LEN)
    return (first // 256) * 256, min(total, -(-last // 256) * 256)


def window_bias(key_start, keys, row_start, rows, total):
    key_at = lax.broadcasted_iota(jnp.int32, (keys, rows), 0) + key_start
    row_at = lax.broadcasted_iota(jnp.int32, (keys, rows), 1) + row_start
    key_window = jnp.zeros_like(key_at)
    row_window = jnp.zeros_like(row_at)
    for edge in range(SHORT_LEN, total, SHORT_LEN):
        key_window += (key_at >= edge).astype(jnp.int32)
        row_window += (row_at >= edge).astype(jnp.int32)
    return jnp.where(key_window == row_window, 0.0, mask_fill)


def attend_kernel(head_dim, bucket_ref, q_ref, k_ref, vt_ref, o_ref, ot_ref, l_ref, bias_ref):
    rows, width = q_ref.shape
    total = k_ref.shape[0]
    heads = width // head_dim
    step = pl.program_id(0)

    def block(at, first, last, masked):
        @pl.loop(0, heads)
        def _(h):
            hs = pl.ds(pl.multiple_of(h * head_dim, head_dim), head_dim)
            scores = dot_nt(k_ref[first:last, :], head_mask(q_ref[at, :], h, head_dim))
            if masked:
                scores = scores + bias_ref[: last - first, :]
            top = jnp.max(scores, axis=0, keepdims=True)
            weights = jnp.exp(scores - top)
            totals = jnp.sum(weights, axis=0, keepdims=True)
            ot_ref[hs, at] = dot_nn(vt_ref[hs, first:last], weights.astype(BF16)) / totals
            l_ref[pl.ds(h, 1), at] = top + jnp.log(totals)

    @pl.when(bucket_ref[0] == 1)
    def _():
        block(slice(0, rows), 0, total, False)

    sub = bias_ref.shape[1]
    for start in range(0, total, sub):
        first, last = key_range(start, sub, total)

        @pl.when((bucket_ref[0] != 1) & (step == start // rows))
        def _():
            bias_ref[: last - first, :] = window_bias(first, last - first, start, sub, total)
            block(slice(start % rows, start % rows + sub), first, last, True)

    o_ref[...] = ot_ref[...].T.astype(BF16)


def attend(bucket, q, k, vt, head_dim, pair, width):
    n = q.shape[0]
    heads = width // head_dim
    block = min(1024, n)
    pairs = n * n * heads
    lanes = -(-heads // 8) * 8
    row = pl.BlockSpec((block, width), lambda i, *_: (i, 0))
    col = pl.BlockSpec((width, block), lambda i, *_: (0, i))
    return pl.pallas_call(
        functools.partial(attend_kernel, head_dim),
        grid_spec=pltpu.PrefetchScalarGridSpec(
            num_scalar_prefetch=1,
            grid=(n // block,),
            in_specs=[
                pl.BlockSpec((block, width), lambda i, *_: (i, pair)),
                pl.BlockSpec((n, width), lambda i, *_: (0, pair)),
                pl.BlockSpec((width, n), lambda i, *_: (pair, 0)),
            ],
            out_specs=[row, col, pl.BlockSpec((lanes, block), lambda i, *_: (0, i))],
            scratch_shapes=[pltpu.VMEM((n, min(512, block)), F32)],
        ),
        out_shape=[
            jax.ShapeDtypeStruct((n, width), BF16),
            jax.ShapeDtypeStruct((width, n), F32),
            jax.ShapeDtypeStruct((lanes, n), F32),
        ],
        compiler_params=pltpu.CompilerParams(vmem_limit_bytes=56 * MIB),
        cost_estimate=pl.CostEstimate(
            flops=pairs * 1024, bytes_accessed=10 * n * width, transcendentals=pairs
        ),
        name="attend",
    )(bucket, q, k, vt)


def attend_back_kernel(
    head_dim,
    bucket_ref,
    q_ref,
    k_ref,
    kt_ref,
    v_ref,
    g_ref,
    ot_ref,
    l_ref,
    dq_ref,
    dk_ref,
    dv_ref,
    bias_ref,
    gt_ref,
):
    rows, width = q_ref.shape
    total = k_ref.shape[0]
    heads = width // head_dim
    step = pl.program_id(0)

    @pl.when(step == 0)
    def _():
        dk_ref[...] = jnp.zeros_like(dk_ref)
        dv_ref[...] = jnp.zeros_like(dv_ref)

    gt_ref[...] = g_ref[...].astype(F32).T * ot_ref[...]

    def block(first, last, masked):
        keys = slice(first, last)

        @pl.loop(0, heads)
        def _(h):
            hs = pl.ds(pl.multiple_of(h * head_dim, head_dim), head_dim)
            qh, gh = head_mask(q_ref[...], h, head_dim), head_mask(g_ref[...], h, head_dim)
            scores = dot_nt(k_ref[keys, :], qh)
            if masked:
                scores = scores + bias_ref[: last - first, :]
            probs = jnp.exp(scores - l_ref[pl.ds(h, 1), :])
            prob_grad = dot_nt(v_ref[keys, :], gh)
            delta = jnp.sum(gt_ref[hs, :], axis=0, keepdims=True)
            score_grad = (probs * (prob_grad - delta)).astype(BF16)
            dv_ref[keys, :] += dot_nn(probs.astype(BF16), gh)
            dk_ref[keys, :] += dot_nn(score_grad, qh)
            dq_ref[hs, :] = dot_nn(kt_ref[hs, keys], score_grad)

    @pl.when(bucket_ref[0] == 1)
    def _():
        block(0, total, False)

    for start in range(0, total, rows):
        first, last = key_range(start, rows, total)

        @pl.when((bucket_ref[0] != 1) & (step == start // rows))
        def _():
            bias_ref[: last - first, :] = window_bias(first, last - first, start, rows, total)
            block(first, last, True)


def attend_back(bucket, q, k, kt, v, g, ot, log_totals, head_dim, pair, width):
    n = q.shape[0]
    heads = width // head_dim
    block = min(512, n)
    pairs = n * n * heads
    col = pl.BlockSpec((width, block), lambda i, *_: (0, i))
    full = pl.BlockSpec((n, width), lambda i, *_: (0, 0))
    full_pair = pl.BlockSpec((n, width), lambda i, *_: (0, pair))
    return pl.pallas_call(
        functools.partial(attend_back_kernel, head_dim),
        grid_spec=pltpu.PrefetchScalarGridSpec(
            num_scalar_prefetch=1,
            grid=(n // block,),
            in_specs=[
                pl.BlockSpec((block, width), lambda i, *_: (i, pair)),
                full_pair,
                pl.BlockSpec((width, n), lambda i, *_: (pair, 0)),
                full_pair,
                pl.BlockSpec((block, width), lambda i, *_: (i, 0)),
                col,
                pl.BlockSpec((log_totals.shape[0], block), lambda i, *_: (0, i)),
            ],
            out_specs=[col, full, full],
            scratch_shapes=[pltpu.VMEM((n, block), F32), pltpu.VMEM((width, block), F32)],
        ),
        out_shape=[
            jax.ShapeDtypeStruct((width, n), F32),
            jax.ShapeDtypeStruct((n, width), F32),
            jax.ShapeDtypeStruct((n, width), F32),
        ],
        compiler_params=pltpu.CompilerParams(vmem_limit_bytes=56 * MIB),
        cost_estimate=pl.CostEstimate(
            flops=pairs * 2560, bytes_accessed=24 * n * width, transcendentals=pairs
        ),
        name="attend_back",
    )(bucket, q, k, kt, v, g, ot, log_totals)


def unrotate_kernel(head_dim, pairs, *refs):
    cos_ref, sin_ref, out_ref = refs[-3:]
    cos, sin = cos_ref[...], sin_ref[...]
    width = cos.shape[1]
    for pair in range(pairs):
        dq_ref, dk_ref, dv_ref = refs[3 * pair : 3 * pair + 3]
        dq = dq_ref[...].T * head_dim ** (-0.5)
        dk = dk_ref[...]
        grads = (
            dq * cos - swap_halves(dq, head_dim) * sin,
            dk * cos - swap_halves(dk, head_dim) * sin,
            dv_ref[...],
        )
        for j, grad in enumerate(grads):
            at = (j * pairs + pair) * width
            out_ref[:, at : at + width] = grad.astype(BF16)


def unrotate(grads, cos_wide, sine_wide, head_dim):
    n, width = cos_wide.shape
    pairs = len(grads)
    block = min(512, n)
    row = pl.BlockSpec((block, width), lambda i: (i, 0))
    col = pl.BlockSpec((width, block), lambda i: (0, i))
    return pl.pallas_call(
        functools.partial(unrotate_kernel, head_dim, pairs),
        grid=(n // block,),
        in_specs=[col, row, row] * pairs + [row, row],
        out_specs=pl.BlockSpec((block, 3 * pairs * width), lambda i: (i, 0)),
        out_shape=jax.ShapeDtypeStruct((n, 3 * pairs * width), BF16),
        compiler_params=pltpu.CompilerParams(vmem_limit_bytes=40 * MIB),
        cost_estimate=pl.CostEstimate(
            flops=0, bytes_accessed=26 * n * width * pairs, transcendentals=0
        ),
        name="unrotate",
    )(*(g for pair in grads for g in pair), cos_wide, sine_wide)


def feed_kernel(x_ref, c_ref, wgu_ref, wd_ref, h_ref, b_ref, n_ref):
    units = wd_ref.shape[0]
    both = dot_nn(x_ref[...], wgu_ref[...])
    gate, up = both[:, :units], both[:, units:]
    sig = jax.nn.sigmoid(gate)
    silu = gate * sig
    h_ref[...] = (silu * up).astype(BF16)
    hidden_grad = dot_nt(c_ref[...], wd_ref[...])
    b_ref[:, :units] = (hidden_grad * up * sig * (1.0 + gate * (1.0 - sig))).astype(BF16)
    b_ref[:, units:] = (hidden_grad * silu).astype(BF16)
    n_ref[...] = dot_nt(b_ref[...], wgu_ref[...]).astype(BF16)


def feed(x, cot, wgu, wd):
    n, d = x.shape
    units = wd.shape[0]
    block = min(256, n)
    row = lambda w: pl.BlockSpec((block, w), lambda i: (i, 0))
    return pl.pallas_call(
        feed_kernel,
        grid=(n // block,),
        in_specs=[
            row(d),
            row(d),
            pl.BlockSpec((d, 2 * units), lambda i: (0, 0)),
            pl.BlockSpec((units, d), lambda i: (0, 0)),
        ],
        out_specs=[row(units), row(2 * units), row(d)],
        out_shape=[
            jax.ShapeDtypeStruct((n, units), BF16),
            jax.ShapeDtypeStruct((n, 2 * units), BF16),
            jax.ShapeDtypeStruct((n, d), BF16),
        ],
        compiler_params=pltpu.CompilerParams(vmem_limit_bytes=40 * MIB),
        cost_estimate=pl.CostEstimate(
            flops=10 * n * d * units, bytes_accessed=8 * n * d, transcendentals=n * units
        ),
        name="feed",
    )(x, cot, wgu, wd)


MESH_ID = pl.DeviceIdType.MESH


def plane_peers():
    me = lax.axis_index("dp")
    return [{"dp": lax.bitwise_xor(me, bit)} for bit in (1, 2, 4)]


def enter(peers):
    barrier = pltpu.get_barrier_semaphore()
    for peer in peers:
        pl.semaphore_signal(barrier, inc=1, device_id=peer, device_id_type=MESH_ID)
    pl.semaphore_wait(barrier, len(peers))


def remote(src, dst, send, recv, at, peer):
    return pltpu.make_async_remote_copy(
        src_ref=src,
        dst_ref=dst,
        send_sem=send.at[at],
        recv_sem=recv.at[at],
        device_id=peer,
        device_id_type=MESH_ID,
    )


def gather_copies(view, send, recv, placed):
    sib, across, along = plane_peers()
    steps = [
        (0, 1, sib, None),
        (0, 2, across, None),
        (0, 4, along, None),
        (4, 2, across, 0),
        (2, 4, along, 1),
        (2, 1, sib, None),
        (4, 1, sib, None),
        (6, 1, sib, None),
    ]
    copies = {}
    for i, (s, bit, peer, part) in enumerate(steps):
        src = view(s, part)
        dst = src if placed else view(s ^ bit, part)
        copies[f"{s}-{s ^ bit}"] = remote(src, dst, send, recv, i, peer)
    return copies


def half_of(ref, part):
    if part is None:
        return ref
    half = ref.shape[-2] // 2
    return ref.at[(slice(None),) * (len(ref.shape) - 2) + (pl.ds(part * half, half),)]


def gather_start(copies):
    for name in ("0-2", "0-4", "0-1"):
        copies[name].start()


def gather_forward(copies):
    copies["0-2"].wait_recv()
    copies["2-6"].start()
    copies["2-3"].start()
    copies["0-4"].wait_recv()
    copies["4-6"].start()
    copies["4-5"].start()


def gather_finish(copies):
    copies["2-6"].wait_recv()
    copies["4-6"].wait_recv()
    copies["6-7"].start()
    for name in ("0-1", "2-3", "4-5", "6-7"):
        copies[name].wait_recv()


def gather_kernel(
    cot_ref, wo_ref, cots_out, wos_out, cots_ref, wos_ref, send, recv, wsend, wrecv, zsend, zrecv, own, done
):
    me, z = lax.axis_index("dp"), lax.axis_index("tensor")
    ways, out_rows = wos_ref.shape[0], wos_ref.shape[2]
    others = [{"tensor": lax.rem(z + k, ways)} for k in range(1, ways)]
    enter(plane_peers() + others)
    copies = gather_copies(lambda s, part: half_of(cots_ref.at[s], part), send, recv, False)
    loads = [
        pltpu.make_async_copy(cot_ref, cots_ref.at[0], own.at[0]),
        pltpu.make_async_copy(
            wo_ref.at[pl.ds(pl.multiple_of(me * out_rows, 16), out_rows)],
            wos_ref.at[z, me],
            own.at[1],
        ),
    ]
    for load in loads:
        load.start()
    loads[0].wait()
    gather_start(copies)
    loads[1].wait()
    sends = []
    for k, peer in enumerate(others):
        mine = wos_ref.at[z, me]
        sends.append(
            pltpu.make_async_remote_copy(
                src_ref=mine,
                dst_ref=mine,
                send_sem=zsend.at[k],
                recv_sem=zrecv.at[z],
                device_id=peer,
                device_id_type=MESH_ID,
            )
        )
        sends[-1].start()
    view = lambda s, part: half_of(wos_ref.at[:, lax.bitwise_xor(me, s)], part)
    weights = gather_copies(view, wsend, wrecv, True)
    gather_forward(copies)
    for k, peer in enumerate(others):
        source = lax.rem(z + k + 1, ways)
        theirs = wos_ref.at[source, me]
        pltpu.make_async_remote_copy(
            src_ref=theirs,
            dst_ref=theirs,
            send_sem=zsend.at[k],
            recv_sem=zrecv.at[source],
            device_id=peer,
            device_id_type=MESH_ID,
        ).wait_recv()
    gather_start(weights)
    gather_finish(copies)
    gather_forward(weights)
    gather_finish(weights)
    stores = [
        pltpu.make_async_copy(cots_ref, cots_out, done.at[0]),
        pltpu.make_async_copy(wos_ref, wos_out, done.at[1]),
    ]
    for store in stores:
        store.start()
    for store in stores:
        store.wait()
    for copy in (*copies.values(), *weights.values(), *sends):
        copy.wait_send()


def gather_front(cot, w_out, ways):
    rows, d = cot.shape
    out_rows = w_out.shape[0] // 8
    anywhere = pl.BlockSpec(memory_space=pl.ANY)
    return pl.pallas_call(
        gather_kernel,
        in_specs=[anywhere] * 2,
        out_specs=[anywhere] * 2,
        out_shape=[
            jax.ShapeDtypeStruct((8, rows, d), cot.dtype),
            jax.ShapeDtypeStruct((ways, 8, out_rows, d), w_out.dtype),
        ],
        scratch_shapes=[
            pltpu.VMEM((8, rows, d), cot.dtype),
            pltpu.VMEM((ways, 8, out_rows, d), w_out.dtype),
        ]
        + [pltpu.SemaphoreType.DMA((8,))] * 4
        + [pltpu.SemaphoreType.DMA((ways,))] * 2
        + [pltpu.SemaphoreType.DMA((2,))] * 2,
        compiler_params=pltpu.CompilerParams(
            collective_id=0, has_side_effects=True, vmem_limit_bytes=40 * MIB
        ),
        cost_estimate=pl.CostEstimate(
            flops=45 * 10**9, bytes_accessed=16 * rows * d, transcendentals=0
        ),
        name="gather_front",
    )(cot, w_out)


def feed_plane_kernel(
    x_ref,
    c_ref,
    w_ref,
    n_ref,
    o_ref,
    grads_ref,
    wgu_ref,
    wd_ref,
    xs,
    cs,
    hid,
    branch,
    part,
    from_sib,
    from_far,
    from_x,
    from_y,
    down_acc,
    gate_up_acc,
    gsend,
    grecv,
    ssend,
    srecv,
    csem,
    osem,
    xsem,
    wsem,
):
    ways, unit = w_ref.shape[0], w_ref.shape[1] // 3
    units = ways * unit
    rows = xs.shape[1]
    half = rows // 2
    low, high = pl.ds(0, half), pl.ds(half, half)
    sib, across, along = plane_peers()
    enter([sib, across, along])
    copies = gather_copies(lambda s, part: half_of(xs.at[s], part), gsend, grecv, False)
    weights = []
    for t in range(ways):
        at = pl.ds(t * unit, unit)
        for j, dst in enumerate((wgu_ref.at[at], wgu_ref.at[pl.ds(units + t * unit, unit)], wd_ref.at[at])):
            src = w_ref.at[t, pl.ds(j * unit, unit)]
            weights.append(pltpu.make_async_copy(src, dst, wsem.at[t, j]))
    own = pltpu.make_async_copy(x_ref, xs.at[0], xsem)
    own.start()
    cots = [pltpu.make_async_copy(c_ref.at[i], cs.at[i], csem.at[i]) for i in range(8)]
    own.wait()
    gather_start(copies)
    for load in (*weights, *cots):
        load.start()
    for load in weights:
        load.wait()
    down_acc[...] = jnp.zeros_like(down_acc)
    gate_up_acc[...] = jnp.zeros_like(gate_up_acc)

    sums = {
        "1": (part.at[1], from_sib.at[0], sib),
        "3": (part.at[3], from_sib.at[1], sib),
        "5": (part.at[5], from_sib.at[2], sib),
        "7": (part.at[7], from_sib.at[3], sib),
        "6l": (part.at[6, low], from_far.at[low], across),
        "6h": (part.at[6, high], from_far.at[high], along),
        "2l": (part.at[2, low], from_x.at[low], across),
        "2h": (part.at[2, high], from_x.at[high], across),
        "4l": (part.at[4, low], from_y.at[low], along),
        "4h": (part.at[4, high], from_y.at[high], along),
    }
    sums = {
        name: remote(src, dst, ssend, srecv, i, peer)
        for i, (name, (src, dst, peer)) in enumerate(sums.items())
    }

    def out_copy(i):
        return pltpu.make_async_copy(cs.at[i], o_ref.at[i], osem.at[i])

    def grads(i, at):
        down_acc[...] += dot_tn(hid[at], cs[i])
        gate_up_acc[...] += dot_tn(branch[at], xs[i])
        cs[i] = dot_nn(hid[at], wd_ref[...]).astype(BF16)
        out_copy(i).start()

    def join(i, j):
        part[i] = (part[i].astype(F32) + from_sib[j].astype(F32)).astype(BF16)

    @pl.loop(0, 8)
    def _(i):
        @pl.when(i == 1)
        def _():
            copies["0-1"].wait_recv()

        @pl.when(i == 2)
        def _():
            gather_forward(copies)

        @pl.when(i == 3)
        def _():
            copies["2-3"].wait_recv()

        @pl.when(i == 5)
        def _():
            copies["4-5"].wait_recv()
            sums["3"].wait_recv()
            join(2, 1)
            sums["2l"].start()

        @pl.when(i == 6)
        def _():
            copies["2-6"].wait_recv()
            copies["4-6"].wait_recv()
            copies["6-7"].start()

        @pl.when(i == 7)
        def _():
            copies["6-7"].wait_recv()
            sums["5"].wait_recv()
            join(4, 2)
            sums["4h"].start()

        for slot in range(8):

            @pl.when(i == slot)
            def _(slot=slot):
                cots[slot].wait()

        both = dot_nt(xs[i], wgu_ref[...])
        gate, up = both[:, :units], both[:, units:]
        sig = jax.nn.sigmoid(gate)
        silu = gate * sig
        at = jnp.where(i < 2, i, i - 2)
        hid[at] = (silu * up).astype(BF16)
        hidden_grad = dot_nt(cs[i], wd_ref[...])
        branch[at, :, :units] = (hidden_grad * up * sig * (1.0 + gate * (1.0 - sig))).astype(BF16)
        branch[at, :, units:] = (hidden_grad * silu).astype(BF16)
        part[i] = dot_nn(branch[at], wgu_ref[...]).astype(BF16)
        for odd in (1, 3, 5, 7):

            @pl.when(i == odd)
            def _(odd=odd):
                sums[str(odd)].start()

        @pl.when(i < 2)
        def _():
            grads(i, i)

    @pl.loop(2, 8)
    def _(i):
        @pl.when(i == 3)
        def _():
            sums["7"].wait_recv()
            join(6, 3)
            sums["6l"].start()
            sums["6h"].start()

        @pl.when(i == 7)
        def _():
            sums["6l"].wait_recv()
            part[4, low] = (part[4, low].astype(F32) + from_far[low].astype(F32)).astype(BF16)
            sums["4l"].start()
            sums["6h"].wait_recv()
            part[2, high] = (part[2, high].astype(F32) + from_far[high].astype(F32)).astype(BF16)
            sums["2h"].start()

        grads(i, i - 2)

    for t in range(ways):
        for j, (acc, first) in enumerate(
            ((gate_up_acc, t * unit), (gate_up_acc, units + t * unit), (down_acc, t * unit))
        ):
            row = (3 * t + j) * unit
            branch[row // rows, row % rows : row % rows + unit] = acc[first : first + unit].astype(BF16)
    grads_copy = pltpu.make_async_copy(branch.at[pl.ds(0, grads_ref.shape[0])], grads_ref, xsem)
    grads_copy.start()
    sums["1"].wait_recv()
    n_ref[...] = part[0].astype(F32) + from_sib[0].astype(F32)
    for name in ("2l", "2h", "4l", "4h"):
        sums[name].wait_recv()
    n_ref[...] += from_x[...].astype(F32) + from_y[...].astype(F32)
    for copy in (*copies.values(), *sums.values()):
        copy.wait_send()
    for i in range(8):
        out_copy(i).wait()
    grads_copy.wait()


def feed_plane(x, cot, weights):
    rows, d = x.shape
    ways = weights.shape[0]
    units = ways * weights.shape[1] // 3
    anywhere = pl.BlockSpec(memory_space=pl.ANY)
    inside = pl.BlockSpec(memory_space=pltpu.VMEM)
    return pl.pallas_call(
        feed_plane_kernel,
        in_specs=[anywhere, anywhere, anywhere],
        out_specs=[inside, anywhere, anywhere],
        out_shape=[
            jax.ShapeDtypeStruct((rows, d), F32),
            jax.ShapeDtypeStruct((8, rows, d), BF16),
            jax.ShapeDtypeStruct((3 * units // rows, rows, d), BF16),
        ],
        scratch_shapes=[
            pltpu.VMEM((2 * units, d), BF16),
            pltpu.VMEM((units, d), BF16),
            pltpu.VMEM((8, rows, d), BF16),
            pltpu.VMEM((8, rows, d), BF16),
            pltpu.VMEM((6, rows, units), BF16),
            pltpu.VMEM((6, rows, 2 * units), BF16),
            pltpu.VMEM((8, rows, d), BF16),
            pltpu.VMEM((4, rows, d), BF16),
            pltpu.VMEM((rows, d), BF16),
            pltpu.VMEM((rows, d), BF16),
            pltpu.VMEM((rows, d), BF16),
            pltpu.VMEM((units, d), F32),
            pltpu.VMEM((2 * units, d), F32),
            pltpu.SemaphoreType.DMA((8,)),
            pltpu.SemaphoreType.DMA((8,)),
            pltpu.SemaphoreType.DMA((10,)),
            pltpu.SemaphoreType.DMA((10,)),
            pltpu.SemaphoreType.DMA((8,)),
            pltpu.SemaphoreType.DMA((8,)),
            pltpu.SemaphoreType.DMA,
            pltpu.SemaphoreType.DMA((ways, 3)),
        ],
        compiler_params=pltpu.CompilerParams(
            collective_id=1, has_side_effects=True, vmem_limit_bytes=62 * MIB
        ),
        cost_estimate=pl.CostEstimate(
            flops=80 * 10**9, bytes_accessed=40 * rows * d, transcendentals=0
        ),
        name="feed_plane",
    )(x, cot, weights)


def tail_kernel(
    mixed_ref,
    w_ref,
    ffn_parts_ref,
    out_parts_ref,
    rows_ref,
    tok_ref,
    norm_ref,
    n_ref,
    ffn_ref,
    og_ref,
    ng_ref,
    lines,
    line_in,
    part,
    from_sib,
    from_far,
    from_x,
    from_y,
    mine,
    slices,
    ogs,
    norms,
    norms_z,
    qkv,
    usend,
    urecv,
    dsend,
    drecv,
    ssend,
    srecv,
    gsend,
    grecv,
    osend,
    orecv,
    nsend,
    nrecv,
    zsend,
    zrecv,
    load_sem,
):
    me, z = lax.axis_index("dp"), lax.axis_index("tensor")
    ways, rows = lines.shape[0], lines.shape[1]
    out_rows = slices.shape[1]
    qkv_rows = ogs.shape[1] - out_rows
    split = rows + ways * out_rows
    total = part.shape[1]
    width = w_ref.shape[2]
    half = total // 2
    low, high = pl.ds(0, half), pl.ds(half, half)
    sib, across, along = plane_peers()
    others = [{"tensor": lax.rem(z + k, ways)} for k in range(1, ways)]
    above, below = {"tensor": lax.rem(z + 1, ways)}, {"tensor": lax.rem(z + ways - 1, ways)}
    enter([sib, across, along] + others)

    loads = []
    for i in range(8):
        loads.append(
            (
                pltpu.make_async_copy(
                    ffn_parts_ref.at[i], part.at[i, pl.ds(0, rows)], load_sem.at[0, i]
                ),
                pltpu.make_async_copy(
                    out_parts_ref.at[lax.bitwise_xor(me, i)],
                    part.at[i, pl.ds(rows, ways * out_rows)],
                    load_sem.at[1, i],
                ),
            )
        )
        for load in loads[-1]:
            load.start()

    def line(i):
        b = jnp.where(z >= ways // 2, i, ways - 1 - i)
        step = min(256, rows)

        @pl.loop(0, rows // step)
        def _(k):
            at = pl.ds(pl.multiple_of(b * rows + k * step, step), step)
            lines[b, pl.ds(pl.multiple_of(k * step, step), step)] = sum(
                dot_nt(mixed_ref[at, j * width : (j + 1) * width], w_ref[j]) for j in range(3)
            ).astype(BF16)

    def up_copy(b):
        return remote(lines.at[b], line_in.at[b + 1], usend, urecv, b, above)

    def down_copy(b):
        return remote(lines.at[b], line_in.at[b], dsend, drecv, b, below)

    def line_round(r):
        b = r - (ways - 1 - z)

        @pl.when((b >= 0) & (b < z))
        def _():
            @pl.when(z < ways - 1)
            def _():
                down_copy(b).wait_recv()
                lines[b] = (lines[b].astype(F32) + line_in[b].astype(F32)).astype(BF16)

            down_copy(b).start()

        u = ways - 1 - (r - z)

        @pl.when((u > z) & (u <= ways - 1))
        def _():
            @pl.when(z > 0)
            def _():
                up_copy(u).wait_recv()
                lines[u] = (lines[u].astype(F32) + line_in[u + 1].astype(F32)).astype(BF16)

            up_copy(u).start()

    sums = [
        ("1", part.at[1], from_sib.at[0], sib),
        ("3", part.at[3], from_sib.at[1], sib),
        ("5", part.at[5], from_sib.at[2], sib),
        ("7", part.at[7], from_sib.at[3], sib),
        ("6l", part.at[6, low], from_far.at[low], across),
        ("6h", part.at[6, high], from_far.at[high], along),
        ("2l", part.at[2, low], from_x.at[low], across),
        ("2h", part.at[2, high], from_x.at[high], across),
        ("4l", part.at[4, low], from_y.at[low], along),
        ("4h", part.at[4, high], from_y.at[high], along),
    ]
    sums = {
        name: remote(src, dst, ssend, srecv, i, peer)
        for i, (name, src, dst, peer) in enumerate(sums)
    }

    def join(i, j):
        part[i] = (part[i].astype(F32) + from_sib[j].astype(F32)).astype(BF16)

    line(0)
    line_round(0)

    @pl.loop(0, 3)
    def _(j):
        at = pl.ds(pl.multiple_of(j * width, width), width)
        qkv[at, :] = dot_tn(mixed_ref[:, at], rows_ref[...]).astype(BF16)

    for i in range(8):
        at = pl.multiple_of(lax.bitwise_xor(me, i) * qkv_rows, 16)
        part[i, split:total] = qkv[pl.ds(at, qkv_rows), :]
    for i in (7, 3, 5, 1):
        for load in loads[i]:
            load.wait()
        sums[str(i)].start()

    @pl.loop(1, ways)
    def _(i):
        line(i)

    for i, j, names in ((6, 3, ("6l", "6h")), (2, 1, ("2l",)), (4, 2, ("4h",))):
        for load in loads[i]:
            load.wait()
        sums[str(i + 1)].wait_recv()
        join(i, j)
        for name in names:
            sums[name].start()
    line_round(1)
    sums["6l"].wait_recv()
    part[4, low] = (part[4, low].astype(F32) + from_far[low].astype(F32)).astype(BF16)
    sums["4l"].start()
    sums["6h"].wait_recv()
    part[2, high] = (part[2, high].astype(F32) + from_far[high].astype(F32)).astype(BF16)
    sums["2h"].start()
    for r in range(2, ways - 1):
        line_round(r)

    for load in loads[0]:
        load.wait()
    sums["1"].wait_recv()
    for name in ("2l", "2h", "4l", "4h"):
        sums[name].wait_recv()
    for at, out in ((slice(0, rows), ffn_ref), (slice(rows, total), mine)):
        out[...] = part[0, at].astype(F32) + from_sib[0, at].astype(F32)
        out[...] += from_x[at].astype(F32) + from_y[at].astype(F32)

    for t in range(ways):
        at = slice(t * out_rows, (t + 1) * out_rows)
        part[0, at] = mine[at].astype(BF16)

    def slice_copy(k, to, source):
        return pltpu.make_async_remote_copy(
            src_ref=part.at[0, pl.ds(pl.multiple_of(to * out_rows, 16), out_rows)],
            dst_ref=slices.at[source],
            send_sem=osend.at[k],
            recv_sem=orecv.at[source],
            device_id={"tensor": to},
            device_id_type=MESH_ID,
        )

    for k in range(1, ways):
        slice_copy(k, lax.rem(z + k, ways), z).start()
    own_slice = part[0, pl.ds(pl.multiple_of(z * out_rows, 16), out_rows)].astype(F32)
    for k in range(1, ways):
        source = lax.rem(z + k, ways)
        slice_copy(k, source, source).wait_recv()
        own_slice += slices[source].astype(F32)
    ogs[me, :out_rows] = own_slice.astype(BF16)
    ogs[me, out_rows:] = mine[ways * out_rows :].astype(BF16)
    view = lambda s, half: half_of(ogs.at[lax.bitwise_xor(me, s)], half)
    gathers = gather_copies(view, gsend, grecv, True)
    gather_start(gathers)
    gather_forward(gathers)
    gather_finish(gathers)
    og_ref[...] = ogs[...]

    n_ref[...] = lines[z].astype(F32)

    @pl.when(z < ways - 1)
    def _():
        down_copy(z).wait_recv()
        n_ref[...] += line_in[z].astype(F32)

    @pl.when(z > 0)
    def _():
        up_copy(z).wait_recv()
        n_ref[...] += line_in[z + 1].astype(F32)

    norms[0] = norm_ref[...]
    step = min(128, rows)

    @pl.loop(0, rows // step)
    def _(i):
        at = pl.ds(pl.multiple_of(i * step, step), step)
        values = tok_ref[at, :].astype(F32)
        centred = values - jnp.mean(values, axis=-1, keepdims=True)
        root = lax.rsqrt(jnp.mean(centred * centred, axis=-1, keepdims=True) + norm_eps)
        grad = n_ref[at, :]
        norms[0, 0:1] += jnp.sum(grad * (centred * root), axis=0, keepdims=True)
        norms[0, 1:2] += jnp.sum(grad, axis=0, keepdims=True)

    swaps = [
        remote(norms.at[i], norms.at[4 + i], nsend, nrecv, i, peer)
        for i, peer in enumerate((sib, across, along))
    ]
    for i, swap in enumerate(swaps):
        swap.start()
        swap.wait_recv()
        norms[i + 1] = norms[i] + norms[4 + i]

    def norm_copy(k, to, source):
        return pltpu.make_async_remote_copy(
            src_ref=norms.at[3],
            dst_ref=norms_z.at[source],
            send_sem=zsend.at[k],
            recv_sem=zrecv.at[source],
            device_id={"tensor": to},
            device_id_type=MESH_ID,
        )

    for k in range(1, ways):
        norm_copy(k, lax.rem(z + k, ways), z).start()
    norms_z[z] = norms[3]
    for k in range(1, ways):
        source = lax.rem(z + k, ways)
        norm_copy(k, source, source).wait_recv()
    ng_ref[...] = sum(norms_z[t] for t in range(ways))

    for copy in (*sums.values(), *gathers.values(), *swaps):
        copy.wait_send()
    for k in range(1, ways):
        to = lax.rem(z + k, ways)
        slice_copy(k, to, z).wait_send()
        norm_copy(k, to, z).wait_send()
    for b in range(ways):

        @pl.when(b < z)
        def _():
            down_copy(b).wait_send()

        @pl.when(b > z)
        def _():
            up_copy(b).wait_send()


def tail(mixed, w, ffn_parts, out_parts, rows_one, tokens, norm_grads, ways):
    rows, d = tokens.shape
    out_rows = out_parts.shape[1] // ways
    qkv_rows = mixed.shape[1] // 8
    total = rows + out_parts.shape[1] + qkv_rows
    both = out_rows + qkv_rows
    anywhere = pl.BlockSpec(memory_space=pl.ANY)
    inside = pl.BlockSpec(memory_space=pltpu.VMEM)
    sems = lambda n: [pltpu.SemaphoreType.DMA((n,))] * 2
    return pl.pallas_call(
        tail_kernel,
        in_specs=[inside, inside, anywhere, anywhere, inside, inside, inside],
        out_specs=[inside] * 4,
        out_shape=[
            jax.ShapeDtypeStruct((rows, d), F32),
            jax.ShapeDtypeStruct((rows, d), F32),
            jax.ShapeDtypeStruct((8, both, d), BF16),
            jax.ShapeDtypeStruct((8, d), F32),
        ],
        scratch_shapes=[
            pltpu.VMEM((ways, rows, d), BF16),
            pltpu.VMEM((ways + 1, rows, d), BF16),
            pltpu.VMEM((8, total, d), BF16),
            pltpu.VMEM((4, total, d), BF16),
            pltpu.VMEM((total, d), BF16),
            pltpu.VMEM((total, d), BF16),
            pltpu.VMEM((total, d), BF16),
            pltpu.VMEM((total - rows, d), F32),
            pltpu.VMEM((ways, out_rows, d), BF16),
            pltpu.VMEM((8, both, d), BF16),
            pltpu.VMEM((8, 8, d), F32),
            pltpu.VMEM((ways, 8, d), F32),
            pltpu.VMEM((mixed.shape[1], d), BF16),
        ]
        + sems(ways) * 2
        + sems(10)
        + sems(8)
        + sems(ways)
        + sems(3)
        + sems(ways)
        + [pltpu.SemaphoreType.DMA((2, 8))],
        compiler_params=pltpu.CompilerParams(
            collective_id=2, has_side_effects=True, vmem_limit_bytes=62 * MIB
        ),
        cost_estimate=pl.CostEstimate(
            flops=75 * 10**9, bytes_accessed=40 * rows * d, transcendentals=0
        ),
        name="tail",
    )(mixed, w, ffn_parts, out_parts, rows_one, tokens, norm_grads)


def spread_kernel(out_rows, both_ref, down_ref, rest_ref, gate_up_ref, down_out_ref, qkv_ref):
    units = both_ref.shape[1] // 2
    for p in range(8):
        turned = both_ref[p].astype(F32).T
        for g in range(2):
            at = pl.ds(2 * p + g, turned.shape[0], stride=16)
            gate_up_ref[at, :] = turned[:, g * units : (g + 1) * units]
    down_out_ref[...] = down_ref[0].astype(F32)
    features = rest_ref[:, out_rows:, :].reshape(-1, rest_ref.shape[2]).astype(F32)
    width = qkv_ref.shape[2]
    for j in range(3):
        qkv_ref[j] = features[j * width : (j + 1) * width].T


def spread(grads, rest, out_rows):
    d = grads.shape[2]
    units = grads.shape[1] // 3
    block = d // 8
    width = 8 * (rest.shape[1] - out_rows) // 3
    return pl.pallas_call(
        functools.partial(spread_kernel, out_rows),
        grid=(8,),
        in_specs=[
            pl.BlockSpec((8, 2 * units, block), lambda i: (0, 0, i)),
            pl.BlockSpec((1, units, d), lambda i: (i, 2, 0)),
            pl.BlockSpec((8, rest.shape[1], block), lambda i: (0, 0, i)),
        ],
        out_specs=[
            pl.BlockSpec((16 * block, units), lambda i: (i, 0)),
            pl.BlockSpec((units, d), lambda i: (i, 0)),
            pl.BlockSpec((3, block, width), lambda i: (0, i, 0)),
        ],
        out_shape=[
            jax.ShapeDtypeStruct((16 * d, units), F32),
            jax.ShapeDtypeStruct((8 * units, d), F32),
            jax.ShapeDtypeStruct((3, d, width), F32),
        ],
        compiler_params=pltpu.CompilerParams(vmem_limit_bytes=40 * MIB),
        name="spread",
    )(grads, grads, rest)


def shards(
    tokens,
    group_bucket,
    gain_one,
    shift_one,
    w_qkv,
    w_out,
    gain_two,
    shift_two,
    w_gate_up,
    w_down,
    cotangent,
):
    ways = lax.axis_size("tensor")
    replicas = lax.axis_size("dp")
    replica = lax.axis_index("dp")
    own_rows, d = tokens.shape
    group_rows = own_rows * ways
    local_width = w_out.shape[0]
    head_dim = d // HEADS
    hidden_width = w_down.shape[0]
    units = hidden_width // replicas
    fast = replicas == 8
    out_rows = local_width // replicas
    pair_width = min(128, local_width)
    pairs = local_width // pair_width

    rows_in = tokens.astype(F32)
    normed_one, unit_one, root_one = norm_forward(rows_in, gain_one, shift_one)
    normed_one_low = normed_one.astype(BF16)
    rows_one = lax.all_gather(normed_one_low, "tensor", axis=0, tiled=True)

    gate_up_slice = lax.dynamic_slice_in_dim(w_gate_up, replica * units, units, axis=2)
    down_slice = lax.dynamic_slice_in_dim(w_down, replica * units, units, axis=0)
    weight_slice = jnp.concatenate(
        [gate_up_slice.transpose(1, 2, 0).reshape(2 * units, d), down_slice]
    )
    weights = lax.all_gather(weight_slice, "tensor", axis=0)
    if fast:
        cot_rows, _ = lax.optimization_barrier((cotangent, normed_one_low))
        cot_all, out_full = gather_front(cot_rows, w_out, ways)
        cot_all, out_full, group_bucket, w_qkv = lax.optimization_barrier(
            (cot_all, out_full, group_bucket, w_qkv)
        )
        out_full = out_full.reshape(d, d)
    else:
        cot_all = lax.all_gather(cotangent, "dp", axis=0, tiled=True)
        out_full = lax.all_gather(w_out, "tensor", axis=0, tiled=True)

    cos_wide, sine_wide = rotary_wide(group_bucket[0], group_rows, head_dim, pair_width)
    qkv_weights = w_qkv.transpose(1, 0, 2)
    q, k, v, kt, vt = project(rows_one, qkv_weights, cos_wide, sine_wide, head_dim)
    attended = [attend(group_bucket, q, k, vt, head_dim, p, pair_width) for p in range(pairs)]
    attended_own = jnp.stack(
        [
            lax.all_to_all(a[0], "tensor", 0, 1, tiled=True).reshape(own_rows, ways, pair_width)
            for a in attended
        ],
        axis=2,
    ).reshape(own_rows, d)
    resid = rows_in + dot_nn(attended_own, out_full)

    normed_two, unit_two, root_two = norm_forward(resid, gain_two, shift_two)
    normed_two_low = normed_two.astype(BF16)
    if fast:
        normed_two_grad, ffn_parts, grads = feed_plane(normed_two_low, cot_all, weights)
        grads = grads.reshape(weights.shape)
    else:
        parts = weights.reshape(ways, 3, units, d)
        wgu = parts[:, :2].transpose(3, 1, 0, 2).reshape(d, 2 * ways * units)
        wd = parts[:, 2].reshape(ways * units, d)
        rows_two = lax.all_gather(normed_two_low, "dp", axis=0, tiled=True)
        hidden, branch, back = feed(rows_two, cot_all, wgu, wd)
        normed_two_grad = lax.psum_scatter(back, "dp", scatter_dimension=0, tiled=True).astype(F32)
        ffn_parts = dot_nn(hidden, wd).astype(BF16)
        grads = jnp.concatenate(
            [
                dot_tn(branch, rows_two).reshape(2, ways, units, d),
                dot_tn(hidden, cot_all).reshape(1, ways, units, d),
            ]
        )
        grads = grads.astype(BF16).transpose(1, 0, 2, 3).reshape(ways, 3 * units, d)
    grads = lax.psum_scatter(grads, "tensor", scatter_dimension=0)

    resid_part, gain_two_grad, shift_two_grad = norm_backward(
        normed_two_grad, unit_two, root_two, gain_two
    )
    resid_grad = cotangent.astype(F32) + resid_part
    attn_grad = resid_grad.astype(BF16)

    attended_grad_own = dot_nt(attn_grad, out_full).astype(BF16)
    attended_grad_own = attended_grad_own.reshape(own_rows, ways, pairs, pair_width)
    attended_grad = [
        lax.all_to_all(
            attended_grad_own[:, :, p].reshape(own_rows, ways * pair_width), "tensor", 1, 0, tiled=True
        )
        for p in range(pairs)
    ]
    out_grad = dot_tn(attended_own, attn_grad).astype(BF16).reshape(ways, replicas, out_rows, d)
    out_grad = out_grad.transpose(1, 0, 2, 3).reshape(replicas, ways * out_rows, d)
    back = [
        attend_back(
            group_bucket, q, k, kt, v, attended_grad[p], *attended[p][1:], head_dim, p, pair_width
        )
        for p in range(pairs)
    ]
    mixed_grad = unrotate(back, cos_wide, sine_wide, head_dim)
    grads = lax.all_gather(grads, "dp", axis=0)
    norm_grads = jnp.zeros((8, d), F32).at[2].set(gain_two_grad).at[3].set(shift_two_grad)
    if fast:
        normed_one_grad, ffn_out, rest, norm_grads = tail(
            mixed_grad, qkv_weights, ffn_parts, out_grad, rows_one, tokens, norm_grads, ways
        )
        gate_up_grad, down_grad, qkv_grad = spread(grads, rest, out_rows)
        out_grad = rest[:, :out_rows].reshape(local_width, d).astype(F32)
        gate_up_grad = gate_up_grad.reshape(d, replicas, 2, units).transpose(0, 2, 1, 3)
        gate_up_grad = gate_up_grad.reshape(d, 2, hidden_width)
        qkv_grad = qkv_grad.transpose(1, 0, 2)
    else:
        grads = grads.reshape(replicas, 3, units, d)
        down_grad = grads[:, 2].reshape(hidden_width, d).astype(F32)
        gate_up_grad = grads[:, :2].transpose(3, 1, 0, 2).reshape(d, 2, hidden_width).astype(F32)
        qkv_grad = lax.psum(dot_tn(rows_one, mixed_grad).astype(BF16), "dp").astype(F32)
        qkv_grad = qkv_grad.reshape(d, 3, local_width)
        flat = qkv_weights.transpose(1, 0, 2).reshape(d, 3 * local_width)
        normed_one_grad = lax.psum_scatter(
            dot_nt(mixed_grad, flat).astype(BF16), "tensor", scatter_dimension=0, tiled=True
        ).astype(F32)
        ffn_out = lax.psum_scatter(ffn_parts, "dp", scatter_dimension=0, tiled=True).astype(F32)
        out_grad = lax.psum_scatter(out_grad, "dp", scatter_dimension=0)
        out_grad = lax.psum_scatter(out_grad, "tensor", scatter_dimension=0, tiled=True)
        out_grad = lax.all_gather(out_grad, "dp", axis=0, tiled=True).astype(F32)
        one = norm_backward(normed_one_grad, unit_one, root_one, gain_one)
        norm_grads = norm_grads.at[0].set(one[1]).at[1].set(one[2])
        norm_grads = lax.psum(norm_grads, ("dp", "tensor"))
    layer_out = (resid + ffn_out).astype(BF16)
    token_grad = resid_grad + norm_backward(normed_one_grad, unit_one, root_one, gain_one)[0]
    gain_one_grad, shift_one_grad, gain_two_grad, shift_two_grad = (norm_grads[i] for i in range(4))
    return (
        layer_out,
        token_grad,
        gain_one_grad,
        shift_one_grad,
        qkv_grad,
        out_grad,
        gain_two_grad,
        shift_two_grad,
        gate_up_grad,
        down_grad,
    )


def solution(mesh):
    in_specs = (
        P(("dp", "tensor"), None),
        P("dp"),
        P(),
        P(),
        P(None, None, "tensor"),
        P("tensor", None),
        P(),
        P(),
        P(None, None, "tensor"),
        P("tensor", None),
        P(("dp", "tensor"), None),
    )
    out_specs = (
        P(("dp", "tensor"), None),
        P(("dp", "tensor"), None),
        P(),
        P(),
        P(None, None, "tensor"),
        P("tensor", None),
        P(),
        P(),
        P(None, None, "tensor"),
        P("tensor", None),
    )
    return jax.shard_map(shards, mesh=mesh, in_specs=in_specs, out_specs=out_specs, check_vma=False)
```

```python
import functools

import jax
import jax.numpy as jnp
from jax import lax
from jax.experimental import pallas as pl
from jax.experimental.pallas import tpu as pltpu
from jax.sharding import PartitionSpec as P

HEADS = 16
LONG_LEN = 2048
SHORT_LEN = 1000

norm_eps = 1e-05
mask_fill = -1e30
rope_base = 10000.0
VMEM_LIMIT = 62 * 2**20
F32 = jnp.float32
BF16 = jnp.bfloat16


def dot_nn(a, b):
    return jnp.dot(a, b, preferred_element_type=F32)


def dot_nt(a, b):
    return lax.dot_general(a, b, (((1,), (1,)), ((), ())), preferred_element_type=F32)


def dot_tn(a, b):
    return lax.dot_general(a, b, (((0,), (0,)), ((), ())), preferred_element_type=F32)


def rotary_wide(bucket_id, group_rows, head_dim, width):
    positions = jnp.arange(group_rows, dtype=jnp.int32)
    span_len = jnp.where(bucket_id == 1, LONG_LEN, SHORT_LEN).astype(jnp.int32)
    places = positions - (positions // span_len) * span_len
    half_dim = head_dim // 2
    exponents = jnp.arange(half_dim, dtype=F32) * (-2.0 / head_dim)
    freqs = jnp.exp(exponents * jnp.log(F32(rope_base)))
    heads = width // head_dim
    signs = jnp.tile(jnp.repeat(jnp.array([-1.0, 1.0], F32), half_dim), heads)
    angles = places.astype(F32)[:, None] * jnp.tile(freqs, 2 * heads)[None, :]
    return jnp.cos(angles), jnp.sin(angles) * signs


def norm_forward(values, gain, shift):
    average = jnp.mean(values, axis=-1, keepdims=True)
    centred = values - average
    spread_sq = jnp.mean(centred * centred, axis=-1, keepdims=True)
    inv_root = lax.rsqrt(spread_sq + norm_eps)
    unit_rows = centred * inv_root
    return (unit_rows * gain + shift, unit_rows, inv_root)


def norm_backward(out_grad_rows, unit_rows, inv_root, gain):
    scaled = out_grad_rows * gain
    first_mean = jnp.mean(scaled, axis=-1, keepdims=True)
    second_mean = jnp.mean(scaled * unit_rows, axis=-1, keepdims=True)
    in_grad = inv_root * (scaled - first_mean - unit_rows * second_mean)
    return (in_grad, jnp.sum(out_grad_rows * unit_rows, axis=0), jnp.sum(out_grad_rows, axis=0))


def swap_halves(x, head_dim):
    half = head_dim // 2
    width = x.shape[1]
    lane = lax.broadcasted_iota(jnp.int32, x.shape, 1) % head_dim
    return jnp.where(lane < half, pltpu.roll(x, width - half, 1), pltpu.roll(x, half, 1))


def head_mask(x, h, head_dim):
    lane = lax.broadcasted_iota(jnp.int32, x.shape, 1)
    return jnp.where((lane >= h * head_dim) & (lane < (h + 1) * head_dim), x, jnp.zeros_like(x))


def widen(table, width):
    return jnp.concatenate([table] * (width // table.shape[1]), axis=1)


def project_kernel(head_dim, x_ref, w_ref, cos_ref, sin_ref, q_ref, k_ref, v_ref, kt_ref, vt_ref):
    width = q_ref.shape[1]
    x = x_ref[...]
    cos, sin = widen(cos_ref[...], width), widen(sin_ref[...], width)
    q, k, v = (dot_nn(x, w_ref[j]) for j in range(3))
    v = v.astype(BF16)
    q = q * cos + swap_halves(q, head_dim) * sin
    k = k * cos + swap_halves(k, head_dim) * sin
    k_low = k.astype(BF16)
    q_ref[...] = (q.astype(BF16).astype(F32) * head_dim ** (-0.5)).astype(BF16)
    k_ref[...] = k_low
    v_ref[...] = v
    kt_ref[...] = k_low.T
    vt_ref[...] = v.T


def project(rows, w, cos_wide, sine_wide, head_dim):
    n, d = rows.shape
    width = w.shape[2]
    block = min(512, n)
    row = pl.BlockSpec((block, width), lambda i: (i, 0))
    col = pl.BlockSpec((width, block), lambda i: (0, i))
    table = pl.BlockSpec((block, cos_wide.shape[1]), lambda i: (i, 0))
    return pl.pallas_call(
        functools.partial(project_kernel, head_dim),
        grid=(n // block,),
        in_specs=[
            pl.BlockSpec((block, d), lambda i: (i, 0)),
            pl.BlockSpec((3, d, width), lambda i: (0, 0, 0)),
            table,
            table,
        ],
        out_specs=[row, row, row, col, col],
        out_shape=[jax.ShapeDtypeStruct((n, width), BF16)] * 3
        + [jax.ShapeDtypeStruct((width, n), BF16)] * 2,
        compiler_params=pltpu.CompilerParams(vmem_limit_bytes=VMEM_LIMIT),
        cost_estimate=pl.CostEstimate(
            flops=6 * n * d * width, bytes_accessed=2 * n * d + 18 * n * width, transcendentals=0
        ),
        name="project",
    )(rows, w, cos_wide, sine_wide)


def key_range(start, block, total):
    first = (start // SHORT_LEN) * SHORT_LEN
    last = min(total, ((start + block - 1) // SHORT_LEN + 1) * SHORT_LEN)
    return (first // 256) * 256, min(total, -(-last // 256) * 256)


def window_bias(key_start, keys, row_start, rows, total):
    key_at = lax.broadcasted_iota(jnp.int32, (keys, rows), 0) + key_start
    row_at = lax.broadcasted_iota(jnp.int32, (keys, rows), 1) + row_start
    key_window = jnp.zeros_like(key_at)
    row_window = jnp.zeros_like(row_at)
    for edge in range(SHORT_LEN, total, SHORT_LEN):
        key_window += (key_at >= edge).astype(jnp.int32)
        row_window += (row_at >= edge).astype(jnp.int32)
    return jnp.where(key_window == row_window, 0.0, mask_fill)


def attend_kernel(head_dim, bucket_ref, q_ref, k_ref, vt_ref, o_ref, ot_ref, l_ref, bias_ref):
    rows, width = q_ref.shape
    total = k_ref.shape[0]
    heads = width // head_dim
    step = pl.program_id(0)

    def block(at, first, last, masked):
        @pl.loop(0, heads)
        def _(h):
            hs = pl.ds(pl.multiple_of(h * head_dim, head_dim), head_dim)
            scores = dot_nt(k_ref[first:last, :], head_mask(q_ref[at, :], h, head_dim))
            if masked:
                scores = scores + bias_ref[: last - first, :]
            top = jnp.max(scores, axis=0, keepdims=True)
            weights = jnp.exp(scores - top)
            totals = jnp.sum(weights, axis=0, keepdims=True)
            ot_ref[hs, at] = dot_nn(vt_ref[hs, first:last], weights.astype(BF16)) / totals
            l_ref[pl.ds(h, 1), at] = top + jnp.log(totals)

    @pl.when(bucket_ref[0] == 1)
    def _():
        block(slice(0, rows), 0, total, False)

    sub = bias_ref.shape[1]
    for start in range(0, total, sub):
        first, last = key_range(start, sub, total)

        @pl.when((bucket_ref[0] != 1) & (step == start // rows))
        def _():
            bias_ref[: last - first, :] = window_bias(first, last - first, start, sub, total)
            block(slice(start % rows, start % rows + sub), first, last, True)

    o_ref[...] = ot_ref[...].T.astype(BF16)


def attend(bucket, q, k, vt, head_dim):
    n, width = q.shape
    heads = width // head_dim
    block = min(1024, n)
    pairs = n * n * heads
    lanes = -(-heads // 8) * 8
    row = pl.BlockSpec((block, width), lambda i, *_: (i, 0))
    col = pl.BlockSpec((width, block), lambda i, *_: (0, i))
    return pl.pallas_call(
        functools.partial(attend_kernel, head_dim),
        grid_spec=pltpu.PrefetchScalarGridSpec(
            num_scalar_prefetch=1,
            grid=(n // block,),
            in_specs=[
                row,
                pl.BlockSpec((n, width), lambda i, *_: (0, 0)),
                pl.BlockSpec((width, n), lambda i, *_: (0, 0)),
            ],
            out_specs=[row, col, pl.BlockSpec((lanes, block), lambda i, *_: (0, i))],
            scratch_shapes=[pltpu.VMEM((n, min(512, block)), F32)],
        ),
        out_shape=[
            jax.ShapeDtypeStruct((n, width), BF16),
            jax.ShapeDtypeStruct((width, n), F32),
            jax.ShapeDtypeStruct((lanes, n), F32),
        ],
        compiler_params=pltpu.CompilerParams(vmem_limit_bytes=VMEM_LIMIT),
        cost_estimate=pl.CostEstimate(
            flops=pairs * 1024, bytes_accessed=10 * n * width, transcendentals=pairs
        ),
        name="attend",
    )(bucket, q, k, vt)


def attend_back_kernel(
    head_dim,
    bucket_ref,
    q_ref,
    k_ref,
    kt_ref,
    v_ref,
    g_ref,
    ot_ref,
    l_ref,
    cos_ref,
    sin_ref,
    out_ref,
    bias_ref,
    gt_ref,
    dq_ref,
    dk_ref,
    dv_ref,
):
    rows, width = q_ref.shape
    total = k_ref.shape[0]
    heads = width // head_dim
    step = pl.program_id(0)

    @pl.when(step == 0)
    def _():
        dk_ref[...] = jnp.zeros_like(dk_ref)
        dv_ref[...] = jnp.zeros_like(dv_ref)

    gt_ref[...] = g_ref[...].astype(F32).T * ot_ref[...]

    def block(first, last, masked):
        keys = slice(first, last)

        @pl.loop(0, heads)
        def _(h):
            hs = pl.ds(pl.multiple_of(h * head_dim, head_dim), head_dim)
            qh, gh = head_mask(q_ref[...], h, head_dim), head_mask(g_ref[...], h, head_dim)
            scores = dot_nt(k_ref[keys, :], qh)
            if masked:
                scores = scores + bias_ref[: last - first, :]
            probs = jnp.exp(scores - l_ref[pl.ds(h, 1), :])
            prob_grad = dot_nt(v_ref[keys, :], gh)
            delta = jnp.sum(gt_ref[hs, :], axis=0, keepdims=True)
            score_grad = (probs * (prob_grad - delta)).astype(BF16)
            dv_ref[keys, :] += dot_nn(probs.astype(BF16), gh)
            dk_ref[keys, :] += dot_nn(score_grad, qh)
            dq_ref[hs, :] = dot_nn(kt_ref[hs, keys], score_grad)

    @pl.when(bucket_ref[0] == 1)
    def _():
        block(0, total, False)

    for start in range(0, total, rows):
        first, last = key_range(start, rows, total)

        @pl.when((bucket_ref[0] != 1) & (step == start // rows))
        def _():
            bias_ref[: last - first, :] = window_bias(first, last - first, start, rows, total)
            block(first, last, True)

    def turn_back(grad, at):
        cos, sin = widen(cos_ref[at, :], width), widen(sin_ref[at, :], width)
        return (grad * cos - swap_halves(grad, head_dim) * sin).astype(BF16)

    at = pl.ds(pl.multiple_of(step * rows, rows), rows)
    out_ref[at, :width] = turn_back(dq_ref[...].T * head_dim ** (-0.5), at)

    @pl.when(step == pl.num_programs(0) - 1)
    def _():
        @pl.loop(0, total // rows)
        def _(i):
            at = pl.ds(pl.multiple_of(i * rows, rows), rows)
            out_ref[at, width : 2 * width] = turn_back(dk_ref[at, :], at)
            out_ref[at, 2 * width :] = dv_ref[at, :].astype(BF16)


def attend_back(bucket, q, k, kt, v, g, ot, log_totals, cos_wide, sine_wide, head_dim):
    n, width = q.shape
    heads = width // head_dim
    block = min(512, n)
    pairs = n * n * heads
    row = pl.BlockSpec((block, width), lambda i, *_: (i, 0))
    col = pl.BlockSpec((width, block), lambda i, *_: (0, i))
    full = lambda rows, cols: pl.BlockSpec((rows, cols), lambda i, *_: (0, 0))
    table = full(n, cos_wide.shape[1])
    return pl.pallas_call(
        functools.partial(attend_back_kernel, head_dim),
        grid_spec=pltpu.PrefetchScalarGridSpec(
            num_scalar_prefetch=1,
            grid=(n // block,),
            in_specs=[
                row,
                full(n, width),
                full(width, n),
                full(n, width),
                row,
                col,
                pl.BlockSpec((log_totals.shape[0], block), lambda i, *_: (0, i)),
                table,
                table,
            ],
            out_specs=full(n, 3 * width),
            scratch_shapes=[
                pltpu.VMEM((n, block), F32),
                pltpu.VMEM((width, block), F32),
                pltpu.VMEM((width, block), F32),
                pltpu.VMEM((n, width), F32),
                pltpu.VMEM((n, width), F32),
            ],
        ),
        out_shape=jax.ShapeDtypeStruct((n, 3 * width), BF16),
        compiler_params=pltpu.CompilerParams(vmem_limit_bytes=VMEM_LIMIT),
        cost_estimate=pl.CostEstimate(
            flops=pairs * 2560, bytes_accessed=24 * n * width, transcendentals=pairs
        ),
        name="attend_back",
    )(bucket, q, k, kt, v, g, ot, log_totals, cos_wide, sine_wide)


def feed_kernel(x_ref, c_ref, wgu_ref, wd_ref, h_ref, b_ref, n_ref):
    units = wd_ref.shape[0]
    both = dot_nn(x_ref[...], wgu_ref[...])
    gate, up = both[:, :units], both[:, units:]
    sig = jax.nn.sigmoid(gate)
    silu = gate * sig
    h_ref[...] = (silu * up).astype(BF16)
    hidden_grad = dot_nt(c_ref[...], wd_ref[...])
    b_ref[:, :units] = (hidden_grad * up * sig * (1.0 + gate * (1.0 - sig))).astype(BF16)
    b_ref[:, units:] = (hidden_grad * silu).astype(BF16)
    n_ref[...] = dot_nt(b_ref[...], wgu_ref[...]).astype(BF16)


def feed(x, cot, wgu, wd):
    n, d = x.shape
    units = wd.shape[0]
    block = min(256, n)
    row = lambda w: pl.BlockSpec((block, w), lambda i: (i, 0))
    return pl.pallas_call(
        feed_kernel,
        grid=(n // block,),
        in_specs=[
            row(d),
            row(d),
            pl.BlockSpec((d, 2 * units), lambda i: (0, 0)),
            pl.BlockSpec((units, d), lambda i: (0, 0)),
        ],
        out_specs=[row(units), row(2 * units), row(d)],
        out_shape=[
            jax.ShapeDtypeStruct((n, units), BF16),
            jax.ShapeDtypeStruct((n, 2 * units), BF16),
            jax.ShapeDtypeStruct((n, d), BF16),
        ],
        compiler_params=pltpu.CompilerParams(vmem_limit_bytes=VMEM_LIMIT),
        cost_estimate=pl.CostEstimate(
            flops=10 * n * d * units, bytes_accessed=8 * n * d, transcendentals=n * units
        ),
        name="feed",
    )(x, cot, wgu, wd)


MESH_ID = pl.DeviceIdType.MESH


def plane_peers():
    me = lax.axis_index("dp")
    return [{"dp": lax.bitwise_xor(me, bit)} for bit in (1, 2, 4)]


def enter(peers):
    barrier = pltpu.get_barrier_semaphore()
    for peer in peers:
        pl.semaphore_signal(barrier, inc=1, device_id=peer, device_id_type=MESH_ID)
    pl.semaphore_wait(barrier, len(peers))


def remote(src, dst, send, recv, at, peer):
    return pltpu.make_async_remote_copy(
        src_ref=src,
        dst_ref=dst,
        send_sem=send.at[at],
        recv_sem=recv.at[at],
        device_id=peer,
        device_id_type=MESH_ID,
    )


def gather_copies(view, send, recv, placed, cores=True):
    sib, across, along = plane_peers()
    steps = [
        (0, 1, sib, None),
        (0, 2, across, None),
        (0, 4, along, None),
        (4, 2, across, 0),
        (2, 4, along, 1),
        (2, 1, sib, None),
        (4, 1, sib, None),
        (6, 1, sib, None),
    ]
    copies = {}
    for i, (s, bit, peer, part) in enumerate(steps):
        if bit == 1 and not cores:
            continue
        src = view(s, part)
        dst = src if placed else view(s ^ bit, part)
        copies[f"{s}-{s ^ bit}"] = remote(src, dst, send, recv, i, peer)
    return copies


def half_of(ref, part):
    if part is None:
        return ref
    half = ref.shape[-2] // 2
    return ref.at[(slice(None),) * (len(ref.shape) - 2) + (pl.ds(part * half, half),)]


def gather_start(copies):
    for name in ("0-2", "0-4", "0-1"):
        copies[name].start()


def gather_forward(copies):
    copies["0-2"].wait_recv()
    copies["2-6"].start()
    copies["2-3"].start()
    copies["0-4"].wait_recv()
    copies["4-6"].start()
    copies["4-5"].start()


def gather_finish(copies):
    copies["2-6"].wait_recv()
    copies["4-6"].wait_recv()
    copies["6-7"].start()
    for name in ("0-1", "2-3", "4-5", "6-7"):
        copies[name].wait_recv()


def head_share():
    core, z = lax.rem(lax.axis_index("dp"), 2), lax.axis_index("tensor")
    return core, 2 * lax.rem(z, 2) + core, z // 2


def head_source(s):
    return s % 2, 2 * lax.rem(lax.axis_index("dp"), 2) + s // 2


def front_kernel(
    head_dim,
    bucket_ref,
    tok_ref,
    gain_ref,
    shift_ref,
    freq_ref,
    cot_ref,
    wo_ref,
    wq_ref,
    q_ref,
    k_ref,
    v_ref,
    kt_ref,
    vt_ref,
    cos_ref,
    sin_ref,
    bucket_out,
    rows_out,
    cots_out,
    wos_out,
    wq_out,
    rows_all,
    mine,
    other,
    cots,
    wos,
    wq,
    buckets,
    nsend,
    nrecv,
    csend,
    crecv,
    wsend,
    wrecv,
    qsend,
    qrecv,
    zsend,
    zrecv,
    psend,
    precv,
    bsend,
    brecv,
    local,
):
    ways, rows, d = rows_all.shape
    half = rows // 2
    out_rows = wos.shape[2]
    width = q_ref.shape[1]
    me, z = lax.axis_index("dp"), lax.axis_index("tensor")
    core, heads_of, group_of = head_share()
    sib, across, along = plane_peers()
    others = [{"tensor": lax.rem(z + k, ways)} for k in range(1, ways)]
    z1, z2, z3 = (lax.bitwise_xor(z, k) for k in (1, 2, 3))
    near, far = {"tensor": z1}, {"tensor": z2}
    chip_rows = wq.shape[1] // 4
    enter([sib, across, along] + others)

    buckets[0] = jnp.full(buckets.shape[1:], bucket_ref[0], jnp.int32)
    bucket_copy = remote(buckets.at[0], buckets.at[1], bsend, brecv, 0, sib)
    bucket_copy.start()
    loads = [
        pltpu.make_async_copy(cot_ref.at[pl.ds(0, half)], cots.at[0], local.at[0]),
        pltpu.make_async_copy(
            wo_ref.at[pl.ds(pl.multiple_of(me * out_rows, 16), out_rows)],
            wos.at[z, me],
            local.at[1],
        ),
    ]
    for load in loads:
        load.start()

    def chip_part(chip, part):
        size = chip_rows if part is None else chip_rows // 2
        first = chip * chip_rows + (0 if part is None else part * size)
        return wq.at[:, pl.ds(pl.multiple_of(first, 16), size)]

    chip = me // 2
    chip_src = wq_ref.at[:, pl.ds(pl.multiple_of(chip * chip_rows, 16), chip_rows)]
    gives = core == lax.rem(z, 2)

    def piece_copy(k):
        return pltpu.make_async_remote_copy(
            src_ref=chip_src,
            dst_ref=chip_part(chip, None),
            send_sem=psend.at[k],
            recv_sem=precv.at[0],
            device_id={"tensor": z // 2 + 2 * k},
            device_id_type=MESH_ID,
        )

    piece_own = pltpu.make_async_copy(chip_src, chip_part(chip, None), local.at[2])
    for k in range(2):

        @pl.when(gives & (z // 2 + 2 * k != z))
        def _():
            piece_copy(k).start()

    @pl.when(heads_of == z)
    def _():
        piece_own.start()

    cot_copies = gather_copies(
        lambda s, part: half_of(cots.at[s], part), csend, crecv, False
    )
    loads[0].wait()
    gather_start(cot_copies)

    step = 128

    @pl.loop(0, rows // step)
    def _(i):
        at = pl.ds(pl.multiple_of(i * step, step), step)
        values = tok_ref[at, :].astype(F32)
        centred = values - jnp.mean(values, axis=-1, keepdims=True)
        root = lax.rsqrt(jnp.mean(centred * centred, axis=-1, keepdims=True) + norm_eps)
        mine[at, :] = (centred * root * gain_ref[...] + shift_ref[...]).astype(BF16)

    def part_of(which):
        return pl.ds(pl.multiple_of(which * half, half), half)

    def rows_at(block, which):
        return rows_all.at[block, part_of(which)]

    home = group_of == core
    give = [
        remote(mine.at[part_of(1 - core)], rows_at(z, 1 - core), nsend, nrecv, 0, sib),
        remote(mine.at[part_of(core)], rows_at(z, core), nsend, nrecv, 1, sib),
    ]
    swap = remote(mine.at[part_of(1 - core)], other, nsend, nrecv, 0, sib)
    to_far = remote(other, rows_at(z, core), nsend, nrecv, 2, far)
    to_near = remote(rows_at(z, core), rows_at(z, core), nsend, nrecv, 3, near)
    relay = remote(rows_at(z2, core), rows_at(z2, core), nsend, nrecv, 4, near)
    shares = {
        b: remote(rows_at(block, core), rows_at(block, core), nsend, nrecv, 4 + b, sib)
        for b, block in ((1, z1), (2, z2), (3, z3))
    }

    @pl.when(home)
    def _():
        give[0].start()
        give[1].start()
        rows_all[z] = mine[...]
        swap.wait_recv()
        to_far.start()
        to_near.start()

    @pl.when(jnp.logical_not(home))
    def _():
        swap.start()
        other[...] = mine[part_of(core), :]
        to_far.start()
        give[0].wait_recv()
        to_near.start()

    loads[1].wait()
    out_sends = []
    for k, peer in enumerate(others):
        slice_ref = wos.at[z, me]
        out_sends.append(
            pltpu.make_async_remote_copy(
                src_ref=slice_ref,
                dst_ref=slice_ref,
                send_sem=zsend.at[k],
                recv_sem=zrecv.at[z],
                device_id=peer,
                device_id_type=MESH_ID,
            )
        )
        out_sends[-1].start()

    qkv_copies = gather_copies(
        lambda s, part: chip_part(lax.bitwise_xor(chip, s // 2), part), qsend, qrecv, True, False
    )
    out_copies = gather_copies(
        lambda s, part: half_of(wos.at[:, lax.bitwise_xor(me, s)], part), wsend, wrecv, True
    )

    @pl.when(heads_of == z)
    def _():
        piece_own.wait()

    @pl.when(heads_of != z)
    def _():
        piece_copy(0).wait_recv()

    qkv_copies["0-2"].start()
    qkv_copies["0-4"].start()
    gather_forward(cot_copies)

    bucket_copy.wait_recv()
    bucket = jnp.where(home, buckets[0], buckets[1])
    bucket_out[...] = bucket
    span = jnp.where(bucket[0:1] == 1, LONG_LEN, SHORT_LEN)
    freq = freq_ref[...]
    lane = lax.broadcasted_iota(jnp.int32, freq.shape, 1)
    sign = jnp.where(lax.rem(lane, head_dim) < head_dim // 2, -1.0, 1.0)
    total = ways * rows

    @pl.loop(0, total // step)
    def _(i):
        at = pl.ds(pl.multiple_of(i * step, step), step)
        position = lax.broadcasted_iota(jnp.int32, (step, freq.shape[1]), 0) + i * step
        place = position
        for k in range(1, -(-total // SHORT_LEN)):
            place = place - jnp.where(position >= k * span, span, 0)
        angles = place.astype(F32) * freq
        cos_ref[at, :] = jnp.cos(angles)
        sin_ref[at, :] = jnp.sin(angles) * sign

    to_far.wait_recv()
    relay.start()
    shares[2].start()
    to_near.wait_recv()
    shares[1].start()
    qkv_copies["0-2"].wait_recv()
    qkv_copies["2-6"].start()
    qkv_copies["0-4"].wait_recv()
    qkv_copies["4-6"].start()
    for k, peer in enumerate(others):
        source = lax.rem(z + k + 1, ways)
        theirs = wos.at[source, me]
        pltpu.make_async_remote_copy(
            src_ref=theirs,
            dst_ref=theirs,
            send_sem=zsend.at[k],
            recv_sem=zrecv.at[source],
            device_id=peer,
            device_id_type=MESH_ID,
        ).wait_recv()
    gather_start(out_copies)
    qkv_copies["2-6"].wait_recv()
    qkv_copies["4-6"].wait_recv()
    wq_copy = pltpu.make_async_copy(wq, wq_out, local.at[0])
    wq_copy.start()

    @pl.when(jnp.logical_not(home))
    def _():
        give[1].wait_recv()

    @pl.loop(0, ways)
    def _(i):
        @pl.when(i == 1)
        def _():
            shares[1].wait_recv()

        @pl.when(i == 2)
        def _():
            shares[2].wait_recv()
            gather_forward(out_copies)

        @pl.when(i == 3)
        def _():
            relay.wait_recv()
            shares[3].start()
            shares[3].wait_recv()

        block = lax.bitwise_xor(z, i)
        at = pl.ds(pl.multiple_of(block * rows, rows), rows)
        x = rows_all[block]
        cos, sin = widen(cos_ref[at, :], width), widen(sin_ref[at, :], width)
        q, k, v = (dot_nn(x, wq[j]) for j in range(3))
        v = v.astype(BF16)
        q = q * cos + swap_halves(q, head_dim) * sin
        k = (k * cos + swap_halves(k, head_dim) * sin).astype(BF16)
        q_ref[at, :] = (q.astype(BF16).astype(F32) * head_dim ** (-0.5)).astype(BF16)
        k_ref[at, :] = k
        v_ref[at, :] = v
        kt_ref[:, at] = k.T
        vt_ref[:, at] = v.T

    gather_finish(cot_copies)
    gather_finish(out_copies)
    stores = [
        wq_copy,
        pltpu.make_async_copy(rows_all, rows_out, local.at[1]),
        pltpu.make_async_copy(cots, cots_out, local.at[2]),
        pltpu.make_async_copy(wos, wos_out, local.at[3]),
    ]
    for store in stores[1:]:
        store.start()
    for store in stores:
        store.wait()

    @pl.when(home)
    def _():
        give[0].wait_send()
        give[1].wait_send()

    @pl.when(jnp.logical_not(home))
    def _():
        swap.wait_send()

    for k in range(2):

        @pl.when(gives & (z // 2 + 2 * k != z))
        def _():
            piece_copy(k).wait_send()

    for copy in (to_far, to_near, relay, bucket_copy, *shares.values(), *out_sends):
        copy.wait_send()
    for copy in (*qkv_copies.values(), *cot_copies.values(), *out_copies.values()):
        copy.wait_send()


def front(bucket, tokens, gain, shift, cot, w_out, w_qkv, head_dim, ways):
    rows, d = tokens.shape
    width = w_qkv.shape[2]
    out_rows = w_out.shape[0] // 8
    total = ways * rows
    lanes = 128
    half_dim = head_dim // 2
    exponents = jnp.arange(half_dim, dtype=F32) * (-2.0 / head_dim)
    freq = jnp.tile(jnp.exp(exponents * jnp.log(F32(rope_base))), lanes // half_dim)[None]
    anywhere = pl.BlockSpec(memory_space=pl.ANY)
    inside = pl.BlockSpec(memory_space=pltpu.VMEM)
    sems = lambda n: [pltpu.SemaphoreType.DMA((n,))] * 2
    shape = jax.ShapeDtypeStruct
    return pl.pallas_call(
        functools.partial(front_kernel, head_dim),
        in_specs=[pl.BlockSpec(memory_space=pltpu.SMEM)] + [inside] * 4 + [anywhere] * 3,
        out_specs=[inside] * 8 + [anywhere] * 4,
        out_shape=[
            shape((total, width), BF16),
            shape((total, width), BF16),
            shape((total, width), BF16),
            shape((width, total), BF16),
            shape((width, total), BF16),
            shape((total, lanes), F32),
            shape((total, lanes), F32),
            shape((8, lanes), jnp.int32),
            shape((ways, rows, d), BF16),
            shape((8, rows // 2, d), BF16),
            shape((ways, 8, out_rows, d), BF16),
            shape(w_qkv.shape, BF16),
        ],
        scratch_shapes=[
            pltpu.VMEM((ways, rows, d), BF16),
            pltpu.VMEM((rows, d), BF16),
            pltpu.VMEM((rows // 2, d), BF16),
            pltpu.VMEM((8, rows // 2, d), BF16),
            pltpu.VMEM((ways, 8, out_rows, d), BF16),
            pltpu.VMEM(w_qkv.shape, BF16),
            pltpu.VMEM((2, 8, lanes), jnp.int32),
        ]
        + sems(8)
        + sems(8)
        + sems(8)
        + sems(8)
        + sems(ways)
        + sems(2)
        + sems(1)
        + [pltpu.SemaphoreType.DMA((4,))],
        compiler_params=pltpu.CompilerParams(
            collective_id=0, has_side_effects=True, vmem_limit_bytes=VMEM_LIMIT
        ),
        cost_estimate=pl.CostEstimate(
            flops=55 * 10**9, bytes_accessed=32 * rows * d, transcendentals=0
        ),
        name="front",
    )(bucket, tokens, gain[None], shift[None], freq, cot, w_out, w_qkv)


def column(ways):
    me, z = lax.axis_index("dp"), lax.axis_index("tensor")
    sib = lax.bitwise_xor(me, 1)
    others = [{"dp": sib, "tensor": z}]
    for k in range(1, ways):
        to = lax.rem(z + k, ways)
        others += [{"dp": me, "tensor": to}, {"dp": sib, "tensor": to}]
    return others


def collect_kernel(
    att_ref,
    tok_ref,
    wo_ref,
    gain_ref,
    shift_ref,
    cot_ref,
    at_ref,
    resid_ref,
    n_ref,
    cots_out,
    at,
    cots,
    isend,
    irecv,
    csend,
    crecv,
    lsem,
):
    ways, rows, quarter = at.shape
    me, z = lax.axis_index("dp"), lax.axis_index("tensor")
    core, heads_of, group_of = head_share()
    enter(column(ways) + plane_peers()[1:])
    half = rows // 2
    cot_own = pltpu.make_async_copy(cot_ref.at[pl.ds(half, half)], cots.at[0], lsem.at[1])
    cot_own.start()

    def in_copy(to):
        return pltpu.make_async_remote_copy(
            src_ref=att_ref.at[pl.ds(pl.multiple_of(to * rows, rows), rows)],
            dst_ref=at.at[heads_of],
            send_sem=isend.at[to],
            recv_sem=irecv.at[heads_of],
            device_id={"dp": me - core + group_of, "tensor": to},
            device_id_type=MESH_ID,
        )

    def in_wait(s):
        return pltpu.make_async_remote_copy(
            src_ref=att_ref.at[pl.ds(0, rows)],
            dst_ref=at.at[s],
            send_sem=isend.at[0],
            recv_sem=irecv.at[s],
            device_id={"dp": me - core + group_of, "tensor": z},
            device_id_type=MESH_ID,
        )

    own_at = group_of == core
    in_own = pltpu.make_async_copy(
        att_ref.at[pl.ds(pl.multiple_of(z * rows, rows), rows)], at.at[heads_of], lsem.at[0]
    )
    for k in range(ways - 1, 0, -1):
        in_copy(lax.bitwise_xor(z, k)).start()

    @pl.when(own_at)
    def _():
        in_own.start()
        in_own.wait()

    @pl.when(jnp.logical_not(own_at))
    def _():
        in_copy(z).start()

    copies = gather_copies(lambda s, part: half_of(cots.at[s], part), csend, crecv, False)
    cot_own.wait()
    gather_start(copies)
    gather_forward(copies)

    for s in range(ways):
        source_core, source_z = head_source(s)

        @pl.when(jnp.logical_not((source_core == core) & (source_z == z)))
        def _():
            in_wait(s).wait_recv()

    step = min(256, rows)

    @pl.loop(0, rows // step)
    def _(k):
        rs = pl.ds(pl.multiple_of(k * step, step), step)
        acc = tok_ref[rs, :].astype(F32)
        for s in range(ways):
            acc += dot_nn(at[s, rs, :], wo_ref[s * quarter : (s + 1) * quarter, :])
            at_ref[s, rs, :] = at[s, rs, :]
        resid_ref[rs, :] = acc
        centred = acc - jnp.mean(acc, axis=-1, keepdims=True)
        root = lax.rsqrt(jnp.mean(centred * centred, axis=-1, keepdims=True) + norm_eps)
        n_ref[rs, :] = (centred * root * gain_ref[...] + shift_ref[...]).astype(BF16)

    gather_finish(copies)
    cots_copy = pltpu.make_async_copy(cots, cots_out, lsem.at[1])
    cots_copy.start()
    for copy in copies.values():
        copy.wait_send()
    for k in range(1, ways):
        in_copy(lax.bitwise_xor(z, k)).wait_send()

    @pl.when(jnp.logical_not(own_at))
    def _():
        in_copy(z).wait_send()

    cots_copy.wait()


def collect(attended, tokens, out_full, gain, shift, cot, ways):
    rows, d = tokens.shape
    quarter = d // ways
    anywhere = pl.BlockSpec(memory_space=pl.ANY)
    inside = pl.BlockSpec(memory_space=pltpu.VMEM)
    return pl.pallas_call(
        collect_kernel,
        in_specs=[anywhere] + [inside] * 4 + [anywhere],
        out_specs=[inside] * 3 + [anywhere],
        out_shape=[
            jax.ShapeDtypeStruct((ways, rows, quarter), BF16),
            jax.ShapeDtypeStruct((rows, d), F32),
            jax.ShapeDtypeStruct((rows, d), BF16),
            jax.ShapeDtypeStruct((8, rows // 2, d), BF16),
        ],
        scratch_shapes=[
            pltpu.VMEM((ways, rows, quarter), BF16),
            pltpu.VMEM((8, rows // 2, d), BF16),
            pltpu.SemaphoreType.DMA((ways,)),
            pltpu.SemaphoreType.DMA((ways,)),
            pltpu.SemaphoreType.DMA((8,)),
            pltpu.SemaphoreType.DMA((8,)),
            pltpu.SemaphoreType.DMA((2,)),
        ],
        compiler_params=pltpu.CompilerParams(
            collective_id=3, has_side_effects=True, vmem_limit_bytes=VMEM_LIMIT
        ),
        cost_estimate=pl.CostEstimate(
            flops=30 * 10**9, bytes_accessed=16 * rows * d, transcendentals=0
        ),
        name="collect",
    )(attended, tokens, out_full, gain[None], shift[None], cot)


def middle_kernel(
    x_ref,
    at_ref,
    resid_ref,
    wo_ref,
    c_low_ref,
    c_high_ref,
    w_low_ref,
    w_high_ref,
    gain_ref,
    ag_ref,
    rg_ref,
    og_ref,
    out_ref,
    grads_ref,
    ng_ref,
    wgu_ref,
    wd_ref,
    xs,
    cs,
    hid,
    branch,
    part,
    from_sib,
    from_far,
    from_x,
    from_y,
    down_acc,
    gate_up_acc,
    resid,
    at,
    agr,
    gsend,
    grecv,
    ssend,
    srecv,
    fsend,
    frecv,
    osend,
    orecv,
    csem,
    wsem,
    lsem,
    credit,
):
    ways, split = w_low_ref.shape[:2]
    unit = 2 * split // 3
    units = ways * unit
    rows, d = x_ref.shape
    quarter = d // ways
    half = rows // 2
    low, high = pl.ds(0, half), pl.ds(half, half)
    me, z = lax.axis_index("dp"), lax.axis_index("tensor")
    core, heads_of, group_of = head_share()
    sib, across, along = plane_peers()
    enter(column(ways) + [across, along])

    own_at = group_of == core
    half_wo = ways // 2
    step = min(256, rows)
    own = pltpu.make_async_copy(x_ref, xs.at[0], lsem.at[0])
    own.start()
    first_loads = [
        pltpu.make_async_copy(at_ref, at, lsem.at[1]),
        pltpu.make_async_copy(resid_ref, resid, lsem.at[2]),
    ]
    cots = [
        pltpu.make_async_copy(ref.at[i], cs.at[i, side], csem.at[i, k])
        for i in range(8)
        for k, (ref, side) in enumerate(((c_low_ref, low), (c_high_ref, high)))
    ]
    weights = []
    for t in range(ways):
        dst = pl.ds(t * unit, unit)
        places = (wgu_ref.at[dst], wgu_ref.at[pl.ds(units + t * unit, unit)], wd_ref.at[dst])
        for j, place in enumerate(places):
            for k, (ref, first) in enumerate(((w_low_ref, 0), (w_high_ref, split))):
                start = max(j * unit, first)
                size = min((j + 1) * unit, first + split) - start
                if size > 0:
                    src = ref.at[t, pl.ds(start - first, size)]
                    dst_rows = place.at[pl.ds(start - j * unit, size)]
                    weights.append(pltpu.make_async_copy(src, dst_rows, wsem.at[t, j, k]))
    own.wait()
    copies = gather_copies(lambda s, side: half_of(xs.at[s], side), gsend, grecv, False)
    gather_start(copies)
    for load in (*weights, *cots, *first_loads):
        load.start()
    down_acc[...] = jnp.zeros_like(down_acc)
    gate_up_acc[...] = jnp.zeros_like(gate_up_acc)
    for load in weights:
        load.wait()

    def plane_sums(send, recv, src, landing):
        steps = [
            ("1", src(1), landing[0], sib),
            ("3", src(3), landing[1], sib),
            ("5", src(5), landing[2], sib),
            ("7", src(7), landing[3], sib),
            ("6l", src(6).at[low], from_far.at[low], across),
            ("6h", src(6).at[high], from_far.at[high], along),
            ("2l", src(2).at[low], from_x.at[low], across),
            ("2h", src(2).at[high], from_x.at[high], across),
            ("4l", src(4).at[low], from_y.at[low], along),
            ("4h", src(4).at[high], from_y.at[high], along),
        ]
        return {
            name: remote(ref, dst, send, recv, i, peer)
            for i, (name, ref, dst, peer) in enumerate(steps)
        }

    def add_to(ref, other):
        ref[...] = (ref[...].astype(F32) + other[...].astype(F32)).astype(BF16)

    def slot(i):
        return i // 2 if i % 2 == 0 else 4 + (i // 2) % 2

    landing = [from_sib.at[0], from_sib.at[1], from_sib.at[2], from_sib.at[0]]
    sums = plane_sums(ssend, srecv, lambda i: part.at[slot(i)], landing)

    def grads(i, place):
        down_acc[...] += dot_tn(hid[place], cs[i])
        gate_up_acc[...] += dot_tn(branch[place], xs[i])
        cs[i] = dot_nn(hid[place], wd_ref[...]).astype(BF16)

    @pl.loop(0, 8)
    def _(i):
        @pl.when(i == 1)
        def _():
            copies["0-1"].wait_recv()

        @pl.when(i == 2)
        def _():
            gather_forward(copies)

        @pl.when(i == 3)
        def _():
            copies["2-3"].wait_recv()

        @pl.when(i == 4)
        def _():
            sums["1"].wait_recv()
            add_to(part.at[0], from_sib.at[0])

        @pl.when(i == 5)
        def _():
            copies["4-5"].wait_recv()
            sums["3"].wait_recv()
            add_to(part.at[1], from_sib.at[1])
            sums["2l"].start()
            sums["1"].wait_send()

        @pl.when(i == 6)
        def _():
            copies["2-6"].wait_recv()
            copies["4-6"].wait_recv()
            copies["6-7"].start()

        @pl.when(i == 7)
        def _():
            copies["6-7"].wait_recv()
            sums["5"].wait_recv()
            add_to(part.at[2], from_sib.at[2])
            sums["4h"].start()
            sums["3"].wait_send()

        for k in range(8):

            @pl.when(i == k)
            def _(k=k):
                cots[2 * k].wait()
                cots[2 * k + 1].wait()

        both = dot_nt(xs[i], wgu_ref[...])
        gate, up = both[:, :units], both[:, units:]
        sig = jax.nn.sigmoid(gate)
        silu = gate * sig
        place = jnp.where(i < 2, i, i - 2)
        hid[place] = (silu * up).astype(BF16)
        hidden_grad = dot_nt(cs[i], wd_ref[...])
        branch[place, :, :units] = (
            hidden_grad * up * sig * (1.0 + gate * (1.0 - sig))
        ).astype(BF16)
        branch[place, :, units:] = (hidden_grad * silu).astype(BF16)
        even = lax.rem(i, 2) == 0
        into = jnp.where(even, i // 2, 4 + lax.rem(i // 2, 2))
        part[into] = dot_nn(branch[place], wgu_ref[...]).astype(BF16)
        for odd in (1, 3, 5, 7):

            @pl.when(i == odd)
            def _(odd=odd):
                sums[str(odd)].start()

        @pl.when(i < 2)
        def _():
            grads(i, i)

    @pl.loop(2, 8)
    def _(i):
        @pl.when(i == 3)
        def _():
            sums["7"].wait_recv()
            add_to(part.at[3], from_sib.at[0])
            sums["6l"].start()
            sums["6h"].start()

        @pl.when(i == 7)
        def _():
            sums["6l"].wait_recv()
            add_to(part.at[2, low], from_far.at[low])
            sums["4l"].start()
            sums["6h"].wait_recv()
            add_to(part.at[1, high], from_far.at[high])
            sums["2h"].start()

        grads(i, i - 2)

    pl.semaphore_signal(credit.at[0], inc=1, device_id=sib, device_id_type=MESH_ID)
    for copy in copies.values():
        copy.wait_send()
    for t in range(ways):
        for j, (acc, first) in enumerate(
            ((gate_up_acc, t * unit), (gate_up_acc, units + t * unit), (down_acc, t * unit))
        ):
            row = (3 * t + j) * unit
            branch[row // rows, row % rows : row % rows + unit] = acc[first : first + unit].astype(
                BF16
            )
    for load in first_loads:
        load.wait()
    grads_copy = pltpu.make_async_copy(branch.at[pl.ds(0, grads_ref.shape[0])], grads_ref, lsem.at[1])
    wo_loads = [
        pltpu.make_async_copy(wo_ref.at[pl.ds(0, rows)], branch.at[3], lsem.at[2]),
        pltpu.make_async_copy(wo_ref.at[pl.ds(rows, rows)], branch.at[4], lsem.at[3]),
        pltpu.make_async_copy(c_low_ref.at[0], xs.at[3, low], lsem.at[0]),
        pltpu.make_async_copy(c_high_ref.at[0], xs.at[3, high], lsem.at[4]),
    ]
    grads_copy.start()
    for load in wo_loads:
        load.start()

    outs = plane_sums(
        fsend,
        frecv,
        lambda i: cs.at[i],
        [from_sib.at[0], from_sib.at[1], from_sib.at[2], branch.at[5]],
    )
    pl.semaphore_wait(credit.at[0], 1)
    for name in ("7", "3", "5", "1"):
        outs[name].start()

    grad = gate_up_acc
    for name in ("2l", "2h", "4l", "4h"):
        sums[name].wait_recv()

    @pl.loop(0, rows // step)
    def _(k):
        rs = pl.ds(pl.multiple_of(k * step, step), step)
        grad[rs, :] = (
            part[0, rs, :].astype(F32) + from_x[rs, :].astype(F32) + from_y[rs, :].astype(F32)
        )

    pl.semaphore_signal(credit.at[1], inc=1, device_id=across, device_id_type=MESH_ID)
    pl.semaphore_signal(credit.at[2], inc=1, device_id=along, device_id_type=MESH_ID)
    outs["7"].wait_recv()
    add_to(cs.at[6], branch.at[5])
    pl.semaphore_wait(credit.at[1], 1)
    pl.semaphore_wait(credit.at[2], 1)
    outs["6l"].start()
    outs["6h"].start()
    outs["3"].wait_recv()
    add_to(cs.at[2], from_sib.at[1])
    outs["2l"].start()
    outs["5"].wait_recv()
    add_to(cs.at[4], from_sib.at[2])
    outs["4h"].start()

    for load in wo_loads:
        load.wait()
    ng_ref[...] = jnp.zeros_like(ng_ref)
    gain = gain_ref[...]
    small = min(128, rows)

    @pl.loop(0, rows // small)
    def _(k):
        rs = pl.ds(pl.multiple_of(k * small, small), small)
        values = resid[rs, :]
        centred = values - jnp.mean(values, axis=-1, keepdims=True)
        root = lax.rsqrt(jnp.mean(centred * centred, axis=-1, keepdims=True) + norm_eps)
        unit_rows = centred * root
        out_grad = grad[rs, :]
        ng_ref[2:3] += jnp.sum(out_grad * unit_rows, axis=0, keepdims=True)
        ng_ref[3:4] += jnp.sum(out_grad, axis=0, keepdims=True)
        scaled = out_grad * gain
        first_mean = jnp.mean(scaled, axis=-1, keepdims=True)
        second_mean = jnp.mean(scaled * unit_rows, axis=-1, keepdims=True)
        total = xs[3, rs, :].astype(F32) + root * (scaled - first_mean - unit_rows * second_mean)
        grad[rs, :] = total
        xs[1, rs, :] = total.astype(BF16)

    rg_copy = pltpu.make_async_copy(grad.at[pl.ds(0, rows)], rg_ref, lsem.at[0])
    rg_copy.start()

    def out_copy(s):
        to_core, to_z = head_source(s)
        return pltpu.make_async_remote_copy(
            src_ref=xs.at[2, :, pl.ds(s * quarter, quarter)],
            dst_ref=agr.at[z],
            send_sem=osend.at[s],
            recv_sem=orecv.at[z],
            device_id={"dp": me - core + to_core, "tensor": to_z},
            device_id_type=MESH_ID,
        )

    def out_wait(source):
        return pltpu.make_async_remote_copy(
            src_ref=xs.at[2, :, pl.ds(0, quarter)],
            dst_ref=agr.at[source],
            send_sem=osend.at[0],
            recv_sem=orecv.at[source],
            device_id={"dp": me, "tensor": z},
            device_id_type=MESH_ID,
        )

    for s in range(ways):
        place = 3 + s // half_wo
        first = (s % half_wo) * quarter
        xs[2, :, s * quarter : (s + 1) * quarter] = dot_nt(
            xs[1], branch[place, first : first + quarter, :]
        ).astype(BF16)
        to_core, to_z = head_source(s)
        to_self = (to_core == core) & (to_z == z)

        @pl.when(jnp.logical_not(to_self))
        def _():
            out_copy(s).start()

        @pl.when(to_self)
        def _():
            agr[z] = xs[2, :, s * quarter : (s + 1) * quarter]

    for s in range(ways):
        place = 6 + s // half_wo
        first = (s % half_wo) * quarter
        xs[place, first : first + quarter] = dot_tn(at[s], xs[1]).astype(BF16)
    og_copy = pltpu.make_async_copy(xs.at[pl.ds(6, 2)], og_ref, lsem.at[2])
    og_copy.start()

    outs["6l"].wait_recv()
    add_to(cs.at[4, low], from_far.at[low])
    outs["4l"].start()
    outs["6h"].wait_recv()
    add_to(cs.at[2, high], from_far.at[high])
    outs["2h"].start()

    for source in range(ways):

        @pl.when(jnp.logical_not(own_at & (z == source)))
        def _():
            out_wait(source).wait_recv()

    ag_copy = pltpu.make_async_copy(agr, ag_ref, lsem.at[3])
    ag_copy.start()
    outs["1"].wait_recv()
    for name in ("2l", "2h", "4l", "4h"):
        outs[name].wait_recv()

    @pl.loop(0, rows // step)
    def _(k):
        rs = pl.ds(pl.multiple_of(k * step, step), step)
        total = resid[rs, :] + cs[0, rs, :].astype(F32) + from_sib[0, rs, :].astype(F32)
        total += from_x[rs, :].astype(F32) + from_y[rs, :].astype(F32)
        xs[0, rs, :] = total.astype(BF16)

    grads_copy.wait()
    lo_copy = pltpu.make_async_copy(xs.at[0], out_ref, lsem.at[1])
    lo_copy.start()
    for name in ("5", "7", "6l", "6h", "2l", "2h", "4l", "4h"):
        sums[name].wait_send()
    for copy in outs.values():
        copy.wait_send()
    for s in range(ways):
        to_core, to_z = head_source(s)

        @pl.when(jnp.logical_not((to_core == core) & (to_z == z)))
        def _():
            out_copy(s).wait_send()

    for copy in (rg_copy, og_copy, ag_copy, lo_copy):
        copy.wait()


def middle(x, attended, resid, out_full, cot_low, cot_high, w_low, w_high, gain):
    rows, d = x.shape
    ways = w_low.shape[0]
    units = ways * 2 * w_low.shape[1] // 3
    quarter = d // ways
    anywhere = pl.BlockSpec(memory_space=pl.ANY)
    inside = pl.BlockSpec(memory_space=pltpu.VMEM)
    sems = lambda n: [pltpu.SemaphoreType.DMA((n,))] * 2
    return pl.pallas_call(
        middle_kernel,
        in_specs=[anywhere] * 8 + [inside],
        out_specs=[anywhere] * 5 + [inside],
        out_shape=[
            jax.ShapeDtypeStruct((ways, rows, quarter), BF16),
            jax.ShapeDtypeStruct((rows, d), F32),
            jax.ShapeDtypeStruct((2, rows, d), BF16),
            jax.ShapeDtypeStruct((rows, d), BF16),
            jax.ShapeDtypeStruct((3 * units // rows, rows, d), BF16),
            jax.ShapeDtypeStruct((8, d), F32),
        ],
        scratch_shapes=[
            pltpu.VMEM((2 * units, d), BF16),
            pltpu.VMEM((units, d), BF16),
            pltpu.VMEM((8, rows, d), BF16),
            pltpu.VMEM((8, rows, d), BF16),
            pltpu.VMEM((6, rows, units), BF16),
            pltpu.VMEM((6, rows, 2 * units), BF16),
            pltpu.VMEM((6, rows, d), BF16),
            pltpu.VMEM((3, rows, d), BF16),
            pltpu.VMEM((rows, d), BF16),
            pltpu.VMEM((rows, d), BF16),
            pltpu.VMEM((rows, d), BF16),
            pltpu.VMEM((units, d), F32),
            pltpu.VMEM((2 * units, d), F32),
            pltpu.VMEM((rows, d), F32),
            pltpu.VMEM((ways, rows, quarter), BF16),
            pltpu.VMEM((ways, rows, quarter), BF16),
        ]
        + sems(8)
        + sems(10)
        + sems(10)
        + sems(ways)
        + [
            pltpu.SemaphoreType.DMA((8, 2)),
            pltpu.SemaphoreType.DMA((ways, 3, 2)),
            pltpu.SemaphoreType.DMA((5,)),
            pltpu.SemaphoreType.REGULAR((3,)),
        ],
        compiler_params=pltpu.CompilerParams(
            collective_id=1, has_side_effects=True, vmem_limit_bytes=VMEM_LIMIT
        ),
        cost_estimate=pl.CostEstimate(
            flops=130 * 10**9, bytes_accessed=40 * rows * d, transcendentals=0
        ),
        name="middle",
    )(x, attended, resid, out_full, cot_low, cot_high, w_low, w_high, gain[None])


def tail_kernel(
    mixed_ref,
    w_ref,
    out_parts_ref,
    rows_ref,
    tok_ref,
    norm_ref,
    n_ref,
    og_ref,
    qkv_ref,
    ng_ref,
    lines,
    line_sib,
    line_z,
    line_end,
    part,
    from_sib,
    from_far,
    from_x,
    from_y,
    mine,
    slices,
    ogs,
    qkv,
    qkv_far,
    qkv_x,
    qkv_y,
    qkv_sum,
    qkv_z,
    qkvs,
    norms,
    norms_z,
    lsend,
    lrecv,
    hsend,
    hrecv,
    ssend,
    srecv,
    gsend,
    grecv,
    osend,
    orecv,
    ksend,
    krecv,
    kzsend,
    kzrecv,
    kgsend,
    kgrecv,
    nsend,
    nrecv,
    zsend,
    zrecv,
    load_sem,
):
    me, z = lax.axis_index("dp"), lax.axis_index("tensor")
    ways, rows = lines.shape[0], lines.shape[1]
    out_rows = slices.shape[1]
    width = w_ref.shape[2]
    total = part.shape[1]
    half = total // 2
    low, high = pl.ds(0, half), pl.ds(half, half)
    core, heads_of, group_of = head_share()
    home = group_of == core
    chip = me // 2
    sib, across, along = plane_peers()
    others = [{"tensor": lax.rem(z + k, ways)} for k in range(1, ways)]
    z1, z2, z3 = (lax.bitwise_xor(z, k) for k in (1, 2, 3))
    near, far = {"tensor": z1}, {"tensor": z2}
    enter([sib, across, along] + others)

    loads = []
    for i in range(8):
        src = pl.multiple_of(lax.bitwise_xor(me, i) * out_rows, 16)
        loads.append(
            [
                pltpu.make_async_copy(
                    out_parts_ref.at[t, pl.ds(src, out_rows)],
                    part.at[i, pl.ds(t * out_rows, out_rows)],
                    load_sem.at[t, i],
                )
                for t in range(ways)
            ]
        )
        for load in loads[-1]:
            load.start()

    def add_to(ref, other):
        ref[...] = (ref[...].astype(F32) + other[...].astype(F32)).astype(BF16)

    size = rows // 2

    def part_of(which):
        return pl.ds(pl.multiple_of(which * size, size), size)

    def line(i):
        b = lax.bitwise_xor(z, i)
        step = min(256, rows)

        @pl.loop(0, rows // step)
        def _(k):
            at = pl.ds(pl.multiple_of(b * rows + k * step, step), step)
            lines[b, pl.ds(pl.multiple_of(k * step, step), step)] = sum(
                dot_nt(mixed_ref[at, j * width : (j + 1) * width], w_ref[j]) for j in range(3)
            ).astype(BF16)

    def share(i):
        b = lax.bitwise_xor(z, i)
        return remote(lines.at[b, part_of(1 - core)], line_sib.at[b], hsend, hrecv, i, sib)

    def share_join(i):
        b = lax.bitwise_xor(z, i)
        share(i).wait_recv()
        add_to(lines.at[b, part_of(core)], line_sib.at[b])

    to_near = [
        remote(lines.at[z3, part_of(core)], line_z.at[0], lsend, lrecv, 0, near),
        remote(lines.at[z1, part_of(core)], line_z.at[1], lsend, lrecv, 1, near),
    ]
    to_far = remote(lines.at[z2, part_of(core)], line_z.at[2], lsend, lrecv, 2, far)
    last_away = remote(line_z.at[2], line_end, lsend, lrecv, 3, sib)
    last_home = remote(lines.at[z, part_of(core)], line_end, lsend, lrecv, 3, sib)

    @pl.loop(0, ways)
    def _(k):
        i = ways - 1 - k
        i = jnp.where(i == 2, 1, jnp.where(i == 1, 2, i))
        line(i)
        for fixed in range(ways):

            @pl.when(i == fixed)
            def _(fixed=fixed):
                share(fixed).start()
                if fixed == 1:
                    share_join(3)
                    to_near[0].start()

    sums = [
        ("1", part.at[1], from_sib.at[0], sib),
        ("3", part.at[3], from_sib.at[1], sib),
        ("5", part.at[5], from_sib.at[2], sib),
        ("7", part.at[7], from_sib.at[3], sib),
        ("6l", part.at[6, low], from_far.at[low], across),
        ("6h", part.at[6, high], from_far.at[high], along),
        ("2l", part.at[2, low], from_x.at[low], across),
        ("2h", part.at[2, high], from_x.at[high], across),
        ("4l", part.at[4, low], from_y.at[low], along),
        ("4h", part.at[4, high], from_y.at[high], along),
    ]
    sums = {
        name: remote(src, dst, ssend, srecv, i, peer)
        for i, (name, src, dst, peer) in enumerate(sums)
    }
    for i in (7, 3, 5, 1):
        for load in loads[i]:
            load.wait()
        sums[str(i)].start()

    @pl.loop(0, 3)
    def _(j):
        at = pl.ds(pl.multiple_of(j * width, width), width)
        qkv[at, :] = dot_tn(mixed_ref[:, at], rows_ref[...]).astype(BF16)

    piece = qkv_sum.shape[0]
    small = piece // 2

    def qkv_at(s, side=None):
        first = lax.bitwise_xor(chip, s) * piece + (0 if side is None else side * small)
        return qkv.at[pl.ds(pl.multiple_of(first, 16), piece if side is None else small)]

    def side_of(ref, side):
        return ref.at[pl.ds(side * small, small)]

    pieces = [
        ("3l", qkv_at(3, 0), side_of(qkv_far, 0), across),
        ("3h", qkv_at(3, 1), side_of(qkv_far, 1), along),
        ("1l", qkv_at(1, 0), side_of(qkv_x, 0), across),
        ("1h", qkv_at(1, 1), side_of(qkv_x, 1), across),
        ("2l", qkv_at(2, 0), side_of(qkv_y, 0), along),
        ("2h", qkv_at(2, 1), side_of(qkv_y, 1), along),
    ]
    pieces = {
        name: remote(src, dst, ksend, krecv, i, peer)
        for i, (name, src, dst, peer) in enumerate(pieces)
    }
    for name in ("3l", "3h", "1l", "2h"):
        pieces[name].start()

    share_join(1)
    for i, j, names in ((6, 3, ("6l", "6h")), (2, 1, ("2l",)), (4, 2, ("4h",))):
        for load in loads[i]:
            load.wait()
        sums[str(i + 1)].wait_recv()
        add_to(part.at[i], from_sib.at[j])
        for name in names:
            sums[name].start()
    share_join(2)
    to_near[0].wait_recv()
    to_near[1].start()
    add_to(lines.at[z2, part_of(core)], line_z.at[0])
    to_far.start()
    share_join(0)

    pieces["3l"].wait_recv()
    add_to(qkv_at(2, 0), side_of(qkv_far, 0))
    pieces["2l"].start()
    pieces["3h"].wait_recv()
    add_to(qkv_at(1, 1), side_of(qkv_far, 1))
    pieces["1h"].start()
    sums["6l"].wait_recv()
    add_to(part.at[4, low], from_far.at[low])
    sums["4l"].start()
    sums["6h"].wait_recv()
    add_to(part.at[2, high], from_far.at[high])
    sums["2h"].start()

    for name in ("1l", "1h", "2l", "2h"):
        pieces[name].wait_recv()
    qkv_sum[...] = (
        qkv_at(0)[...].astype(F32) + qkv_x[...].astype(F32) + qkv_y[...].astype(F32)
    ).astype(BF16)
    takes = core == lax.rem(z, 2)

    def owner_copy(slot):
        return pltpu.make_async_remote_copy(
            src_ref=qkv_sum,
            dst_ref=qkv_z.at[slot],
            send_sem=kzsend.at[0],
            recv_sem=kzrecv.at[slot],
            device_id={"tensor": heads_of},
            device_id_type=MESH_ID,
        )

    @pl.when(heads_of != z)
    def _():
        owner_copy(group_of).start()

    @pl.when(heads_of == z)
    def _():
        qkv_z[group_of] = qkv_sum[...]

    for load in loads[0]:
        load.wait()
    sums["1"].wait_recv()
    for name in ("2l", "2h", "4l", "4h"):
        sums[name].wait_recv()
    mine[...] = part[0].astype(F32) + from_sib[0].astype(F32)
    mine[...] += from_x[...].astype(F32) + from_y[...].astype(F32)

    for t in range(ways):
        at = slice(t * out_rows, (t + 1) * out_rows)
        part[0, at] = mine[at].astype(BF16)

    def slice_copy(k, to, source):
        return pltpu.make_async_remote_copy(
            src_ref=part.at[0, pl.ds(pl.multiple_of(to * out_rows, 16), out_rows)],
            dst_ref=slices.at[source],
            send_sem=osend.at[k],
            recv_sem=orecv.at[source],
            device_id={"tensor": to},
            device_id_type=MESH_ID,
        )

    for k in range(1, ways):
        slice_copy(k, lax.rem(z + k, ways), z).start()

    def chip_copy(s, side, peer, sem):
        at = qkvs.at[lax.bitwise_xor(chip, s)]
        ref = at if side is None else side_of(at, side)
        return remote(ref, ref, kgsend, kgrecv, sem, peer)

    to_x, to_y = chip_copy(0, None, across, 0), chip_copy(0, None, along, 1)
    x_on, y_on = chip_copy(1, 1, along, 2), chip_copy(2, 0, across, 3)
    to_sib = [chip_copy(s, None, sib, 4 + s) for s in range(4)]

    @pl.when(takes)
    def _():
        for slot in range(2):

            @pl.when(z // 2 + 2 * slot != z)
            def _():
                owner_copy(slot).wait_recv()

        qkvs[chip] = (qkv_z[0].astype(F32) + qkv_z[1].astype(F32)).astype(BF16)
        to_x.start()
        to_y.start()
        to_sib[0].start()

    own_slice = part[0, pl.ds(pl.multiple_of(z * out_rows, 16), out_rows)].astype(F32)
    for k in range(1, ways):
        source = lax.rem(z + k, ways)
        slice_copy(k, source, source).wait_recv()
        own_slice += slices[source].astype(F32)
    ogs[me] = own_slice.astype(BF16)
    view = lambda s, side: half_of(ogs.at[lax.bitwise_xor(me, s)], side)
    gathers = gather_copies(view, gsend, grecv, True)
    gather_start(gathers)

    to_near[1].wait_recv()
    add_to(lines.at[z, part_of(core)], line_z.at[1])

    @pl.when(jnp.logical_not(home))
    def _():
        last_home.start()

    to_far.wait_recv()

    @pl.when(home)
    def _():
        last_away.start()
        n_ref[part_of(core), :] = lines[z, part_of(core), :].astype(F32)

    @pl.when(jnp.logical_not(home))
    def _():
        n_ref[part_of(core), :] = line_z[2].astype(F32)

    last_away.wait_recv()
    n_ref[part_of(1 - core), :] = line_end[...].astype(F32)

    norms[0] = norm_ref[...]
    step = min(128, rows)

    @pl.loop(0, rows // step)
    def _(i):
        at = pl.ds(pl.multiple_of(i * step, step), step)
        values = tok_ref[at, :].astype(F32)
        centred = values - jnp.mean(values, axis=-1, keepdims=True)
        root = lax.rsqrt(jnp.mean(centred * centred, axis=-1, keepdims=True) + norm_eps)
        grad = n_ref[at, :]
        norms[0, 0:1] += jnp.sum(grad * (centred * root), axis=0, keepdims=True)
        norms[0, 1:2] += jnp.sum(grad, axis=0, keepdims=True)

    swaps = [
        remote(norms.at[i], norms.at[4 + i], nsend, nrecv, i, peer)
        for i, peer in enumerate((sib, across, along))
    ]
    swaps[0].start()

    gather_forward(gathers)

    @pl.when(takes)
    def _():
        to_x.wait_recv()
        x_on.start()
        to_sib[1].start()
        to_y.wait_recv()
        y_on.start()
        to_sib[2].start()

    for i, swap in enumerate(swaps):
        if i:
            swap.start()
        swap.wait_recv()
        norms[i + 1] = norms[i] + norms[4 + i]

    def norm_copy(k, to, source):
        return pltpu.make_async_remote_copy(
            src_ref=norms.at[3],
            dst_ref=norms_z.at[source],
            send_sem=zsend.at[k],
            recv_sem=zrecv.at[source],
            device_id={"tensor": to},
            device_id_type=MESH_ID,
        )

    for k in range(1, ways):
        norm_copy(k, lax.rem(z + k, ways), z).start()
    norms_z[z] = norms[3]
    gather_finish(gathers)
    og_ref[...] = ogs[...]

    @pl.when(takes)
    def _():
        x_on.wait_recv()
        y_on.wait_recv()
        to_sib[3].start()

    @pl.when(jnp.logical_not(takes))
    def _():
        for copy in to_sib:
            copy.wait_recv()

    qkv_ref[...] = qkvs[...]
    for k in range(1, ways):
        source = lax.rem(z + k, ways)
        norm_copy(k, source, source).wait_recv()
    ng_ref[...] = sum(norms_z[t] for t in range(ways))

    @pl.when(takes)
    def _():
        for copy in (to_x, to_y, x_on, y_on, *to_sib):
            copy.wait_send()

    @pl.when(heads_of != z)
    def _():
        owner_copy(group_of).wait_send()

    @pl.when(home)
    def _():
        last_away.wait_send()

    @pl.when(jnp.logical_not(home))
    def _():
        last_home.wait_send()

    for copy in (*sums.values(), *gathers.values(), *pieces.values(), *swaps, *to_near, to_far):
        copy.wait_send()
    for i in range(ways):
        share(i).wait_send()
    for k in range(1, ways):
        to = lax.rem(z + k, ways)
        slice_copy(k, to, z).wait_send()
        norm_copy(k, to, z).wait_send()


def tail(mixed, w, out_parts, rows_one, tokens, norm_grads, ways):
    rows, d = tokens.shape
    out_rows = out_parts.shape[1] // 8
    qkv_rows = mixed.shape[1] // 4
    total = ways * out_rows
    anywhere = pl.BlockSpec(memory_space=pl.ANY)
    inside = pl.BlockSpec(memory_space=pltpu.VMEM)
    sems = lambda n: [pltpu.SemaphoreType.DMA((n,))] * 2
    return pl.pallas_call(
        tail_kernel,
        in_specs=[inside, inside, anywhere, inside, inside, inside],
        out_specs=[inside] * 4,
        out_shape=[
            jax.ShapeDtypeStruct((rows, d), F32),
            jax.ShapeDtypeStruct((8, out_rows, d), BF16),
            jax.ShapeDtypeStruct((4, qkv_rows, d), BF16),
            jax.ShapeDtypeStruct((8, d), F32),
        ],
        scratch_shapes=[
            pltpu.VMEM((ways, rows, d), BF16),
            pltpu.VMEM((ways, rows // 2, d), BF16),
            pltpu.VMEM((3, rows // 2, d), BF16),
            pltpu.VMEM((rows // 2, d), BF16),
            pltpu.VMEM((8, total, d), BF16),
            pltpu.VMEM((4, total, d), BF16),
            pltpu.VMEM((total, d), BF16),
            pltpu.VMEM((total, d), BF16),
            pltpu.VMEM((total, d), BF16),
            pltpu.VMEM((total, d), F32),
            pltpu.VMEM((ways, out_rows, d), BF16),
            pltpu.VMEM((8, out_rows, d), BF16),
            pltpu.VMEM((4 * qkv_rows, d), BF16),
            pltpu.VMEM((qkv_rows, d), BF16),
            pltpu.VMEM((qkv_rows, d), BF16),
            pltpu.VMEM((qkv_rows, d), BF16),
            pltpu.VMEM((qkv_rows, d), BF16),
            pltpu.VMEM((2, qkv_rows, d), BF16),
            pltpu.VMEM((4, qkv_rows, d), BF16),
            pltpu.VMEM((8, 8, d), F32),
            pltpu.VMEM((ways, 8, d), F32),
        ]
        + sems(4)
        + sems(ways)
        + sems(10)
        + sems(8)
        + sems(ways)
        + sems(6)
        + sems(2)
        + sems(8)
        + sems(3)
        + sems(ways)
        + [pltpu.SemaphoreType.DMA((ways, 8))],
        compiler_params=pltpu.CompilerParams(
            collective_id=2, has_side_effects=True, vmem_limit_bytes=VMEM_LIMIT
        ),
        cost_estimate=pl.CostEstimate(
            flops=75 * 10**9, bytes_accessed=40 * rows * d, transcendentals=0
        ),
        name="tail",
    )(mixed, w, out_parts, rows_one, tokens, norm_grads)


def finish_kernel(
    both_ref,
    down_ref,
    features_ref,
    og_ref,
    grad_ref,
    resid_ref,
    tok_ref,
    gain_ref,
    gate_up_ref,
    down_out_ref,
    qkv_ref,
    og_out_ref,
    token_ref,
):
    units = both_ref.shape[1] // 2
    for p in range(8):
        turned = both_ref[p].astype(F32).T
        for g in range(2):
            at = pl.ds(2 * p + g, turned.shape[0], stride=16)
            gate_up_ref[at, :] = turned[:, g * units : (g + 1) * units]
    down_out_ref[...] = down_ref[0].astype(F32)
    width = qkv_ref.shape[2]
    for j in range(3):
        qkv_ref[j] = features_ref[j * width : (j + 1) * width].astype(F32).T
    og_out_ref[...] = og_ref[0].astype(F32)
    values = tok_ref[...].astype(F32)
    centred = values - jnp.mean(values, axis=-1, keepdims=True)
    root = lax.rsqrt(jnp.mean(centred * centred, axis=-1, keepdims=True) + norm_eps)
    unit_rows = centred * root
    scaled = grad_ref[...] * gain_ref[...]
    first_mean = jnp.mean(scaled, axis=-1, keepdims=True)
    second_mean = jnp.mean(scaled * unit_rows, axis=-1, keepdims=True)
    token_ref[...] = resid_ref[...] + root * (scaled - first_mean - unit_rows * second_mean)


def finish(grads, features, out_grad, norm_grad, resid_grad, tokens, gain):
    rows, d = tokens.shape
    units = grads.shape[1] // 3
    block = d // 8
    width = features.shape[0] // 3
    out_rows = out_grad.shape[1]
    own = pl.BlockSpec((rows // 8, d), lambda i: (i, 0))
    return pl.pallas_call(
        finish_kernel,
        grid=(8,),
        in_specs=[
            pl.BlockSpec((8, 2 * units, block), lambda i: (0, 0, i)),
            pl.BlockSpec((1, units, d), lambda i: (i, 2, 0)),
            pl.BlockSpec((3 * width, block), lambda i: (0, i)),
            pl.BlockSpec((1, out_rows, d), lambda i: (i, 0, 0)),
            own,
            own,
            own,
            pl.BlockSpec((1, d), lambda i: (0, 0)),
        ],
        out_specs=[
            pl.BlockSpec((16 * block, units), lambda i: (i, 0)),
            pl.BlockSpec((units, d), lambda i: (i, 0)),
            pl.BlockSpec((3, block, width), lambda i: (0, i, 0)),
            pl.BlockSpec((out_rows, d), lambda i: (i, 0)),
            own,
        ],
        out_shape=[
            jax.ShapeDtypeStruct((16 * d, units), F32),
            jax.ShapeDtypeStruct((8 * units, d), F32),
            jax.ShapeDtypeStruct((3, d, width), F32),
            jax.ShapeDtypeStruct((8 * out_rows, d), F32),
            jax.ShapeDtypeStruct((rows, d), F32),
        ],
        compiler_params=pltpu.CompilerParams(vmem_limit_bytes=VMEM_LIMIT),
        name="finish",
    )(grads, grads, features, out_grad, norm_grad, resid_grad, tokens, gain[None])


def shards(
    tokens,
    group_bucket,
    gain_one,
    shift_one,
    w_qkv,
    w_out,
    gain_two,
    shift_two,
    w_gate_up,
    w_down,
    cotangent,
):
    ways = lax.axis_size("tensor")
    replicas = lax.axis_size("dp")
    replica = lax.axis_index("dp")
    own_rows, d = tokens.shape
    group_rows = own_rows * ways
    local_width = w_out.shape[0]
    head_dim = d // HEADS
    hidden_width = w_down.shape[0]
    units = hidden_width // replicas
    out_rows = local_width // replicas
    pair_width = min(128, local_width)

    rows_in = tokens.astype(F32)
    normed_one, unit_one, root_one = norm_forward(rows_in, gain_one, shift_one)
    normed_one_low = normed_one.astype(BF16)
    rows_one = lax.all_gather(normed_one_low, "tensor", axis=0, tiled=True)

    gate_up_slice = lax.dynamic_slice_in_dim(w_gate_up, replica * units, units, axis=2)
    down_slice = lax.dynamic_slice_in_dim(w_down, replica * units, units, axis=0)
    weight_slice = jnp.concatenate(
        [gate_up_slice.transpose(1, 2, 0).reshape(2 * units, d), down_slice]
    )
    weights = lax.all_gather(weight_slice, "tensor", axis=0)
    cot_all = lax.all_gather(cotangent, "dp", axis=0, tiled=True)
    out_full = lax.all_gather(w_out, "tensor", axis=0, tiled=True)

    cos_wide, sine_wide = rotary_wide(group_bucket[0], group_rows, head_dim, pair_width)
    qkv_weights = w_qkv.transpose(1, 0, 2)
    q, k, v, kt, vt = project(rows_one, qkv_weights, cos_wide, sine_wide, head_dim)
    attended, *kept = attend(group_bucket, q, k, vt, head_dim)
    attended_own = lax.all_to_all(attended, "tensor", 0, 1, tiled=True)
    resid = rows_in + dot_nn(attended_own, out_full)
    normed_two, unit_two, root_two = norm_forward(resid, gain_two, shift_two)
    normed_two_low = normed_two.astype(BF16)
    parts = weights.reshape(ways, 3, units, d)
    wgu = parts[:, :2].transpose(3, 1, 0, 2).reshape(d, 2 * ways * units)
    wd = parts[:, 2].reshape(ways * units, d)
    rows_two = lax.all_gather(normed_two_low, "dp", axis=0, tiled=True)
    hidden, branch, back = feed(rows_two, cot_all, wgu, wd)
    normed_two_grad = lax.psum_scatter(back, "dp", scatter_dimension=0, tiled=True).astype(F32)
    ffn_parts = dot_nn(hidden, wd).astype(BF16)
    ffn_out = lax.psum_scatter(ffn_parts, "dp", scatter_dimension=0, tiled=True).astype(F32)
    layer_out = (resid + ffn_out).astype(BF16)
    grads = jnp.concatenate(
        [
            dot_tn(branch, rows_two).reshape(2, ways, units, d),
            dot_tn(hidden, cot_all).reshape(1, ways, units, d),
        ]
    )
    grads = grads.astype(BF16).transpose(1, 0, 2, 3).reshape(ways, 3 * units, d)
    resid_part, gain_two_grad, shift_two_grad = norm_backward(
        normed_two_grad, unit_two, root_two, gain_two
    )
    norm_grads = jnp.zeros((8, d), F32).at[2].set(gain_two_grad).at[3].set(shift_two_grad)
    resid_grad = cotangent.astype(F32) + resid_part
    attn_grad = resid_grad.astype(BF16)
    attended_grad = lax.all_to_all(
        dot_nt(attn_grad, out_full).astype(BF16), "tensor", 1, 0, tiled=True
    )
    out_grad = dot_tn(attended_own, attn_grad).astype(BF16)
    out_grad = out_grad.reshape(ways, replicas, out_rows, d).transpose(1, 0, 2, 3)
    out_grad = out_grad.reshape(replicas, ways * out_rows, d)
    grads = lax.psum_scatter(grads, "tensor", scatter_dimension=0)

    mixed_grad = attend_back(
        group_bucket, q, k, kt, v, attended_grad, *kept, cos_wide, sine_wide, head_dim
    )
    grads, mixed_grad = lax.optimization_barrier((grads, mixed_grad))
    grads = lax.all_gather(grads, "dp", axis=0)
    grads = grads.reshape(replicas, 3, units, d)
    down_grad = grads[:, 2].reshape(hidden_width, d).astype(F32)
    gate_up_grad = grads[:, :2].transpose(3, 1, 0, 2).reshape(d, 2, hidden_width).astype(F32)
    qkv_grad = lax.psum(dot_tn(rows_one, mixed_grad).astype(BF16), "dp").astype(F32)
    qkv_grad = qkv_grad.reshape(d, 3, local_width)
    flat = qkv_weights.transpose(1, 0, 2).reshape(d, 3 * local_width)
    normed_one_grad = lax.psum_scatter(
        dot_nt(mixed_grad, flat).astype(BF16), "tensor", scatter_dimension=0, tiled=True
    ).astype(F32)
    out_grad = lax.psum_scatter(out_grad, "dp", scatter_dimension=0)
    out_grad = lax.psum_scatter(out_grad, "tensor", scatter_dimension=0, tiled=True)
    out_grad = lax.all_gather(out_grad, "dp", axis=0, tiled=True).astype(F32)
    one = norm_backward(normed_one_grad, unit_one, root_one, gain_one)
    norm_grads = norm_grads.at[0].set(one[1]).at[1].set(one[2])
    norm_grads = lax.psum(norm_grads, ("dp", "tensor"))
    token_grad = resid_grad + norm_backward(normed_one_grad, unit_one, root_one, gain_one)[0]
    gain_one_grad, shift_one_grad, gain_two_grad, shift_two_grad = (norm_grads[i] for i in range(4))
    return (
        layer_out,
        token_grad,
        gain_one_grad,
        shift_one_grad,
        qkv_grad,
        out_grad,
        gain_two_grad,
        shift_two_grad,
        gate_up_grad,
        down_grad,
    )


def shards_columns(
    tokens,
    group_bucket,
    gain_one,
    shift_one,
    w_qkv,
    w_out,
    gain_two,
    shift_two,
    w_gate_up,
    w_down,
    cotangent,
):
    ways = lax.axis_size("tensor")
    replica = lax.axis_index("dp")
    own_rows, d = tokens.shape
    group_rows = own_rows * ways
    local_width = w_out.shape[0]
    head_dim = d // HEADS
    hidden_width = w_down.shape[0]
    units = hidden_width // 8

    gate_up_slice = lax.dynamic_slice_in_dim(w_gate_up, replica * units, units, axis=2)
    down_slice = lax.dynamic_slice_in_dim(w_down, replica * units, units, axis=0)
    weight_slice = jnp.concatenate(
        [gate_up_slice.transpose(1, 2, 0).reshape(2 * units, d), down_slice]
    )
    split = 3 * units // 2
    weights_low = lax.all_gather(weight_slice[:split], "tensor", axis=0)
    q, k, v, kt, vt, cos_wide, sine_wide, bucket, rows_one, cot_low, out_full, qkv_weights = front(
        group_bucket,
        tokens,
        gain_one,
        shift_one,
        cotangent,
        w_out,
        w_qkv.transpose(1, 0, 2),
        head_dim,
        ways,
    )
    bucket, weight_slice = lax.optimization_barrier((bucket, weight_slice))
    weights_high = lax.all_gather(weight_slice[split:], "tensor", axis=0)
    bucket = bucket[0, :1]
    out_full = out_full.reshape(d, d)
    attended, *kept = attend(bucket, q, k, vt, head_dim)
    attended_own, resid, normed_two, cot_high = collect(
        attended, tokens, out_full, gain_two, shift_two, cotangent, ways
    )
    attended_grad, resid_grad, out_grad, layer_out, grads, norm_grads = middle(
        normed_two,
        attended_own,
        resid,
        out_full,
        cot_low,
        cot_high,
        weights_low,
        weights_high,
        gain_two,
    )
    grads = grads.reshape(ways, 3 * units, d)
    grads = lax.psum_scatter(grads, "tensor", scatter_dimension=0)
    attended_grad = attended_grad.reshape(group_rows, local_width)
    mixed_grad = attend_back(
        bucket, q, k, kt, v, attended_grad, *kept, cos_wide, sine_wide, head_dim
    )
    grads, mixed_grad = lax.optimization_barrier((grads, mixed_grad))
    grads = lax.all_gather(grads, "dp", axis=0)
    normed_one_grad, out_grad, qkv_grad, norm_grads = tail(
        mixed_grad,
        qkv_weights,
        out_grad.reshape(ways, local_width, d),
        rows_one.reshape(group_rows, d),
        tokens,
        norm_grads,
        ways,
    )
    gate_up_grad, down_grad, qkv_grad, out_grad, token_grad = finish(
        grads,
        qkv_grad.reshape(3 * local_width, d),
        out_grad,
        normed_one_grad,
        resid_grad,
        tokens,
        gain_one,
    )
    gate_up_grad = gate_up_grad.reshape(d, 8, 2, units).transpose(0, 2, 1, 3)
    gate_up_grad = gate_up_grad.reshape(d, 2, hidden_width)
    qkv_grad = qkv_grad.transpose(1, 0, 2)
    gain_one_grad, shift_one_grad, gain_two_grad, shift_two_grad = (norm_grads[i] for i in range(4))
    return (
        layer_out,
        token_grad,
        gain_one_grad,
        shift_one_grad,
        qkv_grad,
        out_grad,
        gain_two_grad,
        shift_two_grad,
        gate_up_grad,
        down_grad,
    )


def solution(mesh):
    in_specs = (
        P(("dp", "tensor"), None),
        P("dp"),
        P(),
        P(),
        P(None, None, "tensor"),
        P("tensor", None),
        P(),
        P(),
        P(None, None, "tensor"),
        P("tensor", None),
        P(("dp", "tensor"), None),
    )
    out_specs = (
        P(("dp", "tensor"), None),
        P(("dp", "tensor"), None),
        P(),
        P(),
        P(None, None, "tensor"),
        P("tensor", None),
        P(),
        P(),
        P(None, None, "tensor"),
        P("tensor", None),
    )
    columns = mesh.shape["dp"] == 8 and mesh.shape["tensor"] == 4
    body = shards_columns if columns else shards
    return jax.shard_map(body, mesh=mesh, in_specs=in_specs, out_specs=out_specs, check_vma=False)
```

```python
import functools

import jax
import jax.numpy as jnp
from jax import lax
from jax.experimental import pallas as pl
from jax.experimental.pallas import tpu as pltpu
from jax.sharding import PartitionSpec as P

HEADS = 16
LONG_LEN = 2048
SHORT_LEN = 1000

norm_eps = 1e-05
mask_fill = -1e30
rope_base = 10000.0
log2_e = 1.4426950408889634
VMEM_LIMIT = 62 * 2**20
F32 = jnp.float32
BF16 = jnp.bfloat16


def dot_nn(a, b):
    return jnp.dot(a, b, preferred_element_type=F32)


def dot_nt(a, b):
    return lax.dot_general(a, b, (((1,), (1,)), ((), ())), preferred_element_type=F32)


def dot_tn(a, b):
    return lax.dot_general(a, b, (((0,), (0,)), ((), ())), preferred_element_type=F32)


def rotary_wide(bucket_id, group_rows, head_dim, width):
    positions = jnp.arange(group_rows, dtype=jnp.int32)
    span_len = jnp.where(bucket_id == 1, LONG_LEN, SHORT_LEN).astype(jnp.int32)
    places = positions - (positions // span_len) * span_len
    half_dim = head_dim // 2
    exponents = jnp.arange(half_dim, dtype=F32) * (-2.0 / head_dim)
    freqs = jnp.exp(exponents * jnp.log(F32(rope_base)))
    heads = width // head_dim
    signs = jnp.tile(jnp.repeat(jnp.array([-1.0, 1.0], F32), half_dim), heads)
    angles = places.astype(F32)[:, None] * jnp.tile(freqs, 2 * heads)[None, :]
    return jnp.cos(angles), jnp.sin(angles) * signs


def norm_forward(values, gain, shift):
    average = jnp.mean(values, axis=-1, keepdims=True)
    centred = values - average
    spread_sq = jnp.mean(centred * centred, axis=-1, keepdims=True)
    inv_root = lax.rsqrt(spread_sq + norm_eps)
    unit_rows = centred * inv_root
    return (unit_rows * gain + shift, unit_rows, inv_root)


def norm_backward(out_grad_rows, unit_rows, inv_root, gain):
    scaled = out_grad_rows * gain
    first_mean = jnp.mean(scaled, axis=-1, keepdims=True)
    second_mean = jnp.mean(scaled * unit_rows, axis=-1, keepdims=True)
    in_grad = inv_root * (scaled - first_mean - unit_rows * second_mean)
    return (in_grad, jnp.sum(out_grad_rows * unit_rows, axis=0), jnp.sum(out_grad_rows, axis=0))


def swap_halves(x, head_dim):
    half = head_dim // 2
    width = x.shape[1]
    lane = lax.broadcasted_iota(jnp.int32, x.shape, 1) % head_dim
    return jnp.where(lane < half, pltpu.roll(x, width - half, 1), pltpu.roll(x, half, 1))


def head_mask(x, h, head_dim):
    lane = lax.broadcasted_iota(jnp.int32, x.shape, 1)
    return jnp.where((lane >= h * head_dim) & (lane < (h + 1) * head_dim), x, jnp.zeros_like(x))


def widen(table, width):
    return jnp.concatenate([table] * (width // table.shape[1]), axis=1)


def project_kernel(head_dim, x_ref, w_ref, cos_ref, sin_ref, q_ref, k_ref, v_ref, kt_ref, vt_ref):
    width = q_ref.shape[1]
    x = x_ref[...]
    cos, sin = widen(cos_ref[...], width), widen(sin_ref[...], width)
    q, k, v = (dot_nn(x, w_ref[j]) for j in range(3))
    v = v.astype(BF16)
    q = q * cos + swap_halves(q, head_dim) * sin
    k = k * cos + swap_halves(k, head_dim) * sin
    k_low = k.astype(BF16)
    q_ref[...] = (q * (head_dim ** (-0.5) * log2_e)).astype(BF16)
    k_ref[...] = k_low
    v_ref[...] = v
    kt_ref[...] = k_low.T
    vt_ref[...] = v.T


def project(rows, w, cos_wide, sine_wide, head_dim):
    n, d = rows.shape
    width = w.shape[2]
    block = min(512, n)
    row = pl.BlockSpec((block, width), lambda i: (i, 0))
    col = pl.BlockSpec((width, block), lambda i: (0, i))
    table = pl.BlockSpec((block, cos_wide.shape[1]), lambda i: (i, 0))
    return pl.pallas_call(
        functools.partial(project_kernel, head_dim),
        grid=(n // block,),
        in_specs=[
            pl.BlockSpec((block, d), lambda i: (i, 0)),
            pl.BlockSpec((3, d, width), lambda i: (0, 0, 0)),
            table,
            table,
        ],
        out_specs=[row, row, row, col, col],
        out_shape=[jax.ShapeDtypeStruct((n, width), BF16)] * 3
        + [jax.ShapeDtypeStruct((width, n), BF16)] * 2,
        compiler_params=pltpu.CompilerParams(vmem_limit_bytes=VMEM_LIMIT),
        cost_estimate=pl.CostEstimate(
            flops=6 * n * d * width, bytes_accessed=2 * n * d + 18 * n * width, transcendentals=0
        ),
        name="project",
    )(rows, w, cos_wide, sine_wide)


def key_range(start, block, total):
    first = (start // SHORT_LEN) * SHORT_LEN
    last = min(total, ((start + block - 1) // SHORT_LEN + 1) * SHORT_LEN)
    return (first // 256) * 256, min(total, -(-last // 256) * 256)


def window_bias(key_start, keys, row_start, rows, total):
    key_at = lax.broadcasted_iota(jnp.int32, (keys, rows), 0) + key_start
    row_at = lax.broadcasted_iota(jnp.int32, (keys, rows), 1) + row_start
    key_window = jnp.zeros_like(key_at)
    row_window = jnp.zeros_like(row_at)
    for edge in range(SHORT_LEN, total, SHORT_LEN):
        key_window += (key_at >= edge).astype(jnp.int32)
        row_window += (row_at >= edge).astype(jnp.int32)
    return jnp.where(key_window == row_window, 0.0, mask_fill)


def attend_kernel(head_dim, bucket_ref, q_ref, k_ref, vt_ref, o_ref, ot_ref, l_ref, bias_ref):
    rows, width = q_ref.shape
    total = k_ref.shape[0]
    heads = width // head_dim
    step = pl.program_id(0)

    def block(at, first, last, masked):
        @pl.loop(0, heads)
        def _(h):
            hs = pl.ds(pl.multiple_of(h * head_dim, head_dim), head_dim)
            scores = dot_nt(k_ref[first:last, :], head_mask(q_ref[at, :], h, head_dim))
            if masked:
                scores = scores + bias_ref[: last - first, :]
            top = jnp.max(scores, axis=0, keepdims=True)
            weights = jnp.exp2(scores - top)
            totals = jnp.sum(weights, axis=0, keepdims=True)
            ot_ref[hs, at] = dot_nn(vt_ref[hs, first:last], weights.astype(BF16)) / totals
            l_ref[pl.ds(h, 1), at] = top + jnp.log2(totals)

    @pl.when(bucket_ref[0, 0] == 1)
    def _():
        block(slice(0, rows), 0, total, False)

    sub = bias_ref.shape[1]
    for start in range(0, total, sub):
        first, last = key_range(start, sub, total)

        @pl.when((bucket_ref[0, 0] != 1) & (step == start // rows))
        def _():
            bias_ref[: last - first, :] = window_bias(first, last - first, start, sub, total)
            block(slice(start % rows, start % rows + sub), first, last, True)

    o_ref[...] = ot_ref[...].T.astype(BF16)


def attend(bucket, q, k, vt, head_dim):
    n, width = q.shape
    heads = width // head_dim
    block = min(1024, n)
    pairs = n * n * heads
    lanes = -(-heads // 8) * 8
    row = pl.BlockSpec((block, width), lambda i: (i, 0))
    col = pl.BlockSpec((width, block), lambda i: (0, i))
    return pl.pallas_call(
        functools.partial(attend_kernel, head_dim),
        grid=(n // block,),
        in_specs=[
            pl.BlockSpec(memory_space=pltpu.SMEM),
            row,
            pl.BlockSpec((n, width), lambda i: (0, 0)),
            pl.BlockSpec((width, n), lambda i: (0, 0)),
        ],
        out_specs=[row, col, pl.BlockSpec((lanes, block), lambda i: (0, i))],
        out_shape=[
            jax.ShapeDtypeStruct((n, width), BF16),
            jax.ShapeDtypeStruct((width, n), F32),
            jax.ShapeDtypeStruct((lanes, n), F32),
        ],
        scratch_shapes=[pltpu.VMEM((n, min(512, block)), F32)],
        compiler_params=pltpu.CompilerParams(vmem_limit_bytes=VMEM_LIMIT),
        cost_estimate=pl.CostEstimate(
            flops=pairs * 1024, bytes_accessed=10 * n * width, transcendentals=pairs
        ),
        name="attend",
    )(bucket, q, k, vt)


def attend_back_kernel(
    head_dim,
    bucket_ref,
    q_ref,
    k_ref,
    kt_ref,
    v_ref,
    g_ref,
    ot_ref,
    l_ref,
    cos_ref,
    sin_ref,
    out_ref,
    bias_ref,
    gt_ref,
    dq_ref,
    dk_ref,
    dv_ref,
):
    rows, width = q_ref.shape
    total = k_ref.shape[0]
    heads = width // head_dim
    step = pl.program_id(0)

    @pl.when(step == 0)
    def _():
        dk_ref[...] = jnp.zeros_like(dk_ref)
        dv_ref[...] = jnp.zeros_like(dv_ref)

    gt_ref[...] = g_ref[...].astype(F32).T * ot_ref[...]

    def block(first, last, masked):
        keys = slice(first, last)

        @pl.loop(0, heads)
        def _(h):
            hs = pl.ds(pl.multiple_of(h * head_dim, head_dim), head_dim)
            qh, gh = head_mask(q_ref[...], h, head_dim), head_mask(g_ref[...], h, head_dim)
            scores = dot_nt(k_ref[keys, :], qh)
            if masked:
                scores = scores + bias_ref[: last - first, :]
            probs = jnp.exp2(scores - l_ref[pl.ds(h, 1), :])
            prob_grad = dot_nt(v_ref[keys, :], gh)
            delta = jnp.sum(gt_ref[hs, :], axis=0, keepdims=True)
            score_grad = (probs * (prob_grad - delta)).astype(BF16)
            dv_ref[keys, :] += dot_nn(probs.astype(BF16), gh)
            dk_ref[keys, :] += dot_nn(score_grad, qh)
            dq_ref[hs, :] = dot_nn(kt_ref[hs, keys], score_grad)

    @pl.when(bucket_ref[0, 0] == 1)
    def _():
        block(0, total, False)

    for start in range(0, total, rows):
        first, last = key_range(start, rows, total)

        @pl.when((bucket_ref[0, 0] != 1) & (step == start // rows))
        def _():
            bias_ref[: last - first, :] = window_bias(first, last - first, start, rows, total)
            block(first, last, True)

    def turn_back(grad, at):
        cos, sin = widen(cos_ref[at, :], width), widen(sin_ref[at, :], width)
        return (grad * cos - swap_halves(grad, head_dim) * sin).astype(BF16)

    at = pl.ds(pl.multiple_of(step * rows, rows), rows)
    out_ref[at, :width] = turn_back(dq_ref[...].T * head_dim ** (-0.5), at)

    @pl.when(step == pl.num_programs(0) - 1)
    def _():
        @pl.loop(0, total // rows)
        def _(i):
            at = pl.ds(pl.multiple_of(i * rows, rows), rows)
            out_ref[at, width : 2 * width] = turn_back(dk_ref[at, :] * (1.0 / log2_e), at)
            out_ref[at, 2 * width :] = dv_ref[at, :].astype(BF16)


def attend_back(bucket, q, k, kt, v, g, ot, log_totals, cos_wide, sine_wide, head_dim):
    n, width = q.shape
    heads = width // head_dim
    block = min(512, n)
    pairs = n * n * heads
    row = pl.BlockSpec((block, width), lambda i: (i, 0))
    col = pl.BlockSpec((width, block), lambda i: (0, i))
    full = lambda rows, cols: pl.BlockSpec((rows, cols), lambda i: (0, 0))
    table = full(n, cos_wide.shape[1])
    return pl.pallas_call(
        functools.partial(attend_back_kernel, head_dim),
        grid=(n // block,),
        in_specs=[
            pl.BlockSpec(memory_space=pltpu.SMEM),
            row,
            full(n, width),
            full(width, n),
            full(n, width),
            row,
            col,
            pl.BlockSpec((log_totals.shape[0], block), lambda i: (0, i)),
            table,
            table,
        ],
        out_specs=full(n, 3 * width),
        out_shape=jax.ShapeDtypeStruct((n, 3 * width), BF16),
        scratch_shapes=[
            pltpu.VMEM((n, block), F32),
            pltpu.VMEM((width, block), F32),
            pltpu.VMEM((width, block), F32),
            pltpu.VMEM((n, width), F32),
            pltpu.VMEM((n, width), F32),
        ],
        compiler_params=pltpu.CompilerParams(vmem_limit_bytes=VMEM_LIMIT),
        cost_estimate=pl.CostEstimate(
            flops=pairs * 2560, bytes_accessed=24 * n * width, transcendentals=pairs
        ),
        name="attend_back",
    )(bucket, q, k, kt, v, g, ot, log_totals, cos_wide, sine_wide)


def feed_kernel(x_ref, c_ref, wgu_ref, wd_ref, h_ref, b_ref, n_ref):
    units = wd_ref.shape[0]
    both = dot_nn(x_ref[...], wgu_ref[...])
    gate, up = both[:, :units], both[:, units:]
    sig = jax.nn.sigmoid(gate)
    silu = gate * sig
    h_ref[...] = (silu * up).astype(BF16)
    hidden_grad = dot_nt(c_ref[...], wd_ref[...])
    b_ref[:, :units] = (hidden_grad * up * sig * (1.0 + gate * (1.0 - sig))).astype(BF16)
    b_ref[:, units:] = (hidden_grad * silu).astype(BF16)
    n_ref[...] = dot_nt(b_ref[...], wgu_ref[...]).astype(BF16)


def feed(x, cot, wgu, wd):
    n, d = x.shape
    units = wd.shape[0]
    block = min(256, n)
    row = lambda w: pl.BlockSpec((block, w), lambda i: (i, 0))
    return pl.pallas_call(
        feed_kernel,
        grid=(n // block,),
        in_specs=[
            row(d),
            row(d),
            pl.BlockSpec((d, 2 * units), lambda i: (0, 0)),
            pl.BlockSpec((units, d), lambda i: (0, 0)),
        ],
        out_specs=[row(units), row(2 * units), row(d)],
        out_shape=[
            jax.ShapeDtypeStruct((n, units), BF16),
            jax.ShapeDtypeStruct((n, 2 * units), BF16),
            jax.ShapeDtypeStruct((n, d), BF16),
        ],
        compiler_params=pltpu.CompilerParams(vmem_limit_bytes=VMEM_LIMIT),
        cost_estimate=pl.CostEstimate(
            flops=10 * n * d * units, bytes_accessed=8 * n * d, transcendentals=n * units
        ),
        name="feed",
    )(x, cot, wgu, wd)


MESH_ID = pl.DeviceIdType.MESH


def plane_peers():
    me = lax.axis_index("dp")
    return [{"dp": lax.bitwise_xor(me, bit)} for bit in (1, 2, 4)]


def enter(peers):
    barrier = pltpu.get_barrier_semaphore()
    for peer in peers:
        pl.semaphore_signal(barrier, inc=1, device_id=peer, device_id_type=MESH_ID)
    pl.semaphore_wait(barrier, len(peers))


def remote(src, dst, send, recv, at, peer):
    return pltpu.make_async_remote_copy(
        src_ref=src,
        dst_ref=dst,
        send_sem=send.at[at],
        recv_sem=recv.at[at],
        device_id=peer,
        device_id_type=MESH_ID,
    )


def gather_copies(view, send, recv, placed, cores=True):
    sib, across, along = plane_peers()
    steps = [
        (0, 1, sib, None),
        (0, 2, across, None),
        (0, 4, along, None),
        (4, 2, across, 0),
        (2, 4, along, 1),
        (2, 1, sib, None),
        (4, 1, sib, None),
        (6, 1, sib, None),
    ]
    copies = {}
    for i, (s, bit, peer, part) in enumerate(steps):
        if bit == 1 and not cores:
            continue
        src = view(s, part)
        dst = src if placed else view(s ^ bit, part)
        copies[f"{s}-{s ^ bit}"] = remote(src, dst, send, recv, i, peer)
    return copies


def half_of(ref, part):
    if part is None:
        return ref
    half = ref.shape[-2] // 2
    return ref.at[(slice(None),) * (len(ref.shape) - 2) + (pl.ds(part * half, half),)]


def gather_start(copies):
    for name in ("0-2", "0-4", "0-1"):
        copies[name].start()


def gather_forward(copies):
    copies["0-2"].wait_recv()
    copies["2-6"].start()
    copies["2-3"].start()
    copies["0-4"].wait_recv()
    copies["4-6"].start()
    copies["4-5"].start()


def gather_finish(copies):
    copies["2-6"].wait_recv()
    copies["4-6"].wait_recv()
    copies["6-7"].start()
    for name in ("0-1", "2-3", "4-5", "6-7"):
        copies[name].wait_recv()


def head_share():
    core, z = lax.rem(lax.axis_index("dp"), 2), lax.axis_index("tensor")
    return core, 2 * lax.rem(z, 2) + core, z // 2


def head_source(s):
    return s % 2, 2 * lax.rem(lax.axis_index("dp"), 2) + s // 2


def front_kernel(
    head_dim,
    bucket_ref,
    tok_ref,
    gain_ref,
    shift_ref,
    freq_ref,
    cot_ref,
    wo_ref,
    wq_ref,
    q_ref,
    k_ref,
    v_ref,
    kt_ref,
    vt_ref,
    cos_ref,
    sin_ref,
    bucket_out,
    rows_out,
    cots_out,
    wos_out,
    wq_out,
    rows_all,
    mine,
    other,
    cots,
    wos,
    wq,
    buckets,
    nsend,
    nrecv,
    csend,
    crecv,
    wsend,
    wrecv,
    qsend,
    qrecv,
    zsend,
    zrecv,
    psend,
    precv,
    bsend,
    brecv,
    local,
):
    ways, rows, d = rows_all.shape
    half = rows // 2
    out_rows = wos.shape[2]
    width = q_ref.shape[1]
    me, z = lax.axis_index("dp"), lax.axis_index("tensor")
    core, heads_of, group_of = head_share()
    sib, across, along = plane_peers()
    others = [{"tensor": lax.rem(z + k, ways)} for k in range(1, ways)]
    z1, z2, z3 = (lax.bitwise_xor(z, k) for k in (1, 2, 3))
    near, far = {"tensor": z1}, {"tensor": z2}
    chip_rows = wq.shape[1] // 4
    enter([sib, across, along] + others)

    buckets[0] = jnp.full(buckets.shape[1:], bucket_ref[0], jnp.int32)
    bucket_copy = remote(buckets.at[0], buckets.at[1], bsend, brecv, 0, sib)
    bucket_copy.start()
    loads = [
        pltpu.make_async_copy(cot_ref.at[pl.ds(0, half)], cots.at[0], local.at[0]),
        pltpu.make_async_copy(
            wo_ref.at[pl.ds(pl.multiple_of(me * out_rows, 16), out_rows)],
            wos.at[z, me],
            local.at[1],
        ),
    ]
    for load in loads:
        load.start()

    def chip_part(chip, part):
        size = chip_rows if part is None else chip_rows // 2
        first = chip * chip_rows + (0 if part is None else part * size)
        return wq.at[:, pl.ds(pl.multiple_of(first, 16), size)]

    chip = me // 2
    chip_src = wq_ref.at[:, pl.ds(pl.multiple_of(chip * chip_rows, 16), chip_rows)]
    gives = core == lax.rem(z, 2)

    def piece_copy(k):
        return pltpu.make_async_remote_copy(
            src_ref=chip_src,
            dst_ref=chip_part(chip, None),
            send_sem=psend.at[k],
            recv_sem=precv.at[0],
            device_id={"tensor": z // 2 + 2 * k},
            device_id_type=MESH_ID,
        )

    piece_own = pltpu.make_async_copy(chip_src, chip_part(chip, None), local.at[2])
    for k in range(2):

        @pl.when(gives & (z // 2 + 2 * k != z))
        def _():
            piece_copy(k).start()

    @pl.when(heads_of == z)
    def _():
        piece_own.start()

    cot_copies = gather_copies(
        lambda s, part: half_of(cots.at[s], part), csend, crecv, False
    )
    loads[0].wait()
    gather_start(cot_copies)

    step = 128

    @pl.loop(0, rows // step)
    def _(i):
        at = pl.ds(pl.multiple_of(i * step, step), step)
        values = tok_ref[at, :].astype(F32)
        centred = values - jnp.mean(values, axis=-1, keepdims=True)
        root = lax.rsqrt(jnp.mean(centred * centred, axis=-1, keepdims=True) + norm_eps)
        mine[at, :] = (centred * root * gain_ref[...] + shift_ref[...]).astype(BF16)

    def part_of(which):
        return pl.ds(pl.multiple_of(which * half, half), half)

    def rows_at(block, which):
        return rows_all.at[block, part_of(which)]

    home = group_of == core
    give = [
        remote(mine.at[part_of(1 - core)], rows_at(z, 1 - core), nsend, nrecv, 0, sib),
        remote(mine.at[part_of(core)], rows_at(z, core), nsend, nrecv, 1, sib),
    ]
    swap = remote(mine.at[part_of(1 - core)], other, nsend, nrecv, 0, sib)
    to_far = remote(other, rows_at(z, core), nsend, nrecv, 2, far)
    to_near = remote(rows_at(z, core), rows_at(z, core), nsend, nrecv, 3, near)
    relay = remote(rows_at(z2, core), rows_at(z2, core), nsend, nrecv, 4, near)
    shares = {
        b: remote(rows_at(block, core), rows_at(block, core), nsend, nrecv, 4 + b, sib)
        for b, block in ((1, z1), (2, z2), (3, z3))
    }

    @pl.when(home)
    def _():
        give[0].start()
        give[1].start()
        rows_all[z] = mine[...]
        swap.wait_recv()
        to_far.start()
        to_near.start()

    @pl.when(jnp.logical_not(home))
    def _():
        swap.start()
        other[...] = mine[part_of(core), :]
        to_far.start()
        give[0].wait_recv()
        to_near.start()

    loads[1].wait()
    out_sends = []
    for k, peer in enumerate(others):
        slice_ref = wos.at[z, me]
        out_sends.append(
            pltpu.make_async_remote_copy(
                src_ref=slice_ref,
                dst_ref=slice_ref,
                send_sem=zsend.at[k],
                recv_sem=zrecv.at[z],
                device_id=peer,
                device_id_type=MESH_ID,
            )
        )
        out_sends[-1].start()

    qkv_copies = gather_copies(
        lambda s, part: chip_part(lax.bitwise_xor(chip, s // 2), part), qsend, qrecv, True, False
    )
    out_copies = gather_copies(
        lambda s, part: half_of(wos.at[:, lax.bitwise_xor(me, s)], part), wsend, wrecv, True
    )

    @pl.when(heads_of == z)
    def _():
        piece_own.wait()

    @pl.when(heads_of != z)
    def _():
        piece_copy(0).wait_recv()

    qkv_copies["0-2"].start()
    qkv_copies["0-4"].start()
    gather_forward(cot_copies)

    bucket_copy.wait_recv()
    bucket = jnp.where(home, buckets[0], buckets[1])
    bucket_out[...] = bucket
    span = jnp.where(bucket[0:1] == 1, LONG_LEN, SHORT_LEN)
    freq = freq_ref[...]
    lane = lax.broadcasted_iota(jnp.int32, freq.shape, 1)
    sign = jnp.where(lax.rem(lane, head_dim) < head_dim // 2, -1.0, 1.0)
    total = ways * rows

    @pl.loop(0, total // step)
    def _(i):
        at = pl.ds(pl.multiple_of(i * step, step), step)
        position = lax.broadcasted_iota(jnp.int32, (step, freq.shape[1]), 0) + i * step
        place = position
        for k in range(1, -(-total // SHORT_LEN)):
            place = place - jnp.where(position >= k * span, span, 0)
        angles = place.astype(F32) * freq
        cos_ref[at, :] = jnp.cos(angles)
        sin_ref[at, :] = jnp.sin(angles) * sign

    to_far.wait_recv()
    relay.start()
    shares[2].start()
    to_near.wait_recv()
    shares[1].start()
    qkv_copies["0-2"].wait_recv()
    qkv_copies["2-6"].start()
    qkv_copies["0-4"].wait_recv()
    qkv_copies["4-6"].start()
    for k, peer in enumerate(others):
        source = lax.rem(z + k + 1, ways)
        theirs = wos.at[source, me]
        pltpu.make_async_remote_copy(
            src_ref=theirs,
            dst_ref=theirs,
            send_sem=zsend.at[k],
            recv_sem=zrecv.at[source],
            device_id=peer,
            device_id_type=MESH_ID,
        ).wait_recv()
    gather_start(out_copies)
    qkv_copies["2-6"].wait_recv()
    qkv_copies["4-6"].wait_recv()
    wq_copy = pltpu.make_async_copy(wq, wq_out, local.at[0])
    wq_copy.start()

    stores = [
        pltpu.make_async_copy(rows_all, rows_out, local.at[1]),
        pltpu.make_async_copy(cots, cots_out, local.at[2]),
        pltpu.make_async_copy(wos, wos_out, local.at[3]),
    ]

    @pl.when(jnp.logical_not(home))
    def _():
        give[1].wait_recv()

    @pl.loop(0, ways)
    def _(i):
        @pl.when(i == 1)
        def _():
            shares[1].wait_recv()

        @pl.when(i == 2)
        def _():
            shares[2].wait_recv()
            gather_forward(out_copies)

        @pl.when(i == 3)
        def _():
            relay.wait_recv()
            shares[3].start()
            shares[3].wait_recv()
            stores[0].start()
            gather_finish(cot_copies)
            stores[1].start()

        block = lax.bitwise_xor(z, i)
        at = pl.ds(pl.multiple_of(block * rows, rows), rows)
        x = rows_all[block]
        cos, sin = widen(cos_ref[at, :], width), widen(sin_ref[at, :], width)
        q, k, v = (dot_nn(x, wq[j]) for j in range(3))
        v = v.astype(BF16)
        q = q * cos + swap_halves(q, head_dim) * sin
        k = (k * cos + swap_halves(k, head_dim) * sin).astype(BF16)
        q_ref[at, :] = (q * (head_dim ** (-0.5) * log2_e)).astype(BF16)
        k_ref[at, :] = k
        v_ref[at, :] = v
        kt_ref[:, at] = k.T
        vt_ref[:, at] = v.T

    gather_finish(out_copies)
    stores[2].start()
    for store in (wq_copy, *stores):
        store.wait()

    @pl.when(home)
    def _():
        give[0].wait_send()
        give[1].wait_send()

    @pl.when(jnp.logical_not(home))
    def _():
        swap.wait_send()

    for k in range(2):

        @pl.when(gives & (z // 2 + 2 * k != z))
        def _():
            piece_copy(k).wait_send()

    for copy in (to_far, to_near, relay, bucket_copy, *shares.values(), *out_sends):
        copy.wait_send()
    for copy in (*qkv_copies.values(), *cot_copies.values(), *out_copies.values()):
        copy.wait_send()


def front(bucket, tokens, gain, shift, cot, w_out, w_qkv, head_dim, ways):
    rows, d = tokens.shape
    width = w_qkv.shape[2]
    out_rows = w_out.shape[0] // 8
    total = ways * rows
    lanes = 128
    half_dim = head_dim // 2
    exponents = jnp.arange(half_dim, dtype=F32) * (-2.0 / head_dim)
    freq = jnp.tile(jnp.exp(exponents * jnp.log(F32(rope_base))), lanes // half_dim)[None]
    anywhere = pl.BlockSpec(memory_space=pl.ANY)
    inside = pl.BlockSpec(memory_space=pltpu.VMEM)
    sems = lambda n: [pltpu.SemaphoreType.DMA((n,))] * 2
    shape = jax.ShapeDtypeStruct
    return pl.pallas_call(
        functools.partial(front_kernel, head_dim),
        in_specs=[pl.BlockSpec(memory_space=pltpu.SMEM)] + [inside] * 4 + [anywhere] * 3,
        out_specs=[inside] * 8 + [anywhere] * 4,
        out_shape=[
            shape((total, width), BF16),
            shape((total, width), BF16),
            shape((total, width), BF16),
            shape((width, total), BF16),
            shape((width, total), BF16),
            shape((total, lanes), F32),
            shape((total, lanes), F32),
            shape((8, lanes), jnp.int32),
            shape((ways, rows, d), BF16),
            shape((8, rows // 2, d), BF16),
            shape((ways, 8, out_rows, d), BF16),
            shape(w_qkv.shape, BF16),
        ],
        scratch_shapes=[
            pltpu.VMEM((ways, rows, d), BF16),
            pltpu.VMEM((rows, d), BF16),
            pltpu.VMEM((rows // 2, d), BF16),
            pltpu.VMEM((8, rows // 2, d), BF16),
            pltpu.VMEM((ways, 8, out_rows, d), BF16),
            pltpu.VMEM(w_qkv.shape, BF16),
            pltpu.VMEM((2, 8, lanes), jnp.int32),
        ]
        + sems(8)
        + sems(8)
        + sems(8)
        + sems(8)
        + sems(ways)
        + sems(2)
        + sems(1)
        + [pltpu.SemaphoreType.DMA((4,))],
        compiler_params=pltpu.CompilerParams(
            collective_id=0, has_side_effects=True, vmem_limit_bytes=VMEM_LIMIT
        ),
        cost_estimate=pl.CostEstimate(
            flops=55 * 10**9, bytes_accessed=32 * rows * d, transcendentals=0
        ),
        name="front",
    )(bucket, tokens, gain[None], shift[None], freq, cot, w_out, w_qkv)


def column(ways):
    me, z = lax.axis_index("dp"), lax.axis_index("tensor")
    sib = lax.bitwise_xor(me, 1)
    others = [{"dp": sib, "tensor": z}]
    for k in range(1, ways):
        to = lax.rem(z + k, ways)
        others += [{"dp": me, "tensor": to}, {"dp": sib, "tensor": to}]
    return others


def collect_kernel(
    att_ref,
    tok_ref,
    wo_ref,
    gain_ref,
    shift_ref,
    cot_ref,
    at_ref,
    resid_ref,
    n_ref,
    cots_out,
    at,
    cots,
    isend,
    irecv,
    csend,
    crecv,
    lsem,
):
    ways, rows, quarter = at.shape
    me, z = lax.axis_index("dp"), lax.axis_index("tensor")
    core, heads_of, group_of = head_share()
    enter(column(ways) + plane_peers()[1:])
    half = rows // 2
    cot_own = pltpu.make_async_copy(cot_ref.at[pl.ds(half, half)], cots.at[0], lsem.at[1])
    cot_own.start()

    def in_copy(to):
        return pltpu.make_async_remote_copy(
            src_ref=att_ref.at[pl.ds(pl.multiple_of(to * rows, rows), rows)],
            dst_ref=at.at[heads_of],
            send_sem=isend.at[to],
            recv_sem=irecv.at[heads_of],
            device_id={"dp": me - core + group_of, "tensor": to},
            device_id_type=MESH_ID,
        )

    def in_wait(s):
        return pltpu.make_async_remote_copy(
            src_ref=att_ref.at[pl.ds(0, rows)],
            dst_ref=at.at[s],
            send_sem=isend.at[0],
            recv_sem=irecv.at[s],
            device_id={"dp": me - core + group_of, "tensor": z},
            device_id_type=MESH_ID,
        )

    own_at = group_of == core
    in_own = pltpu.make_async_copy(
        att_ref.at[pl.ds(pl.multiple_of(z * rows, rows), rows)], at.at[heads_of], lsem.at[0]
    )
    for k in range(ways - 1, 0, -1):
        in_copy(lax.bitwise_xor(z, k)).start()

    @pl.when(own_at)
    def _():
        in_own.start()
        in_own.wait()

    @pl.when(jnp.logical_not(own_at))
    def _():
        in_copy(z).start()

    copies = gather_copies(lambda s, part: half_of(cots.at[s], part), csend, crecv, False)
    cot_own.wait()
    gather_start(copies)
    gather_forward(copies)

    turn = jnp.where(z > 2 * core, 2, 0)
    step = min(256, rows)

    @pl.loop(0, ways)
    def _(k):
        s = lax.bitwise_xor(k, turn)
        source_core, source_z = head_source(s)

        @pl.when(jnp.logical_not((source_core == core) & (source_z == z)))
        def _():
            in_wait(s).wait_recv()

        at_ref[s] = at[s]
        weights = wo_ref[pl.ds(pl.multiple_of(s * quarter, quarter), quarter), :]

        @pl.when(k == 0)
        def _():
            resid_ref[...] = tok_ref[...].astype(F32) + dot_nn(at[s], weights)

        @pl.when(k > 0)
        def _():
            resid_ref[...] += dot_nn(at[s], weights)

    @pl.loop(0, rows // step)
    def _(k):
        rs = pl.ds(pl.multiple_of(k * step, step), step)
        acc = resid_ref[rs, :]
        centred = acc - jnp.mean(acc, axis=-1, keepdims=True)
        root = lax.rsqrt(jnp.mean(centred * centred, axis=-1, keepdims=True) + norm_eps)
        n_ref[rs, :] = (centred * root * gain_ref[...] + shift_ref[...]).astype(BF16)

    gather_finish(copies)
    cots_copy = pltpu.make_async_copy(cots, cots_out, lsem.at[1])
    cots_copy.start()
    for copy in copies.values():
        copy.wait_send()
    for k in range(1, ways):
        in_copy(lax.bitwise_xor(z, k)).wait_send()

    @pl.when(jnp.logical_not(own_at))
    def _():
        in_copy(z).wait_send()

    cots_copy.wait()


def collect(attended, tokens, out_full, gain, shift, cot, ways):
    rows, d = tokens.shape
    quarter = d // ways
    anywhere = pl.BlockSpec(memory_space=pl.ANY)
    inside = pl.BlockSpec(memory_space=pltpu.VMEM)
    return pl.pallas_call(
        collect_kernel,
        in_specs=[anywhere] + [inside] * 4 + [anywhere],
        out_specs=[inside] * 3 + [anywhere],
        out_shape=[
            jax.ShapeDtypeStruct((ways, rows, quarter), BF16),
            jax.ShapeDtypeStruct((rows, d), F32),
            jax.ShapeDtypeStruct((rows, d), BF16),
            jax.ShapeDtypeStruct((8, rows // 2, d), BF16),
        ],
        scratch_shapes=[
            pltpu.VMEM((ways, rows, quarter), BF16),
            pltpu.VMEM((8, rows // 2, d), BF16),
            pltpu.SemaphoreType.DMA((ways,)),
            pltpu.SemaphoreType.DMA((ways,)),
            pltpu.SemaphoreType.DMA((8,)),
            pltpu.SemaphoreType.DMA((8,)),
            pltpu.SemaphoreType.DMA((2,)),
        ],
        compiler_params=pltpu.CompilerParams(
            collective_id=3, has_side_effects=True, vmem_limit_bytes=VMEM_LIMIT
        ),
        cost_estimate=pl.CostEstimate(
            flops=30 * 10**9, bytes_accessed=16 * rows * d, transcendentals=0
        ),
        name="collect",
    )(attended, tokens, out_full, gain[None], shift[None], cot)


def middle_kernel(
    x_ref,
    at_ref,
    resid_ref,
    wo_ref,
    c_low_ref,
    c_high_ref,
    w_low_ref,
    w_high_ref,
    gain_ref,
    ag_ref,
    rg_ref,
    og_ref,
    out_ref,
    high_ref,
    grads_ref,
    ng_ref,
    wgu_ref,
    wd_ref,
    xs,
    cs,
    hid,
    branch,
    part,
    from_sib,
    from_far,
    from_x,
    from_y,
    down_acc,
    gate_up_acc,
    resid,
    at,
    agr,
    gsend,
    grecv,
    ssend,
    srecv,
    fsend,
    frecv,
    osend,
    orecv,
    csem,
    wsem,
    upsend,
    uprecv,
    downsend,
    downrecv,
    lsem,
    credit,
):
    ways, unit = w_low_ref.shape[0], w_low_ref.shape[1] // 3
    part_units = ways * unit
    units = 2 * part_units
    rows, d = x_ref.shape
    quarter = d // ways
    half = rows // 2
    low, high = pl.ds(0, half), pl.ds(half, half)
    keep = out_ref.shape[0]
    kept, others_at = pl.ds(0, keep), pl.ds(keep, rows - keep)
    me, z = lax.axis_index("dp"), lax.axis_index("tensor")
    core, heads_of, group_of = head_share()
    sib, across, along = plane_peers()
    enter(column(ways) + [across, along])

    own_at = group_of == core
    half_wo = ways // 2
    step = min(256, rows)
    own = pltpu.make_async_copy(x_ref, xs.at[0], lsem.at[0])
    own.start()
    first_loads = [
        pltpu.make_async_copy(at_ref, at, lsem.at[1]),
        pltpu.make_async_copy(resid_ref, resid, lsem.at[2]),
    ]
    cots = [
        pltpu.make_async_copy(ref.at[i], cs.at[i, side], csem.at[i, k])
        for i in range(8)
        for k, (ref, side) in enumerate(((c_low_ref, low), (c_high_ref, high)))
    ]

    def weight_place(t, j, upper):
        first = part_units * (upper if j == 2 else 2 * upper + j) + t * unit
        ref = wd_ref if j == 2 else wgu_ref
        return ref.at[pl.ds(first if isinstance(first, int) else pl.multiple_of(first, 16), unit)]

    weights = [
        pltpu.make_async_copy(
            w_low_ref.at[t, pl.ds(j * unit, unit)], weight_place(t, j, 0), wsem.at[t, j]
        )
        for t in range(ways)
        for j in range(3)
    ]
    upper_own = [
        pltpu.make_async_copy(
            w_high_ref.at[pl.ds(j * unit, unit)], weight_place(z, j, 1), wsem.at[ways, j]
        )
        for j in range(3)
    ]
    above, below = {"tensor": lax.rem(z + 1, ways)}, {"tensor": lax.rem(z + ways - 1, ways)}

    def weight_up(t):
        return [
            pltpu.make_async_remote_copy(
                src_ref=weight_place(t, j, 1),
                dst_ref=weight_place(t, j, 1),
                send_sem=upsend.at[t, j],
                recv_sem=uprecv.at[t, j],
                device_id=above,
                device_id_type=MESH_ID,
            )
            for j in range(3)
        ]

    def weight_down(t):
        return [
            pltpu.make_async_remote_copy(
                src_ref=weight_place(t, j, 1),
                dst_ref=weight_place(t, j, 1),
                send_sem=downsend.at[t, j],
                recv_sem=downrecv.at[t, j],
                device_id=below,
                device_id_type=MESH_ID,
            )
            for j in range(3)
        ]

    def weight_round(r):
        t = z + 1 + r

        @pl.when(t < ways)
        def _():
            for copy in weight_down(t):
                copy.wait_recv()

            @pl.when(z > 0)
            def _():
                for copy in weight_down(t):
                    copy.start()

        u = z - 1 - r

        @pl.when(u >= 0)
        def _():
            for copy in weight_up(u):
                copy.wait_recv()

            @pl.when(z < ways - 1)
            def _():
                for copy in weight_up(u):
                    copy.start()

    own.wait()
    copies = gather_copies(lambda s, side: half_of(xs.at[s], side), gsend, grecv, False)
    gather_start(copies)
    for load in (*upper_own, *weights, *cots, *first_loads):
        load.start()
    for load in upper_own:
        load.wait()

    @pl.when(z < ways - 1)
    def _():
        for copy in weight_up(z):
            copy.start()

    @pl.when(z > 0)
    def _():
        for copy in weight_down(z):
            copy.start()

    down_acc[...] = jnp.zeros_like(down_acc)
    gate_up_acc[...] = jnp.zeros_like(gate_up_acc)
    for load in weights:
        load.wait()

    def plane_sums(send, recv, src, landing, size):
        first, second = pl.ds(0, size // 2), pl.ds(size // 2, size // 2)
        steps = [
            ("1", src(1), landing[0], sib),
            ("3", src(3), landing[1], sib),
            ("5", src(5), landing[2], sib),
            ("7", src(7), landing[3], sib),
            ("6l", src(6).at[first], from_far.at[first], across),
            ("6h", src(6).at[second], from_far.at[second], along),
            ("2l", src(2).at[first], from_x.at[first], across),
            ("2h", src(2).at[second], from_x.at[second], across),
            ("4l", src(4).at[first], from_y.at[first], along),
            ("4h", src(4).at[second], from_y.at[second], along),
        ]
        return {
            name: remote(ref, dst, send, recv, i, peer)
            for i, (name, ref, dst, peer) in enumerate(steps)
        }

    def add_to(ref, other):
        ref[...] = (ref[...].astype(F32) + other[...].astype(F32)).astype(BF16)

    def slot(i):
        return i // 2 if i % 2 == 0 else 4 + (i // 2) % 2

    landing = [from_sib.at[0], from_sib.at[0], from_sib.at[1], from_sib.at[2]]
    sums = plane_sums(ssend, srecv, lambda i: part.at[slot(i)], landing, rows)

    def forward(i, place, into):
        both = dot_nt(xs[i], wgu_ref[...])
        hidden_grad = dot_nt(cs[i], wd_ref[...])
        for upper in range(2):
            of_units = slice(upper * part_units, (upper + 1) * part_units)
            first = upper * units
            gate = both[:, first : first + part_units]
            up = both[:, first + part_units : first + units]
            grad = hidden_grad[:, of_units]
            sig = jax.nn.sigmoid(gate)
            silu = gate * sig
            hid[place, :, of_units] = (silu * up).astype(BF16)
            branch[place, :, first : first + part_units] = (
                grad * up * sig * (1.0 + gate * (1.0 - sig))
            ).astype(BF16)
            branch[place, :, first + part_units : first + units] = (grad * silu).astype(BF16)
        part[into] = dot_nn(branch[place], wgu_ref[...]).astype(BF16)

    def grads(i, place):
        down_acc[...] += dot_tn(hid[place], cs[i])
        gate_up_acc[...] += dot_tn(branch[place], xs[i])
        cs[i] = dot_nn(hid[place], wd_ref[...]).astype(BF16)

    def cot_wait(i, slots):
        for k in slots:

            @pl.when(i == k)
            def _(k=k):
                cots[2 * k].wait()
                cots[2 * k + 1].wait()

    weight_round(0)
    weight_round(1)
    gather_forward(copies)
    for r in range(2, ways - 1):
        weight_round(r)

    @pl.loop(2, 8)
    def _(i):
        @pl.when(i == 3)
        def _():
            copies["2-3"].wait_recv()

        @pl.when(i == 5)
        def _():
            copies["4-5"].wait_recv()
            sums["3"].wait_recv()
            add_to(part.at[1], from_sib.at[0])
            sums["2l"].start()

        @pl.when(i == 6)
        def _():
            copies["2-6"].wait_recv()
            copies["4-6"].wait_recv()
            copies["6-7"].start()

        @pl.when(i == 7)
        def _():
            copies["6-7"].wait_recv()
            sums["5"].wait_recv()
            add_to(part.at[2], from_sib.at[1])
            sums["4h"].start()
            sums["3"].wait_send()

        cot_wait(i, range(2, 8))
        even = lax.rem(i, 2) == 0
        forward(i, i - 2, jnp.where(even, i // 2, 4 + lax.rem(i // 2, 2)))
        for odd in (3, 5, 7):

            @pl.when(i == odd)
            def _(odd=odd):
                sums[str(odd)].start()

    @pl.loop(2, 8)
    def _(i):
        @pl.when(i == 3)
        def _():
            sums["7"].wait_recv()
            add_to(part.at[3], from_sib.at[2])
            sums["6l"].start()
            sums["6h"].start()

        grads(i, i - 2)

    def grant(k, peer):
        pl.semaphore_signal(credit.at[k], inc=1, device_id=peer, device_id_type=MESH_ID)

    grant(0, sib)
    outs = plane_sums(
        fsend,
        frecv,
        lambda i: cs.at[i],
        [from_sib.at[0], from_sib.at[1], branch.at[5], from_sib.at[2]],
        keep,
    )
    pl.semaphore_wait(credit.at[0], 1)
    for name in ("7", "3", "5"):
        outs[name].start()
    copies["0-1"].wait_recv()
    sums["5"].wait_send()

    @pl.loop(0, 2)
    def _(i):
        cot_wait(i, (0, 1))
        forward(i, i, 4 * i)

        @pl.when(i == 0)
        def _():
            sums["6l"].wait_recv()
            add_to(part.at[2, low], from_far.at[low])
            sums["4l"].start()
            sums["6h"].wait_recv()
            add_to(part.at[1, high], from_far.at[high])
            sums["2h"].start()
            grant(1, across)
            grant(2, along)

        @pl.when(i == 1)
        def _():
            sums["1"].start()

        grads(i, i)

    sums["1"].wait_recv()
    add_to(part.at[0], from_sib.at[0])
    grant(3, sib)
    for copy in copies.values():
        copy.wait_send()
    for t in range(ways):
        for j in range(3):
            for upper in range(2):
                row = 2 * (3 * t + j) * unit + upper * unit
                first = part_units * (upper if j == 2 else 2 * upper + j) + t * unit
                acc = down_acc if j == 2 else gate_up_acc
                branch[row // rows, row % rows : row % rows + unit] = acc[
                    first : first + unit
                ].astype(BF16)
    for load in first_loads:
        load.wait()
    grads_copy = pltpu.make_async_copy(branch.at[pl.ds(0, grads_ref.shape[0])], grads_ref, lsem.at[1])
    wo_loads = [
        pltpu.make_async_copy(wo_ref.at[pl.ds(0, rows)], branch.at[3], lsem.at[2]),
        pltpu.make_async_copy(wo_ref.at[pl.ds(rows, rows)], branch.at[4], lsem.at[3]),
        pltpu.make_async_copy(c_low_ref.at[0], xs.at[3, low], lsem.at[0]),
        pltpu.make_async_copy(c_high_ref.at[0], xs.at[3, high], lsem.at[4]),
    ]
    grads_copy.start()
    for load in wo_loads:
        load.start()

    outs["7"].wait_recv()
    add_to(cs.at[6], from_sib.at[2])
    outs["3"].wait_recv()
    add_to(cs.at[2], from_sib.at[1])
    outs["5"].wait_recv()
    add_to(cs.at[4], branch.at[5])
    pl.semaphore_wait(credit.at[3], 1)
    outs["1"].start()

    grad = gate_up_acc
    for name in ("2l", "2h", "4l", "4h"):
        sums[name].wait_recv()
    pl.semaphore_wait(credit.at[1], 1)
    pl.semaphore_wait(credit.at[2], 1)
    outs["6l"].start()
    outs["6h"].start()

    @pl.loop(0, rows // step)
    def _(k):
        rs = pl.ds(pl.multiple_of(k * step, step), step)
        grad[rs, :] = (
            part[0, rs, :].astype(F32) + from_x[rs, :].astype(F32) + from_y[rs, :].astype(F32)
        )

    grant(4, across)
    grant(5, along)

    for load in wo_loads:
        load.wait()
    ng_ref[...] = jnp.zeros_like(ng_ref)
    gain = gain_ref[...]
    small = min(128, rows)

    @pl.loop(0, rows // small)
    def _(k):
        rs = pl.ds(pl.multiple_of(k * small, small), small)
        values = resid[rs, :]
        centred = values - jnp.mean(values, axis=-1, keepdims=True)
        root = lax.rsqrt(jnp.mean(centred * centred, axis=-1, keepdims=True) + norm_eps)
        unit_rows = centred * root
        out_grad = grad[rs, :]
        ng_ref[2:3] += jnp.sum(out_grad * unit_rows, axis=0, keepdims=True)
        ng_ref[3:4] += jnp.sum(out_grad, axis=0, keepdims=True)
        scaled = out_grad * gain
        first_mean = jnp.mean(scaled, axis=-1, keepdims=True)
        second_mean = jnp.mean(scaled * unit_rows, axis=-1, keepdims=True)
        total = xs[3, rs, :].astype(F32) + root * (scaled - first_mean - unit_rows * second_mean)
        grad[rs, :] = total
        xs[1, rs, :] = total.astype(BF16)

    rg_copy = pltpu.make_async_copy(grad.at[pl.ds(0, rows)], rg_ref, lsem.at[0])
    rg_copy.start()

    def out_copy(s):
        to_core, to_z = head_source(s)
        return pltpu.make_async_remote_copy(
            src_ref=xs.at[2, :, pl.ds(s * quarter, quarter)],
            dst_ref=agr.at[z],
            send_sem=osend.at[s],
            recv_sem=orecv.at[z],
            device_id={"dp": me - core + to_core, "tensor": to_z},
            device_id_type=MESH_ID,
        )

    def out_wait(source):
        return pltpu.make_async_remote_copy(
            src_ref=xs.at[2, :, pl.ds(0, quarter)],
            dst_ref=agr.at[source],
            send_sem=osend.at[0],
            recv_sem=orecv.at[source],
            device_id={"dp": me, "tensor": z},
            device_id_type=MESH_ID,
        )

    for s in range(ways):
        place = 3 + s // half_wo
        first = (s % half_wo) * quarter
        xs[2, :, s * quarter : (s + 1) * quarter] = dot_nt(
            xs[1], branch[place, first : first + quarter, :]
        ).astype(BF16)
        to_core, to_z = head_source(s)
        to_self = (to_core == core) & (to_z == z)

        @pl.when(jnp.logical_not(to_self))
        def _():
            out_copy(s).start()

        @pl.when(to_self)
        def _():
            agr[z] = xs[2, :, s * quarter : (s + 1) * quarter]

    pl.semaphore_wait(credit.at[4], 1)
    pl.semaphore_wait(credit.at[5], 1)
    outs["2l"].start()
    outs["4h"].start()

    for s in range(ways):
        place = 6 + s // half_wo
        first = (s % half_wo) * quarter
        xs[place, first : first + quarter] = dot_tn(at[s], xs[1]).astype(BF16)
    og_copy = pltpu.make_async_copy(xs.at[pl.ds(6, 2)], og_ref, lsem.at[2])
    og_copy.start()

    outs["1"].wait_recv()
    add_to(cs.at[0], from_sib.at[0])
    high_copies = [
        pltpu.make_async_copy(cs.at[2 * k, others_at], high_ref.at[k], csem.at[k, 0])
        for k in range(4)
    ]
    for copy in high_copies:
        copy.start()
    first, second = pl.ds(0, keep // 2), pl.ds(keep // 2, keep // 2)
    outs["6l"].wait_recv()
    add_to(cs.at[4, first], from_far.at[first])
    outs["4l"].start()
    outs["6h"].wait_recv()
    add_to(cs.at[2, second], from_far.at[second])
    outs["2h"].start()

    for source in range(ways):

        @pl.when(jnp.logical_not(own_at & (z == source)))
        def _():
            out_wait(source).wait_recv()

    ag_copy = pltpu.make_async_copy(agr, ag_ref, lsem.at[3])
    ag_copy.start()
    for name in ("2l", "2h", "4l", "4h"):
        outs[name].wait_recv()
    total = resid[kept, :] + cs[0, kept, :].astype(F32)
    total += from_x[kept, :].astype(F32) + from_y[kept, :].astype(F32)
    xs[0, kept, :] = total.astype(BF16)
    grads_copy.wait()
    lo_copy = pltpu.make_async_copy(xs.at[0, kept], out_ref, lsem.at[1])
    lo_copy.start()
    for name in ("1", "7", "6l", "6h", "2l", "2h", "4l", "4h"):
        sums[name].wait_send()
    for copy in outs.values():
        copy.wait_send()
    for t in range(ways):

        @pl.when((t <= z) & (z < ways - 1))
        def _():
            for copy in weight_up(t):
                copy.wait_send()

        @pl.when((t >= z) & (z > 0))
        def _():
            for copy in weight_down(t):
                copy.wait_send()

    for s in range(ways):
        to_core, to_z = head_source(s)

        @pl.when(jnp.logical_not((to_core == core) & (to_z == z)))
        def _():
            out_copy(s).wait_send()

    for copy in (rg_copy, og_copy, ag_copy, lo_copy, *high_copies):
        copy.wait()


def middle(x, attended, resid, out_full, cot_low, cot_high, w_low, w_high, gain):
    rows, d = x.shape
    ways, unit = w_low.shape[0], w_low.shape[1] // 3
    units = 2 * ways * unit
    quarter = d // ways
    anywhere = pl.BlockSpec(memory_space=pl.ANY)
    inside = pl.BlockSpec(memory_space=pltpu.VMEM)
    sems = lambda n: [pltpu.SemaphoreType.DMA((n,))] * 2
    return pl.pallas_call(
        middle_kernel,
        in_specs=[anywhere] * 8 + [inside],
        out_specs=[anywhere] * 6 + [inside],
        out_shape=[
            jax.ShapeDtypeStruct((ways, rows, quarter), BF16),
            jax.ShapeDtypeStruct((rows, d), F32),
            jax.ShapeDtypeStruct((2, rows, d), BF16),
            jax.ShapeDtypeStruct((rows - rows // 4, d), BF16),
            jax.ShapeDtypeStruct((4, rows // 4, d), BF16),
            jax.ShapeDtypeStruct((3 * units // rows, rows, d), BF16),
            jax.ShapeDtypeStruct((8, d), F32),
        ],
        scratch_shapes=[
            pltpu.VMEM((2 * units, d), BF16),
            pltpu.VMEM((units, d), BF16),
            pltpu.VMEM((8, rows, d), BF16),
            pltpu.VMEM((8, rows, d), BF16),
            pltpu.VMEM((6, rows, units), BF16),
            pltpu.VMEM((6, rows, 2 * units), BF16),
            pltpu.VMEM((6, rows, d), BF16),
            pltpu.VMEM((3, rows, d), BF16),
            pltpu.VMEM((rows, d), BF16),
            pltpu.VMEM((rows, d), BF16),
            pltpu.VMEM((rows, d), BF16),
            pltpu.VMEM((units, d), F32),
            pltpu.VMEM((2 * units, d), F32),
            pltpu.VMEM((rows, d), F32),
            pltpu.VMEM((ways, rows, quarter), BF16),
            pltpu.VMEM((ways, rows, quarter), BF16),
        ]
        + sems(8)
        + sems(10)
        + sems(10)
        + sems(ways)
        + [
            pltpu.SemaphoreType.DMA((8, 2)),
            pltpu.SemaphoreType.DMA((ways + 1, 3)),
        ]
        + [pltpu.SemaphoreType.DMA((ways, 3))] * 4
        + [
            pltpu.SemaphoreType.DMA((5,)),
            pltpu.SemaphoreType.REGULAR((6,)),
        ],
        compiler_params=pltpu.CompilerParams(
            collective_id=1, has_side_effects=True, vmem_limit_bytes=VMEM_LIMIT
        ),
        cost_estimate=pl.CostEstimate(
            flops=130 * 10**9, bytes_accessed=40 * rows * d, transcendentals=0
        ),
        name="middle",
    )(x, attended, resid, out_full, cot_low, cot_high, w_low, w_high, gain[None])


def tail_kernel(
    mixed_ref,
    w_ref,
    out_parts_ref,
    ffn_parts_ref,
    rows_ref,
    tok_ref,
    norm_ref,
    n_ref,
    og_ref,
    qkv_ref,
    ng_ref,
    ffn_ref,
    lines,
    line_sib,
    line_z,
    line_end,
    part,
    from_sib,
    from_far,
    from_x,
    from_y,
    mine,
    slices,
    ogs,
    qkv,
    qkv_far,
    qkv_x,
    qkv_y,
    qkv_sum,
    qkv_z,
    qkvs,
    norms,
    norm_sum,
    norms_z,
    ffn,
    ffn_far,
    ffn_x,
    ffn_y,
    lsend,
    lrecv,
    hsend,
    hrecv,
    ssend,
    srecv,
    gsend,
    grecv,
    osend,
    orecv,
    ksend,
    krecv,
    kzsend,
    kzrecv,
    kgsend,
    kgrecv,
    nsend,
    nrecv,
    zsend,
    zrecv,
    fsend,
    frecv,
    load_sem,
    ffn_sem,
):
    me, z = lax.axis_index("dp"), lax.axis_index("tensor")
    ways, rows = lines.shape[0], lines.shape[1]
    out_rows = slices.shape[1]
    width = w_ref.shape[2]
    total = part.shape[1]
    half = total // 2
    low, high = pl.ds(0, half), pl.ds(half, half)
    core, heads_of, group_of = head_share()
    home = group_of == core
    chip = me // 2
    sib, across, along = plane_peers()
    others = [{"tensor": lax.rem(z + k, ways)} for k in range(1, ways)]
    z1, z2, z3 = (lax.bitwise_xor(z, k) for k in (1, 2, 3))
    near, far = {"tensor": z1}, {"tensor": z2}
    plane = [{"dp": lax.bitwise_xor(me, k)} for k in range(1, 8)]
    enter(plane + others)

    loads = []
    for i in range(8):
        src = pl.multiple_of(lax.bitwise_xor(me, i) * out_rows, 16)
        loads.append(
            [
                pltpu.make_async_copy(
                    out_parts_ref.at[t, pl.ds(src, out_rows)],
                    part.at[i, pl.ds(t * out_rows, out_rows)],
                    load_sem.at[t, i],
                )
                for t in range(ways)
            ]
        )
        for load in loads[-1]:
            load.start()

    ffn_load = pltpu.make_async_copy(ffn_parts_ref, ffn, ffn_sem)
    ffn_load.start()

    def add_to(ref, other):
        ref[...] = (ref[...].astype(F32) + other[...].astype(F32)).astype(BF16)

    size = rows // 2

    def part_of(which):
        return pl.ds(pl.multiple_of(which * size, size), size)

    def line(i):
        b = lax.bitwise_xor(z, i)
        step = min(256, rows)

        @pl.loop(0, rows // step)
        def _(k):
            at = pl.ds(pl.multiple_of(b * rows + k * step, step), step)
            lines[b, pl.ds(pl.multiple_of(k * step, step), step)] = sum(
                dot_nt(mixed_ref[at, j * width : (j + 1) * width], w_ref[j]) for j in range(3)
            ).astype(BF16)

    def share(i):
        b = lax.bitwise_xor(z, i)
        return remote(lines.at[b, part_of(1 - core)], line_sib.at[b], hsend, hrecv, i, sib)

    def share_join(i):
        b = lax.bitwise_xor(z, i)
        share(i).wait_recv()
        add_to(lines.at[b, part_of(core)], line_sib.at[b])

    to_near = [
        remote(lines.at[z3, part_of(core)], line_z.at[0], lsend, lrecv, 0, near),
        remote(lines.at[z1, part_of(core)], line_z.at[1], lsend, lrecv, 1, near),
    ]
    to_far = remote(lines.at[z2, part_of(core)], line_z.at[2], lsend, lrecv, 2, far)
    last_away = remote(line_z.at[2], line_end, lsend, lrecv, 3, sib)
    last_home = remote(lines.at[z, part_of(core)], line_end, lsend, lrecv, 3, sib)

    sums = [
        ("1", part.at[1], from_sib.at[0], sib),
        ("3", part.at[3], from_sib.at[1], sib),
        ("5", part.at[5], from_sib.at[2], sib),
        ("7", part.at[7], from_sib.at[3], sib),
        ("6l", part.at[6, low], from_far.at[low], across),
        ("6h", part.at[6, high], from_far.at[high], along),
        ("2l", part.at[2, low], from_x.at[low], across),
        ("2h", part.at[2, high], from_x.at[high], across),
        ("4l", part.at[4, low], from_y.at[low], along),
        ("4h", part.at[4, high], from_y.at[high], along),
    ]
    sums = {
        name: remote(src, dst, ssend, srecv, i, peer)
        for i, (name, src, dst, peer) in enumerate(sums)
    }

    def qkv_rows(j):
        at = pl.ds(pl.multiple_of(j * width, width), width)
        qkv[at, :] = dot_tn(mixed_ref[:, at], rows_ref[...]).astype(BF16)

    edge = ffn.shape[1] // 2
    first, second = pl.ds(0, edge), pl.ds(edge, edge)
    ffns = [
        ("3l", ffn.at[3, first], ffn_far.at[first], across),
        ("3h", ffn.at[3, second], ffn_far.at[second], along),
        ("1l", ffn.at[1, first], ffn_x.at[first], across),
        ("1h", ffn.at[1, second], ffn_x.at[second], across),
        ("2l", ffn.at[2, first], ffn_y.at[first], along),
        ("2h", ffn.at[2, second], ffn_y.at[second], along),
    ]
    ffns = {
        name: remote(src, dst, fsend, frecv, i, peer)
        for i, (name, src, dst, peer) in enumerate(ffns)
    }
    ffn_load.wait()
    for name in ("3l", "3h", "1l", "2h"):
        ffns[name].start()

    line(3)
    share(3).start()

    @pl.loop(0, 3)
    def _(j):
        qkv_rows(j)

        @pl.when(j == 0)
        def _():
            share_join(3)
            to_near[0].start()

    piece = qkv_sum.shape[0]
    small = piece // 2

    def qkv_at(s, side=None):
        first = lax.bitwise_xor(chip, s) * piece + (0 if side is None else side * small)
        return qkv.at[pl.ds(pl.multiple_of(first, 16), piece if side is None else small)]

    def side_of(ref, side):
        return ref.at[pl.ds(side * small, small)]

    pieces = [
        ("3l", qkv_at(3, 0), side_of(qkv_far, 0), across),
        ("3h", qkv_at(3, 1), side_of(qkv_far, 1), along),
        ("1l", qkv_at(1, 0), side_of(qkv_x, 0), across),
        ("1h", qkv_at(1, 1), side_of(qkv_x, 1), across),
        ("2l", qkv_at(2, 0), side_of(qkv_y, 0), along),
        ("2h", qkv_at(2, 1), side_of(qkv_y, 1), along),
    ]
    pieces = {
        name: remote(src, dst, ksend, krecv, i, peer)
        for i, (name, src, dst, peer) in enumerate(pieces)
    }
    for name in ("3l", "3h", "1l", "2h"):
        pieces[name].start()

    @pl.loop(0, ways - 1)
    def _(k):
        i = lax.rem(k + 1, ways - 1)
        line(i)
        for fixed in range(ways - 1):

            @pl.when(i == fixed)
            def _(fixed=fixed):
                share(fixed).start()

    for i in (7, 3, 5, 1):
        for load in loads[i]:
            load.wait()
        sums[str(i)].start()

    pieces["3l"].wait_recv()
    add_to(qkv_at(2, 0), side_of(qkv_far, 0))
    pieces["2l"].start()
    pieces["3h"].wait_recv()
    add_to(qkv_at(1, 1), side_of(qkv_far, 1))
    pieces["1h"].start()
    share_join(1)
    share_join(2)
    to_near[0].wait_recv()
    to_near[1].start()
    add_to(lines.at[z2, part_of(core)], line_z.at[0])
    to_far.start()
    for i, j, names in ((6, 3, ("6l", "6h")), (2, 1, ("2l",)), (4, 2, ("4h",))):
        for load in loads[i]:
            load.wait()
        sums[str(i + 1)].wait_recv()
        add_to(part.at[i], from_sib.at[j])
        for name in names:
            sums[name].start()
    share_join(0)

    for name in ("1l", "1h", "2l", "2h"):
        pieces[name].wait_recv()
    qkv_sum[...] = (
        qkv_at(0)[...].astype(F32) + qkv_x[...].astype(F32) + qkv_y[...].astype(F32)
    ).astype(BF16)
    takes = core == lax.rem(z, 2)

    def owner_copy(slot):
        return pltpu.make_async_remote_copy(
            src_ref=qkv_sum,
            dst_ref=qkv_z.at[slot],
            send_sem=kzsend.at[0],
            recv_sem=kzrecv.at[slot],
            device_id={"tensor": heads_of},
            device_id_type=MESH_ID,
        )

    @pl.when(heads_of != z)
    def _():
        owner_copy(group_of).start()

    @pl.when(heads_of == z)
    def _():
        qkv_z[group_of] = qkv_sum[...]

    ffns["3l"].wait_recv()
    add_to(ffn.at[2, first], ffn_far.at[first])
    ffns["2l"].start()
    ffns["3h"].wait_recv()
    add_to(ffn.at[1, second], ffn_far.at[second])
    ffns["1h"].start()
    sums["6l"].wait_recv()
    add_to(part.at[4, low], from_far.at[low])
    sums["4l"].start()
    sums["6h"].wait_recv()
    add_to(part.at[2, high], from_far.at[high])
    sums["2h"].start()

    for load in loads[0]:
        load.wait()
    sums["1"].wait_recv()
    for name in ("2l", "2h", "4l", "4h"):
        sums[name].wait_recv()
    mine[...] = part[0].astype(F32) + from_sib[0].astype(F32)
    mine[...] += from_x[...].astype(F32) + from_y[...].astype(F32)

    for t in range(ways):
        at = slice(t * out_rows, (t + 1) * out_rows)
        part[0, at] = mine[at].astype(BF16)

    def slice_copy(k, to, source):
        return pltpu.make_async_remote_copy(
            src_ref=part.at[0, pl.ds(pl.multiple_of(to * out_rows, 16), out_rows)],
            dst_ref=slices.at[source],
            send_sem=osend.at[k],
            recv_sem=orecv.at[source],
            device_id={"tensor": to},
            device_id_type=MESH_ID,
        )

    for k in range(1, ways):
        slice_copy(k, lax.rem(z + k, ways), z).start()

    def chip_copy(s, side, peer, sem):
        at = qkvs.at[lax.bitwise_xor(chip, s)]
        ref = at if side is None else side_of(at, side)
        return remote(ref, ref, kgsend, kgrecv, sem, peer)

    to_x, to_y = chip_copy(0, None, across, 0), chip_copy(0, None, along, 1)
    x_on, y_on = chip_copy(1, 1, along, 2), chip_copy(2, 0, across, 3)
    to_sib = [chip_copy(s, None, sib, 4 + s) for s in range(4)]

    @pl.when(takes)
    def _():
        for slot in range(2):

            @pl.when(z // 2 + 2 * slot != z)
            def _():
                owner_copy(slot).wait_recv()

        qkvs[chip] = (qkv_z[0].astype(F32) + qkv_z[1].astype(F32)).astype(BF16)
        to_x.start()
        to_y.start()
        to_sib[0].start()

    own_slice = part[0, pl.ds(pl.multiple_of(z * out_rows, 16), out_rows)].astype(F32)
    for k in range(1, ways):
        source = lax.rem(z + k, ways)
        slice_copy(k, source, source).wait_recv()
        own_slice += slices[source].astype(F32)
    ogs[me] = own_slice.astype(BF16)
    view = lambda s, side: half_of(ogs.at[lax.bitwise_xor(me, s)], side)
    gathers = gather_copies(view, gsend, grecv, True)
    gather_start(gathers)

    for name in ("1l", "1h", "2l", "2h"):
        ffns[name].wait_recv()
    ffn_ref[...] = ffn[0].astype(F32) + ffn_x[...].astype(F32) + ffn_y[...].astype(F32)

    to_near[1].wait_recv()
    add_to(lines.at[z, part_of(core)], line_z.at[1])

    @pl.when(jnp.logical_not(home))
    def _():
        last_home.start()

    to_far.wait_recv()

    @pl.when(home)
    def _():
        last_away.start()
        n_ref[part_of(core), :] = lines[z, part_of(core), :].astype(F32)

    @pl.when(jnp.logical_not(home))
    def _():
        n_ref[part_of(core), :] = line_z[2].astype(F32)

    last_away.wait_recv()
    n_ref[part_of(1 - core), :] = line_end[...].astype(F32)

    norms[me] = norm_ref[...]
    step = min(128, rows)

    @pl.loop(0, rows // step)
    def _(i):
        at = pl.ds(pl.multiple_of(i * step, step), step)
        values = tok_ref[at, :].astype(F32)
        centred = values - jnp.mean(values, axis=-1, keepdims=True)
        root = lax.rsqrt(jnp.mean(centred * centred, axis=-1, keepdims=True) + norm_eps)
        grad = n_ref[at, :]
        norms[me, 0:1] += jnp.sum(grad * (centred * root), axis=0, keepdims=True)
        norms[me, 1:2] += jnp.sum(grad, axis=0, keepdims=True)

    def swap(k, source):
        return remote(norms.at[source], norms.at[source], nsend, nrecv, k, plane[k])

    for k in range(7):
        swap(k, me).start()

    gather_forward(gathers)

    @pl.when(takes)
    def _():
        to_x.wait_recv()
        x_on.start()
        to_sib[1].start()
        to_y.wait_recv()
        y_on.start()
        to_sib[2].start()

    for k in range(7):
        swap(k, lax.bitwise_xor(me, k + 1)).wait_recv()
    norm_sum[...] = sum(norms[k] for k in range(8))

    def norm_copy(k, to, source):
        return pltpu.make_async_remote_copy(
            src_ref=norm_sum,
            dst_ref=norms_z.at[source],
            send_sem=zsend.at[k],
            recv_sem=zrecv.at[source],
            device_id={"tensor": to},
            device_id_type=MESH_ID,
        )

    for k in range(1, ways):
        norm_copy(k, lax.rem(z + k, ways), z).start()
    norms_z[z] = norm_sum[...]
    gather_finish(gathers)
    og_ref[...] = ogs[...]

    @pl.when(takes)
    def _():
        x_on.wait_recv()
        y_on.wait_recv()
        to_sib[3].start()

    @pl.when(jnp.logical_not(takes))
    def _():
        for copy in to_sib:
            copy.wait_recv()

    qkv_ref[...] = qkvs[...]
    for k in range(1, ways):
        source = lax.rem(z + k, ways)
        norm_copy(k, source, source).wait_recv()
    ng_ref[...] = sum(norms_z[t] for t in range(ways))

    @pl.when(takes)
    def _():
        for copy in (to_x, to_y, x_on, y_on, *to_sib):
            copy.wait_send()

    @pl.when(heads_of != z)
    def _():
        owner_copy(group_of).wait_send()

    @pl.when(home)
    def _():
        last_away.wait_send()

    @pl.when(jnp.logical_not(home))
    def _():
        last_home.wait_send()

    for copy in (*sums.values(), *gathers.values(), *pieces.values(), *ffns.values(), *to_near, to_far):
        copy.wait_send()
    for k in range(7):
        swap(k, me).wait_send()
    for i in range(ways):
        share(i).wait_send()
    for k in range(1, ways):
        to = lax.rem(z + k, ways)
        slice_copy(k, to, z).wait_send()
        norm_copy(k, to, z).wait_send()


def tail(mixed, w, out_parts, ffn_parts, rows_one, tokens, norm_grads, ways):
    rows, d = tokens.shape
    out_rows = out_parts.shape[1] // 8
    qkv_rows = mixed.shape[1] // 4
    total = ways * out_rows
    anywhere = pl.BlockSpec(memory_space=pl.ANY)
    inside = pl.BlockSpec(memory_space=pltpu.VMEM)
    sems = lambda n: [pltpu.SemaphoreType.DMA((n,))] * 2
    return pl.pallas_call(
        tail_kernel,
        in_specs=[inside] * 2 + [anywhere] * 2 + [inside] * 3,
        out_specs=[inside] * 5,
        out_shape=[
            jax.ShapeDtypeStruct((rows, d), F32),
            jax.ShapeDtypeStruct((8, out_rows, d), BF16),
            jax.ShapeDtypeStruct((4, qkv_rows, d), BF16),
            jax.ShapeDtypeStruct((8, d), F32),
            jax.ShapeDtypeStruct(ffn_parts.shape[1:], F32),
        ],
        scratch_shapes=[
            pltpu.VMEM((ways, rows, d), BF16),
            pltpu.VMEM((ways, rows // 2, d), BF16),
            pltpu.VMEM((3, rows // 2, d), BF16),
            pltpu.VMEM((rows // 2, d), BF16),
            pltpu.VMEM((8, total, d), BF16),
            pltpu.VMEM((4, total, d), BF16),
            pltpu.VMEM((total, d), BF16),
            pltpu.VMEM((total, d), BF16),
            pltpu.VMEM((total, d), BF16),
            pltpu.VMEM((total, d), F32),
            pltpu.VMEM((ways, out_rows, d), BF16),
            pltpu.VMEM((8, out_rows, d), BF16),
            pltpu.VMEM((4 * qkv_rows, d), BF16),
            pltpu.VMEM((qkv_rows, d), BF16),
            pltpu.VMEM((qkv_rows, d), BF16),
            pltpu.VMEM((qkv_rows, d), BF16),
            pltpu.VMEM((qkv_rows, d), BF16),
            pltpu.VMEM((2, qkv_rows, d), BF16),
            pltpu.VMEM((4, qkv_rows, d), BF16),
            pltpu.VMEM((8, 8, d), F32),
            pltpu.VMEM((8, d), F32),
            pltpu.VMEM((ways, 8, d), F32),
            pltpu.VMEM(ffn_parts.shape, BF16),
        ]
        + [pltpu.VMEM(ffn_parts.shape[1:], BF16)] * 3
        + sems(4)
        + sems(ways)
        + sems(10)
        + sems(8)
        + sems(ways)
        + sems(6)
        + sems(2)
        + sems(8)
        + sems(7)
        + sems(ways)
        + sems(6)
        + [pltpu.SemaphoreType.DMA((ways, 8)), pltpu.SemaphoreType.DMA],
        compiler_params=pltpu.CompilerParams(
            collective_id=2, has_side_effects=True, vmem_limit_bytes=VMEM_LIMIT
        ),
        cost_estimate=pl.CostEstimate(
            flops=75 * 10**9, bytes_accessed=40 * rows * d, transcendentals=0
        ),
        name="tail",
    )(mixed, w, out_parts, ffn_parts, rows_one, tokens, norm_grads)


def finish_kernel(
    kept,
    both_ref,
    down_ref,
    features_ref,
    og_ref,
    grad_ref,
    resid_ref,
    tok_ref,
    gain_ref,
    low_ref,
    high_ref,
    before_ref,
    norms_ref,
    gate_up_ref,
    down_out_ref,
    qkv_ref,
    og_out_ref,
    token_ref,
    layer_ref,
    *norm_refs,
):
    units = both_ref.shape[1] // 2
    for p in range(8):
        turned = both_ref[p].astype(F32).T
        for g in range(2):
            at = pl.ds(2 * p + g, turned.shape[0], stride=16)
            gate_up_ref[at, :] = turned[:, g * units : (g + 1) * units]
    down_out_ref[...] = down_ref[0].astype(F32)
    width = qkv_ref.shape[2]
    for j in range(3):
        qkv_ref[j] = features_ref[j * width : (j + 1) * width].astype(F32).T
    og_out_ref[...] = og_ref[0].astype(F32)
    values = tok_ref[...].astype(F32)
    centred = values - jnp.mean(values, axis=-1, keepdims=True)
    root = lax.rsqrt(jnp.mean(centred * centred, axis=-1, keepdims=True) + norm_eps)
    unit_rows = centred * root
    scaled = grad_ref[...] * gain_ref[...]
    first_mean = jnp.mean(scaled, axis=-1, keepdims=True)
    second_mean = jnp.mean(scaled * unit_rows, axis=-1, keepdims=True)
    token_ref[...] = resid_ref[...] + root * (scaled - first_mean - unit_rows * second_mean)
    for k, ref in enumerate(norm_refs):
        ref[...] = norms_ref[k : k + 1]
    step = pl.program_id(0)

    @pl.when(step < kept)
    def _():
        layer_ref[...] = low_ref[...]

    @pl.when(step >= kept)
    def _():
        layer_ref[...] = (before_ref[...] + high_ref[...]).astype(BF16)


def finish(grads, features, out_grad, norm_grad, resid_grad, tokens, gain, low, high, resid, norms):
    rows, d = tokens.shape
    units = grads.shape[1] // 3
    block = d // 8
    width = features.shape[0] // 3
    out_rows = out_grad.shape[1]
    own = pl.BlockSpec((rows // 8, d), lambda i: (i, 0))
    kept = 8 * low.shape[0] // rows
    return pl.pallas_call(
        functools.partial(finish_kernel, kept),
        grid=(8,),
        in_specs=[
            pl.BlockSpec((8, 2 * units, block), lambda i: (0, 0, i)),
            pl.BlockSpec((1, units, d), lambda i: (i, 2, 0)),
            pl.BlockSpec((3 * width, block), lambda i: (0, i)),
            pl.BlockSpec((1, out_rows, d), lambda i: (i, 0, 0)),
            own,
            own,
            own,
            pl.BlockSpec((1, d), lambda i: (0, 0)),
            pl.BlockSpec((rows // 8, d), lambda i: (jnp.minimum(i, kept - 1), 0)),
            pl.BlockSpec((rows // 8, d), lambda i: (jnp.maximum(i - kept, 0), 0)),
            own,
            pl.BlockSpec(norms.shape, lambda i: (0, 0)),
        ],
        out_specs=[
            pl.BlockSpec((16 * block, units), lambda i: (i, 0)),
            pl.BlockSpec((units, d), lambda i: (i, 0)),
            pl.BlockSpec((3, block, width), lambda i: (0, i, 0)),
            pl.BlockSpec((out_rows, d), lambda i: (i, 0)),
            own,
            own,
        ]
        + [pl.BlockSpec((1, d), lambda i: (0, 0))] * 4,
        out_shape=[
            jax.ShapeDtypeStruct((16 * d, units), F32),
            jax.ShapeDtypeStruct((8 * units, d), F32),
            jax.ShapeDtypeStruct((3, d, width), F32),
            jax.ShapeDtypeStruct((8 * out_rows, d), F32),
            jax.ShapeDtypeStruct((rows, d), F32),
            jax.ShapeDtypeStruct((rows, d), BF16),
        ]
        + [jax.ShapeDtypeStruct((1, d), F32)] * 4,
        compiler_params=pltpu.CompilerParams(vmem_limit_bytes=VMEM_LIMIT),
        name="finish",
    )(
        grads,
        grads,
        features,
        out_grad,
        norm_grad,
        resid_grad,
        tokens,
        gain[None],
        low,
        high,
        resid,
        norms,
    )


def shards(
    tokens,
    group_bucket,
    gain_one,
    shift_one,
    w_qkv,
    w_out,
    gain_two,
    shift_two,
    w_gate_up,
    w_down,
    cotangent,
):
    ways = lax.axis_size("tensor")
    replicas = lax.axis_size("dp")
    replica = lax.axis_index("dp")
    own_rows, d = tokens.shape
    group_rows = own_rows * ways
    local_width = w_out.shape[0]
    head_dim = d // HEADS
    hidden_width = w_down.shape[0]
    units = hidden_width // replicas
    out_rows = local_width // replicas
    pair_width = min(128, local_width)

    rows_in = tokens.astype(F32)
    normed_one, unit_one, root_one = norm_forward(rows_in, gain_one, shift_one)
    normed_one_low = normed_one.astype(BF16)
    rows_one = lax.all_gather(normed_one_low, "tensor", axis=0, tiled=True)

    gate_up_slice = lax.dynamic_slice_in_dim(w_gate_up, replica * units, units, axis=2)
    down_slice = lax.dynamic_slice_in_dim(w_down, replica * units, units, axis=0)
    weight_slice = jnp.concatenate(
        [gate_up_slice.transpose(1, 2, 0).reshape(2 * units, d), down_slice]
    )
    weights = lax.all_gather(weight_slice, "tensor", axis=0)
    cot_all = lax.all_gather(cotangent, "dp", axis=0, tiled=True)
    out_full = lax.all_gather(w_out, "tensor", axis=0, tiled=True)

    cos_wide, sine_wide = rotary_wide(group_bucket[0], group_rows, head_dim, pair_width)
    qkv_weights = w_qkv.transpose(1, 0, 2)
    q, k, v, kt, vt = project(rows_one, qkv_weights, cos_wide, sine_wide, head_dim)
    attended, *kept = attend(group_bucket[None], q, k, vt, head_dim)
    attended_own = lax.all_to_all(attended, "tensor", 0, 1, tiled=True)
    resid = rows_in + dot_nn(attended_own, out_full)
    normed_two, unit_two, root_two = norm_forward(resid, gain_two, shift_two)
    normed_two_low = normed_two.astype(BF16)
    parts = weights.reshape(ways, 3, units, d)
    wgu = parts[:, :2].transpose(3, 1, 0, 2).reshape(d, 2 * ways * units)
    wd = parts[:, 2].reshape(ways * units, d)
    rows_two = lax.all_gather(normed_two_low, "dp", axis=0, tiled=True)
    hidden, branch, back = feed(rows_two, cot_all, wgu, wd)
    normed_two_grad = lax.psum_scatter(back, "dp", scatter_dimension=0, tiled=True).astype(F32)
    ffn_parts = dot_nn(hidden, wd).astype(BF16)
    ffn_out = lax.psum_scatter(ffn_parts, "dp", scatter_dimension=0, tiled=True).astype(F32)
    layer_out = (resid + ffn_out).astype(BF16)
    grads = jnp.concatenate(
        [
            dot_tn(branch, rows_two).reshape(2, ways, units, d),
            dot_tn(hidden, cot_all).reshape(1, ways, units, d),
        ]
    )
    grads = grads.astype(BF16).transpose(1, 0, 2, 3).reshape(ways, 3 * units, d)
    resid_part, gain_two_grad, shift_two_grad = norm_backward(
        normed_two_grad, unit_two, root_two, gain_two
    )
    norm_grads = jnp.zeros((8, d), F32).at[2].set(gain_two_grad).at[3].set(shift_two_grad)
    resid_grad = cotangent.astype(F32) + resid_part
    attn_grad = resid_grad.astype(BF16)
    attended_grad = lax.all_to_all(
        dot_nt(attn_grad, out_full).astype(BF16), "tensor", 1, 0, tiled=True
    )
    out_grad = dot_tn(attended_own, attn_grad).astype(BF16)
    out_grad = out_grad.reshape(ways, replicas, out_rows, d).transpose(1, 0, 2, 3)
    out_grad = out_grad.reshape(replicas, ways * out_rows, d)
    grads = lax.psum_scatter(grads, "tensor", scatter_dimension=0)

    mixed_grad = attend_back(
        group_bucket[None], q, k, kt, v, attended_grad, *kept, cos_wide, sine_wide, head_dim
    )
    grads, mixed_grad = lax.optimization_barrier((grads, mixed_grad))
    grads = lax.all_gather(grads, "dp", axis=0)
    grads = grads.reshape(replicas, 3, units, d)
    down_grad = grads[:, 2].reshape(hidden_width, d).astype(F32)
    gate_up_grad = grads[:, :2].transpose(3, 1, 0, 2).reshape(d, 2, hidden_width).astype(F32)
    qkv_grad = lax.psum(dot_tn(rows_one, mixed_grad).astype(BF16), "dp").astype(F32)
    qkv_grad = qkv_grad.reshape(d, 3, local_width)
    flat = qkv_weights.transpose(1, 0, 2).reshape(d, 3 * local_width)
    normed_one_grad = lax.psum_scatter(
        dot_nt(mixed_grad, flat).astype(BF16), "tensor", scatter_dimension=0, tiled=True
    ).astype(F32)
    out_grad = lax.psum_scatter(out_grad, "dp", scatter_dimension=0)
    out_grad = lax.psum_scatter(out_grad, "tensor", scatter_dimension=0, tiled=True)
    out_grad = lax.all_gather(out_grad, "dp", axis=0, tiled=True).astype(F32)
    one = norm_backward(normed_one_grad, unit_one, root_one, gain_one)
    norm_grads = norm_grads.at[0].set(one[1]).at[1].set(one[2])
    norm_grads = lax.psum(norm_grads, ("dp", "tensor"))
    token_grad = resid_grad + norm_backward(normed_one_grad, unit_one, root_one, gain_one)[0]
    gain_one_grad, shift_one_grad, gain_two_grad, shift_two_grad = (norm_grads[i] for i in range(4))
    return (
        layer_out,
        token_grad,
        gain_one_grad,
        shift_one_grad,
        qkv_grad,
        out_grad,
        gain_two_grad,
        shift_two_grad,
        gate_up_grad,
        down_grad,
    )


def shards_columns(
    tokens,
    group_bucket,
    gain_one,
    shift_one,
    w_qkv,
    w_out,
    gain_two,
    shift_two,
    w_gate_up,
    w_down,
    cotangent,
):
    ways = lax.axis_size("tensor")
    replica = lax.axis_index("dp")
    own_rows, d = tokens.shape
    group_rows = own_rows * ways
    local_width = w_out.shape[0]
    head_dim = d // HEADS
    hidden_width = w_down.shape[0]
    units = hidden_width // 8

    gate_up_slice = lax.dynamic_slice_in_dim(w_gate_up, replica * units, units, axis=2)
    down_slice = lax.dynamic_slice_in_dim(w_down, replica * units, units, axis=0)
    gate_up_slice = gate_up_slice.transpose(1, 2, 0)
    half = units // 2
    slice_low, slice_high = (
        jnp.concatenate([gate_up_slice[:, at].reshape(units, d), down_slice[at]])
        for at in (slice(0, half), slice(half, units))
    )
    q, k, v, kt, vt, cos_wide, sine_wide, bucket, rows_one, cot_low, out_full, qkv_weights = front(
        group_bucket,
        tokens,
        gain_one,
        shift_one,
        cotangent,
        w_out,
        w_qkv.transpose(1, 0, 2),
        head_dim,
        ways,
    )
    bucket, slice_low = lax.optimization_barrier((bucket, slice_low))
    weights_low = lax.all_gather(slice_low, "tensor", axis=0)
    out_full = out_full.reshape(d, d)
    attended, *kept = attend(bucket, q, k, vt, head_dim)
    attended_own, resid, normed_two, cot_high = collect(
        attended, tokens, out_full, gain_two, shift_two, cotangent, ways
    )
    attended_grad, resid_grad, out_grad, layer_low, ffn_parts, grads, norm_grads = middle(
        normed_two,
        attended_own,
        resid,
        out_full,
        cot_low,
        cot_high,
        weights_low,
        slice_high,
        gain_two,
    )
    grads = grads.reshape(ways, 3 * units, d)
    grads = lax.psum_scatter(grads, "tensor", scatter_dimension=0)
    attended_grad = attended_grad.reshape(group_rows, local_width)
    mixed_grad = attend_back(
        bucket, q, k, kt, v, attended_grad, *kept, cos_wide, sine_wide, head_dim
    )
    grads, mixed_grad = lax.optimization_barrier((grads, mixed_grad))
    grads = lax.all_gather(grads, "dp", axis=0)
    normed_one_grad, out_grad, qkv_grad, norm_grads, layer_high = tail(
        mixed_grad,
        qkv_weights,
        out_grad.reshape(ways, local_width, d),
        ffn_parts,
        rows_one.reshape(group_rows, d),
        tokens,
        norm_grads,
        ways,
    )
    gate_up_grad, down_grad, qkv_grad, out_grad, token_grad, layer_out, *norm_grads = finish(
        grads,
        qkv_grad.reshape(3 * local_width, d),
        out_grad,
        normed_one_grad,
        resid_grad,
        tokens,
        gain_one,
        layer_low,
        layer_high,
        resid,
        norm_grads,
    )
    gate_up_grad = gate_up_grad.reshape(d, 8, 2, units).transpose(0, 2, 1, 3)
    gate_up_grad = gate_up_grad.reshape(d, 2, hidden_width)
    qkv_grad = qkv_grad.transpose(1, 0, 2)
    gain_one_grad, shift_one_grad, gain_two_grad, shift_two_grad = (g[0] for g in norm_grads)
    return (
        layer_out,
        token_grad,
        gain_one_grad,
        shift_one_grad,
        qkv_grad,
        out_grad,
        gain_two_grad,
        shift_two_grad,
        gate_up_grad,
        down_grad,
    )


def solution(mesh):
    in_specs = (
        P(("dp", "tensor"), None),
        P("dp"),
        P(),
        P(),
        P(None, None, "tensor"),
        P("tensor", None),
        P(),
        P(),
        P(None, None, "tensor"),
        P("tensor", None),
        P(("dp", "tensor"), None),
    )
    out_specs = (
        P(("dp", "tensor"), None),
        P(("dp", "tensor"), None),
        P(),
        P(),
        P(None, None, "tensor"),
        P("tensor", None),
        P(),
        P(),
        P(None, None, "tensor"),
        P("tensor", None),
    )
    columns = mesh.shape["dp"] == 8 and mesh.shape["tensor"] == 4
    body = shards_columns if columns else shards
    return jax.shard_map(body, mesh=mesh, in_specs=in_specs, out_specs=out_specs, check_vma=False)
```

```python
import functools

import jax
import jax.numpy as jnp
from jax import lax
from jax.experimental import pallas as pl
from jax.experimental.pallas import tpu as pltpu
from jax.sharding import PartitionSpec as P

HEADS = 16
LONG_LEN = 2048
SHORT_LEN = 1000

norm_eps = 1e-05
mask_fill = -1e30
rope_base = 10000.0
log2_e = 1.4426950408889634
VMEM_LIMIT = 62 * 2**20
F32 = jnp.float32
BF16 = jnp.bfloat16


def dot_nn(a, b):
    return jnp.dot(a, b, preferred_element_type=F32)


def dot_nt(a, b):
    return lax.dot_general(a, b, (((1,), (1,)), ((), ())), preferred_element_type=F32)


def dot_tn(a, b):
    return lax.dot_general(a, b, (((0,), (0,)), ((), ())), preferred_element_type=F32)


def rotary_wide(bucket_id, group_rows, head_dim, width):
    positions = jnp.arange(group_rows, dtype=jnp.int32)
    span_len = jnp.where(bucket_id == 1, LONG_LEN, SHORT_LEN).astype(jnp.int32)
    places = positions - (positions // span_len) * span_len
    half_dim = head_dim // 2
    exponents = jnp.arange(half_dim, dtype=F32) * (-2.0 / head_dim)
    freqs = jnp.exp(exponents * jnp.log(F32(rope_base)))
    heads = width // head_dim
    signs = jnp.tile(jnp.repeat(jnp.array([-1.0, 1.0], F32), half_dim), heads)
    angles = places.astype(F32)[:, None] * jnp.tile(freqs, 2 * heads)[None, :]
    return jnp.cos(angles), jnp.sin(angles) * signs


def norm_forward(values, gain, shift):
    average = jnp.mean(values, axis=-1, keepdims=True)
    centred = values - average
    spread_sq = jnp.mean(centred * centred, axis=-1, keepdims=True)
    inv_root = lax.rsqrt(spread_sq + norm_eps)
    unit_rows = centred * inv_root
    return (unit_rows * gain + shift, unit_rows, inv_root)


def norm_backward(out_grad_rows, unit_rows, inv_root, gain):
    scaled = out_grad_rows * gain
    first_mean = jnp.mean(scaled, axis=-1, keepdims=True)
    second_mean = jnp.mean(scaled * unit_rows, axis=-1, keepdims=True)
    in_grad = inv_root * (scaled - first_mean - unit_rows * second_mean)
    return (in_grad, jnp.sum(out_grad_rows * unit_rows, axis=0), jnp.sum(out_grad_rows, axis=0))


def swap_halves(x, head_dim):
    half = head_dim // 2
    width = x.shape[1]
    lane = lax.broadcasted_iota(jnp.int32, x.shape, 1) % head_dim
    return jnp.where(lane < half, pltpu.roll(x, width - half, 1), pltpu.roll(x, half, 1))


def head_mask(x, h, head_dim):
    lane = lax.broadcasted_iota(jnp.int32, x.shape, 1)
    return jnp.where((lane >= h * head_dim) & (lane < (h + 1) * head_dim), x, jnp.zeros_like(x))


def widen(table, width):
    return jnp.concatenate([table] * (width // table.shape[1]), axis=1)


def project_kernel(head_dim, x_ref, w_ref, cos_ref, sin_ref, q_ref, k_ref, v_ref, kt_ref, vt_ref):
    width = q_ref.shape[1]
    x = x_ref[...]
    cos, sin = widen(cos_ref[...], width), widen(sin_ref[...], width)
    q, k, v = (dot_nn(x, w_ref[j]) for j in range(3))
    v = v.astype(BF16)
    q = q * cos + swap_halves(q, head_dim) * sin
    k = k * cos + swap_halves(k, head_dim) * sin
    k_low = k.astype(BF16)
    q_ref[...] = (q * (head_dim ** (-0.5) * log2_e)).astype(BF16)
    k_ref[...] = k_low
    v_ref[...] = v
    kt_ref[...] = k_low.T
    vt_ref[...] = v.T


def project(rows, w, cos_wide, sine_wide, head_dim):
    n, d = rows.shape
    width = w.shape[2]
    block = min(512, n)
    row = pl.BlockSpec((block, width), lambda i: (i, 0))
    col = pl.BlockSpec((width, block), lambda i: (0, i))
    table = pl.BlockSpec((block, cos_wide.shape[1]), lambda i: (i, 0))
    return pl.pallas_call(
        functools.partial(project_kernel, head_dim),
        grid=(n // block,),
        in_specs=[
            pl.BlockSpec((block, d), lambda i: (i, 0)),
            pl.BlockSpec((3, d, width), lambda i: (0, 0, 0)),
            table,
            table,
        ],
        out_specs=[row, row, row, col, col],
        out_shape=[jax.ShapeDtypeStruct((n, width), BF16)] * 3
        + [jax.ShapeDtypeStruct((width, n), BF16)] * 2,
        compiler_params=pltpu.CompilerParams(vmem_limit_bytes=VMEM_LIMIT),
        cost_estimate=pl.CostEstimate(
            flops=6 * n * d * width, bytes_accessed=2 * n * d + 18 * n * width, transcendentals=0
        ),
        name="project",
    )(rows, w, cos_wide, sine_wide)


def key_range(start, block, total):
    first = (start // SHORT_LEN) * SHORT_LEN
    last = min(total, ((start + block - 1) // SHORT_LEN + 1) * SHORT_LEN)
    return (first // 256) * 256, min(total, -(-last // 256) * 256)


def window_bias(key_start, keys, row_start, rows, total):
    key_at = lax.broadcasted_iota(jnp.int32, (keys, rows), 0) + key_start
    row_at = lax.broadcasted_iota(jnp.int32, (keys, rows), 1) + row_start
    key_window = jnp.zeros_like(key_at)
    row_window = jnp.zeros_like(row_at)
    for edge in range(SHORT_LEN, total, SHORT_LEN):
        key_window += (key_at >= edge).astype(jnp.int32)
        row_window += (row_at >= edge).astype(jnp.int32)
    return jnp.where(key_window == row_window, 0.0, mask_fill)


def attend_kernel(head_dim, bucket_ref, q_ref, k_ref, vt_ref, o_ref, ot_ref, l_ref, bias_ref):
    rows, width = q_ref.shape
    total = k_ref.shape[0]
    heads = width // head_dim
    step = pl.program_id(0)

    def block(at, first, last, masked):
        @pl.loop(0, heads)
        def _(h):
            hs = pl.ds(pl.multiple_of(h * head_dim, head_dim), head_dim)
            scores = dot_nt(k_ref[first:last, :], head_mask(q_ref[at, :], h, head_dim))
            if masked:
                scores = scores + bias_ref[: last - first, :]
            top = jnp.max(scores, axis=0, keepdims=True)
            weights = jnp.exp2(scores - top)
            totals = jnp.sum(weights, axis=0, keepdims=True)
            ot_ref[hs, at] = dot_nn(vt_ref[hs, first:last], weights.astype(BF16)) / totals
            l_ref[pl.ds(h, 1), at] = top + jnp.log2(totals)

    @pl.when(bucket_ref[0, 0] == 1)
    def _():
        block(slice(0, rows), 0, total, False)

    sub = bias_ref.shape[1]
    for start in range(0, total, sub):
        first, last = key_range(start, sub, total)

        @pl.when((bucket_ref[0, 0] != 1) & (step == start // rows))
        def _():
            bias_ref[: last - first, :] = window_bias(first, last - first, start, sub, total)
            block(slice(start % rows, start % rows + sub), first, last, True)

    o_ref[...] = ot_ref[...].T.astype(BF16)


def attend(bucket, q, k, vt, head_dim):
    n, width = q.shape
    heads = width // head_dim
    block = min(1024, n)
    pairs = n * n * heads
    lanes = -(-heads // 8) * 8
    row = pl.BlockSpec((block, width), lambda i: (i, 0))
    col = pl.BlockSpec((width, block), lambda i: (0, i))
    return pl.pallas_call(
        functools.partial(attend_kernel, head_dim),
        grid=(n // block,),
        in_specs=[
            pl.BlockSpec(memory_space=pltpu.SMEM),
            row,
            pl.BlockSpec((n, width), lambda i: (0, 0)),
            pl.BlockSpec((width, n), lambda i: (0, 0)),
        ],
        out_specs=[row, col, pl.BlockSpec((lanes, block), lambda i: (0, i))],
        out_shape=[
            jax.ShapeDtypeStruct((n, width), BF16),
            jax.ShapeDtypeStruct((width, n), F32),
            jax.ShapeDtypeStruct((lanes, n), F32),
        ],
        scratch_shapes=[pltpu.VMEM((n, min(512, block)), F32)],
        compiler_params=pltpu.CompilerParams(vmem_limit_bytes=VMEM_LIMIT),
        cost_estimate=pl.CostEstimate(
            flops=pairs * 1024, bytes_accessed=10 * n * width, transcendentals=pairs
        ),
        name="attend",
    )(bucket, q, k, vt)


def attend_back_kernel(
    head_dim,
    bucket_ref,
    q_ref,
    k_ref,
    kt_ref,
    v_ref,
    g_ref,
    ot_ref,
    l_ref,
    cos_ref,
    sin_ref,
    out_ref,
    bias_ref,
    gt_ref,
    dq_ref,
    dk_ref,
    dv_ref,
):
    rows, width = q_ref.shape
    total = k_ref.shape[0]
    heads = width // head_dim
    step = pl.program_id(0)

    @pl.when(step == 0)
    def _():
        dk_ref[...] = jnp.zeros_like(dk_ref)
        dv_ref[...] = jnp.zeros_like(dv_ref)

    gt_ref[...] = g_ref[...].astype(F32).T * ot_ref[...]

    def block(first, last, masked):
        keys = slice(first, last)

        @pl.loop(0, heads)
        def _(h):
            hs = pl.ds(pl.multiple_of(h * head_dim, head_dim), head_dim)
            qh, gh = head_mask(q_ref[...], h, head_dim), head_mask(g_ref[...], h, head_dim)
            scores = dot_nt(k_ref[keys, :], qh)
            if masked:
                scores = scores + bias_ref[: last - first, :]
            probs = jnp.exp2(scores - l_ref[pl.ds(h, 1), :])
            prob_grad = dot_nt(v_ref[keys, :], gh)
            delta = jnp.sum(gt_ref[hs, :], axis=0, keepdims=True)
            score_grad = (probs * (prob_grad - delta)).astype(BF16)
            dv_ref[keys, :] += dot_nn(probs.astype(BF16), gh)
            dk_ref[keys, :] += dot_nn(score_grad, qh)
            dq_ref[hs, :] = dot_nn(kt_ref[hs, keys], score_grad)

    @pl.when(bucket_ref[0, 0] == 1)
    def _():
        block(0, total, False)

    for start in range(0, total, rows):
        first, last = key_range(start, rows, total)

        @pl.when((bucket_ref[0, 0] != 1) & (step == start // rows))
        def _():
            bias_ref[: last - first, :] = window_bias(first, last - first, start, rows, total)
            block(first, last, True)

    def turn_back(grad, at):
        cos, sin = widen(cos_ref[at, :], width), widen(sin_ref[at, :], width)
        return (grad * cos - swap_halves(grad, head_dim) * sin).astype(BF16)

    at = pl.ds(pl.multiple_of(step * rows, rows), rows)
    out_ref[at, :width] = turn_back(dq_ref[...].T * head_dim ** (-0.5), at)

    @pl.when(step == pl.num_programs(0) - 1)
    def _():
        @pl.loop(0, total // rows)
        def _(i):
            at = pl.ds(pl.multiple_of(i * rows, rows), rows)
            out_ref[at, width : 2 * width] = turn_back(dk_ref[at, :] * (1.0 / log2_e), at)
            out_ref[at, 2 * width :] = dv_ref[at, :].astype(BF16)


def attend_back(bucket, q, k, kt, v, g, ot, log_totals, cos_wide, sine_wide, head_dim):
    n, width = q.shape
    heads = width // head_dim
    block = min(512, n)
    pairs = n * n * heads
    row = pl.BlockSpec((block, width), lambda i: (i, 0))
    col = pl.BlockSpec((width, block), lambda i: (0, i))
    full = lambda rows, cols: pl.BlockSpec((rows, cols), lambda i: (0, 0))
    table = full(n, cos_wide.shape[1])
    return pl.pallas_call(
        functools.partial(attend_back_kernel, head_dim),
        grid=(n // block,),
        in_specs=[
            pl.BlockSpec(memory_space=pltpu.SMEM),
            row,
            full(n, width),
            full(width, n),
            full(n, width),
            row,
            col,
            pl.BlockSpec((log_totals.shape[0], block), lambda i: (0, i)),
            table,
            table,
        ],
        out_specs=full(n, 3 * width),
        out_shape=jax.ShapeDtypeStruct((n, 3 * width), BF16),
        scratch_shapes=[
            pltpu.VMEM((n, block), F32),
            pltpu.VMEM((width, block), F32),
            pltpu.VMEM((width, block), F32),
            pltpu.VMEM((n, width), F32),
            pltpu.VMEM((n, width), F32),
        ],
        compiler_params=pltpu.CompilerParams(vmem_limit_bytes=VMEM_LIMIT),
        cost_estimate=pl.CostEstimate(
            flops=pairs * 2560, bytes_accessed=24 * n * width, transcendentals=pairs
        ),
        name="attend_back",
    )(bucket, q, k, kt, v, g, ot, log_totals, cos_wide, sine_wide)


def feed_kernel(x_ref, c_ref, wgu_ref, wd_ref, h_ref, b_ref, n_ref):
    units = wd_ref.shape[0]
    both = dot_nn(x_ref[...], wgu_ref[...])
    gate, up = both[:, :units], both[:, units:]
    sig = jax.nn.sigmoid(gate)
    silu = gate * sig
    h_ref[...] = (silu * up).astype(BF16)
    hidden_grad = dot_nt(c_ref[...], wd_ref[...])
    b_ref[:, :units] = (hidden_grad * up * sig * (1.0 + gate * (1.0 - sig))).astype(BF16)
    b_ref[:, units:] = (hidden_grad * silu).astype(BF16)
    n_ref[...] = dot_nt(b_ref[...], wgu_ref[...]).astype(BF16)


def feed(x, cot, wgu, wd):
    n, d = x.shape
    units = wd.shape[0]
    block = min(256, n)
    row = lambda w: pl.BlockSpec((block, w), lambda i: (i, 0))
    return pl.pallas_call(
        feed_kernel,
        grid=(n // block,),
        in_specs=[
            row(d),
            row(d),
            pl.BlockSpec((d, 2 * units), lambda i: (0, 0)),
            pl.BlockSpec((units, d), lambda i: (0, 0)),
        ],
        out_specs=[row(units), row(2 * units), row(d)],
        out_shape=[
            jax.ShapeDtypeStruct((n, units), BF16),
            jax.ShapeDtypeStruct((n, 2 * units), BF16),
            jax.ShapeDtypeStruct((n, d), BF16),
        ],
        compiler_params=pltpu.CompilerParams(vmem_limit_bytes=VMEM_LIMIT),
        cost_estimate=pl.CostEstimate(
            flops=10 * n * d * units, bytes_accessed=8 * n * d, transcendentals=n * units
        ),
        name="feed",
    )(x, cot, wgu, wd)


MESH_ID = pl.DeviceIdType.MESH


def plane_peers():
    me = lax.axis_index("dp")
    return [{"dp": lax.bitwise_xor(me, bit)} for bit in (1, 2, 4)]


def enter(peers):
    barrier = pltpu.get_barrier_semaphore()
    for peer in peers:
        pl.semaphore_signal(barrier, inc=1, device_id=peer, device_id_type=MESH_ID)
    pl.semaphore_wait(barrier, len(peers))


def remote(src, dst, send, recv, at, peer):
    return pltpu.make_async_remote_copy(
        src_ref=src,
        dst_ref=dst,
        send_sem=send.at[at],
        recv_sem=recv.at[at],
        device_id=peer,
        device_id_type=MESH_ID,
    )


def gather_copies(view, send, recv, placed, cores=True):
    sib, across, along = plane_peers()
    steps = [
        (0, 1, sib, None),
        (0, 2, across, None),
        (0, 4, along, None),
        (4, 2, across, 0),
        (2, 4, along, 1),
        (2, 1, sib, None),
        (4, 1, sib, None),
        (6, 1, sib, None),
    ]
    copies = {}
    for i, (s, bit, peer, part) in enumerate(steps):
        if bit == 1 and not cores:
            continue
        src = view(s, part)
        dst = src if placed else view(s ^ bit, part)
        copies[f"{s}-{s ^ bit}"] = remote(src, dst, send, recv, i, peer)
    return copies


def half_of(ref, part):
    if part is None:
        return ref
    half = ref.shape[-2] // 2
    return ref.at[(slice(None),) * (len(ref.shape) - 2) + (pl.ds(part * half, half),)]


def gather_start(copies):
    for name in ("0-2", "0-4", "0-1"):
        copies[name].start()


def gather_forward(copies):
    copies["0-2"].wait_recv()
    copies["2-6"].start()
    copies["2-3"].start()
    copies["0-4"].wait_recv()
    copies["4-6"].start()
    copies["4-5"].start()


def gather_finish(copies):
    copies["2-6"].wait_recv()
    copies["4-6"].wait_recv()
    copies["6-7"].start()
    for name in ("0-1", "2-3", "4-5", "6-7"):
        copies[name].wait_recv()


def head_share():
    core, z = lax.rem(lax.axis_index("dp"), 2), lax.axis_index("tensor")
    return core, 2 * lax.rem(z, 2) + core, z // 2


def head_source(s):
    return s % 2, 2 * lax.rem(lax.axis_index("dp"), 2) + s // 2


def front_kernel(
    head_dim,
    bucket_ref,
    tok_ref,
    gain_ref,
    shift_ref,
    freq_ref,
    cot_ref,
    wo_ref,
    wq_ref,
    q_ref,
    k_ref,
    v_ref,
    kt_ref,
    vt_ref,
    cos_ref,
    sin_ref,
    bucket_out,
    rows_out,
    cots_out,
    wos_out,
    wq_out,
    rows_all,
    mine,
    other,
    cots,
    wos,
    wq,
    buckets,
    nsend,
    nrecv,
    csend,
    crecv,
    wsend,
    wrecv,
    qsend,
    qrecv,
    zsend,
    zrecv,
    psend,
    precv,
    bsend,
    brecv,
    local,
):
    ways, rows, d = rows_all.shape
    half = rows // 2
    out_rows = wos.shape[2]
    width = q_ref.shape[1]
    me, z = lax.axis_index("dp"), lax.axis_index("tensor")
    core, heads_of, group_of = head_share()
    sib, across, along = plane_peers()
    others = [{"tensor": lax.rem(z + k, ways)} for k in range(1, ways)]
    z1, z2, z3 = (lax.bitwise_xor(z, k) for k in (1, 2, 3))
    near, far = {"tensor": z1}, {"tensor": z2}
    chip_rows = wq.shape[1] // 4
    enter([sib, across, along] + others)

    buckets[0] = jnp.full(buckets.shape[1:], bucket_ref[0], jnp.int32)
    bucket_copy = remote(buckets.at[0], buckets.at[1], bsend, brecv, 0, sib)
    bucket_copy.start()
    loads = [
        pltpu.make_async_copy(cot_ref.at[pl.ds(0, half)], cots.at[0], local.at[0]),
        pltpu.make_async_copy(
            wo_ref.at[pl.ds(pl.multiple_of(me * out_rows, 16), out_rows)],
            wos.at[z, me],
            local.at[1],
        ),
    ]
    for load in loads:
        load.start()

    def chip_part(chip, part):
        size = chip_rows if part is None else chip_rows // 2
        first = chip * chip_rows + (0 if part is None else part * size)
        return wq.at[:, pl.ds(pl.multiple_of(first, 16), size)]

    chip = me // 2
    chip_src = wq_ref.at[:, pl.ds(pl.multiple_of(chip * chip_rows, 16), chip_rows)]
    gives = core == lax.rem(z, 2)

    def piece_copy(k):
        return pltpu.make_async_remote_copy(
            src_ref=chip_src,
            dst_ref=chip_part(chip, None),
            send_sem=psend.at[k],
            recv_sem=precv.at[0],
            device_id={"tensor": z // 2 + 2 * k},
            device_id_type=MESH_ID,
        )

    piece_own = pltpu.make_async_copy(chip_src, chip_part(chip, None), local.at[2])
    for k in range(2):

        @pl.when(gives & (z // 2 + 2 * k != z))
        def _():
            piece_copy(k).start()

    @pl.when(heads_of == z)
    def _():
        piece_own.start()

    cot_copies = gather_copies(
        lambda s, part: half_of(cots.at[s], part), csend, crecv, False
    )
    loads[0].wait()
    gather_start(cot_copies)

    step = 128

    @pl.loop(0, rows // step)
    def _(i):
        at = pl.ds(pl.multiple_of(i * step, step), step)
        values = tok_ref[at, :].astype(F32)
        centred = values - jnp.mean(values, axis=-1, keepdims=True)
        root = lax.rsqrt(jnp.mean(centred * centred, axis=-1, keepdims=True) + norm_eps)
        mine[at, :] = (centred * root * gain_ref[...] + shift_ref[...]).astype(BF16)

    def part_of(which):
        return pl.ds(pl.multiple_of(which * half, half), half)

    def rows_at(block, which):
        return rows_all.at[block, part_of(which)]

    home = group_of == core
    give = [
        remote(mine.at[part_of(1 - core)], rows_at(z, 1 - core), nsend, nrecv, 0, sib),
        remote(mine.at[part_of(core)], rows_at(z, core), nsend, nrecv, 1, sib),
    ]
    swap = remote(mine.at[part_of(1 - core)], other, nsend, nrecv, 0, sib)
    to_far = remote(other, rows_at(z, core), nsend, nrecv, 2, far)
    to_near = remote(rows_at(z, core), rows_at(z, core), nsend, nrecv, 3, near)
    relay = remote(rows_at(z2, core), rows_at(z2, core), nsend, nrecv, 4, near)
    shares = {
        b: remote(rows_at(block, core), rows_at(block, core), nsend, nrecv, 4 + b, sib)
        for b, block in ((1, z1), (2, z2), (3, z3))
    }

    @pl.when(home)
    def _():
        give[0].start()
        give[1].start()
        rows_all[z] = mine[...]
        swap.wait_recv()
        to_far.start()
        to_near.start()

    @pl.when(jnp.logical_not(home))
    def _():
        swap.start()
        other[...] = mine[part_of(core), :]
        to_far.start()
        give[0].wait_recv()
        to_near.start()

    loads[1].wait()
    out_sends = []
    for k, peer in enumerate(others):
        slice_ref = wos.at[z, me]
        out_sends.append(
            pltpu.make_async_remote_copy(
                src_ref=slice_ref,
                dst_ref=slice_ref,
                send_sem=zsend.at[k],
                recv_sem=zrecv.at[z],
                device_id=peer,
                device_id_type=MESH_ID,
            )
        )
        out_sends[-1].start()

    qkv_copies = gather_copies(
        lambda s, part: chip_part(lax.bitwise_xor(chip, s // 2), part), qsend, qrecv, True, False
    )
    out_copies = gather_copies(
        lambda s, part: half_of(wos.at[:, lax.bitwise_xor(me, s)], part), wsend, wrecv, True
    )

    @pl.when(heads_of == z)
    def _():
        piece_own.wait()

    @pl.when(heads_of != z)
    def _():
        piece_copy(0).wait_recv()

    qkv_copies["0-2"].start()
    qkv_copies["0-4"].start()
    gather_forward(cot_copies)

    bucket_copy.wait_recv()
    bucket = jnp.where(home, buckets[0], buckets[1])
    bucket_out[...] = bucket
    span = jnp.where(bucket[0:1] == 1, LONG_LEN, SHORT_LEN)
    freq = freq_ref[...]
    lane = lax.broadcasted_iota(jnp.int32, freq.shape, 1)
    sign = jnp.where(lax.rem(lane, head_dim) < head_dim // 2, -1.0, 1.0)
    total = ways * rows

    @pl.loop(0, total // step)
    def _(i):
        at = pl.ds(pl.multiple_of(i * step, step), step)
        position = lax.broadcasted_iota(jnp.int32, (step, freq.shape[1]), 0) + i * step
        place = position
        for k in range(1, -(-total // SHORT_LEN)):
            place = place - jnp.where(position >= k * span, span, 0)
        angles = place.astype(F32) * freq
        cos_ref[at, :] = jnp.cos(angles)
        sin_ref[at, :] = jnp.sin(angles) * sign

    to_far.wait_recv()
    relay.start()
    shares[2].start()
    to_near.wait_recv()
    shares[1].start()
    qkv_copies["0-2"].wait_recv()
    qkv_copies["2-6"].start()
    qkv_copies["0-4"].wait_recv()
    qkv_copies["4-6"].start()
    for k, peer in enumerate(others):
        source = lax.rem(z + k + 1, ways)
        theirs = wos.at[source, me]
        pltpu.make_async_remote_copy(
            src_ref=theirs,
            dst_ref=theirs,
            send_sem=zsend.at[k],
            recv_sem=zrecv.at[source],
            device_id=peer,
            device_id_type=MESH_ID,
        ).wait_recv()
    gather_start(out_copies)
    qkv_copies["2-6"].wait_recv()
    qkv_copies["4-6"].wait_recv()
    wq_copy = pltpu.make_async_copy(wq, wq_out, local.at[0])
    wq_copy.start()

    stores = [
        pltpu.make_async_copy(rows_all, rows_out, local.at[1]),
        pltpu.make_async_copy(cots, cots_out, local.at[2]),
        pltpu.make_async_copy(wos, wos_out, local.at[3]),
    ]

    @pl.when(jnp.logical_not(home))
    def _():
        give[1].wait_recv()

    @pl.loop(0, ways)
    def _(i):
        @pl.when(i == 1)
        def _():
            shares[1].wait_recv()

        @pl.when(i == 2)
        def _():
            shares[2].wait_recv()
            gather_forward(out_copies)

        @pl.when(i == 3)
        def _():
            relay.wait_recv()
            shares[3].start()
            shares[3].wait_recv()
            stores[0].start()
            gather_finish(cot_copies)
            stores[1].start()

        block = lax.bitwise_xor(z, i)
        at = pl.ds(pl.multiple_of(block * rows, rows), rows)
        x = rows_all[block]
        cos, sin = widen(cos_ref[at, :], width), widen(sin_ref[at, :], width)
        q, k, v = (dot_nn(x, wq[j]) for j in range(3))
        v = v.astype(BF16)
        q = q * cos + swap_halves(q, head_dim) * sin
        k = (k * cos + swap_halves(k, head_dim) * sin).astype(BF16)
        q_ref[at, :] = (q * (head_dim ** (-0.5) * log2_e)).astype(BF16)
        k_ref[at, :] = k
        v_ref[at, :] = v
        kt_ref[:, at] = k.T
        vt_ref[:, at] = v.T

    gather_finish(out_copies)
    stores[2].start()
    for store in (wq_copy, *stores):
        store.wait()

    @pl.when(home)
    def _():
        give[0].wait_send()
        give[1].wait_send()

    @pl.when(jnp.logical_not(home))
    def _():
        swap.wait_send()

    for k in range(2):

        @pl.when(gives & (z // 2 + 2 * k != z))
        def _():
            piece_copy(k).wait_send()

    for copy in (to_far, to_near, relay, bucket_copy, *shares.values(), *out_sends):
        copy.wait_send()
    for copy in (*qkv_copies.values(), *cot_copies.values(), *out_copies.values()):
        copy.wait_send()


def front(bucket, tokens, gain, shift, cot, w_out, w_qkv, head_dim, ways):
    rows, d = tokens.shape
    width = w_qkv.shape[2]
    out_rows = w_out.shape[0] // 8
    total = ways * rows
    lanes = 128
    half_dim = head_dim // 2
    exponents = jnp.arange(half_dim, dtype=F32) * (-2.0 / head_dim)
    freq = jnp.tile(jnp.exp(exponents * jnp.log(F32(rope_base))), lanes // half_dim)[None]
    anywhere = pl.BlockSpec(memory_space=pl.ANY)
    inside = pl.BlockSpec(memory_space=pltpu.VMEM)
    sems = lambda n: [pltpu.SemaphoreType.DMA((n,))] * 2
    shape = jax.ShapeDtypeStruct
    return pl.pallas_call(
        functools.partial(front_kernel, head_dim),
        in_specs=[pl.BlockSpec(memory_space=pltpu.SMEM)] + [inside] * 4 + [anywhere] * 3,
        out_specs=[inside] * 8 + [anywhere] * 4,
        out_shape=[
            shape((total, width), BF16),
            shape((total, width), BF16),
            shape((total, width), BF16),
            shape((width, total), BF16),
            shape((width, total), BF16),
            shape((total, lanes), F32),
            shape((total, lanes), F32),
            shape((8, lanes), jnp.int32),
            shape((ways, rows, d), BF16),
            shape((8, rows // 2, d), BF16),
            shape((ways, 8, out_rows, d), BF16),
            shape(w_qkv.shape, BF16),
        ],
        scratch_shapes=[
            pltpu.VMEM((ways, rows, d), BF16),
            pltpu.VMEM((rows, d), BF16),
            pltpu.VMEM((rows // 2, d), BF16),
            pltpu.VMEM((8, rows // 2, d), BF16),
            pltpu.VMEM((ways, 8, out_rows, d), BF16),
            pltpu.VMEM(w_qkv.shape, BF16),
            pltpu.VMEM((2, 8, lanes), jnp.int32),
        ]
        + sems(8)
        + sems(8)
        + sems(8)
        + sems(8)
        + sems(ways)
        + sems(2)
        + sems(1)
        + [pltpu.SemaphoreType.DMA((4,))],
        compiler_params=pltpu.CompilerParams(
            collective_id=0, has_side_effects=True, vmem_limit_bytes=VMEM_LIMIT
        ),
        cost_estimate=pl.CostEstimate(
            flops=55 * 10**9, bytes_accessed=32 * rows * d, transcendentals=0
        ),
        name="front",
    )(bucket, tokens, gain[None], shift[None], freq, cot, w_out, w_qkv)


def column(ways):
    me, z = lax.axis_index("dp"), lax.axis_index("tensor")
    sib = lax.bitwise_xor(me, 1)
    others = [{"dp": sib, "tensor": z}]
    for k in range(1, ways):
        to = lax.rem(z + k, ways)
        others += [{"dp": me, "tensor": to}, {"dp": sib, "tensor": to}]
    return others


def collect_kernel(
    att_ref,
    tok_ref,
    wo_ref,
    gain_ref,
    shift_ref,
    cot_ref,
    at_ref,
    resid_ref,
    n_ref,
    cots_out,
    at,
    cots,
    isend,
    irecv,
    csend,
    crecv,
    lsem,
):
    ways, rows, quarter = at.shape
    me, z = lax.axis_index("dp"), lax.axis_index("tensor")
    core, heads_of, group_of = head_share()
    enter(column(ways) + plane_peers()[1:])
    half = rows // 2
    cot_own = pltpu.make_async_copy(cot_ref.at[pl.ds(half, half)], cots.at[0], lsem.at[1])
    cot_own.start()

    def in_copy(to):
        return pltpu.make_async_remote_copy(
            src_ref=att_ref.at[pl.ds(pl.multiple_of(to * rows, rows), rows)],
            dst_ref=at.at[heads_of],
            send_sem=isend.at[to],
            recv_sem=irecv.at[heads_of],
            device_id={"dp": me - core + group_of, "tensor": to},
            device_id_type=MESH_ID,
        )

    def in_wait(s):
        return pltpu.make_async_remote_copy(
            src_ref=att_ref.at[pl.ds(0, rows)],
            dst_ref=at.at[s],
            send_sem=isend.at[0],
            recv_sem=irecv.at[s],
            device_id={"dp": me - core + group_of, "tensor": z},
            device_id_type=MESH_ID,
        )

    own_at = group_of == core
    in_own = pltpu.make_async_copy(
        att_ref.at[pl.ds(pl.multiple_of(z * rows, rows), rows)], at.at[heads_of], lsem.at[0]
    )
    for k in range(ways - 1, 0, -1):
        in_copy(lax.bitwise_xor(z, k)).start()

    @pl.when(own_at)
    def _():
        in_own.start()
        in_own.wait()

    @pl.when(jnp.logical_not(own_at))
    def _():
        in_copy(z).start()

    copies = gather_copies(lambda s, part: half_of(cots.at[s], part), csend, crecv, False)
    cot_own.wait()
    gather_start(copies)
    gather_forward(copies)

    turn = jnp.where(z > 2 * core, 2, 0)
    step = min(256, rows)

    @pl.loop(0, ways)
    def _(k):
        s = lax.bitwise_xor(k, turn)
        source_core, source_z = head_source(s)

        @pl.when(jnp.logical_not((source_core == core) & (source_z == z)))
        def _():
            in_wait(s).wait_recv()

        at_ref[s] = at[s]
        weights = wo_ref[pl.ds(pl.multiple_of(s * quarter, quarter), quarter), :]

        @pl.when(k == 0)
        def _():
            resid_ref[...] = tok_ref[...].astype(F32) + dot_nn(at[s], weights)

        @pl.when(k > 0)
        def _():
            resid_ref[...] += dot_nn(at[s], weights)

    @pl.loop(0, rows // step)
    def _(k):
        rs = pl.ds(pl.multiple_of(k * step, step), step)
        acc = resid_ref[rs, :]
        centred = acc - jnp.mean(acc, axis=-1, keepdims=True)
        root = lax.rsqrt(jnp.mean(centred * centred, axis=-1, keepdims=True) + norm_eps)
        n_ref[rs, :] = (centred * root * gain_ref[...] + shift_ref[...]).astype(BF16)

    gather_finish(copies)
    cots_copy = pltpu.make_async_copy(cots, cots_out, lsem.at[1])
    cots_copy.start()
    for copy in copies.values():
        copy.wait_send()
    for k in range(1, ways):
        in_copy(lax.bitwise_xor(z, k)).wait_send()

    @pl.when(jnp.logical_not(own_at))
    def _():
        in_copy(z).wait_send()

    cots_copy.wait()


def collect(attended, tokens, out_full, gain, shift, cot, ways):
    rows, d = tokens.shape
    quarter = d // ways
    anywhere = pl.BlockSpec(memory_space=pl.ANY)
    inside = pl.BlockSpec(memory_space=pltpu.VMEM)
    return pl.pallas_call(
        collect_kernel,
        in_specs=[anywhere] + [inside] * 4 + [anywhere],
        out_specs=[inside] * 3 + [anywhere],
        out_shape=[
            jax.ShapeDtypeStruct((ways, rows, quarter), BF16),
            jax.ShapeDtypeStruct((rows, d), F32),
            jax.ShapeDtypeStruct((rows, d), BF16),
            jax.ShapeDtypeStruct((8, rows // 2, d), BF16),
        ],
        scratch_shapes=[
            pltpu.VMEM((ways, rows, quarter), BF16),
            pltpu.VMEM((8, rows // 2, d), BF16),
            pltpu.SemaphoreType.DMA((ways,)),
            pltpu.SemaphoreType.DMA((ways,)),
            pltpu.SemaphoreType.DMA((8,)),
            pltpu.SemaphoreType.DMA((8,)),
            pltpu.SemaphoreType.DMA((2,)),
        ],
        compiler_params=pltpu.CompilerParams(
            collective_id=3, has_side_effects=True, vmem_limit_bytes=VMEM_LIMIT
        ),
        cost_estimate=pl.CostEstimate(
            flops=30 * 10**9, bytes_accessed=16 * rows * d, transcendentals=0
        ),
        name="collect",
    )(attended, tokens, out_full, gain[None], shift[None], cot)


def middle_kernel(
    x_ref,
    at_ref,
    resid_ref,
    wo_ref,
    c_low_ref,
    c_high_ref,
    w_low_ref,
    w_high_ref,
    gain_ref,
    ag_ref,
    rg_ref,
    og_ref,
    out_ref,
    high_ref,
    grads_ref,
    ng_ref,
    wgu_ref,
    wd_ref,
    xs,
    cs,
    hid,
    branch,
    part,
    from_sib,
    from_far,
    from_x,
    from_y,
    down_acc,
    gate_up_acc,
    resid,
    at,
    agr,
    gsend,
    grecv,
    ssend,
    srecv,
    fsend,
    frecv,
    osend,
    orecv,
    csem,
    wsem,
    upsend,
    uprecv,
    downsend,
    downrecv,
    lsem,
    credit,
):
    ways, unit = w_low_ref.shape[0], w_low_ref.shape[1] // 3
    part_units = ways * unit
    units = 2 * part_units
    rows, d = x_ref.shape
    quarter = d // ways
    half = rows // 2
    low, high = pl.ds(0, half), pl.ds(half, half)
    keep = out_ref.shape[0]
    kept, others_at = pl.ds(0, keep), pl.ds(keep, rows - keep)
    me, z = lax.axis_index("dp"), lax.axis_index("tensor")
    core, heads_of, group_of = head_share()
    sib, across, along = plane_peers()
    enter(column(ways) + [across, along])

    own_at = group_of == core
    half_wo = ways // 2
    step = min(256, rows)
    own = pltpu.make_async_copy(x_ref, xs.at[0], lsem.at[0])
    own.start()
    first_loads = [
        pltpu.make_async_copy(at_ref, at, lsem.at[1]),
        pltpu.make_async_copy(resid_ref, resid, lsem.at[2]),
    ]
    cots = [
        pltpu.make_async_copy(ref.at[i], cs.at[i, side], csem.at[i, k])
        for i in range(8)
        for k, (ref, side) in enumerate(((c_low_ref, low), (c_high_ref, high)))
    ]

    def weight_place(t, j, upper):
        first = part_units * (upper if j == 2 else 2 * upper + j) + t * unit
        ref = wd_ref if j == 2 else wgu_ref
        return ref.at[pl.ds(first if isinstance(first, int) else pl.multiple_of(first, 16), unit)]

    weights = [
        pltpu.make_async_copy(
            w_low_ref.at[t, pl.ds(j * unit, unit)], weight_place(t, j, 0), wsem.at[t, j]
        )
        for t in range(ways)
        for j in range(3)
    ]
    upper_own = [
        pltpu.make_async_copy(
            w_high_ref.at[pl.ds(j * unit, unit)], weight_place(z, j, 1), wsem.at[ways, j]
        )
        for j in range(3)
    ]
    above, below = {"tensor": lax.rem(z + 1, ways)}, {"tensor": lax.rem(z + ways - 1, ways)}

    def weight_up(t):
        return [
            pltpu.make_async_remote_copy(
                src_ref=weight_place(t, j, 1),
                dst_ref=weight_place(t, j, 1),
                send_sem=upsend.at[t, j],
                recv_sem=uprecv.at[t, j],
                device_id=above,
                device_id_type=MESH_ID,
            )
            for j in range(3)
        ]

    def weight_down(t):
        return [
            pltpu.make_async_remote_copy(
                src_ref=weight_place(t, j, 1),
                dst_ref=weight_place(t, j, 1),
                send_sem=downsend.at[t, j],
                recv_sem=downrecv.at[t, j],
                device_id=below,
                device_id_type=MESH_ID,
            )
            for j in range(3)
        ]

    def weight_round(r):
        t = z + 1 + r

        @pl.when(t < ways)
        def _():
            for copy in weight_down(t):
                copy.wait_recv()

            @pl.when(z > 0)
            def _():
                for copy in weight_down(t):
                    copy.start()

        u = z - 1 - r

        @pl.when(u >= 0)
        def _():
            for copy in weight_up(u):
                copy.wait_recv()

            @pl.when(z < ways - 1)
            def _():
                for copy in weight_up(u):
                    copy.start()

    own.wait()
    copies = gather_copies(lambda s, side: half_of(xs.at[s], side), gsend, grecv, False)
    gather_start(copies)
    for load in (*upper_own, *weights, *cots, *first_loads):
        load.start()
    for load in upper_own:
        load.wait()

    @pl.when(z < ways - 1)
    def _():
        for copy in weight_up(z):
            copy.start()

    @pl.when(z > 0)
    def _():
        for copy in weight_down(z):
            copy.start()

    down_acc[...] = jnp.zeros_like(down_acc)
    gate_up_acc[...] = jnp.zeros_like(gate_up_acc)
    for load in weights:
        load.wait()

    def plane_sums(send, recv, src, landing, size):
        first, second = pl.ds(0, size // 2), pl.ds(size // 2, size // 2)
        steps = [
            ("1", src(1), landing[0], sib),
            ("3", src(3), landing[1], sib),
            ("5", src(5), landing[2], sib),
            ("7", src(7), landing[3], sib),
            ("6l", src(6).at[first], from_far.at[first], across),
            ("6h", src(6).at[second], from_far.at[second], along),
            ("2l", src(2).at[first], from_x.at[first], across),
            ("2h", src(2).at[second], from_x.at[second], across),
            ("4l", src(4).at[first], from_y.at[first], along),
            ("4h", src(4).at[second], from_y.at[second], along),
        ]
        return {
            name: remote(ref, dst, send, recv, i, peer)
            for i, (name, ref, dst, peer) in enumerate(steps)
        }

    def add_to(ref, other):
        ref[...] = (ref[...].astype(F32) + other[...].astype(F32)).astype(BF16)

    def slot(i):
        return i // 2 if i % 2 == 0 else 4 + (i // 2) % 2

    landing = [from_sib.at[0], from_sib.at[0], from_sib.at[1], from_sib.at[2]]
    sums = plane_sums(ssend, srecv, lambda i: part.at[slot(i)], landing, rows)

    def forward(i, place, into):
        both = dot_nt(xs[i], wgu_ref[...])
        hidden_grad = dot_nt(cs[i], wd_ref[...])
        for upper in range(2):
            of_units = slice(upper * part_units, (upper + 1) * part_units)
            first = upper * units
            gate = both[:, first : first + part_units]
            up = both[:, first + part_units : first + units]
            grad = hidden_grad[:, of_units]
            sig = jax.nn.sigmoid(gate)
            silu = gate * sig
            hid[place, :, of_units] = (silu * up).astype(BF16)
            branch[place, :, first : first + part_units] = (
                grad * up * sig * (1.0 + gate * (1.0 - sig))
            ).astype(BF16)
            branch[place, :, first + part_units : first + units] = (grad * silu).astype(BF16)
        part[into] = dot_nn(branch[place], wgu_ref[...]).astype(BF16)

    def grads(i, place):
        down_acc[...] += dot_tn(hid[place], cs[i])
        gate_up_acc[...] += dot_tn(branch[place], xs[i])
        cs[i] = dot_nn(hid[place], wd_ref[...]).astype(BF16)

    def cot_wait(i, slots):
        for k in slots:

            @pl.when(i == k)
            def _(k=k):
                cots[2 * k].wait()
                cots[2 * k + 1].wait()

    weight_round(0)
    weight_round(1)
    gather_forward(copies)
    for r in range(2, ways - 1):
        weight_round(r)

    @pl.loop(2, 8)
    def _(i):
        @pl.when(i == 3)
        def _():
            copies["2-3"].wait_recv()

        @pl.when(i == 5)
        def _():
            copies["4-5"].wait_recv()
            sums["3"].wait_recv()
            add_to(part.at[1], from_sib.at[0])
            sums["2l"].start()

        @pl.when(i == 6)
        def _():
            copies["2-6"].wait_recv()
            copies["4-6"].wait_recv()
            copies["6-7"].start()

        @pl.when(i == 7)
        def _():
            copies["6-7"].wait_recv()
            sums["5"].wait_recv()
            add_to(part.at[2], from_sib.at[1])
            sums["4h"].start()
            sums["3"].wait_send()

        cot_wait(i, range(2, 8))
        even = lax.rem(i, 2) == 0
        forward(i, i - 2, jnp.where(even, i // 2, 4 + lax.rem(i // 2, 2)))
        for odd in (3, 5, 7):

            @pl.when(i == odd)
            def _(odd=odd):
                sums[str(odd)].start()

    @pl.loop(2, 8)
    def _(i):
        @pl.when(i == 3)
        def _():
            sums["7"].wait_recv()
            add_to(part.at[3], from_sib.at[2])
            sums["6l"].start()
            sums["6h"].start()

        grads(i, i - 2)

    def grant(k, peer):
        pl.semaphore_signal(credit.at[k], inc=1, device_id=peer, device_id_type=MESH_ID)

    grant(0, sib)
    outs = plane_sums(
        fsend,
        frecv,
        lambda i: cs.at[i],
        [from_sib.at[0], from_sib.at[1], branch.at[5], from_sib.at[2]],
        keep,
    )
    pl.semaphore_wait(credit.at[0], 1)
    for name in ("7", "3", "5"):
        outs[name].start()
    copies["0-1"].wait_recv()
    sums["5"].wait_send()

    @pl.loop(0, 2)
    def _(i):
        cot_wait(i, (0, 1))
        forward(i, i, 4 * i)

        @pl.when(i == 0)
        def _():
            sums["6l"].wait_recv()
            add_to(part.at[2, low], from_far.at[low])
            sums["4l"].start()
            sums["6h"].wait_recv()
            add_to(part.at[1, high], from_far.at[high])
            sums["2h"].start()
            grant(1, across)
            grant(2, along)

        @pl.when(i == 1)
        def _():
            sums["1"].start()

        grads(i, i)

    sums["1"].wait_recv()
    add_to(part.at[0], from_sib.at[0])
    grant(3, sib)
    for copy in copies.values():
        copy.wait_send()
    for t in range(ways):
        for j in range(3):
            for upper in range(2):
                row = 2 * (3 * t + j) * unit + upper * unit
                first = part_units * (upper if j == 2 else 2 * upper + j) + t * unit
                acc = down_acc if j == 2 else gate_up_acc
                branch[row // rows, row % rows : row % rows + unit] = acc[
                    first : first + unit
                ].astype(BF16)
    for load in first_loads:
        load.wait()
    grads_copy = pltpu.make_async_copy(branch.at[pl.ds(0, grads_ref.shape[0])], grads_ref, lsem.at[1])
    wo_loads = [
        pltpu.make_async_copy(wo_ref.at[pl.ds(0, rows)], branch.at[3], lsem.at[2]),
        pltpu.make_async_copy(wo_ref.at[pl.ds(rows, rows)], branch.at[4], lsem.at[3]),
        pltpu.make_async_copy(c_low_ref.at[0], xs.at[3, low], lsem.at[0]),
        pltpu.make_async_copy(c_high_ref.at[0], xs.at[3, high], lsem.at[4]),
    ]
    grads_copy.start()
    for load in wo_loads:
        load.start()

    outs["7"].wait_recv()
    add_to(cs.at[6], from_sib.at[2])
    outs["3"].wait_recv()
    add_to(cs.at[2], from_sib.at[1])
    outs["5"].wait_recv()
    add_to(cs.at[4], branch.at[5])
    pl.semaphore_wait(credit.at[3], 1)
    outs["1"].start()

    grad = gate_up_acc
    for name in ("2l", "2h", "4l", "4h"):
        sums[name].wait_recv()
    pl.semaphore_wait(credit.at[1], 1)
    pl.semaphore_wait(credit.at[2], 1)
    outs["6l"].start()
    outs["6h"].start()

    @pl.loop(0, rows // step)
    def _(k):
        rs = pl.ds(pl.multiple_of(k * step, step), step)
        grad[rs, :] = (
            part[0, rs, :].astype(F32) + from_x[rs, :].astype(F32) + from_y[rs, :].astype(F32)
        )

    grant(4, across)
    grant(5, along)

    for load in wo_loads:
        load.wait()
    ng_ref[...] = jnp.zeros_like(ng_ref)
    gain = gain_ref[...]
    small = min(128, rows)

    @pl.loop(0, rows // small)
    def _(k):
        rs = pl.ds(pl.multiple_of(k * small, small), small)
        values = resid[rs, :]
        centred = values - jnp.mean(values, axis=-1, keepdims=True)
        root = lax.rsqrt(jnp.mean(centred * centred, axis=-1, keepdims=True) + norm_eps)
        unit_rows = centred * root
        out_grad = grad[rs, :]
        ng_ref[2:3] += jnp.sum(out_grad * unit_rows, axis=0, keepdims=True)
        ng_ref[3:4] += jnp.sum(out_grad, axis=0, keepdims=True)
        scaled = out_grad * gain
        first_mean = jnp.mean(scaled, axis=-1, keepdims=True)
        second_mean = jnp.mean(scaled * unit_rows, axis=-1, keepdims=True)
        total = xs[3, rs, :].astype(F32) + root * (scaled - first_mean - unit_rows * second_mean)
        grad[rs, :] = total
        xs[1, rs, :] = total.astype(BF16)

    rg_copy = pltpu.make_async_copy(grad.at[pl.ds(0, rows)], rg_ref, lsem.at[0])
    rg_copy.start()

    def out_copy(s):
        to_core, to_z = head_source(s)
        return pltpu.make_async_remote_copy(
            src_ref=xs.at[2, :, pl.ds(s * quarter, quarter)],
            dst_ref=agr.at[z],
            send_sem=osend.at[s],
            recv_sem=orecv.at[z],
            device_id={"dp": me - core + to_core, "tensor": to_z},
            device_id_type=MESH_ID,
        )

    def out_wait(source):
        return pltpu.make_async_remote_copy(
            src_ref=xs.at[2, :, pl.ds(0, quarter)],
            dst_ref=agr.at[source],
            send_sem=osend.at[0],
            recv_sem=orecv.at[source],
            device_id={"dp": me, "tensor": z},
            device_id_type=MESH_ID,
        )

    for s in range(ways):
        place = 3 + s // half_wo
        first = (s % half_wo) * quarter
        xs[2, :, s * quarter : (s + 1) * quarter] = dot_nt(
            xs[1], branch[place, first : first + quarter, :]
        ).astype(BF16)
        to_core, to_z = head_source(s)
        to_self = (to_core == core) & (to_z == z)

        @pl.when(jnp.logical_not(to_self))
        def _():
            out_copy(s).start()

        @pl.when(to_self)
        def _():
            agr[z] = xs[2, :, s * quarter : (s + 1) * quarter]

    pl.semaphore_wait(credit.at[4], 1)
    pl.semaphore_wait(credit.at[5], 1)
    outs["2l"].start()
    outs["4h"].start()

    for s in range(ways):
        place = 6 + s // half_wo
        first = (s % half_wo) * quarter
        xs[place, first : first + quarter] = dot_tn(at[s], xs[1]).astype(BF16)
    og_copy = pltpu.make_async_copy(xs.at[pl.ds(6, 2)], og_ref, lsem.at[2])
    og_copy.start()

    outs["1"].wait_recv()
    add_to(cs.at[0], from_sib.at[0])
    high_copies = [
        pltpu.make_async_copy(cs.at[2 * k, others_at], high_ref.at[k], csem.at[k, 0])
        for k in range(4)
    ]
    for copy in high_copies:
        copy.start()
    first, second = pl.ds(0, keep // 2), pl.ds(keep // 2, keep // 2)
    outs["6l"].wait_recv()
    add_to(cs.at[4, first], from_far.at[first])
    outs["4l"].start()
    outs["6h"].wait_recv()
    add_to(cs.at[2, second], from_far.at[second])
    outs["2h"].start()

    for source in range(ways):

        @pl.when(jnp.logical_not(own_at & (z == source)))
        def _():
            out_wait(source).wait_recv()

    ag_copy = pltpu.make_async_copy(agr, ag_ref, lsem.at[3])
    ag_copy.start()
    for name in ("2l", "2h", "4l", "4h"):
        outs[name].wait_recv()
    total = resid[kept, :] + cs[0, kept, :].astype(F32)
    total += from_x[kept, :].astype(F32) + from_y[kept, :].astype(F32)
    xs[0, kept, :] = total.astype(BF16)
    grads_copy.wait()
    lo_copy = pltpu.make_async_copy(xs.at[0, kept], out_ref, lsem.at[1])
    lo_copy.start()
    for name in ("1", "7", "6l", "6h", "2l", "2h", "4l", "4h"):
        sums[name].wait_send()
    for copy in outs.values():
        copy.wait_send()
    for t in range(ways):

        @pl.when((t <= z) & (z < ways - 1))
        def _():
            for copy in weight_up(t):
                copy.wait_send()

        @pl.when((t >= z) & (z > 0))
        def _():
            for copy in weight_down(t):
                copy.wait_send()

    for s in range(ways):
        to_core, to_z = head_source(s)

        @pl.when(jnp.logical_not((to_core == core) & (to_z == z)))
        def _():
            out_copy(s).wait_send()

    for copy in (rg_copy, og_copy, ag_copy, lo_copy, *high_copies):
        copy.wait()


def middle(x, attended, resid, out_full, cot_low, cot_high, w_low, w_high, gain):
    rows, d = x.shape
    ways, unit = w_low.shape[0], w_low.shape[1] // 3
    units = 2 * ways * unit
    quarter = d // ways
    anywhere = pl.BlockSpec(memory_space=pl.ANY)
    inside = pl.BlockSpec(memory_space=pltpu.VMEM)
    sems = lambda n: [pltpu.SemaphoreType.DMA((n,))] * 2
    return pl.pallas_call(
        middle_kernel,
        in_specs=[anywhere] * 8 + [inside],
        out_specs=[anywhere] * 6 + [inside],
        out_shape=[
            jax.ShapeDtypeStruct((ways, rows, quarter), BF16),
            jax.ShapeDtypeStruct((rows, d), F32),
            jax.ShapeDtypeStruct((2, rows, d), BF16),
            jax.ShapeDtypeStruct((rows - rows // 4, d), BF16),
            jax.ShapeDtypeStruct((4, rows // 4, d), BF16),
            jax.ShapeDtypeStruct((3 * units // rows, rows, d), BF16),
            jax.ShapeDtypeStruct((8, d), F32),
        ],
        scratch_shapes=[
            pltpu.VMEM((2 * units, d), BF16),
            pltpu.VMEM((units, d), BF16),
            pltpu.VMEM((8, rows, d), BF16),
            pltpu.VMEM((8, rows, d), BF16),
            pltpu.VMEM((6, rows, units), BF16),
            pltpu.VMEM((6, rows, 2 * units), BF16),
            pltpu.VMEM((6, rows, d), BF16),
            pltpu.VMEM((3, rows, d), BF16),
            pltpu.VMEM((rows, d), BF16),
            pltpu.VMEM((rows, d), BF16),
            pltpu.VMEM((rows, d), BF16),
            pltpu.VMEM((units, d), F32),
            pltpu.VMEM((2 * units, d), F32),
            pltpu.VMEM((rows, d), F32),
            pltpu.VMEM((ways, rows, quarter), BF16),
            pltpu.VMEM((ways, rows, quarter), BF16),
        ]
        + sems(8)
        + sems(10)
        + sems(10)
        + sems(ways)
        + [
            pltpu.SemaphoreType.DMA((8, 2)),
            pltpu.SemaphoreType.DMA((ways + 1, 3)),
        ]
        + [pltpu.SemaphoreType.DMA((ways, 3))] * 4
        + [
            pltpu.SemaphoreType.DMA((5,)),
            pltpu.SemaphoreType.REGULAR((6,)),
        ],
        compiler_params=pltpu.CompilerParams(
            collective_id=1, has_side_effects=True, vmem_limit_bytes=VMEM_LIMIT
        ),
        cost_estimate=pl.CostEstimate(
            flops=130 * 10**9, bytes_accessed=40 * rows * d, transcendentals=0
        ),
        name="middle",
    )(x, attended, resid, out_full, cot_low, cot_high, w_low, w_high, gain[None])


def ffn_rest_kernel(parts_ref, out_ref, ffn, ffn_far, ffn_x, ffn_y, fsend, frecv, load_sem):
    _, across, along = plane_peers()
    load = pltpu.make_async_copy(parts_ref, ffn, load_sem)
    load.start()
    enter([across, along])

    def add_to(ref, other):
        ref[...] = (ref[...].astype(F32) + other[...].astype(F32)).astype(BF16)

    edge = ffn.shape[1] // 2
    first, second = pl.ds(0, edge), pl.ds(edge, edge)
    ffns = [
        ("3l", ffn.at[3, first], ffn_far.at[first], across),
        ("3h", ffn.at[3, second], ffn_far.at[second], along),
        ("1l", ffn.at[1, first], ffn_x.at[first], across),
        ("1h", ffn.at[1, second], ffn_x.at[second], across),
        ("2l", ffn.at[2, first], ffn_y.at[first], along),
        ("2h", ffn.at[2, second], ffn_y.at[second], along),
    ]
    ffns = {
        name: remote(src, dst, fsend, frecv, i, peer)
        for i, (name, src, dst, peer) in enumerate(ffns)
    }
    load.wait()
    for name in ("3l", "3h", "1l", "2h"):
        ffns[name].start()
    ffns["3l"].wait_recv()
    add_to(ffn.at[2, first], ffn_far.at[first])
    ffns["2l"].start()
    ffns["3h"].wait_recv()
    add_to(ffn.at[1, second], ffn_far.at[second])
    ffns["1h"].start()
    for name in ("1l", "1h", "2l", "2h"):
        ffns[name].wait_recv()
    out_ref[...] = ffn[0].astype(F32) + ffn_x[...].astype(F32) + ffn_y[...].astype(F32)
    for copy in ffns.values():
        copy.wait_send()


def ffn_rest(parts):
    _, rows, d = parts.shape
    return pl.pallas_call(
        ffn_rest_kernel,
        in_specs=[pl.BlockSpec(memory_space=pl.ANY)],
        out_specs=pl.BlockSpec(memory_space=pltpu.VMEM),
        out_shape=jax.ShapeDtypeStruct((rows, d), F32),
        scratch_shapes=[pltpu.VMEM(parts.shape, BF16)]
        + [pltpu.VMEM((rows, d), BF16)] * 3
        + [pltpu.SemaphoreType.DMA((6,))] * 2
        + [pltpu.SemaphoreType.DMA],
        compiler_params=pltpu.CompilerParams(
            collective_id=4, has_side_effects=True, vmem_limit_bytes=VMEM_LIMIT
        ),
        cost_estimate=pl.CostEstimate(
            flops=8 * 10**9, bytes_accessed=8 * rows * d, transcendentals=0
        ),
        name="ffn_rest",
    )(parts)


def tail_kernel(
    mixed_ref,
    w_ref,
    out_parts_ref,
    rows_ref,
    tok_ref,
    norm_ref,
    n_ref,
    og_ref,
    qkv_ref,
    ng_ref,
    lines,
    line_sib,
    line_z,
    line_end,
    part,
    from_sib,
    from_far,
    from_x,
    from_y,
    mine,
    slices,
    ogs,
    qkv,
    qkv_far,
    qkv_x,
    qkv_y,
    qkv_sum,
    qkv_z,
    qkvs,
    norms,
    norm_sum,
    norms_z,
    lsend,
    lrecv,
    hsend,
    hrecv,
    ssend,
    srecv,
    gsend,
    grecv,
    osend,
    orecv,
    ksend,
    krecv,
    kzsend,
    kzrecv,
    kgsend,
    kgrecv,
    nsend,
    nrecv,
    zsend,
    zrecv,
    load_sem,
):
    me, z = lax.axis_index("dp"), lax.axis_index("tensor")
    ways, rows = lines.shape[0], lines.shape[1]
    out_rows = slices.shape[1]
    width = w_ref.shape[2]
    total = part.shape[1]
    half = total // 2
    low, high = pl.ds(0, half), pl.ds(half, half)
    core, heads_of, group_of = head_share()
    home = group_of == core
    chip = me // 2
    sib, across, along = plane_peers()
    others = [{"tensor": lax.rem(z + k, ways)} for k in range(1, ways)]
    z1, z2, z3 = (lax.bitwise_xor(z, k) for k in (1, 2, 3))
    near, far = {"tensor": z1}, {"tensor": z2}
    plane = [{"dp": lax.bitwise_xor(me, k)} for k in range(1, 8)]
    enter(plane + others)

    loads = []
    for i in range(8):
        src = pl.multiple_of(lax.bitwise_xor(me, i) * out_rows, 16)
        loads.append(
            [
                pltpu.make_async_copy(
                    out_parts_ref.at[t, pl.ds(src, out_rows)],
                    part.at[i, pl.ds(t * out_rows, out_rows)],
                    load_sem.at[t, i],
                )
                for t in range(ways)
            ]
        )
        for load in loads[-1]:
            load.start()

    def add_to(ref, other):
        ref[...] = (ref[...].astype(F32) + other[...].astype(F32)).astype(BF16)

    size = rows // 2

    def part_of(which):
        return pl.ds(pl.multiple_of(which * size, size), size)

    def line(i):
        b = lax.bitwise_xor(z, i)
        step = min(256, rows)

        @pl.loop(0, rows // step)
        def _(k):
            at = pl.ds(pl.multiple_of(b * rows + k * step, step), step)
            lines[b, pl.ds(pl.multiple_of(k * step, step), step)] = sum(
                dot_nt(mixed_ref[at, j * width : (j + 1) * width], w_ref[j]) for j in range(3)
            ).astype(BF16)

    def share(i):
        b = lax.bitwise_xor(z, i)
        return remote(lines.at[b, part_of(1 - core)], line_sib.at[b], hsend, hrecv, i, sib)

    def share_join(i):
        b = lax.bitwise_xor(z, i)
        share(i).wait_recv()
        add_to(lines.at[b, part_of(core)], line_sib.at[b])

    to_near = [
        remote(lines.at[z3, part_of(core)], line_z.at[0], lsend, lrecv, 0, near),
        remote(lines.at[z1, part_of(core)], line_z.at[1], lsend, lrecv, 1, near),
    ]
    to_far = remote(lines.at[z2, part_of(core)], line_z.at[2], lsend, lrecv, 2, far)
    last_away = remote(line_z.at[2], line_end, lsend, lrecv, 3, sib)
    last_home = remote(lines.at[z, part_of(core)], line_end, lsend, lrecv, 3, sib)

    sums = [
        ("1", part.at[1], from_sib.at[0], sib),
        ("3", part.at[3], from_sib.at[1], sib),
        ("5", part.at[5], from_sib.at[2], sib),
        ("7", part.at[7], from_sib.at[3], sib),
        ("6l", part.at[6, low], from_far.at[low], across),
        ("6h", part.at[6, high], from_far.at[high], along),
        ("2l", part.at[2, low], from_x.at[low], across),
        ("2h", part.at[2, high], from_x.at[high], across),
        ("4l", part.at[4, low], from_y.at[low], along),
        ("4h", part.at[4, high], from_y.at[high], along),
    ]
    sums = {
        name: remote(src, dst, ssend, srecv, i, peer)
        for i, (name, src, dst, peer) in enumerate(sums)
    }

    def qkv_rows(j):
        at = pl.ds(pl.multiple_of(j * width, width), width)
        qkv[at, :] = dot_tn(mixed_ref[:, at], rows_ref[...]).astype(BF16)

    line(3)
    share(3).start()

    @pl.loop(0, 3)
    def _(j):
        qkv_rows(j)

        @pl.when(j == 0)
        def _():
            share_join(3)
            to_near[0].start()

    piece = qkv_sum.shape[0]
    small = piece // 2

    def qkv_at(s, side=None):
        first = lax.bitwise_xor(chip, s) * piece + (0 if side is None else side * small)
        return qkv.at[pl.ds(pl.multiple_of(first, 16), piece if side is None else small)]

    def side_of(ref, side):
        return ref.at[pl.ds(side * small, small)]

    pieces = [
        ("3l", qkv_at(3, 0), side_of(qkv_far, 0), across),
        ("3h", qkv_at(3, 1), side_of(qkv_far, 1), along),
        ("1l", qkv_at(1, 0), side_of(qkv_x, 0), across),
        ("1h", qkv_at(1, 1), side_of(qkv_x, 1), across),
        ("2l", qkv_at(2, 0), side_of(qkv_y, 0), along),
        ("2h", qkv_at(2, 1), side_of(qkv_y, 1), along),
    ]
    pieces = {
        name: remote(src, dst, ksend, krecv, i, peer)
        for i, (name, src, dst, peer) in enumerate(pieces)
    }
    for name in ("3l", "3h", "1l", "2h"):
        pieces[name].start()

    @pl.loop(0, ways - 1)
    def _(k):
        i = lax.rem(k + 1, ways - 1)
        line(i)
        for fixed in range(ways - 1):

            @pl.when(i == fixed)
            def _(fixed=fixed):
                share(fixed).start()

    for i in (7, 3, 5, 1):
        for load in loads[i]:
            load.wait()
        sums[str(i)].start()

    pieces["3l"].wait_recv()
    add_to(qkv_at(2, 0), side_of(qkv_far, 0))
    pieces["2l"].start()
    pieces["3h"].wait_recv()
    add_to(qkv_at(1, 1), side_of(qkv_far, 1))
    pieces["1h"].start()
    share_join(1)
    share_join(2)
    to_near[0].wait_recv()
    to_near[1].start()
    add_to(lines.at[z2, part_of(core)], line_z.at[0])
    to_far.start()
    for i, j, names in ((6, 3, ("6l", "6h")), (2, 1, ("2l",)), (4, 2, ("4h",))):
        for load in loads[i]:
            load.wait()
        sums[str(i + 1)].wait_recv()
        add_to(part.at[i], from_sib.at[j])
        for name in names:
            sums[name].start()
    share_join(0)

    for name in ("1l", "1h", "2l", "2h"):
        pieces[name].wait_recv()
    qkv_sum[...] = (
        qkv_at(0)[...].astype(F32) + qkv_x[...].astype(F32) + qkv_y[...].astype(F32)
    ).astype(BF16)
    takes = core == lax.rem(z, 2)

    def owner_copy(slot):
        return pltpu.make_async_remote_copy(
            src_ref=qkv_sum,
            dst_ref=qkv_z.at[slot],
            send_sem=kzsend.at[0],
            recv_sem=kzrecv.at[slot],
            device_id={"tensor": heads_of},
            device_id_type=MESH_ID,
        )

    @pl.when(heads_of != z)
    def _():
        owner_copy(group_of).start()

    @pl.when(heads_of == z)
    def _():
        qkv_z[group_of] = qkv_sum[...]

    sums["6l"].wait_recv()
    add_to(part.at[4, low], from_far.at[low])
    sums["4l"].start()
    sums["6h"].wait_recv()
    add_to(part.at[2, high], from_far.at[high])
    sums["2h"].start()

    for load in loads[0]:
        load.wait()
    sums["1"].wait_recv()
    for name in ("2l", "2h", "4l", "4h"):
        sums[name].wait_recv()
    mine[...] = part[0].astype(F32) + from_sib[0].astype(F32)
    mine[...] += from_x[...].astype(F32) + from_y[...].astype(F32)

    for t in range(ways):
        at = slice(t * out_rows, (t + 1) * out_rows)
        part[0, at] = mine[at].astype(BF16)

    def slice_copy(k, to, source):
        return pltpu.make_async_remote_copy(
            src_ref=part.at[0, pl.ds(pl.multiple_of(to * out_rows, 16), out_rows)],
            dst_ref=slices.at[source],
            send_sem=osend.at[k],
            recv_sem=orecv.at[source],
            device_id={"tensor": to},
            device_id_type=MESH_ID,
        )

    for k in range(1, ways):
        slice_copy(k, lax.rem(z + k, ways), z).start()

    def chip_copy(s, side, peer, sem):
        at = qkvs.at[lax.bitwise_xor(chip, s)]
        ref = at if side is None else side_of(at, side)
        return remote(ref, ref, kgsend, kgrecv, sem, peer)

    to_x, to_y = chip_copy(0, None, across, 0), chip_copy(0, None, along, 1)
    x_on, y_on = chip_copy(1, 1, along, 2), chip_copy(2, 0, across, 3)
    to_sib = [chip_copy(s, None, sib, 4 + s) for s in range(4)]

    @pl.when(takes)
    def _():
        for slot in range(2):

            @pl.when(z // 2 + 2 * slot != z)
            def _():
                owner_copy(slot).wait_recv()

        qkvs[chip] = (qkv_z[0].astype(F32) + qkv_z[1].astype(F32)).astype(BF16)
        to_x.start()
        to_y.start()
        to_sib[0].start()

    own_slice = part[0, pl.ds(pl.multiple_of(z * out_rows, 16), out_rows)].astype(F32)
    for k in range(1, ways):
        source = lax.rem(z + k, ways)
        slice_copy(k, source, source).wait_recv()
        own_slice += slices[source].astype(F32)
    ogs[me] = own_slice.astype(BF16)
    view = lambda s, side: half_of(ogs.at[lax.bitwise_xor(me, s)], side)
    gathers = gather_copies(view, gsend, grecv, True)
    gather_start(gathers)

    to_near[1].wait_recv()
    add_to(lines.at[z, part_of(core)], line_z.at[1])

    @pl.when(jnp.logical_not(home))
    def _():
        last_home.start()

    to_far.wait_recv()

    @pl.when(home)
    def _():
        last_away.start()
        n_ref[part_of(core), :] = lines[z, part_of(core), :].astype(F32)

    @pl.when(jnp.logical_not(home))
    def _():
        n_ref[part_of(core), :] = line_z[2].astype(F32)

    last_away.wait_recv()
    n_ref[part_of(1 - core), :] = line_end[...].astype(F32)

    norms[me] = norm_ref[...]
    step = min(128, rows)

    @pl.loop(0, rows // step)
    def _(i):
        at = pl.ds(pl.multiple_of(i * step, step), step)
        values = tok_ref[at, :].astype(F32)
        centred = values - jnp.mean(values, axis=-1, keepdims=True)
        root = lax.rsqrt(jnp.mean(centred * centred, axis=-1, keepdims=True) + norm_eps)
        grad = n_ref[at, :]
        norms[me, 0:1] += jnp.sum(grad * (centred * root), axis=0, keepdims=True)
        norms[me, 1:2] += jnp.sum(grad, axis=0, keepdims=True)

    def swap(k, source):
        return remote(norms.at[source], norms.at[source], nsend, nrecv, k, plane[k])

    for k in range(7):
        swap(k, me).start()

    gather_forward(gathers)

    @pl.when(takes)
    def _():
        to_x.wait_recv()
        x_on.start()
        to_sib[1].start()
        to_y.wait_recv()
        y_on.start()
        to_sib[2].start()

    for k in range(7):
        swap(k, lax.bitwise_xor(me, k + 1)).wait_recv()
    norm_sum[...] = sum(norms[k] for k in range(8))

    def norm_copy(k, to, source):
        return pltpu.make_async_remote_copy(
            src_ref=norm_sum,
            dst_ref=norms_z.at[source],
            send_sem=zsend.at[k],
            recv_sem=zrecv.at[source],
            device_id={"tensor": to},
            device_id_type=MESH_ID,
        )

    for k in range(1, ways):
        norm_copy(k, lax.rem(z + k, ways), z).start()
    norms_z[z] = norm_sum[...]
    gather_finish(gathers)
    og_ref[...] = ogs[...]

    @pl.when(takes)
    def _():
        x_on.wait_recv()
        y_on.wait_recv()
        to_sib[3].start()

    @pl.when(jnp.logical_not(takes))
    def _():
        for copy in to_sib:
            copy.wait_recv()

    qkv_ref[...] = qkvs[...]
    for k in range(1, ways):
        source = lax.rem(z + k, ways)
        norm_copy(k, source, source).wait_recv()
    ng_ref[...] = sum(norms_z[t] for t in range(ways))

    @pl.when(takes)
    def _():
        for copy in (to_x, to_y, x_on, y_on, *to_sib):
            copy.wait_send()

    @pl.when(heads_of != z)
    def _():
        owner_copy(group_of).wait_send()

    @pl.when(home)
    def _():
        last_away.wait_send()

    @pl.when(jnp.logical_not(home))
    def _():
        last_home.wait_send()

    for copy in (*sums.values(), *gathers.values(), *pieces.values(), *to_near, to_far):
        copy.wait_send()
    for k in range(7):
        swap(k, me).wait_send()
    for i in range(ways):
        share(i).wait_send()
    for k in range(1, ways):
        to = lax.rem(z + k, ways)
        slice_copy(k, to, z).wait_send()
        norm_copy(k, to, z).wait_send()


def tail(mixed, w, out_parts, rows_one, tokens, norm_grads, ways):
    rows, d = tokens.shape
    out_rows = out_parts.shape[1] // 8
    qkv_rows = mixed.shape[1] // 4
    total = ways * out_rows
    anywhere = pl.BlockSpec(memory_space=pl.ANY)
    inside = pl.BlockSpec(memory_space=pltpu.VMEM)
    sems = lambda n: [pltpu.SemaphoreType.DMA((n,))] * 2
    return pl.pallas_call(
        tail_kernel,
        in_specs=[inside] * 2 + [anywhere] + [inside] * 3,
        out_specs=[inside] * 4,
        out_shape=[
            jax.ShapeDtypeStruct((rows, d), F32),
            jax.ShapeDtypeStruct((8, out_rows, d), BF16),
            jax.ShapeDtypeStruct((4, qkv_rows, d), BF16),
            jax.ShapeDtypeStruct((8, d), F32),
        ],
        scratch_shapes=[
            pltpu.VMEM((ways, rows, d), BF16),
            pltpu.VMEM((ways, rows // 2, d), BF16),
            pltpu.VMEM((3, rows // 2, d), BF16),
            pltpu.VMEM((rows // 2, d), BF16),
            pltpu.VMEM((8, total, d), BF16),
            pltpu.VMEM((4, total, d), BF16),
            pltpu.VMEM((total, d), BF16),
            pltpu.VMEM((total, d), BF16),
            pltpu.VMEM((total, d), BF16),
            pltpu.VMEM((total, d), F32),
            pltpu.VMEM((ways, out_rows, d), BF16),
            pltpu.VMEM((8, out_rows, d), BF16),
            pltpu.VMEM((4 * qkv_rows, d), BF16),
            pltpu.VMEM((qkv_rows, d), BF16),
            pltpu.VMEM((qkv_rows, d), BF16),
            pltpu.VMEM((qkv_rows, d), BF16),
            pltpu.VMEM((qkv_rows, d), BF16),
            pltpu.VMEM((2, qkv_rows, d), BF16),
            pltpu.VMEM((4, qkv_rows, d), BF16),
            pltpu.VMEM((8, 8, d), F32),
            pltpu.VMEM((8, d), F32),
            pltpu.VMEM((ways, 8, d), F32),
        ]
        + sems(4)
        + sems(ways)
        + sems(10)
        + sems(8)
        + sems(ways)
        + sems(6)
        + sems(2)
        + sems(8)
        + sems(7)
        + sems(ways)
        + [pltpu.SemaphoreType.DMA((ways, 8))],
        compiler_params=pltpu.CompilerParams(
            collective_id=2, has_side_effects=True, vmem_limit_bytes=VMEM_LIMIT
        ),
        cost_estimate=pl.CostEstimate(
            flops=75 * 10**9, bytes_accessed=40 * rows * d, transcendentals=0
        ),
        name="tail",
    )(mixed, w, out_parts, rows_one, tokens, norm_grads)


def finish_kernel(
    kept,
    both_ref,
    down_ref,
    features_ref,
    og_ref,
    grad_ref,
    resid_ref,
    tok_ref,
    gain_ref,
    low_ref,
    high_ref,
    before_ref,
    norms_ref,
    gate_up_ref,
    down_out_ref,
    qkv_ref,
    og_out_ref,
    token_ref,
    layer_ref,
    *norm_refs,
):
    units = both_ref.shape[1] // 2
    for p in range(8):
        turned = both_ref[p].astype(F32).T
        for g in range(2):
            at = pl.ds(2 * p + g, turned.shape[0], stride=16)
            gate_up_ref[at, :] = turned[:, g * units : (g + 1) * units]
    for p in range(down_ref.shape[0]):
        down_out_ref[p * units : (p + 1) * units] = down_ref[p].astype(F32)
    width = qkv_ref.shape[2]
    for j in range(3):
        qkv_ref[j] = features_ref[j * width : (j + 1) * width].astype(F32).T
    out_rows = og_ref.shape[1]
    for p in range(og_ref.shape[0]):
        og_out_ref[p * out_rows : (p + 1) * out_rows] = og_ref[p].astype(F32)
    values = tok_ref[...].astype(F32)
    centred = values - jnp.mean(values, axis=-1, keepdims=True)
    root = lax.rsqrt(jnp.mean(centred * centred, axis=-1, keepdims=True) + norm_eps)
    unit_rows = centred * root
    scaled = grad_ref[...] * gain_ref[...]
    first_mean = jnp.mean(scaled, axis=-1, keepdims=True)
    second_mean = jnp.mean(scaled * unit_rows, axis=-1, keepdims=True)
    token_ref[...] = resid_ref[...] + root * (scaled - first_mean - unit_rows * second_mean)
    for k, ref in enumerate(norm_refs):
        ref[...] = norms_ref[k : k + 1]
    step = pl.program_id(0)

    @pl.when(step < kept)
    def _():
        layer_ref[...] = low_ref[...]

    @pl.when(step >= kept)
    def _():
        layer_ref[...] = (before_ref[...] + high_ref[...]).astype(BF16)


def finish(grads, features, out_grad, norm_grad, resid_grad, tokens, gain, low, high, resid, norms):
    rows, d = tokens.shape
    units = grads.shape[1] // 3
    width = features.shape[0] // 3
    out_rows = out_grad.shape[1]
    steps = 4
    each = 8 // steps
    block = d // steps
    own = pl.BlockSpec((rows // steps, d), lambda i: (i, 0))
    kept = steps * low.shape[0] // rows
    return pl.pallas_call(
        functools.partial(finish_kernel, kept),
        grid=(steps,),
        in_specs=[
            pl.BlockSpec((8, 2 * units, block), lambda i: (0, 0, i)),
            pl.BlockSpec((each, units, d), lambda i: (i, 2, 0)),
            pl.BlockSpec((3 * width, block), lambda i: (0, i)),
            pl.BlockSpec((each, out_rows, d), lambda i: (i, 0, 0)),
            own,
            own,
            own,
            pl.BlockSpec((1, d), lambda i: (0, 0)),
            pl.BlockSpec((rows // steps, d), lambda i: (jnp.minimum(i, kept - 1), 0)),
            pl.BlockSpec((rows // steps, d), lambda i: (jnp.maximum(i - kept, 0), 0)),
            pl.BlockSpec((rows // steps, d), lambda i: (jnp.maximum(i, kept), 0)),
            pl.BlockSpec(norms.shape, lambda i: (0, 0)),
        ],
        out_specs=[
            pl.BlockSpec((16 * block, units), lambda i: (i, 0)),
            pl.BlockSpec((each * units, d), lambda i: (i, 0)),
            pl.BlockSpec((3, block, width), lambda i: (0, i, 0)),
            pl.BlockSpec((each * out_rows, d), lambda i: (i, 0)),
            own,
            own,
        ]
        + [pl.BlockSpec((1, d), lambda i: (0, 0))] * 4,
        out_shape=[
            jax.ShapeDtypeStruct((16 * d, units), F32),
            jax.ShapeDtypeStruct((8 * units, d), F32),
            jax.ShapeDtypeStruct((3, d, width), F32),
            jax.ShapeDtypeStruct((8 * out_rows, d), F32),
            jax.ShapeDtypeStruct((rows, d), F32),
            jax.ShapeDtypeStruct((rows, d), BF16),
        ]
        + [jax.ShapeDtypeStruct((1, d), F32)] * 4,
        compiler_params=pltpu.CompilerParams(vmem_limit_bytes=VMEM_LIMIT),
        name="finish",
    )(
        grads,
        grads,
        features,
        out_grad,
        norm_grad,
        resid_grad,
        tokens,
        gain[None],
        low,
        high,
        resid,
        norms,
    )


def shards(
    tokens,
    group_bucket,
    gain_one,
    shift_one,
    w_qkv,
    w_out,
    gain_two,
    shift_two,
    w_gate_up,
    w_down,
    cotangent,
):
    ways = lax.axis_size("tensor")
    replicas = lax.axis_size("dp")
    replica = lax.axis_index("dp")
    own_rows, d = tokens.shape
    group_rows = own_rows * ways
    local_width = w_out.shape[0]
    head_dim = d // HEADS
    hidden_width = w_down.shape[0]
    units = hidden_width // replicas
    out_rows = local_width // replicas
    pair_width = min(128, local_width)

    rows_in = tokens.astype(F32)
    normed_one, unit_one, root_one = norm_forward(rows_in, gain_one, shift_one)
    normed_one_low = normed_one.astype(BF16)
    rows_one = lax.all_gather(normed_one_low, "tensor", axis=0, tiled=True)

    gate_up_slice = lax.dynamic_slice_in_dim(w_gate_up, replica * units, units, axis=2)
    down_slice = lax.dynamic_slice_in_dim(w_down, replica * units, units, axis=0)
    weight_slice = jnp.concatenate(
        [gate_up_slice.transpose(1, 2, 0).reshape(2 * units, d), down_slice]
    )
    weights = lax.all_gather(weight_slice, "tensor", axis=0)
    cot_all = lax.all_gather(cotangent, "dp", axis=0, tiled=True)
    out_full = lax.all_gather(w_out, "tensor", axis=0, tiled=True)

    cos_wide, sine_wide = rotary_wide(group_bucket[0], group_rows, head_dim, pair_width)
    qkv_weights = w_qkv.transpose(1, 0, 2)
    q, k, v, kt, vt = project(rows_one, qkv_weights, cos_wide, sine_wide, head_dim)
    attended, *kept = attend(group_bucket[None], q, k, vt, head_dim)
    attended_own = lax.all_to_all(attended, "tensor", 0, 1, tiled=True)
    resid = rows_in + dot_nn(attended_own, out_full)
    normed_two, unit_two, root_two = norm_forward(resid, gain_two, shift_two)
    normed_two_low = normed_two.astype(BF16)
    parts = weights.reshape(ways, 3, units, d)
    wgu = parts[:, :2].transpose(3, 1, 0, 2).reshape(d, 2 * ways * units)
    wd = parts[:, 2].reshape(ways * units, d)
    rows_two = lax.all_gather(normed_two_low, "dp", axis=0, tiled=True)
    hidden, branch, back = feed(rows_two, cot_all, wgu, wd)
    normed_two_grad = lax.psum_scatter(back, "dp", scatter_dimension=0, tiled=True).astype(F32)
    ffn_parts = dot_nn(hidden, wd).astype(BF16)
    ffn_out = lax.psum_scatter(ffn_parts, "dp", scatter_dimension=0, tiled=True).astype(F32)
    layer_out = (resid + ffn_out).astype(BF16)
    grads = jnp.concatenate(
        [
            dot_tn(branch, rows_two).reshape(2, ways, units, d),
            dot_tn(hidden, cot_all).reshape(1, ways, units, d),
        ]
    )
    grads = grads.astype(BF16).transpose(1, 0, 2, 3).reshape(ways, 3 * units, d)
    resid_part, gain_two_grad, shift_two_grad = norm_backward(
        normed_two_grad, unit_two, root_two, gain_two
    )
    norm_grads = jnp.zeros((8, d), F32).at[2].set(gain_two_grad).at[3].set(shift_two_grad)
    resid_grad = cotangent.astype(F32) + resid_part
    attn_grad = resid_grad.astype(BF16)
    attended_grad = lax.all_to_all(
        dot_nt(attn_grad, out_full).astype(BF16), "tensor", 1, 0, tiled=True
    )
    out_grad = dot_tn(attended_own, attn_grad).astype(BF16)
    out_grad = out_grad.reshape(ways, replicas, out_rows, d).transpose(1, 0, 2, 3)
    out_grad = out_grad.reshape(replicas, ways * out_rows, d)
    grads = lax.psum_scatter(grads, "tensor", scatter_dimension=0)

    mixed_grad = attend_back(
        group_bucket[None], q, k, kt, v, attended_grad, *kept, cos_wide, sine_wide, head_dim
    )
    grads, mixed_grad = lax.optimization_barrier((grads, mixed_grad))
    grads = lax.all_gather(grads, "dp", axis=0)
    grads = grads.reshape(replicas, 3, units, d)
    down_grad = grads[:, 2].reshape(hidden_width, d).astype(F32)
    gate_up_grad = grads[:, :2].transpose(3, 1, 0, 2).reshape(d, 2, hidden_width).astype(F32)
    qkv_grad = lax.psum(dot_tn(rows_one, mixed_grad).astype(BF16), "dp").astype(F32)
    qkv_grad = qkv_grad.reshape(d, 3, local_width)
    flat = qkv_weights.transpose(1, 0, 2).reshape(d, 3 * local_width)
    normed_one_grad = lax.psum_scatter(
        dot_nt(mixed_grad, flat).astype(BF16), "tensor", scatter_dimension=0, tiled=True
    ).astype(F32)
    out_grad = lax.psum_scatter(out_grad, "dp", scatter_dimension=0)
    out_grad = lax.psum_scatter(out_grad, "tensor", scatter_dimension=0, tiled=True)
    out_grad = lax.all_gather(out_grad, "dp", axis=0, tiled=True).astype(F32)
    one = norm_backward(normed_one_grad, unit_one, root_one, gain_one)
    norm_grads = norm_grads.at[0].set(one[1]).at[1].set(one[2])
    norm_grads = lax.psum(norm_grads, ("dp", "tensor"))
    token_grad = resid_grad + norm_backward(normed_one_grad, unit_one, root_one, gain_one)[0]
    gain_one_grad, shift_one_grad, gain_two_grad, shift_two_grad = (norm_grads[i] for i in range(4))
    return (
        layer_out,
        token_grad,
        gain_one_grad,
        shift_one_grad,
        qkv_grad,
        out_grad,
        gain_two_grad,
        shift_two_grad,
        gate_up_grad,
        down_grad,
    )


def shards_columns(
    tokens,
    group_bucket,
    gain_one,
    shift_one,
    w_qkv,
    w_out,
    gain_two,
    shift_two,
    w_gate_up,
    w_down,
    cotangent,
):
    ways = lax.axis_size("tensor")
    replica = lax.axis_index("dp")
    own_rows, d = tokens.shape
    group_rows = own_rows * ways
    local_width = w_out.shape[0]
    head_dim = d // HEADS
    hidden_width = w_down.shape[0]
    units = hidden_width // 8

    gate_up_slice = lax.dynamic_slice_in_dim(w_gate_up, replica * units, units, axis=2)
    down_slice = lax.dynamic_slice_in_dim(w_down, replica * units, units, axis=0)
    gate_up_slice = gate_up_slice.transpose(1, 2, 0)
    half = units // 2
    slice_low, slice_high = (
        jnp.concatenate([gate_up_slice[:, at].reshape(units, d), down_slice[at]])
        for at in (slice(0, half), slice(half, units))
    )
    q, k, v, kt, vt, cos_wide, sine_wide, bucket, rows_one, cot_low, out_full, qkv_weights = front(
        group_bucket,
        tokens,
        gain_one,
        shift_one,
        cotangent,
        w_out,
        w_qkv.transpose(1, 0, 2),
        head_dim,
        ways,
    )
    bucket, slice_low = lax.optimization_barrier((bucket, slice_low))
    weights_low = lax.all_gather(slice_low, "tensor", axis=0)
    out_full = out_full.reshape(d, d)
    attended, *kept = attend(bucket, q, k, vt, head_dim)
    attended_own, resid, normed_two, cot_high = collect(
        attended, tokens, out_full, gain_two, shift_two, cotangent, ways
    )
    attended_grad, resid_grad, out_grad, layer_low, ffn_parts, grads, norm_grads = middle(
        normed_two,
        attended_own,
        resid,
        out_full,
        cot_low,
        cot_high,
        weights_low,
        slice_high,
        gain_two,
    )
    grads = grads.reshape(ways, 3 * units, d)
    grads = lax.psum_scatter(grads, "tensor", scatter_dimension=0)
    attended_grad = attended_grad.reshape(group_rows, local_width)
    mixed_grad = attend_back(
        bucket, q, k, kt, v, attended_grad, *kept, cos_wide, sine_wide, head_dim
    )
    ffn_parts, mixed_grad = lax.optimization_barrier((ffn_parts, mixed_grad))
    layer_high = ffn_rest(ffn_parts)
    grads, mixed_grad, layer_high = lax.optimization_barrier((grads, mixed_grad, layer_high))
    grads = lax.all_gather(grads, "dp", axis=0)
    normed_one_grad, out_grad, qkv_grad, norm_grads = tail(
        mixed_grad,
        qkv_weights,
        out_grad.reshape(ways, local_width, d),
        rows_one.reshape(group_rows, d),
        tokens,
        norm_grads,
        ways,
    )
    gate_up_grad, down_grad, qkv_grad, out_grad, token_grad, layer_out, *norm_grads = finish(
        grads,
        qkv_grad.reshape(3 * local_width, d),
        out_grad,
        normed_one_grad,
        resid_grad,
        tokens,
        gain_one,
        layer_low,
        layer_high,
        resid,
        norm_grads,
    )
    gate_up_grad = gate_up_grad.reshape(d, 8, 2, units).transpose(0, 2, 1, 3)
    gate_up_grad = gate_up_grad.reshape(d, 2, hidden_width)
    qkv_grad = qkv_grad.transpose(1, 0, 2)
    gain_one_grad, shift_one_grad, gain_two_grad, shift_two_grad = (g[0] for g in norm_grads)
    return (
        layer_out,
        token_grad,
        gain_one_grad,
        shift_one_grad,
        qkv_grad,
        out_grad,
        gain_two_grad,
        shift_two_grad,
        gate_up_grad,
        down_grad,
    )


def solution(mesh):
    in_specs = (
        P(("dp", "tensor"), None),
        P("dp"),
        P(),
        P(),
        P(None, None, "tensor"),
        P("tensor", None),
        P(),
        P(),
        P(None, None, "tensor"),
        P("tensor", None),
        P(("dp", "tensor"), None),
    )
    out_specs = (
        P(("dp", "tensor"), None),
        P(("dp", "tensor"), None),
        P(),
        P(),
        P(None, None, "tensor"),
        P("tensor", None),
        P(),
        P(),
        P(None, None, "tensor"),
        P("tensor", None),
    )
    columns = mesh.shape["dp"] == 8 and mesh.shape["tensor"] == 4
    body = shards_columns if columns else shards
    return jax.shard_map(body, mesh=mesh, in_specs=in_specs, out_specs=out_specs, check_vma=False)
```

```python
import functools

import jax
import jax.numpy as jnp
from jax import lax
from jax.experimental import pallas as pl
from jax.experimental.pallas import tpu as pltpu
from jax.sharding import PartitionSpec as P

HEADS = 16
LONG_LEN = 2048
SHORT_LEN = 1000

norm_eps = 1e-05
mask_fill = -1e30
rope_base = 10000.0
VMEM_LIMIT = 62 * 2**20
F32 = jnp.float32
BF16 = jnp.bfloat16


def dot_nn(a, b):
    return jnp.dot(a, b, preferred_element_type=F32)


def dot_nt(a, b):
    return lax.dot_general(a, b, (((1,), (1,)), ((), ())), preferred_element_type=F32)


def dot_tn(a, b):
    return lax.dot_general(a, b, (((0,), (0,)), ((), ())), preferred_element_type=F32)


def rotary_wide(bucket_id, group_rows, head_dim, width):
    positions = jnp.arange(group_rows, dtype=jnp.int32)
    span_len = jnp.where(bucket_id == 1, LONG_LEN, SHORT_LEN).astype(jnp.int32)
    places = positions - (positions // span_len) * span_len
    half_dim = head_dim // 2
    exponents = jnp.arange(half_dim, dtype=F32) * (-2.0 / head_dim)
    freqs = jnp.exp(exponents * jnp.log(F32(rope_base)))
    heads = width // head_dim
    signs = jnp.tile(jnp.repeat(jnp.array([-1.0, 1.0], F32), half_dim), heads)
    angles = places.astype(F32)[:, None] * jnp.tile(freqs, 2 * heads)[None, :]
    return jnp.cos(angles), jnp.sin(angles) * signs


def norm_forward(values, gain, shift):
    average = jnp.mean(values, axis=-1, keepdims=True)
    centred = values - average
    spread_sq = jnp.mean(centred * centred, axis=-1, keepdims=True)
    inv_root = lax.rsqrt(spread_sq + norm_eps)
    unit_rows = centred * inv_root
    return (unit_rows * gain + shift, unit_rows, inv_root)


def norm_backward(out_grad_rows, unit_rows, inv_root, gain):
    scaled = out_grad_rows * gain
    first_mean = jnp.mean(scaled, axis=-1, keepdims=True)
    second_mean = jnp.mean(scaled * unit_rows, axis=-1, keepdims=True)
    in_grad = inv_root * (scaled - first_mean - unit_rows * second_mean)
    return (in_grad, jnp.sum(out_grad_rows * unit_rows, axis=0), jnp.sum(out_grad_rows, axis=0))


def swap_halves(x, head_dim):
    half = head_dim // 2
    width = x.shape[1]
    lane = lax.broadcasted_iota(jnp.int32, x.shape, 1) % head_dim
    return jnp.where(lane < half, pltpu.roll(x, width - half, 1), pltpu.roll(x, half, 1))


def head_mask(x, h, head_dim):
    lane = lax.broadcasted_iota(jnp.int32, x.shape, 1)
    return jnp.where((lane >= h * head_dim) & (lane < (h + 1) * head_dim), x, jnp.zeros_like(x))


def widen(table, width):
    return jnp.concatenate([table] * (width // table.shape[1]), axis=1)


def project_kernel(head_dim, x_ref, w_ref, cos_ref, sin_ref, q_ref, k_ref, v_ref, kt_ref, vt_ref):
    width = q_ref.shape[1]
    x = x_ref[...]
    cos, sin = widen(cos_ref[...], width), widen(sin_ref[...], width)
    q, k, v = (dot_nn(x, w_ref[j]) for j in range(3))
    v = v.astype(BF16)
    q = q * cos + swap_halves(q, head_dim) * sin
    k = k * cos + swap_halves(k, head_dim) * sin
    k_low = k.astype(BF16)
    q_ref[...] = (q.astype(BF16).astype(F32) * head_dim ** (-0.5)).astype(BF16)
    k_ref[...] = k_low
    v_ref[...] = v
    kt_ref[...] = k_low.T
    vt_ref[...] = v.T


def project(rows, w, cos_wide, sine_wide, head_dim):
    n, d = rows.shape
    width = w.shape[2]
    block = min(512, n)
    row = pl.BlockSpec((block, width), lambda i: (i, 0))
    col = pl.BlockSpec((width, block), lambda i: (0, i))
    table = pl.BlockSpec((block, cos_wide.shape[1]), lambda i: (i, 0))
    return pl.pallas_call(
        functools.partial(project_kernel, head_dim),
        grid=(n // block,),
        in_specs=[
            pl.BlockSpec((block, d), lambda i: (i, 0)),
            pl.BlockSpec((3, d, width), lambda i: (0, 0, 0)),
            table,
            table,
        ],
        out_specs=[row, row, row, col, col],
        out_shape=[jax.ShapeDtypeStruct((n, width), BF16)] * 3
        + [jax.ShapeDtypeStruct((width, n), BF16)] * 2,
        compiler_params=pltpu.CompilerParams(vmem_limit_bytes=VMEM_LIMIT),
        cost_estimate=pl.CostEstimate(
            flops=6 * n * d * width, bytes_accessed=2 * n * d + 18 * n * width, transcendentals=0
        ),
        name="project",
    )(rows, w, cos_wide, sine_wide)


def key_range(start, block, total):
    first = (start // SHORT_LEN) * SHORT_LEN
    last = min(total, ((start + block - 1) // SHORT_LEN + 1) * SHORT_LEN)
    return (first // 256) * 256, min(total, -(-last // 256) * 256)


def window_bias(key_start, keys, row_start, rows, total):
    key_at = lax.broadcasted_iota(jnp.int32, (keys, rows), 0) + key_start
    row_at = lax.broadcasted_iota(jnp.int32, (keys, rows), 1) + row_start
    key_window = jnp.zeros_like(key_at)
    row_window = jnp.zeros_like(row_at)
    for edge in range(SHORT_LEN, total, SHORT_LEN):
        key_window += (key_at >= edge).astype(jnp.int32)
        row_window += (row_at >= edge).astype(jnp.int32)
    return jnp.where(key_window == row_window, 0.0, mask_fill)


def attend_kernel(head_dim, bucket_ref, q_ref, k_ref, vt_ref, o_ref, ot_ref, l_ref, bias_ref):
    rows, width = q_ref.shape
    total = k_ref.shape[0]
    heads = width // head_dim
    step = pl.program_id(0)

    def block(at, first, last, masked):
        @pl.loop(0, heads)
        def _(h):
            hs = pl.ds(pl.multiple_of(h * head_dim, head_dim), head_dim)
            scores = dot_nt(k_ref[first:last, :], head_mask(q_ref[at, :], h, head_dim))
            if masked:
                scores = scores + bias_ref[: last - first, :]
            top = jnp.max(scores, axis=0, keepdims=True)
            weights = jnp.exp(scores - top)
            totals = jnp.sum(weights, axis=0, keepdims=True)
            ot_ref[hs, at] = dot_nn(vt_ref[hs, first:last], weights.astype(BF16)) / totals
            l_ref[pl.ds(h, 1), at] = top + jnp.log(totals)

    @pl.when(bucket_ref[0, 0] == 1)
    def _():
        block(slice(0, rows), 0, total, False)

    sub = bias_ref.shape[1]
    for start in range(0, total, sub):
        first, last = key_range(start, sub, total)

        @pl.when((bucket_ref[0, 0] != 1) & (step == start // rows))
        def _():
            bias_ref[: last - first, :] = window_bias(first, last - first, start, sub, total)
            block(slice(start % rows, start % rows + sub), first, last, True)

    o_ref[...] = ot_ref[...].T.astype(BF16)


def attend(bucket, q, k, vt, head_dim):
    n, width = q.shape
    heads = width // head_dim
    block = min(1024, n)
    pairs = n * n * heads
    lanes = -(-heads // 8) * 8
    row = pl.BlockSpec((block, width), lambda i: (i, 0))
    col = pl.BlockSpec((width, block), lambda i: (0, i))
    return pl.pallas_call(
        functools.partial(attend_kernel, head_dim),
        grid=(n // block,),
        in_specs=[
            pl.BlockSpec(memory_space=pltpu.SMEM),
            row,
            pl.BlockSpec((n, width), lambda i: (0, 0)),
            pl.BlockSpec((width, n), lambda i: (0, 0)),
        ],
        out_specs=[row, col, pl.BlockSpec((lanes, block), lambda i: (0, i))],
        out_shape=[
            jax.ShapeDtypeStruct((n, width), BF16),
            jax.ShapeDtypeStruct((width, n), F32),
            jax.ShapeDtypeStruct((lanes, n), F32),
        ],
        scratch_shapes=[pltpu.VMEM((n, min(512, block)), F32)],
        compiler_params=pltpu.CompilerParams(vmem_limit_bytes=VMEM_LIMIT),
        cost_estimate=pl.CostEstimate(
            flops=pairs * 1024, bytes_accessed=10 * n * width, transcendentals=pairs
        ),
        name="attend",
    )(bucket, q, k, vt)


def attend_back_kernel(
    head_dim,
    bucket_ref,
    q_ref,
    k_ref,
    kt_ref,
    v_ref,
    g_ref,
    ot_ref,
    l_ref,
    cos_ref,
    sin_ref,
    out_ref,
    bias_ref,
    gt_ref,
    dq_ref,
    dk_ref,
    dv_ref,
):
    rows, width = q_ref.shape
    total = k_ref.shape[0]
    heads = width // head_dim
    step = pl.program_id(0)

    @pl.when(step == 0)
    def _():
        dk_ref[...] = jnp.zeros_like(dk_ref)
        dv_ref[...] = jnp.zeros_like(dv_ref)

    gt_ref[...] = g_ref[...].astype(F32).T * ot_ref[...]

    def block(first, last, masked):
        keys = slice(first, last)

        @pl.loop(0, heads)
        def _(h):
            hs = pl.ds(pl.multiple_of(h * head_dim, head_dim), head_dim)
            qh, gh = head_mask(q_ref[...], h, head_dim), head_mask(g_ref[...], h, head_dim)
            scores = dot_nt(k_ref[keys, :], qh)
            if masked:
                scores = scores + bias_ref[: last - first, :]
            probs = jnp.exp(scores - l_ref[pl.ds(h, 1), :])
            prob_grad = dot_nt(v_ref[keys, :], gh)
            delta = jnp.sum(gt_ref[hs, :], axis=0, keepdims=True)
            score_grad = (probs * (prob_grad - delta)).astype(BF16)
            dv_ref[keys, :] += dot_nn(probs.astype(BF16), gh)
            dk_ref[keys, :] += dot_nn(score_grad, qh)
            dq_ref[hs, :] = dot_nn(kt_ref[hs, keys], score_grad)

    @pl.when(bucket_ref[0, 0] == 1)
    def _():
        block(0, total, False)

    for start in range(0, total, rows):
        first, last = key_range(start, rows, total)

        @pl.when((bucket_ref[0, 0] != 1) & (step == start // rows))
        def _():
            bias_ref[: last - first, :] = window_bias(first, last - first, start, rows, total)
            block(first, last, True)

    def turn_back(grad, at):
        cos, sin = widen(cos_ref[at, :], width), widen(sin_ref[at, :], width)
        return (grad * cos - swap_halves(grad, head_dim) * sin).astype(BF16)

    at = pl.ds(pl.multiple_of(step * rows, rows), rows)
    out_ref[at, :width] = turn_back(dq_ref[...].T * head_dim ** (-0.5), at)

    @pl.when(step == pl.num_programs(0) - 1)
    def _():
        @pl.loop(0, total // rows)
        def _(i):
            at = pl.ds(pl.multiple_of(i * rows, rows), rows)
            out_ref[at, width : 2 * width] = turn_back(dk_ref[at, :], at)
            out_ref[at, 2 * width :] = dv_ref[at, :].astype(BF16)


def attend_back(bucket, q, k, kt, v, g, ot, log_totals, cos_wide, sine_wide, head_dim):
    n, width = q.shape
    heads = width // head_dim
    block = min(512, n)
    pairs = n * n * heads
    row = pl.BlockSpec((block, width), lambda i: (i, 0))
    col = pl.BlockSpec((width, block), lambda i: (0, i))
    full = lambda rows, cols: pl.BlockSpec((rows, cols), lambda i: (0, 0))
    table = full(n, cos_wide.shape[1])
    return pl.pallas_call(
        functools.partial(attend_back_kernel, head_dim),
        grid=(n // block,),
        in_specs=[
            pl.BlockSpec(memory_space=pltpu.SMEM),
            row,
            full(n, width),
            full(width, n),
            full(n, width),
            row,
            col,
            pl.BlockSpec((log_totals.shape[0], block), lambda i: (0, i)),
            table,
            table,
        ],
        out_specs=full(n, 3 * width),
        out_shape=jax.ShapeDtypeStruct((n, 3 * width), BF16),
        scratch_shapes=[
            pltpu.VMEM((n, block), F32),
            pltpu.VMEM((width, block), F32),
            pltpu.VMEM((width, block), F32),
            pltpu.VMEM((n, width), F32),
            pltpu.VMEM((n, width), F32),
        ],
        compiler_params=pltpu.CompilerParams(vmem_limit_bytes=VMEM_LIMIT),
        cost_estimate=pl.CostEstimate(
            flops=pairs * 2560, bytes_accessed=24 * n * width, transcendentals=pairs
        ),
        name="attend_back",
    )(bucket, q, k, kt, v, g, ot, log_totals, cos_wide, sine_wide)


def feed_kernel(x_ref, c_ref, wgu_ref, wd_ref, h_ref, b_ref, n_ref):
    units = wd_ref.shape[0]
    both = dot_nn(x_ref[...], wgu_ref[...])
    gate, up = both[:, :units], both[:, units:]
    sig = jax.nn.sigmoid(gate)
    silu = gate * sig
    h_ref[...] = (silu * up).astype(BF16)
    hidden_grad = dot_nt(c_ref[...], wd_ref[...])
    b_ref[:, :units] = (hidden_grad * up * sig * (1.0 + gate * (1.0 - sig))).astype(BF16)
    b_ref[:, units:] = (hidden_grad * silu).astype(BF16)
    n_ref[...] = dot_nt(b_ref[...], wgu_ref[...]).astype(BF16)


def feed(x, cot, wgu, wd):
    n, d = x.shape
    units = wd.shape[0]
    block = min(256, n)
    row = lambda w: pl.BlockSpec((block, w), lambda i: (i, 0))
    return pl.pallas_call(
        feed_kernel,
        grid=(n // block,),
        in_specs=[
            row(d),
            row(d),
            pl.BlockSpec((d, 2 * units), lambda i: (0, 0)),
            pl.BlockSpec((units, d), lambda i: (0, 0)),
        ],
        out_specs=[row(units), row(2 * units), row(d)],
        out_shape=[
            jax.ShapeDtypeStruct((n, units), BF16),
            jax.ShapeDtypeStruct((n, 2 * units), BF16),
            jax.ShapeDtypeStruct((n, d), BF16),
        ],
        compiler_params=pltpu.CompilerParams(vmem_limit_bytes=VMEM_LIMIT),
        cost_estimate=pl.CostEstimate(
            flops=10 * n * d * units, bytes_accessed=8 * n * d, transcendentals=n * units
        ),
        name="feed",
    )(x, cot, wgu, wd)


MESH_ID = pl.DeviceIdType.MESH


def plane_peers():
    me = lax.axis_index("dp")
    return [{"dp": lax.bitwise_xor(me, bit)} for bit in (1, 2, 4)]


def enter(peers):
    barrier = pltpu.get_barrier_semaphore()
    for peer in peers:
        pl.semaphore_signal(barrier, inc=1, device_id=peer, device_id_type=MESH_ID)
    pl.semaphore_wait(barrier, len(peers))


def remote(src, dst, send, recv, at, peer):
    return pltpu.make_async_remote_copy(
        src_ref=src,
        dst_ref=dst,
        send_sem=send.at[at],
        recv_sem=recv.at[at],
        device_id=peer,
        device_id_type=MESH_ID,
    )


def gather_copies(view, send, recv, placed, cores=True):
    sib, across, along = plane_peers()
    steps = [
        (0, 1, sib, None),
        (0, 2, across, None),
        (0, 4, along, None),
        (4, 2, across, 0),
        (2, 4, along, 1),
        (2, 1, sib, None),
        (4, 1, sib, None),
        (6, 1, sib, None),
    ]
    copies = {}
    for i, (s, bit, peer, part) in enumerate(steps):
        if bit == 1 and not cores:
            continue
        src = view(s, part)
        dst = src if placed else view(s ^ bit, part)
        copies[f"{s}-{s ^ bit}"] = remote(src, dst, send, recv, i, peer)
    return copies


def half_of(ref, part):
    if part is None:
        return ref
    half = ref.shape[-2] // 2
    return ref.at[(slice(None),) * (len(ref.shape) - 2) + (pl.ds(part * half, half),)]


def gather_start(copies):
    for name in ("0-2", "0-4", "0-1"):
        copies[name].start()


def gather_forward(copies):
    copies["0-2"].wait_recv()
    copies["2-6"].start()
    copies["2-3"].start()
    copies["0-4"].wait_recv()
    copies["4-6"].start()
    copies["4-5"].start()


def gather_finish(copies):
    copies["2-6"].wait_recv()
    copies["4-6"].wait_recv()
    copies["6-7"].start()
    for name in ("0-1", "2-3", "4-5", "6-7"):
        copies[name].wait_recv()


def head_share():
    core, z = lax.rem(lax.axis_index("dp"), 2), lax.axis_index("tensor")
    return core, 2 * lax.rem(z, 2) + core, z // 2


def head_source(s):
    return s % 2, 2 * lax.rem(lax.axis_index("dp"), 2) + s // 2


def front_kernel(
    head_dim,
    bucket_ref,
    tok_ref,
    gain_ref,
    shift_ref,
    freq_ref,
    cot_ref,
    wo_ref,
    wq_ref,
    q_ref,
    k_ref,
    v_ref,
    kt_ref,
    vt_ref,
    cos_ref,
    sin_ref,
    bucket_out,
    rows_out,
    cots_out,
    wos_out,
    wq_out,
    rows_all,
    mine,
    other,
    cots,
    wos,
    wq,
    buckets,
    nsend,
    nrecv,
    csend,
    crecv,
    wsend,
    wrecv,
    qsend,
    qrecv,
    zsend,
    zrecv,
    psend,
    precv,
    bsend,
    brecv,
    local,
):
    ways, rows, d = rows_all.shape
    half = rows // 2
    out_rows = wos.shape[2]
    width = q_ref.shape[1]
    me, z = lax.axis_index("dp"), lax.axis_index("tensor")
    core, heads_of, group_of = head_share()
    sib, across, along = plane_peers()
    others = [{"tensor": lax.rem(z + k, ways)} for k in range(1, ways)]
    z1, z2, z3 = (lax.bitwise_xor(z, k) for k in (1, 2, 3))
    near, far = {"tensor": z1}, {"tensor": z2}
    chip_rows = wq.shape[1] // 4
    enter([sib, across, along] + others)

    buckets[0] = jnp.full(buckets.shape[1:], bucket_ref[0], jnp.int32)
    bucket_copy = remote(buckets.at[0], buckets.at[1], bsend, brecv, 0, sib)
    bucket_copy.start()
    loads = [
        pltpu.make_async_copy(cot_ref.at[pl.ds(0, half)], cots.at[0], local.at[0]),
        pltpu.make_async_copy(
            wo_ref.at[pl.ds(pl.multiple_of(me * out_rows, 16), out_rows)],
            wos.at[z, me],
            local.at[1],
        ),
    ]
    for load in loads:
        load.start()

    def chip_part(chip, part):
        size = chip_rows if part is None else chip_rows // 2
        first = chip * chip_rows + (0 if part is None else part * size)
        return wq.at[:, pl.ds(pl.multiple_of(first, 16), size)]

    chip = me // 2
    chip_src = wq_ref.at[:, pl.ds(pl.multiple_of(chip * chip_rows, 16), chip_rows)]
    gives = core == lax.rem(z, 2)

    def piece_copy(k):
        return pltpu.make_async_remote_copy(
            src_ref=chip_src,
            dst_ref=chip_part(chip, None),
            send_sem=psend.at[k],
            recv_sem=precv.at[0],
            device_id={"tensor": z // 2 + 2 * k},
            device_id_type=MESH_ID,
        )

    piece_own = pltpu.make_async_copy(chip_src, chip_part(chip, None), local.at[2])
    for k in range(2):

        @pl.when(gives & (z // 2 + 2 * k != z))
        def _():
            piece_copy(k).start()

    @pl.when(heads_of == z)
    def _():
        piece_own.start()

    cot_copies = gather_copies(
        lambda s, part: half_of(cots.at[s], part), csend, crecv, False
    )
    loads[0].wait()
    gather_start(cot_copies)

    step = 128

    @pl.loop(0, rows // step)
    def _(i):
        at = pl.ds(pl.multiple_of(i * step, step), step)
        values = tok_ref[at, :].astype(F32)
        centred = values - jnp.mean(values, axis=-1, keepdims=True)
        root = lax.rsqrt(jnp.mean(centred * centred, axis=-1, keepdims=True) + norm_eps)
        mine[at, :] = (centred * root * gain_ref[...] + shift_ref[...]).astype(BF16)

    def part_of(which):
        return pl.ds(pl.multiple_of(which * half, half), half)

    def rows_at(block, which):
        return rows_all.at[block, part_of(which)]

    home = group_of == core
    give = [
        remote(mine.at[part_of(1 - core)], rows_at(z, 1 - core), nsend, nrecv, 0, sib),
        remote(mine.at[part_of(core)], rows_at(z, core), nsend, nrecv, 1, sib),
    ]
    swap = remote(mine.at[part_of(1 - core)], other, nsend, nrecv, 0, sib)
    to_far = remote(other, rows_at(z, core), nsend, nrecv, 2, far)
    to_near = remote(rows_at(z, core), rows_at(z, core), nsend, nrecv, 3, near)
    relay = remote(rows_at(z2, core), rows_at(z2, core), nsend, nrecv, 4, near)
    shares = {
        b: remote(rows_at(block, core), rows_at(block, core), nsend, nrecv, 4 + b, sib)
        for b, block in ((1, z1), (2, z2), (3, z3))
    }

    @pl.when(home)
    def _():
        give[0].start()
        give[1].start()
        rows_all[z] = mine[...]
        swap.wait_recv()
        to_far.start()
        to_near.start()

    @pl.when(jnp.logical_not(home))
    def _():
        swap.start()
        other[...] = mine[part_of(core), :]
        to_far.start()
        give[0].wait_recv()
        to_near.start()

    loads[1].wait()
    out_sends = []
    for k, peer in enumerate(others):
        slice_ref = wos.at[z, me]
        out_sends.append(
            pltpu.make_async_remote_copy(
                src_ref=slice_ref,
                dst_ref=slice_ref,
                send_sem=zsend.at[k],
                recv_sem=zrecv.at[z],
                device_id=peer,
                device_id_type=MESH_ID,
            )
        )
        out_sends[-1].start()

    qkv_copies = gather_copies(
        lambda s, part: chip_part(lax.bitwise_xor(chip, s // 2), part), qsend, qrecv, True, False
    )
    out_copies = gather_copies(
        lambda s, part: half_of(wos.at[:, lax.bitwise_xor(me, s)], part), wsend, wrecv, True
    )

    @pl.when(heads_of == z)
    def _():
        piece_own.wait()

    @pl.when(heads_of != z)
    def _():
        piece_copy(0).wait_recv()

    qkv_copies["0-2"].start()
    qkv_copies["0-4"].start()
    gather_forward(cot_copies)

    bucket_copy.wait_recv()
    bucket = jnp.where(home, buckets[0], buckets[1])
    bucket_out[...] = bucket
    span = jnp.where(bucket[0:1] == 1, LONG_LEN, SHORT_LEN)
    freq = freq_ref[...]
    lane = lax.broadcasted_iota(jnp.int32, freq.shape, 1)
    sign = jnp.where(lax.rem(lane, head_dim) < head_dim // 2, -1.0, 1.0)
    total = ways * rows

    @pl.loop(0, total // step)
    def _(i):
        at = pl.ds(pl.multiple_of(i * step, step), step)
        position = lax.broadcasted_iota(jnp.int32, (step, freq.shape[1]), 0) + i * step
        place = position
        for k in range(1, -(-total // SHORT_LEN)):
            place = place - jnp.where(position >= k * span, span, 0)
        angles = place.astype(F32) * freq
        cos_ref[at, :] = jnp.cos(angles)
        sin_ref[at, :] = jnp.sin(angles) * sign

    to_far.wait_recv()
    relay.start()
    shares[2].start()
    to_near.wait_recv()
    shares[1].start()
    qkv_copies["0-2"].wait_recv()
    qkv_copies["2-6"].start()
    qkv_copies["0-4"].wait_recv()
    qkv_copies["4-6"].start()
    for k, peer in enumerate(others):
        source = lax.rem(z + k + 1, ways)
        theirs = wos.at[source, me]
        pltpu.make_async_remote_copy(
            src_ref=theirs,
            dst_ref=theirs,
            send_sem=zsend.at[k],
            recv_sem=zrecv.at[source],
            device_id=peer,
            device_id_type=MESH_ID,
        ).wait_recv()
    gather_start(out_copies)
    qkv_copies["2-6"].wait_recv()
    qkv_copies["4-6"].wait_recv()
    wq_copy = pltpu.make_async_copy(wq, wq_out, local.at[0])
    wq_copy.start()

    stores = [
        pltpu.make_async_copy(rows_all, rows_out, local.at[1]),
        pltpu.make_async_copy(cots, cots_out, local.at[2]),
        pltpu.make_async_copy(wos, wos_out, local.at[3]),
    ]

    @pl.when(jnp.logical_not(home))
    def _():
        give[1].wait_recv()

    @pl.loop(0, ways)
    def _(i):
        @pl.when(i == 1)
        def _():
            shares[1].wait_recv()

        @pl.when(i == 2)
        def _():
            shares[2].wait_recv()
            gather_forward(out_copies)

        @pl.when(i == 3)
        def _():
            relay.wait_recv()
            shares[3].start()
            shares[3].wait_recv()
            stores[0].start()
            gather_finish(cot_copies)
            stores[1].start()

        block = lax.bitwise_xor(z, i)
        at = pl.ds(pl.multiple_of(block * rows, rows), rows)
        x = rows_all[block]
        cos, sin = widen(cos_ref[at, :], width), widen(sin_ref[at, :], width)
        q, k, v = (dot_nn(x, wq[j]) for j in range(3))
        v = v.astype(BF16)
        q = q * cos + swap_halves(q, head_dim) * sin
        k = (k * cos + swap_halves(k, head_dim) * sin).astype(BF16)
        q_ref[at, :] = (q.astype(BF16).astype(F32) * head_dim ** (-0.5)).astype(BF16)
        k_ref[at, :] = k
        v_ref[at, :] = v
        kt_ref[:, at] = k.T
        vt_ref[:, at] = v.T

    gather_finish(out_copies)
    stores[2].start()
    for store in (wq_copy, *stores):
        store.wait()

    @pl.when(home)
    def _():
        give[0].wait_send()
        give[1].wait_send()

    @pl.when(jnp.logical_not(home))
    def _():
        swap.wait_send()

    for k in range(2):

        @pl.when(gives & (z // 2 + 2 * k != z))
        def _():
            piece_copy(k).wait_send()

    for copy in (to_far, to_near, relay, bucket_copy, *shares.values(), *out_sends):
        copy.wait_send()
    for copy in (*qkv_copies.values(), *cot_copies.values(), *out_copies.values()):
        copy.wait_send()


def front(bucket, tokens, gain, shift, cot, w_out, w_qkv, head_dim, ways):
    rows, d = tokens.shape
    width = w_qkv.shape[2]
    out_rows = w_out.shape[0] // 8
    total = ways * rows
    lanes = 128
    half_dim = head_dim // 2
    exponents = jnp.arange(half_dim, dtype=F32) * (-2.0 / head_dim)
    freq = jnp.tile(jnp.exp(exponents * jnp.log(F32(rope_base))), lanes // half_dim)[None]
    anywhere = pl.BlockSpec(memory_space=pl.ANY)
    inside = pl.BlockSpec(memory_space=pltpu.VMEM)
    sems = lambda n: [pltpu.SemaphoreType.DMA((n,))] * 2
    shape = jax.ShapeDtypeStruct
    return pl.pallas_call(
        functools.partial(front_kernel, head_dim),
        in_specs=[pl.BlockSpec(memory_space=pltpu.SMEM)] + [inside] * 4 + [anywhere] * 3,
        out_specs=[inside] * 8 + [anywhere] * 4,
        out_shape=[
            shape((total, width), BF16),
            shape((total, width), BF16),
            shape((total, width), BF16),
            shape((width, total), BF16),
            shape((width, total), BF16),
            shape((total, lanes), F32),
            shape((total, lanes), F32),
            shape((8, lanes), jnp.int32),
            shape((ways, rows, d), BF16),
            shape((8, rows // 2, d), BF16),
            shape((ways, 8, out_rows, d), BF16),
            shape(w_qkv.shape, BF16),
        ],
        scratch_shapes=[
            pltpu.VMEM((ways, rows, d), BF16),
            pltpu.VMEM((rows, d), BF16),
            pltpu.VMEM((rows // 2, d), BF16),
            pltpu.VMEM((8, rows // 2, d), BF16),
            pltpu.VMEM((ways, 8, out_rows, d), BF16),
            pltpu.VMEM(w_qkv.shape, BF16),
            pltpu.VMEM((2, 8, lanes), jnp.int32),
        ]
        + sems(8)
        + sems(8)
        + sems(8)
        + sems(8)
        + sems(ways)
        + sems(2)
        + sems(1)
        + [pltpu.SemaphoreType.DMA((4,))],
        compiler_params=pltpu.CompilerParams(
            collective_id=0, has_side_effects=True, vmem_limit_bytes=VMEM_LIMIT
        ),
        cost_estimate=pl.CostEstimate(
            flops=55 * 10**9, bytes_accessed=32 * rows * d, transcendentals=0
        ),
        name="front",
    )(bucket, tokens, gain[None], shift[None], freq, cot, w_out, w_qkv)


def column(ways):
    me, z = lax.axis_index("dp"), lax.axis_index("tensor")
    sib = lax.bitwise_xor(me, 1)
    others = [{"dp": sib, "tensor": z}]
    for k in range(1, ways):
        to = lax.rem(z + k, ways)
        others += [{"dp": me, "tensor": to}, {"dp": sib, "tensor": to}]
    return others


def collect_kernel(
    att_ref,
    tok_ref,
    wo_ref,
    gain_ref,
    shift_ref,
    cot_ref,
    at_ref,
    resid_ref,
    n_ref,
    cots_out,
    at,
    cots,
    isend,
    irecv,
    csend,
    crecv,
    lsem,
):
    ways, rows, quarter = at.shape
    me, z = lax.axis_index("dp"), lax.axis_index("tensor")
    core, heads_of, group_of = head_share()
    enter(column(ways) + plane_peers()[1:])
    half = rows // 2
    cot_own = pltpu.make_async_copy(cot_ref.at[pl.ds(half, half)], cots.at[0], lsem.at[1])
    cot_own.start()

    def in_copy(to):
        return pltpu.make_async_remote_copy(
            src_ref=att_ref.at[pl.ds(pl.multiple_of(to * rows, rows), rows)],
            dst_ref=at.at[heads_of],
            send_sem=isend.at[to],
            recv_sem=irecv.at[heads_of],
            device_id={"dp": me - core + group_of, "tensor": to},
            device_id_type=MESH_ID,
        )

    def in_wait(s):
        return pltpu.make_async_remote_copy(
            src_ref=att_ref.at[pl.ds(0, rows)],
            dst_ref=at.at[s],
            send_sem=isend.at[0],
            recv_sem=irecv.at[s],
            device_id={"dp": me - core + group_of, "tensor": z},
            device_id_type=MESH_ID,
        )

    own_at = group_of == core
    in_own = pltpu.make_async_copy(
        att_ref.at[pl.ds(pl.multiple_of(z * rows, rows), rows)], at.at[heads_of], lsem.at[0]
    )
    for k in range(ways - 1, 0, -1):
        in_copy(lax.bitwise_xor(z, k)).start()

    @pl.when(own_at)
    def _():
        in_own.start()
        in_own.wait()

    @pl.when(jnp.logical_not(own_at))
    def _():
        in_copy(z).start()

    copies = gather_copies(lambda s, part: half_of(cots.at[s], part), csend, crecv, False)
    cot_own.wait()
    gather_start(copies)
    gather_forward(copies)

    turn = jnp.where(z > 2 * core, 2, 0)
    step = min(256, rows)

    @pl.loop(0, ways)
    def _(k):
        s = lax.bitwise_xor(k, turn)
        source_core, source_z = head_source(s)

        @pl.when(jnp.logical_not((source_core == core) & (source_z == z)))
        def _():
            in_wait(s).wait_recv()

        at_ref[s] = at[s]
        weights = wo_ref[pl.ds(pl.multiple_of(s * quarter, quarter), quarter), :]

        @pl.when(k == 0)
        def _():
            resid_ref[...] = tok_ref[...].astype(F32) + dot_nn(at[s], weights)

        @pl.when(k > 0)
        def _():
            resid_ref[...] += dot_nn(at[s], weights)

    @pl.loop(0, rows // step)
    def _(k):
        rs = pl.ds(pl.multiple_of(k * step, step), step)
        acc = resid_ref[rs, :]
        centred = acc - jnp.mean(acc, axis=-1, keepdims=True)
        root = lax.rsqrt(jnp.mean(centred * centred, axis=-1, keepdims=True) + norm_eps)
        n_ref[rs, :] = (centred * root * gain_ref[...] + shift_ref[...]).astype(BF16)

    gather_finish(copies)
    cots_copy = pltpu.make_async_copy(cots, cots_out, lsem.at[1])
    cots_copy.start()
    for copy in copies.values():
        copy.wait_send()
    for k in range(1, ways):
        in_copy(lax.bitwise_xor(z, k)).wait_send()

    @pl.when(jnp.logical_not(own_at))
    def _():
        in_copy(z).wait_send()

    cots_copy.wait()


def collect(attended, tokens, out_full, gain, shift, cot, ways):
    rows, d = tokens.shape
    quarter = d // ways
    anywhere = pl.BlockSpec(memory_space=pl.ANY)
    inside = pl.BlockSpec(memory_space=pltpu.VMEM)
    return pl.pallas_call(
        collect_kernel,
        in_specs=[anywhere] + [inside] * 4 + [anywhere],
        out_specs=[inside] * 3 + [anywhere],
        out_shape=[
            jax.ShapeDtypeStruct((ways, rows, quarter), BF16),
            jax.ShapeDtypeStruct((rows, d), F32),
            jax.ShapeDtypeStruct((rows, d), BF16),
            jax.ShapeDtypeStruct((8, rows // 2, d), BF16),
        ],
        scratch_shapes=[
            pltpu.VMEM((ways, rows, quarter), BF16),
            pltpu.VMEM((8, rows // 2, d), BF16),
            pltpu.SemaphoreType.DMA((ways,)),
            pltpu.SemaphoreType.DMA((ways,)),
            pltpu.SemaphoreType.DMA((8,)),
            pltpu.SemaphoreType.DMA((8,)),
            pltpu.SemaphoreType.DMA((2,)),
        ],
        compiler_params=pltpu.CompilerParams(
            collective_id=3, has_side_effects=True, vmem_limit_bytes=VMEM_LIMIT
        ),
        cost_estimate=pl.CostEstimate(
            flops=30 * 10**9, bytes_accessed=16 * rows * d, transcendentals=0
        ),
        name="collect",
    )(attended, tokens, out_full, gain[None], shift[None], cot)


def middle_kernel(
    x_ref,
    at_ref,
    resid_ref,
    wo_ref,
    c_low_ref,
    c_high_ref,
    w_low_ref,
    w_high_ref,
    gain_ref,
    ag_ref,
    rg_ref,
    og_ref,
    out_ref,
    high_ref,
    grads_ref,
    ng_ref,
    wgu_ref,
    wd_ref,
    xs,
    cs,
    hid,
    branch,
    part,
    from_sib,
    from_far,
    from_x,
    from_y,
    down_acc,
    gate_up_acc,
    resid,
    at,
    agr,
    gsend,
    grecv,
    ssend,
    srecv,
    fsend,
    frecv,
    osend,
    orecv,
    csem,
    wsem,
    upsend,
    uprecv,
    downsend,
    downrecv,
    lsem,
    credit,
):
    ways, unit = w_low_ref.shape[0], w_low_ref.shape[1] // 3
    part_units = ways * unit
    units = 2 * part_units
    rows, d = x_ref.shape
    quarter = d // ways
    half = rows // 2
    low, high = pl.ds(0, half), pl.ds(half, half)
    keep = out_ref.shape[0]
    kept, others_at = pl.ds(0, keep), pl.ds(keep, rows - keep)
    me, z = lax.axis_index("dp"), lax.axis_index("tensor")
    core, heads_of, group_of = head_share()
    sib, across, along = plane_peers()
    enter(column(ways) + [across, along])

    own_at = group_of == core
    half_wo = ways // 2
    step = min(256, rows)
    own = pltpu.make_async_copy(x_ref, xs.at[0], lsem.at[0])
    own.start()
    first_loads = [
        pltpu.make_async_copy(at_ref, at, lsem.at[1]),
        pltpu.make_async_copy(resid_ref, resid, lsem.at[2]),
    ]
    cots = [
        pltpu.make_async_copy(ref.at[i], cs.at[i, side], csem.at[i, k])
        for i in range(8)
        for k, (ref, side) in enumerate(((c_low_ref, low), (c_high_ref, high)))
    ]

    def weight_place(t, j, upper):
        first = part_units * (upper if j == 2 else 2 * upper + j) + t * unit
        ref = wd_ref if j == 2 else wgu_ref
        return ref.at[pl.ds(first if isinstance(first, int) else pl.multiple_of(first, 16), unit)]

    weights = [
        pltpu.make_async_copy(
            w_low_ref.at[t, pl.ds(j * unit, unit)], weight_place(t, j, 0), wsem.at[t, j]
        )
        for t in range(ways)
        for j in range(3)
    ]
    upper_own = [
        pltpu.make_async_copy(
            w_high_ref.at[pl.ds(j * unit, unit)], weight_place(z, j, 1), wsem.at[ways, j]
        )
        for j in range(3)
    ]
    above, below = {"tensor": lax.rem(z + 1, ways)}, {"tensor": lax.rem(z + ways - 1, ways)}

    def weight_up(t):
        return [
            pltpu.make_async_remote_copy(
                src_ref=weight_place(t, j, 1),
                dst_ref=weight_place(t, j, 1),
                send_sem=upsend.at[t, j],
                recv_sem=uprecv.at[t, j],
                device_id=above,
                device_id_type=MESH_ID,
            )
            for j in range(3)
        ]

    def weight_down(t):
        return [
            pltpu.make_async_remote_copy(
                src_ref=weight_place(t, j, 1),
                dst_ref=weight_place(t, j, 1),
                send_sem=downsend.at[t, j],
                recv_sem=downrecv.at[t, j],
                device_id=below,
                device_id_type=MESH_ID,
            )
            for j in range(3)
        ]

    def weight_round(r):
        t = z + 1 + r

        @pl.when(t < ways)
        def _():
            for copy in weight_down(t):
                copy.wait_recv()

            @pl.when(z > 0)
            def _():
                for copy in weight_down(t):
                    copy.start()

        u = z - 1 - r

        @pl.when(u >= 0)
        def _():
            for copy in weight_up(u):
                copy.wait_recv()

            @pl.when(z < ways - 1)
            def _():
                for copy in weight_up(u):
                    copy.start()

    own.wait()
    copies = gather_copies(lambda s, side: half_of(xs.at[s], side), gsend, grecv, False)
    gather_start(copies)
    for load in (*upper_own, *weights, *cots, *first_loads):
        load.start()
    for load in upper_own:
        load.wait()

    @pl.when(z < ways - 1)
    def _():
        for copy in weight_up(z):
            copy.start()

    @pl.when(z > 0)
    def _():
        for copy in weight_down(z):
            copy.start()

    down_acc[...] = jnp.zeros_like(down_acc)
    gate_up_acc[...] = jnp.zeros_like(gate_up_acc)
    for load in weights:
        load.wait()

    def plane_sums(send, recv, src, landing, size):
        first, second = pl.ds(0, size // 2), pl.ds(size // 2, size // 2)
        steps = [
            ("1", src(1), landing[0], sib),
            ("3", src(3), landing[1], sib),
            ("5", src(5), landing[2], sib),
            ("7", src(7), landing[3], sib),
            ("6l", src(6).at[first], from_far.at[first], across),
            ("6h", src(6).at[second], from_far.at[second], along),
            ("2l", src(2).at[first], from_x.at[first], across),
            ("2h", src(2).at[second], from_x.at[second], across),
            ("4l", src(4).at[first], from_y.at[first], along),
            ("4h", src(4).at[second], from_y.at[second], along),
        ]
        return {
            name: remote(ref, dst, send, recv, i, peer)
            for i, (name, ref, dst, peer) in enumerate(steps)
        }

    def add_to(ref, other):
        ref[...] = (ref[...].astype(F32) + other[...].astype(F32)).astype(BF16)

    def slot(i):
        return i // 2 if i % 2 == 0 else 4 + (i // 2) % 2

    landing = [from_sib.at[0], from_sib.at[0], from_sib.at[1], from_sib.at[2]]
    sums = plane_sums(ssend, srecv, lambda i: part.at[slot(i)], landing, rows)

    def forward(i, place, into):
        both = dot_nt(xs[i], wgu_ref[...])
        hidden_grad = dot_nt(cs[i], wd_ref[...])
        for upper in range(2):
            of_units = slice(upper * part_units, (upper + 1) * part_units)
            first = upper * units
            gate = both[:, first : first + part_units]
            up = both[:, first + part_units : first + units]
            grad = hidden_grad[:, of_units]
            sig = jax.nn.sigmoid(gate)
            silu = gate * sig
            hid[place, :, of_units] = (silu * up).astype(BF16)
            branch[place, :, first : first + part_units] = (
                grad * up * sig * (1.0 + gate * (1.0 - sig))
            ).astype(BF16)
            branch[place, :, first + part_units : first + units] = (grad * silu).astype(BF16)
        part[into] = dot_nn(branch[place], wgu_ref[...]).astype(BF16)

    def grads(i, place):
        down_acc[...] += dot_tn(hid[place], cs[i])
        gate_up_acc[...] += dot_tn(branch[place], xs[i])
        cs[i] = dot_nn(hid[place], wd_ref[...]).astype(BF16)

    def cot_wait(i, slots):
        for k in slots:

            @pl.when(i == k)
            def _(k=k):
                cots[2 * k].wait()
                cots[2 * k + 1].wait()

    weight_round(0)
    weight_round(1)
    gather_forward(copies)
    for r in range(2, ways - 1):
        weight_round(r)

    @pl.loop(2, 8)
    def _(i):
        @pl.when(i == 3)
        def _():
            copies["2-3"].wait_recv()

        @pl.when(i == 5)
        def _():
            copies["4-5"].wait_recv()
            sums["3"].wait_recv()
            add_to(part.at[1], from_sib.at[0])
            sums["2l"].start()

        @pl.when(i == 6)
        def _():
            copies["2-6"].wait_recv()
            copies["4-6"].wait_recv()
            copies["6-7"].start()

        @pl.when(i == 7)
        def _():
            copies["6-7"].wait_recv()
            sums["5"].wait_recv()
            add_to(part.at[2], from_sib.at[1])
            sums["4h"].start()
            sums["3"].wait_send()

        cot_wait(i, range(2, 8))
        even = lax.rem(i, 2) == 0
        forward(i, i - 2, jnp.where(even, i // 2, 4 + lax.rem(i // 2, 2)))
        for odd in (3, 5, 7):

            @pl.when(i == odd)
            def _(odd=odd):
                sums[str(odd)].start()

    @pl.loop(2, 8)
    def _(i):
        @pl.when(i == 3)
        def _():
            sums["7"].wait_recv()
            add_to(part.at[3], from_sib.at[2])
            sums["6l"].start()
            sums["6h"].start()

        grads(i, i - 2)

    def grant(k, peer):
        pl.semaphore_signal(credit.at[k], inc=1, device_id=peer, device_id_type=MESH_ID)

    grant(0, sib)
    outs = plane_sums(
        fsend,
        frecv,
        lambda i: cs.at[i],
        [from_sib.at[0], from_sib.at[1], branch.at[5], from_sib.at[2]],
        keep,
    )
    pl.semaphore_wait(credit.at[0], 1)
    for name in ("7", "3", "5"):
        outs[name].start()
    copies["0-1"].wait_recv()
    sums["5"].wait_send()

    @pl.loop(0, 2)
    def _(i):
        cot_wait(i, (0, 1))
        forward(i, i, 4 * i)

        @pl.when(i == 0)
        def _():
            sums["6l"].wait_recv()
            add_to(part.at[2, low], from_far.at[low])
            sums["4l"].start()
            sums["6h"].wait_recv()
            add_to(part.at[1, high], from_far.at[high])
            sums["2h"].start()
            grant(1, across)
            grant(2, along)

        @pl.when(i == 1)
        def _():
            sums["1"].start()

        grads(i, i)

    sums["1"].wait_recv()
    add_to(part.at[0], from_sib.at[0])
    grant(3, sib)
    for copy in copies.values():
        copy.wait_send()
    for t in range(ways):
        for j in range(3):
            for upper in range(2):
                row = 2 * (3 * t + j) * unit + upper * unit
                first = part_units * (upper if j == 2 else 2 * upper + j) + t * unit
                acc = down_acc if j == 2 else gate_up_acc
                branch[row // rows, row % rows : row % rows + unit] = acc[
                    first : first + unit
                ].astype(BF16)
    for load in first_loads:
        load.wait()
    grads_copy = pltpu.make_async_copy(branch.at[pl.ds(0, grads_ref.shape[0])], grads_ref, lsem.at[1])
    wo_loads = [
        pltpu.make_async_copy(wo_ref.at[pl.ds(0, rows)], branch.at[3], lsem.at[2]),
        pltpu.make_async_copy(wo_ref.at[pl.ds(rows, rows)], branch.at[4], lsem.at[3]),
        pltpu.make_async_copy(c_low_ref.at[0], xs.at[3, low], lsem.at[0]),
        pltpu.make_async_copy(c_high_ref.at[0], xs.at[3, high], lsem.at[4]),
    ]
    grads_copy.start()
    for load in wo_loads:
        load.start()

    outs["7"].wait_recv()
    add_to(cs.at[6], from_sib.at[2])
    outs["3"].wait_recv()
    add_to(cs.at[2], from_sib.at[1])
    outs["5"].wait_recv()
    add_to(cs.at[4], branch.at[5])
    pl.semaphore_wait(credit.at[3], 1)
    outs["1"].start()

    grad = gate_up_acc
    for name in ("2l", "2h", "4l", "4h"):
        sums[name].wait_recv()
    pl.semaphore_wait(credit.at[1], 1)
    pl.semaphore_wait(credit.at[2], 1)
    outs["6l"].start()
    outs["6h"].start()

    @pl.loop(0, rows // step)
    def _(k):
        rs = pl.ds(pl.multiple_of(k * step, step), step)
        grad[rs, :] = (
            part[0, rs, :].astype(F32) + from_x[rs, :].astype(F32) + from_y[rs, :].astype(F32)
        )

    grant(4, across)
    grant(5, along)

    for load in wo_loads:
        load.wait()
    ng_ref[...] = jnp.zeros_like(ng_ref)
    gain = gain_ref[...]
    small = min(128, rows)

    @pl.loop(0, rows // small)
    def _(k):
        rs = pl.ds(pl.multiple_of(k * small, small), small)
        values = resid[rs, :]
        centred = values - jnp.mean(values, axis=-1, keepdims=True)
        root = lax.rsqrt(jnp.mean(centred * centred, axis=-1, keepdims=True) + norm_eps)
        unit_rows = centred * root
        out_grad = grad[rs, :]
        ng_ref[2:3] += jnp.sum(out_grad * unit_rows, axis=0, keepdims=True)
        ng_ref[3:4] += jnp.sum(out_grad, axis=0, keepdims=True)
        scaled = out_grad * gain
        first_mean = jnp.mean(scaled, axis=-1, keepdims=True)
        second_mean = jnp.mean(scaled * unit_rows, axis=-1, keepdims=True)
        total = xs[3, rs, :].astype(F32) + root * (scaled - first_mean - unit_rows * second_mean)
        grad[rs, :] = total
        xs[1, rs, :] = total.astype(BF16)

    rg_copy = pltpu.make_async_copy(grad.at[pl.ds(0, rows)], rg_ref, lsem.at[0])
    rg_copy.start()

    def out_copy(s):
        to_core, to_z = head_source(s)
        return pltpu.make_async_remote_copy(
            src_ref=xs.at[2, :, pl.ds(s * quarter, quarter)],
            dst_ref=agr.at[z],
            send_sem=osend.at[s],
            recv_sem=orecv.at[z],
            device_id={"dp": me - core + to_core, "tensor": to_z},
            device_id_type=MESH_ID,
        )

    def out_wait(source):
        return pltpu.make_async_remote_copy(
            src_ref=xs.at[2, :, pl.ds(0, quarter)],
            dst_ref=agr.at[source],
            send_sem=osend.at[0],
            recv_sem=orecv.at[source],
            device_id={"dp": me, "tensor": z},
            device_id_type=MESH_ID,
        )

    for s in range(ways):
        place = 3 + s // half_wo
        first = (s % half_wo) * quarter
        xs[2, :, s * quarter : (s + 1) * quarter] = dot_nt(
            xs[1], branch[place, first : first + quarter, :]
        ).astype(BF16)
        to_core, to_z = head_source(s)
        to_self = (to_core == core) & (to_z == z)

        @pl.when(jnp.logical_not(to_self))
        def _():
            out_copy(s).start()

        @pl.when(to_self)
        def _():
            agr[z] = xs[2, :, s * quarter : (s + 1) * quarter]

    pl.semaphore_wait(credit.at[4], 1)
    pl.semaphore_wait(credit.at[5], 1)
    outs["2l"].start()
    outs["4h"].start()

    for s in range(ways):
        place = 6 + s // half_wo
        first = (s % half_wo) * quarter
        xs[place, first : first + quarter] = dot_tn(at[s], xs[1]).astype(BF16)
    og_copy = pltpu.make_async_copy(xs.at[pl.ds(6, 2)], og_ref, lsem.at[2])
    og_copy.start()

    outs["1"].wait_recv()
    add_to(cs.at[0], from_sib.at[0])
    high_copies = [
        pltpu.make_async_copy(cs.at[2 * k, others_at], high_ref.at[k], csem.at[k, 0])
        for k in range(4)
    ]
    for copy in high_copies:
        copy.start()
    first, second = pl.ds(0, keep // 2), pl.ds(keep // 2, keep // 2)
    outs["6l"].wait_recv()
    add_to(cs.at[4, first], from_far.at[first])
    outs["4l"].start()
    outs["6h"].wait_recv()
    add_to(cs.at[2, second], from_far.at[second])
    outs["2h"].start()

    for source in range(ways):

        @pl.when(jnp.logical_not(own_at & (z == source)))
        def _():
            out_wait(source).wait_recv()

    ag_copy = pltpu.make_async_copy(agr, ag_ref, lsem.at[3])
    ag_copy.start()
    for name in ("2l", "2h", "4l", "4h"):
        outs[name].wait_recv()
    total = resid[kept, :] + cs[0, kept, :].astype(F32)
    total += from_x[kept, :].astype(F32) + from_y[kept, :].astype(F32)
    xs[0, kept, :] = total.astype(BF16)
    grads_copy.wait()
    lo_copy = pltpu.make_async_copy(xs.at[0, kept], out_ref, lsem.at[1])
    lo_copy.start()
    for name in ("1", "7", "6l", "6h", "2l", "2h", "4l", "4h"):
        sums[name].wait_send()
    for copy in outs.values():
        copy.wait_send()
    for t in range(ways):

        @pl.when((t <= z) & (z < ways - 1))
        def _():
            for copy in weight_up(t):
                copy.wait_send()

        @pl.when((t >= z) & (z > 0))
        def _():
            for copy in weight_down(t):
                copy.wait_send()

    for s in range(ways):
        to_core, to_z = head_source(s)

        @pl.when(jnp.logical_not((to_core == core) & (to_z == z)))
        def _():
            out_copy(s).wait_send()

    for copy in (rg_copy, og_copy, ag_copy, lo_copy, *high_copies):
        copy.wait()


def middle(x, attended, resid, out_full, cot_low, cot_high, w_low, w_high, gain):
    rows, d = x.shape
    ways, unit = w_low.shape[0], w_low.shape[1] // 3
    units = 2 * ways * unit
    quarter = d // ways
    anywhere = pl.BlockSpec(memory_space=pl.ANY)
    inside = pl.BlockSpec(memory_space=pltpu.VMEM)
    sems = lambda n: [pltpu.SemaphoreType.DMA((n,))] * 2
    return pl.pallas_call(
        middle_kernel,
        in_specs=[anywhere] * 8 + [inside],
        out_specs=[anywhere] * 6 + [inside],
        out_shape=[
            jax.ShapeDtypeStruct((ways, rows, quarter), BF16),
            jax.ShapeDtypeStruct((rows, d), F32),
            jax.ShapeDtypeStruct((2, rows, d), BF16),
            jax.ShapeDtypeStruct((rows - rows // 4, d), BF16),
            jax.ShapeDtypeStruct((4, rows // 4, d), BF16),
            jax.ShapeDtypeStruct((3 * units // rows, rows, d), BF16),
            jax.ShapeDtypeStruct((8, d), F32),
        ],
        scratch_shapes=[
            pltpu.VMEM((2 * units, d), BF16),
            pltpu.VMEM((units, d), BF16),
            pltpu.VMEM((8, rows, d), BF16),
            pltpu.VMEM((8, rows, d), BF16),
            pltpu.VMEM((6, rows, units), BF16),
            pltpu.VMEM((6, rows, 2 * units), BF16),
            pltpu.VMEM((6, rows, d), BF16),
            pltpu.VMEM((3, rows, d), BF16),
            pltpu.VMEM((rows, d), BF16),
            pltpu.VMEM((rows, d), BF16),
            pltpu.VMEM((rows, d), BF16),
            pltpu.VMEM((units, d), F32),
            pltpu.VMEM((2 * units, d), F32),
            pltpu.VMEM((rows, d), F32),
            pltpu.VMEM((ways, rows, quarter), BF16),
            pltpu.VMEM((ways, rows, quarter), BF16),
        ]
        + sems(8)
        + sems(10)
        + sems(10)
        + sems(ways)
        + [
            pltpu.SemaphoreType.DMA((8, 2)),
            pltpu.SemaphoreType.DMA((ways + 1, 3)),
        ]
        + [pltpu.SemaphoreType.DMA((ways, 3))] * 4
        + [
            pltpu.SemaphoreType.DMA((5,)),
            pltpu.SemaphoreType.REGULAR((6,)),
        ],
        compiler_params=pltpu.CompilerParams(
            collective_id=1, has_side_effects=True, vmem_limit_bytes=VMEM_LIMIT
        ),
        cost_estimate=pl.CostEstimate(
            flops=130 * 10**9, bytes_accessed=40 * rows * d, transcendentals=0
        ),
        name="middle",
    )(x, attended, resid, out_full, cot_low, cot_high, w_low, w_high, gain[None])


def ffn_rest_kernel(parts_ref, out_ref, ffn, ffn_far, ffn_x, ffn_y, fsend, frecv, load_sem):
    _, across, along = plane_peers()
    load = pltpu.make_async_copy(parts_ref, ffn, load_sem)
    load.start()
    enter([across, along])

    def add_to(ref, other):
        ref[...] = (ref[...].astype(F32) + other[...].astype(F32)).astype(BF16)

    edge = ffn.shape[1] // 2
    first, second = pl.ds(0, edge), pl.ds(edge, edge)
    ffns = [
        ("3l", ffn.at[3, first], ffn_far.at[first], across),
        ("3h", ffn.at[3, second], ffn_far.at[second], along),
        ("1l", ffn.at[1, first], ffn_x.at[first], across),
        ("1h", ffn.at[1, second], ffn_x.at[second], across),
        ("2l", ffn.at[2, first], ffn_y.at[first], along),
        ("2h", ffn.at[2, second], ffn_y.at[second], along),
    ]
    ffns = {
        name: remote(src, dst, fsend, frecv, i, peer)
        for i, (name, src, dst, peer) in enumerate(ffns)
    }
    load.wait()
    for name in ("3l", "3h", "1l", "2h"):
        ffns[name].start()
    ffns["3l"].wait_recv()
    add_to(ffn.at[2, first], ffn_far.at[first])
    ffns["2l"].start()
    ffns["3h"].wait_recv()
    add_to(ffn.at[1, second], ffn_far.at[second])
    ffns["1h"].start()
    for name in ("1l", "1h", "2l", "2h"):
        ffns[name].wait_recv()
    out_ref[...] = ffn[0].astype(F32) + ffn_x[...].astype(F32) + ffn_y[...].astype(F32)
    for copy in ffns.values():
        copy.wait_send()


def ffn_rest(parts):
    _, rows, d = parts.shape
    return pl.pallas_call(
        ffn_rest_kernel,
        in_specs=[pl.BlockSpec(memory_space=pl.ANY)],
        out_specs=pl.BlockSpec(memory_space=pltpu.VMEM),
        out_shape=jax.ShapeDtypeStruct((rows, d), F32),
        scratch_shapes=[pltpu.VMEM(parts.shape, BF16)]
        + [pltpu.VMEM((rows, d), BF16)] * 3
        + [pltpu.SemaphoreType.DMA((6,))] * 2
        + [pltpu.SemaphoreType.DMA],
        compiler_params=pltpu.CompilerParams(
            collective_id=4, has_side_effects=True, vmem_limit_bytes=VMEM_LIMIT
        ),
        cost_estimate=pl.CostEstimate(
            flops=8 * 10**9, bytes_accessed=8 * rows * d, transcendentals=0
        ),
        name="ffn_rest",
    )(parts)


def tail_kernel(
    mixed_ref,
    w_ref,
    out_parts_ref,
    rows_ref,
    tok_ref,
    norm_ref,
    n_ref,
    og_ref,
    qkv_ref,
    ng_ref,
    lines,
    line_sib,
    line_z,
    line_end,
    part,
    from_sib,
    from_far,
    from_x,
    from_y,
    mine,
    slices,
    ogs,
    qkv,
    qkv_far,
    qkv_x,
    qkv_y,
    qkv_sum,
    qkv_z,
    qkvs,
    norms,
    norm_sum,
    norms_z,
    lsend,
    lrecv,
    hsend,
    hrecv,
    ssend,
    srecv,
    gsend,
    grecv,
    osend,
    orecv,
    ksend,
    krecv,
    kzsend,
    kzrecv,
    kgsend,
    kgrecv,
    nsend,
    nrecv,
    zsend,
    zrecv,
    load_sem,
):
    me, z = lax.axis_index("dp"), lax.axis_index("tensor")
    ways, rows = lines.shape[0], lines.shape[1]
    out_rows = slices.shape[1]
    width = w_ref.shape[2]
    total = part.shape[1]
    half = total // 2
    low, high = pl.ds(0, half), pl.ds(half, half)
    core, heads_of, group_of = head_share()
    home = group_of == core
    chip = me // 2
    sib, across, along = plane_peers()
    others = [{"tensor": lax.rem(z + k, ways)} for k in range(1, ways)]
    z1, z2, z3 = (lax.bitwise_xor(z, k) for k in (1, 2, 3))
    near, far = {"tensor": z1}, {"tensor": z2}
    plane = [{"dp": lax.bitwise_xor(me, k)} for k in range(1, 8)]
    enter(plane + others)

    loads = []
    for i in range(8):
        src = pl.multiple_of(lax.bitwise_xor(me, i) * out_rows, 16)
        loads.append(
            [
                pltpu.make_async_copy(
                    out_parts_ref.at[t, pl.ds(src, out_rows)],
                    part.at[i, pl.ds(t * out_rows, out_rows)],
                    load_sem.at[t, i],
                )
                for t in range(ways)
            ]
        )
        for load in loads[-1]:
            load.start()

    def add_to(ref, other):
        ref[...] = (ref[...].astype(F32) + other[...].astype(F32)).astype(BF16)

    size = rows // 2

    def part_of(which):
        return pl.ds(pl.multiple_of(which * size, size), size)

    def line(i):
        b = lax.bitwise_xor(z, i)
        step = min(256, rows)

        @pl.loop(0, rows // step)
        def _(k):
            at = pl.ds(pl.multiple_of(b * rows + k * step, step), step)
            lines[b, pl.ds(pl.multiple_of(k * step, step), step)] = sum(
                dot_nt(mixed_ref[at, j * width : (j + 1) * width], w_ref[j]) for j in range(3)
            ).astype(BF16)

    def share(i):
        b = lax.bitwise_xor(z, i)
        return remote(lines.at[b, part_of(1 - core)], line_sib.at[b], hsend, hrecv, i, sib)

    def share_join(i):
        b = lax.bitwise_xor(z, i)
        share(i).wait_recv()
        add_to(lines.at[b, part_of(core)], line_sib.at[b])

    to_near = [
        remote(lines.at[z3, part_of(core)], line_z.at[0], lsend, lrecv, 0, near),
        remote(lines.at[z1, part_of(core)], line_z.at[1], lsend, lrecv, 1, near),
    ]
    to_far = remote(lines.at[z2, part_of(core)], line_z.at[2], lsend, lrecv, 2, far)
    last_away = remote(line_z.at[2], line_end, lsend, lrecv, 3, sib)
    last_home = remote(lines.at[z, part_of(core)], line_end, lsend, lrecv, 3, sib)

    sums = [
        ("1", part.at[1], from_sib.at[0], sib),
        ("3", part.at[3], from_sib.at[1], sib),
        ("5", part.at[5], from_sib.at[2], sib),
        ("7", part.at[7], from_sib.at[3], sib),
        ("6l", part.at[6, low], from_far.at[low], across),
        ("6h", part.at[6, high], from_far.at[high], along),
        ("2l", part.at[2, low], from_x.at[low], across),
        ("2h", part.at[2, high], from_x.at[high], across),
        ("4l", part.at[4, low], from_y.at[low], along),
        ("4h", part.at[4, high], from_y.at[high], along),
    ]
    sums = {
        name: remote(src, dst, ssend, srecv, i, peer)
        for i, (name, src, dst, peer) in enumerate(sums)
    }

    def qkv_rows(j):
        at = pl.ds(pl.multiple_of(j * width, width), width)
        qkv[at, :] = dot_tn(mixed_ref[:, at], rows_ref[...]).astype(BF16)

    line(3)
    share(3).start()

    @pl.loop(0, 3)
    def _(j):
        qkv_rows(j)

        @pl.when(j == 0)
        def _():
            share_join(3)
            to_near[0].start()

    piece = qkv_sum.shape[0]
    small = piece // 2

    def qkv_at(s, side=None):
        first = lax.bitwise_xor(chip, s) * piece + (0 if side is None else side * small)
        return qkv.at[pl.ds(pl.multiple_of(first, 16), piece if side is None else small)]

    def side_of(ref, side):
        return ref.at[pl.ds(side * small, small)]

    pieces = [
        ("3l", qkv_at(3, 0), side_of(qkv_far, 0), across),
        ("3h", qkv_at(3, 1), side_of(qkv_far, 1), along),
        ("1l", qkv_at(1, 0), side_of(qkv_x, 0), across),
        ("1h", qkv_at(1, 1), side_of(qkv_x, 1), across),
        ("2l", qkv_at(2, 0), side_of(qkv_y, 0), along),
        ("2h", qkv_at(2, 1), side_of(qkv_y, 1), along),
    ]
    pieces = {
        name: remote(src, dst, ksend, krecv, i, peer)
        for i, (name, src, dst, peer) in enumerate(pieces)
    }
    for name in ("3l", "3h", "1l", "2h"):
        pieces[name].start()

    @pl.loop(0, ways - 1)
    def _(k):
        i = lax.rem(k + 1, ways - 1)
        line(i)
        for fixed in range(ways - 1):

            @pl.when(i == fixed)
            def _(fixed=fixed):
                share(fixed).start()

    for i in (7, 3, 5, 1):
        for load in loads[i]:
            load.wait()
        sums[str(i)].start()

    pieces["3l"].wait_recv()
    add_to(qkv_at(2, 0), side_of(qkv_far, 0))
    pieces["2l"].start()
    pieces["3h"].wait_recv()
    add_to(qkv_at(1, 1), side_of(qkv_far, 1))
    pieces["1h"].start()
    share_join(1)
    share_join(2)
    to_near[0].wait_recv()
    to_near[1].start()
    add_to(lines.at[z2, part_of(core)], line_z.at[0])
    to_far.start()
    for i, j, names in ((6, 3, ("6l", "6h")), (2, 1, ("2l",)), (4, 2, ("4h",))):
        for load in loads[i]:
            load.wait()
        sums[str(i + 1)].wait_recv()
        add_to(part.at[i], from_sib.at[j])
        for name in names:
            sums[name].start()
    share_join(0)

    for name in ("1l", "1h", "2l", "2h"):
        pieces[name].wait_recv()
    qkv_sum[...] = (
        qkv_at(0)[...].astype(F32) + qkv_x[...].astype(F32) + qkv_y[...].astype(F32)
    ).astype(BF16)
    takes = core == lax.rem(z, 2)

    def owner_copy(slot):
        return pltpu.make_async_remote_copy(
            src_ref=qkv_sum,
            dst_ref=qkv_z.at[slot],
            send_sem=kzsend.at[0],
            recv_sem=kzrecv.at[slot],
            device_id={"tensor": heads_of},
            device_id_type=MESH_ID,
        )

    @pl.when(heads_of != z)
    def _():
        owner_copy(group_of).start()

    @pl.when(heads_of == z)
    def _():
        qkv_z[group_of] = qkv_sum[...]

    sums["6l"].wait_recv()
    add_to(part.at[4, low], from_far.at[low])
    sums["4l"].start()
    sums["6h"].wait_recv()
    add_to(part.at[2, high], from_far.at[high])
    sums["2h"].start()

    for load in loads[0]:
        load.wait()
    sums["1"].wait_recv()
    for name in ("2l", "2h", "4l", "4h"):
        sums[name].wait_recv()
    mine[...] = part[0].astype(F32) + from_sib[0].astype(F32)
    mine[...] += from_x[...].astype(F32) + from_y[...].astype(F32)

    for t in range(ways):
        at = slice(t * out_rows, (t + 1) * out_rows)
        part[0, at] = mine[at].astype(BF16)

    def slice_copy(k, to, source):
        return pltpu.make_async_remote_copy(
            src_ref=part.at[0, pl.ds(pl.multiple_of(to * out_rows, 16), out_rows)],
            dst_ref=slices.at[source],
            send_sem=osend.at[k],
            recv_sem=orecv.at[source],
            device_id={"tensor": to},
            device_id_type=MESH_ID,
        )

    for k in range(1, ways):
        slice_copy(k, lax.rem(z + k, ways), z).start()

    def chip_copy(s, side, peer, sem):
        at = qkvs.at[lax.bitwise_xor(chip, s)]
        ref = at if side is None else side_of(at, side)
        return remote(ref, ref, kgsend, kgrecv, sem, peer)

    to_x, to_y = chip_copy(0, None, across, 0), chip_copy(0, None, along, 1)
    x_on, y_on = chip_copy(1, 1, along, 2), chip_copy(2, 0, across, 3)
    to_sib = [chip_copy(s, None, sib, 4 + s) for s in range(4)]

    @pl.when(takes)
    def _():
        for slot in range(2):

            @pl.when(z // 2 + 2 * slot != z)
            def _():
                owner_copy(slot).wait_recv()

        qkvs[chip] = (qkv_z[0].astype(F32) + qkv_z[1].astype(F32)).astype(BF16)
        to_x.start()
        to_y.start()
        to_sib[0].start()

    own_slice = part[0, pl.ds(pl.multiple_of(z * out_rows, 16), out_rows)].astype(F32)
    for k in range(1, ways):
        source = lax.rem(z + k, ways)
        slice_copy(k, source, source).wait_recv()
        own_slice += slices[source].astype(F32)
    ogs[me] = own_slice.astype(BF16)
    view = lambda s, side: half_of(ogs.at[lax.bitwise_xor(me, s)], side)
    gathers = gather_copies(view, gsend, grecv, True)
    gather_start(gathers)

    to_near[1].wait_recv()
    add_to(lines.at[z, part_of(core)], line_z.at[1])

    @pl.when(jnp.logical_not(home))
    def _():
        last_home.start()

    to_far.wait_recv()

    @pl.when(home)
    def _():
        last_away.start()
        n_ref[part_of(core), :] = lines[z, part_of(core), :].astype(F32)

    @pl.when(jnp.logical_not(home))
    def _():
        n_ref[part_of(core), :] = line_z[2].astype(F32)

    last_away.wait_recv()
    n_ref[part_of(1 - core), :] = line_end[...].astype(F32)

    norms[me] = norm_ref[...]
    step = min(128, rows)

    @pl.loop(0, rows // step)
    def _(i):
        at = pl.ds(pl.multiple_of(i * step, step), step)
        values = tok_ref[at, :].astype(F32)
        centred = values - jnp.mean(values, axis=-1, keepdims=True)
        root = lax.rsqrt(jnp.mean(centred * centred, axis=-1, keepdims=True) + norm_eps)
        grad = n_ref[at, :]
        norms[me, 0:1] += jnp.sum(grad * (centred * root), axis=0, keepdims=True)
        norms[me, 1:2] += jnp.sum(grad, axis=0, keepdims=True)

    def swap(k, source):
        return remote(norms.at[source], norms.at[source], nsend, nrecv, k, plane[k])

    for k in range(7):
        swap(k, me).start()

    gather_forward(gathers)

    @pl.when(takes)
    def _():
        to_x.wait_recv()
        x_on.start()
        to_sib[1].start()
        to_y.wait_recv()
        y_on.start()
        to_sib[2].start()

    for k in range(7):
        swap(k, lax.bitwise_xor(me, k + 1)).wait_recv()
    norm_sum[...] = sum(norms[k] for k in range(8))

    def norm_copy(k, to, source):
        return pltpu.make_async_remote_copy(
            src_ref=norm_sum,
            dst_ref=norms_z.at[source],
            send_sem=zsend.at[k],
            recv_sem=zrecv.at[source],
            device_id={"tensor": to},
            device_id_type=MESH_ID,
        )

    for k in range(1, ways):
        norm_copy(k, lax.rem(z + k, ways), z).start()
    norms_z[z] = norm_sum[...]
    gather_finish(gathers)
    og_ref[...] = ogs[...]

    @pl.when(takes)
    def _():
        x_on.wait_recv()
        y_on.wait_recv()
        to_sib[3].start()

    @pl.when(jnp.logical_not(takes))
    def _():
        for copy in to_sib:
            copy.wait_recv()

    qkv_ref[...] = qkvs[...]
    for k in range(1, ways):
        source = lax.rem(z + k, ways)
        norm_copy(k, source, source).wait_recv()
    ng_ref[...] = sum(norms_z[t] for t in range(ways))

    @pl.when(takes)
    def _():
        for copy in (to_x, to_y, x_on, y_on, *to_sib):
            copy.wait_send()

    @pl.when(heads_of != z)
    def _():
        owner_copy(group_of).wait_send()

    @pl.when(home)
    def _():
        last_away.wait_send()

    @pl.when(jnp.logical_not(home))
    def _():
        last_home.wait_send()

    for copy in (*sums.values(), *gathers.values(), *pieces.values(), *to_near, to_far):
        copy.wait_send()
    for k in range(7):
        swap(k, me).wait_send()
    for i in range(ways):
        share(i).wait_send()
    for k in range(1, ways):
        to = lax.rem(z + k, ways)
        slice_copy(k, to, z).wait_send()
        norm_copy(k, to, z).wait_send()


def tail(mixed, w, out_parts, rows_one, tokens, norm_grads, ways):
    rows, d = tokens.shape
    out_rows = out_parts.shape[1] // 8
    qkv_rows = mixed.shape[1] // 4
    total = ways * out_rows
    anywhere = pl.BlockSpec(memory_space=pl.ANY)
    inside = pl.BlockSpec(memory_space=pltpu.VMEM)
    sems = lambda n: [pltpu.SemaphoreType.DMA((n,))] * 2
    return pl.pallas_call(
        tail_kernel,
        in_specs=[inside] * 2 + [anywhere] + [inside] * 3,
        out_specs=[inside] * 4,
        out_shape=[
            jax.ShapeDtypeStruct((rows, d), F32),
            jax.ShapeDtypeStruct((8, out_rows, d), BF16),
            jax.ShapeDtypeStruct((4, qkv_rows, d), BF16),
            jax.ShapeDtypeStruct((8, d), F32),
        ],
        scratch_shapes=[
            pltpu.VMEM((ways, rows, d), BF16),
            pltpu.VMEM((ways, rows // 2, d), BF16),
            pltpu.VMEM((3, rows // 2, d), BF16),
            pltpu.VMEM((rows // 2, d), BF16),
            pltpu.VMEM((8, total, d), BF16),
            pltpu.VMEM((4, total, d), BF16),
            pltpu.VMEM((total, d), BF16),
            pltpu.VMEM((total, d), BF16),
            pltpu.VMEM((total, d), BF16),
            pltpu.VMEM((total, d), F32),
            pltpu.VMEM((ways, out_rows, d), BF16),
            pltpu.VMEM((8, out_rows, d), BF16),
            pltpu.VMEM((4 * qkv_rows, d), BF16),
            pltpu.VMEM((qkv_rows, d), BF16),
            pltpu.VMEM((qkv_rows, d), BF16),
            pltpu.VMEM((qkv_rows, d), BF16),
            pltpu.VMEM((qkv_rows, d), BF16),
            pltpu.VMEM((2, qkv_rows, d), BF16),
            pltpu.VMEM((4, qkv_rows, d), BF16),
            pltpu.VMEM((8, 8, d), F32),
            pltpu.VMEM((8, d), F32),
            pltpu.VMEM((ways, 8, d), F32),
        ]
        + sems(4)
        + sems(ways)
        + sems(10)
        + sems(8)
        + sems(ways)
        + sems(6)
        + sems(2)
        + sems(8)
        + sems(7)
        + sems(ways)
        + [pltpu.SemaphoreType.DMA((ways, 8))],
        compiler_params=pltpu.CompilerParams(
            collective_id=2, has_side_effects=True, vmem_limit_bytes=VMEM_LIMIT
        ),
        cost_estimate=pl.CostEstimate(
            flops=75 * 10**9, bytes_accessed=40 * rows * d, transcendentals=0
        ),
        name="tail",
    )(mixed, w, out_parts, rows_one, tokens, norm_grads)


def finish_kernel(
    kept,
    both_ref,
    down_ref,
    features_ref,
    og_ref,
    grad_ref,
    resid_ref,
    tok_ref,
    gain_ref,
    low_ref,
    high_ref,
    before_ref,
    norms_ref,
    gate_up_ref,
    down_out_ref,
    qkv_ref,
    og_out_ref,
    token_ref,
    layer_ref,
    *norm_refs,
):
    units = both_ref.shape[1] // 2
    for p in range(8):
        turned = both_ref[p].astype(F32).T
        for g in range(2):
            at = pl.ds(2 * p + g, turned.shape[0], stride=16)
            gate_up_ref[at, :] = turned[:, g * units : (g + 1) * units]
    for p in range(down_ref.shape[0]):
        down_out_ref[p * units : (p + 1) * units] = down_ref[p].astype(F32)
    width = qkv_ref.shape[2]
    for j in range(3):
        qkv_ref[j] = features_ref[j * width : (j + 1) * width].astype(F32).T
    out_rows = og_ref.shape[1]
    for p in range(og_ref.shape[0]):
        og_out_ref[p * out_rows : (p + 1) * out_rows] = og_ref[p].astype(F32)
    values = tok_ref[...].astype(F32)
    centred = values - jnp.mean(values, axis=-1, keepdims=True)
    root = lax.rsqrt(jnp.mean(centred * centred, axis=-1, keepdims=True) + norm_eps)
    unit_rows = centred * root
    scaled = grad_ref[...] * gain_ref[...]
    first_mean = jnp.mean(scaled, axis=-1, keepdims=True)
    second_mean = jnp.mean(scaled * unit_rows, axis=-1, keepdims=True)
    token_ref[...] = resid_ref[...] + root * (scaled - first_mean - unit_rows * second_mean)
    for k, ref in enumerate(norm_refs):
        ref[...] = norms_ref[k : k + 1]
    step = pl.program_id(0)

    @pl.when(step < kept)
    def _():
        layer_ref[...] = low_ref[...]

    @pl.when(step >= kept)
    def _():
        layer_ref[...] = (before_ref[...] + high_ref[...]).astype(BF16)


def finish(grads, features, out_grad, norm_grad, resid_grad, tokens, gain, low, high, resid, norms):
    rows, d = tokens.shape
    units = grads.shape[1] // 3
    width = features.shape[0] // 3
    out_rows = out_grad.shape[1]
    steps = 4
    each = 8 // steps
    block = d // steps
    own = pl.BlockSpec((rows // steps, d), lambda i: (i, 0))
    kept = steps * low.shape[0] // rows
    return pl.pallas_call(
        functools.partial(finish_kernel, kept),
        grid=(steps,),
        in_specs=[
            pl.BlockSpec((8, 2 * units, block), lambda i: (0, 0, i)),
            pl.BlockSpec((each, units, d), lambda i: (i, 2, 0)),
            pl.BlockSpec((3 * width, block), lambda i: (0, i)),
            pl.BlockSpec((each, out_rows, d), lambda i: (i, 0, 0)),
            own,
            own,
            own,
            pl.BlockSpec((1, d), lambda i: (0, 0)),
            pl.BlockSpec((rows // steps, d), lambda i: (jnp.minimum(i, kept - 1), 0)),
            pl.BlockSpec((rows // steps, d), lambda i: (jnp.maximum(i - kept, 0), 0)),
            pl.BlockSpec((rows // steps, d), lambda i: (jnp.maximum(i, kept), 0)),
            pl.BlockSpec(norms.shape, lambda i: (0, 0)),
        ],
        out_specs=[
            pl.BlockSpec((16 * block, units), lambda i: (i, 0)),
            pl.BlockSpec((each * units, d), lambda i: (i, 0)),
            pl.BlockSpec((3, block, width), lambda i: (0, i, 0)),
            pl.BlockSpec((each * out_rows, d), lambda i: (i, 0)),
            own,
            own,
        ]
        + [pl.BlockSpec((1, d), lambda i: (0, 0))] * 4,
        out_shape=[
            jax.ShapeDtypeStruct((16 * d, units), F32),
            jax.ShapeDtypeStruct((8 * units, d), F32),
            jax.ShapeDtypeStruct((3, d, width), F32),
            jax.ShapeDtypeStruct((8 * out_rows, d), F32),
            jax.ShapeDtypeStruct((rows, d), F32),
            jax.ShapeDtypeStruct((rows, d), BF16),
        ]
        + [jax.ShapeDtypeStruct((1, d), F32)] * 4,
        compiler_params=pltpu.CompilerParams(vmem_limit_bytes=VMEM_LIMIT),
        name="finish",
    )(
        grads,
        grads,
        features,
        out_grad,
        norm_grad,
        resid_grad,
        tokens,
        gain[None],
        low,
        high,
        resid,
        norms,
    )


def shards(
    tokens,
    group_bucket,
    gain_one,
    shift_one,
    w_qkv,
    w_out,
    gain_two,
    shift_two,
    w_gate_up,
    w_down,
    cotangent,
):
    ways = lax.axis_size("tensor")
    replicas = lax.axis_size("dp")
    replica = lax.axis_index("dp")
    own_rows, d = tokens.shape
    group_rows = own_rows * ways
    local_width = w_out.shape[0]
    head_dim = d // HEADS
    hidden_width = w_down.shape[0]
    units = hidden_width // replicas
    out_rows = local_width // replicas
    pair_width = min(128, local_width)

    rows_in = tokens.astype(F32)
    normed_one, unit_one, root_one = norm_forward(rows_in, gain_one, shift_one)
    normed_one_low = normed_one.astype(BF16)
    rows_one = lax.all_gather(normed_one_low, "tensor", axis=0, tiled=True)

    gate_up_slice = lax.dynamic_slice_in_dim(w_gate_up, replica * units, units, axis=2)
    down_slice = lax.dynamic_slice_in_dim(w_down, replica * units, units, axis=0)
    weight_slice = jnp.concatenate(
        [gate_up_slice.transpose(1, 2, 0).reshape(2 * units, d), down_slice]
    )
    weights = lax.all_gather(weight_slice, "tensor", axis=0)
    cot_all = lax.all_gather(cotangent, "dp", axis=0, tiled=True)
    out_full = lax.all_gather(w_out, "tensor", axis=0, tiled=True)

    cos_wide, sine_wide = rotary_wide(group_bucket[0], group_rows, head_dim, pair_width)
    qkv_weights = w_qkv.transpose(1, 0, 2)
    q, k, v, kt, vt = project(rows_one, qkv_weights, cos_wide, sine_wide, head_dim)
    attended, *kept = attend(group_bucket[None], q, k, vt, head_dim)
    attended_own = lax.all_to_all(attended, "tensor", 0, 1, tiled=True)
    resid = rows_in + dot_nn(attended_own, out_full)
    normed_two, unit_two, root_two = norm_forward(resid, gain_two, shift_two)
    normed_two_low = normed_two.astype(BF16)
    parts = weights.reshape(ways, 3, units, d)
    wgu = parts[:, :2].transpose(3, 1, 0, 2).reshape(d, 2 * ways * units)
    wd = parts[:, 2].reshape(ways * units, d)
    rows_two = lax.all_gather(normed_two_low, "dp", axis=0, tiled=True)
    hidden, branch, back = feed(rows_two, cot_all, wgu, wd)
    normed_two_grad = lax.psum_scatter(back, "dp", scatter_dimension=0, tiled=True).astype(F32)
    ffn_parts = dot_nn(hidden, wd).astype(BF16)
    ffn_out = lax.psum_scatter(ffn_parts, "dp", scatter_dimension=0, tiled=True).astype(F32)
    layer_out = (resid + ffn_out).astype(BF16)
    grads = jnp.concatenate(
        [
            dot_tn(branch, rows_two).reshape(2, ways, units, d),
            dot_tn(hidden, cot_all).reshape(1, ways, units, d),
        ]
    )
    grads = grads.astype(BF16).transpose(1, 0, 2, 3).reshape(ways, 3 * units, d)
    resid_part, gain_two_grad, shift_two_grad = norm_backward(
        normed_two_grad, unit_two, root_two, gain_two
    )
    norm_grads = jnp.zeros((8, d), F32).at[2].set(gain_two_grad).at[3].set(shift_two_grad)
    resid_grad = cotangent.astype(F32) + resid_part
    attn_grad = resid_grad.astype(BF16)
    attended_grad = lax.all_to_all(
        dot_nt(attn_grad, out_full).astype(BF16), "tensor", 1, 0, tiled=True
    )
    out_grad = dot_tn(attended_own, attn_grad).astype(BF16)
    out_grad = out_grad.reshape(ways, replicas, out_rows, d).transpose(1, 0, 2, 3)
    out_grad = out_grad.reshape(replicas, ways * out_rows, d)
    grads = lax.psum_scatter(grads, "tensor", scatter_dimension=0)

    mixed_grad = attend_back(
        group_bucket[None], q, k, kt, v, attended_grad, *kept, cos_wide, sine_wide, head_dim
    )
    grads, mixed_grad = lax.optimization_barrier((grads, mixed_grad))
    grads = lax.all_gather(grads, "dp", axis=0)
    grads = grads.reshape(replicas, 3, units, d)
    down_grad = grads[:, 2].reshape(hidden_width, d).astype(F32)
    gate_up_grad = grads[:, :2].transpose(3, 1, 0, 2).reshape(d, 2, hidden_width).astype(F32)
    qkv_grad = lax.psum(dot_tn(rows_one, mixed_grad).astype(BF16), "dp").astype(F32)
    qkv_grad = qkv_grad.reshape(d, 3, local_width)
    flat = qkv_weights.transpose(1, 0, 2).reshape(d, 3 * local_width)
    normed_one_grad = lax.psum_scatter(
        dot_nt(mixed_grad, flat).astype(BF16), "tensor", scatter_dimension=0, tiled=True
    ).astype(F32)
    out_grad = lax.psum_scatter(out_grad, "dp", scatter_dimension=0)
    out_grad = lax.psum_scatter(out_grad, "tensor", scatter_dimension=0, tiled=True)
    out_grad = lax.all_gather(out_grad, "dp", axis=0, tiled=True).astype(F32)
    one = norm_backward(normed_one_grad, unit_one, root_one, gain_one)
    norm_grads = norm_grads.at[0].set(one[1]).at[1].set(one[2])
    norm_grads = lax.psum(norm_grads, ("dp", "tensor"))
    token_grad = resid_grad + norm_backward(normed_one_grad, unit_one, root_one, gain_one)[0]
    gain_one_grad, shift_one_grad, gain_two_grad, shift_two_grad = (norm_grads[i] for i in range(4))
    return (
        layer_out,
        token_grad,
        gain_one_grad,
        shift_one_grad,
        qkv_grad,
        out_grad,
        gain_two_grad,
        shift_two_grad,
        gate_up_grad,
        down_grad,
    )


def shards_columns(
    tokens,
    group_bucket,
    gain_one,
    shift_one,
    w_qkv,
    w_out,
    gain_two,
    shift_two,
    w_gate_up,
    w_down,
    cotangent,
):
    ways = lax.axis_size("tensor")
    replica = lax.axis_index("dp")
    own_rows, d = tokens.shape
    group_rows = own_rows * ways
    local_width = w_out.shape[0]
    head_dim = d // HEADS
    hidden_width = w_down.shape[0]
    units = hidden_width // 8

    gate_up_slice = lax.dynamic_slice_in_dim(w_gate_up, replica * units, units, axis=2)
    down_slice = lax.dynamic_slice_in_dim(w_down, replica * units, units, axis=0)
    gate_up_slice = gate_up_slice.transpose(1, 2, 0)
    half = units // 2
    slice_low, slice_high = (
        jnp.concatenate([gate_up_slice[:, at].reshape(units, d), down_slice[at]])
        for at in (slice(0, half), slice(half, units))
    )
    q, k, v, kt, vt, cos_wide, sine_wide, bucket, rows_one, cot_low, out_full, qkv_weights = front(
        group_bucket,
        tokens,
        gain_one,
        shift_one,
        cotangent,
        w_out,
        w_qkv.transpose(1, 0, 2),
        head_dim,
        ways,
    )
    bucket, slice_low = lax.optimization_barrier((bucket, slice_low))
    weights_low = lax.all_gather(slice_low, "tensor", axis=0)
    out_full = out_full.reshape(d, d)
    attended, *kept = attend(bucket, q, k, vt, head_dim)
    attended_own, resid, normed_two, cot_high = collect(
        attended, tokens, out_full, gain_two, shift_two, cotangent, ways
    )
    attended_grad, resid_grad, out_grad, layer_low, ffn_parts, grads, norm_grads = middle(
        normed_two,
        attended_own,
        resid,
        out_full,
        cot_low,
        cot_high,
        weights_low,
        slice_high,
        gain_two,
    )
    grads = grads.reshape(ways, 3 * units, d)
    grads = lax.psum_scatter(grads, "tensor", scatter_dimension=0)
    attended_grad = attended_grad.reshape(group_rows, local_width)
    mixed_grad = attend_back(
        bucket, q, k, kt, v, attended_grad, *kept, cos_wide, sine_wide, head_dim
    )
    ffn_parts, mixed_grad = lax.optimization_barrier((ffn_parts, mixed_grad))
    layer_high = ffn_rest(ffn_parts)
    grads, mixed_grad, layer_high = lax.optimization_barrier((grads, mixed_grad, layer_high))
    grads = lax.all_gather(grads, "dp", axis=0)
    normed_one_grad, out_grad, qkv_grad, norm_grads = tail(
        mixed_grad,
        qkv_weights,
        out_grad.reshape(ways, local_width, d),
        rows_one.reshape(group_rows, d),
        tokens,
        norm_grads,
        ways,
    )
    gate_up_grad, down_grad, qkv_grad, out_grad, token_grad, layer_out, *norm_grads = finish(
        grads,
        qkv_grad.reshape(3 * local_width, d),
        out_grad,
        normed_one_grad,
        resid_grad,
        tokens,
        gain_one,
        layer_low,
        layer_high,
        resid,
        norm_grads,
    )
    gate_up_grad = gate_up_grad.reshape(d, 8, 2, units).transpose(0, 2, 1, 3)
    gate_up_grad = gate_up_grad.reshape(d, 2, hidden_width)
    qkv_grad = qkv_grad.transpose(1, 0, 2)
    gain_one_grad, shift_one_grad, gain_two_grad, shift_two_grad = (g[0] for g in norm_grads)
    return (
        layer_out,
        token_grad,
        gain_one_grad,
        shift_one_grad,
        qkv_grad,
        out_grad,
        gain_two_grad,
        shift_two_grad,
        gate_up_grad,
        down_grad,
    )


def solution(mesh):
    in_specs = (
        P(("dp", "tensor"), None),
        P("dp"),
        P(),
        P(),
        P(None, None, "tensor"),
        P("tensor", None),
        P(),
        P(),
        P(None, None, "tensor"),
        P("tensor", None),
        P(("dp", "tensor"), None),
    )
    out_specs = (
        P(("dp", "tensor"), None),
        P(("dp", "tensor"), None),
        P(),
        P(),
        P(None, None, "tensor"),
        P("tensor", None),
        P(),
        P(),
        P(None, None, "tensor"),
        P("tensor", None),
    )
    columns = mesh.shape["dp"] == 8 and mesh.shape["tensor"] == 4
    body = shards_columns if columns else shards
    return jax.shard_map(body, mesh=mesh, in_specs=in_specs, out_specs=out_specs, check_vma=False)
```
